32 devices in a mesh: dp: 4 (over y, x), ctx: 8 (over z, core).
Axes of the slice: x: 2, y: 2, z: 4, core: 2. Of those that a mesh axis runs over, the one named last changes fastest.
Arguments:
- projected: bfloat16 [4, 1024, 3, 8192], P('dp', 'ctx'), may hold values from -6 to 6
- short_filter: float32 [3, 7, 8192], replicated, may hold values from -2.4 to 2.4
- residues: float32 [512, 16], replicated, may hold values from -0.06 to 0.06
- decay_rates: float32 [512, 16], replicated, may hold values from 9.765625e-05 to 0.03125
- skip_gain: float32 [8192], replicated, may hold values from 0.5 to 1.5
- cotangent: bfloat16 [4, 1024, 8192], P('dp', 'ctx'), may hold values from -6 to 6
Outputs:
- output: bfloat16 [4, 1024, 8192], P('dp', 'ctx')
- grad_projected: bfloat16 [4, 1024, 3, 8192], P('dp', 'ctx')
- grad_short: float32 [3, 7, 8192], replicated
- grad_skip: float32 [8192], replicated
The draws below stay inside these ranges and needn't reach their ends.
All inputs are finite; a program needn't handle non-finite values.
Results may differ from the reference program's by a relative error of at most 0.001.
Values may be sent and summed in bfloat16 or wider, within the bound.
No kernel may reach another device: no remote copies, remote signals or barrier semaphores. Data moves between devices by JAX's collectives and lax.ppermute only.
A program may use at most 320 MiB of HBM per device.

```python
import math
import jax
import jax.numpy as jnp
from jax import lax

D = 8192
POLES = 16
GROUPS = 512
SHORT = 7
BLK = 64
SEQ = 1024
SEQS = 4


def block_levels(key, shape, shards, smallest, top_value):
    loudness, own = 1.0, jax.random.fold_in(key, 6)
    for dim, parts in shards:
        draws = jnp.exp(jax.random.uniform(jax.random.fold_in(own, dim), (parts,), jnp.float32, smallest / len(shards), top_value / len(shards)))
        loudness = loudness * jnp.repeat(draws, shape[dim] // parts).reshape([-1 if axis == dim else 1 for axis in range(len(shape))])
    return loudness


def gaussian(stream_key, extent, scale, bound, shards=(), kind=jnp.bfloat16):
    factor_of = block_levels(stream_key, extent, shards, -0.22, 0.18) if shards else 1.0
    result = jax.random.normal(stream_key, extent, jnp.float32) * scale * factor_of
    return jnp.minimum(jnp.maximum(result, -bound), bound).astype(kind)


def setup_inputs(seed: int = 0) -> dict:
    key_list = jax.random.split(jax.random.key(seed), 7)
    return {
        "projected": gaussian(key_list[0], (SEQS, SEQ, 3, D), 1.0, 6.0, ((0, 4), (1, 8))),
        "short_filter": gaussian(key_list[1], (3, SHORT, D), 0.4, 2.4, (), jnp.float32),
        "residues": gaussian(key_list[2], (GROUPS, POLES), 0.01, 0.06, (), jnp.float32),
        "decay_rates": jnp.clip(jnp.exp(jax.random.uniform(key_list[3], (GROUPS, POLES), jnp.float32, math.log(9.765625145519152e-05), math.log(0.03125))), 9.765625145519152e-05, 0.03125),
        "skip_gain": jnp.clip(1.0 + 0.1 * jax.random.normal(key_list[4], (D,), jnp.float32), 0.5, 1.5),
        "cotangent": gaussian(key_list[5], (SEQS, SEQ, D), 1.0, 6.0, ((0, 4), (1, 8))),
    }


HIGHEST = lax.Precision.HIGHEST

def edge_tables(residues, decay_rates, span):
    offsets = jnp.arange(span).astype(jnp.float32)
    carry_fwd = residues[:, None, :] * jnp.exp(-decay_rates[:, None, :] * (offsets[None, :, None] + 1.0))
    carry_bwd = residues[:, None, :] * jnp.exp(-decay_rates[:, None, :] * (span - offsets)[None, :, None])
    decay_factor = jnp.exp(-decay_rates * span)
    return (carry_fwd, carry_bwd, decay_factor)

def block_tables(residues, decay_rates, block_rows):
    offsets = jnp.arange(block_rows).astype(jnp.float32)
    powers = jnp.exp(-decay_rates[:, :, None] * offsets[None, None, :])
    lag_filter = lax.optimization_barrier(jnp.sum(residues[:, :, None] * powers, axis=1))
    lag_index = (jnp.arange(block_rows)[:, None] - jnp.arange(block_rows)[None, :]).astype(jnp.int32)
    toeplitz = jnp.where(lag_index >= 0, lag_filter[:, jnp.maximum(lag_index, 0)], 0.0)
    carry_fwd, carry_bwd, decay_factor = edge_tables(residues, decay_rates, block_rows)
    return (toeplitz, powers[:, :, ::-1], powers, carry_fwd, carry_bwd, decay_factor)

def forward_local(inputs, tables):
    toeplitz, end_weights, start_weights, carry_fwd, carry_bwd, decay_factor = tables
    local_out = jnp.einsum('gts,bkswg->bktwg', toeplitz, inputs, precision=HIGHEST)
    block_ends = jnp.einsum('gns,bkswg->bknwg', end_weights, inputs, precision=HIGHEST)
    factor = decay_factor.T[:, None, :]

    def advance(carried, block_term):
        return (factor * carried + block_term, carried)
    final_state, entering = lax.scan(advance, jnp.zeros_like(block_ends[:, 0]), jnp.moveaxis(block_ends, 1, 0))
    entering = jnp.moveaxis(entering, 0, 1)
    local_out = local_out + jnp.einsum('gjn,bknwg->bkjwg', carry_fwd, entering, precision=HIGHEST)
    return (local_out, final_state)

def backward_local(grads, tables):
    toeplitz, end_weights, start_weights, carry_fwd, carry_bwd, decay_factor = tables
    local_grad = jnp.einsum('gts,bktwg->bkswg', toeplitz, grads, precision=HIGHEST)
    block_starts = jnp.einsum('gnt,bktwg->bknwg', start_weights, grads, precision=HIGHEST)
    factor = decay_factor.T[:, None, :]

    def advance(carried, block_term):
        return (factor * carried + block_term, carried)
    final_adjoint, following = lax.scan(advance, jnp.zeros_like(block_starts[:, 0]), jnp.moveaxis(block_starts, 1, 0), reverse=True)
    following = jnp.moveaxis(following, 0, 1)
    local_grad = local_grad + jnp.einsum('gsn,bknwg->bkswg', carry_bwd, following, precision=HIGHEST)
    return (local_grad, final_adjoint)

def short_conv(padded, short_filter, count):
    tap_count = short_filter.shape[1]
    total = jnp.zeros((padded.shape[0], count) + padded.shape[2:], jnp.float32)
    for offset in range(tap_count):
        begin = tap_count - 1 - offset
        total = total + short_filter[:, offset, :] * padded[:, begin:begin + count].astype(jnp.float32)
    return total

def short_conv_grad(ahead, short_filter, count):
    tap_count = short_filter.shape[1]
    total = jnp.zeros((ahead.shape[0], count) + ahead.shape[2:], jnp.float32)
    for offset in range(tap_count):
        total = total + short_filter[:, offset, :] * ahead[:, offset:offset + count]
    return total

def filter_grad(grad_mixed, padded, tap_count, count):
    terms = []
    for offset in range(tap_count):
        begin = tap_count - 1 - offset
        terms.append(lax.optimization_barrier(jnp.sum(grad_mixed * padded[:, begin:begin + count].astype(jnp.float32), axis=(0, 1))))
    return jnp.stack(terms, axis=1)

def sequence_pass(projected, cotangent, short_filter, residues, decay_rates, skip_gain):
    length = projected.shape[1]
    channels = projected.shape[3]
    filter_groups = residues.shape[0]
    tap_count = short_filter.shape[1]
    padded = jnp.concatenate([jnp.zeros((1, tap_count - 1) + projected.shape[2:], projected.dtype), projected], axis=1)
    mixed = short_conv(padded, short_filter, length)
    query_part = mixed[:, :, 0]
    key_part = mixed[:, :, 1]
    value_part = mixed[:, :, 2]
    gated = key_part * value_part
    tables = block_tables(residues, decay_rates, BLK)
    block_shape = (1, length // BLK, BLK, channels // filter_groups, filter_groups)
    conv_out, final_state = forward_local(gated.reshape(block_shape), tables)
    filtered = conv_out.reshape(gated.shape) + skip_gain * gated
    output = (query_part * filtered).astype(jnp.bfloat16)
    upstream = cotangent.astype(jnp.float32)
    grad_query = upstream * filtered
    grad_filtered = upstream * query_part
    conv_grad, final_adjoint = backward_local(grad_filtered.reshape(block_shape), tables)
    grad_gated = conv_grad.reshape(gated.shape) + skip_gain * grad_filtered
    grad_mixed = jnp.stack([grad_query, grad_gated * value_part, grad_gated * key_part], axis=2)
    ahead = jnp.concatenate([grad_mixed, jnp.zeros((1, tap_count - 1, 3, channels), jnp.float32)], axis=1)
    grad_projected = short_conv_grad(ahead, short_filter, length).astype(jnp.bfloat16)
    grad_short = filter_grad(grad_mixed, padded, tap_count, length)
    grad_skip = lax.optimization_barrier(jnp.sum(grad_filtered * gated, axis=(0, 1)))
    return (output[0], grad_projected[0], grad_short, grad_skip)

def reference(projected, short_filter, residues, decay_rates, skip_gain, cotangent):

    def single(sequence_pair):
        return sequence_pass(sequence_pair[0][None], sequence_pair[1][None], short_filter, residues, decay_rates, skip_gain)
    outputs, grads_projected, shorts, skips = lax.map(single, (projected, cotangent))
    return (outputs, grads_projected, lax.optimization_barrier(jnp.sum(shorts, axis=0)), lax.optimization_barrier(jnp.sum(skips, axis=0)))
```

```python
import functools

import jax
import jax.numpy as jnp
import numpy as np
from jax import lax
from jax.experimental import pallas as pl
from jax.experimental.pallas import tpu as pltpu
from jax.sharding import PartitionSpec as P

LANES = 128
SUB = 8
F32 = jnp.float32
BF16 = jnp.bfloat16


def split(value):
    high = value.astype(BF16)
    return high, (value - high.astype(F32)).astype(BF16)


def fourier(rows):
    run = rows // SUB
    row = np.arange(rows)
    time = run * (row % SUB) + row // SUB
    angle = 2.0 * np.pi * (np.arange(rows)[:, None] + 0.5) * time[None, :] / (2 * rows)
    ahead = np.concatenate([np.cos(angle), -np.sin(angle)], axis=0)
    back = ahead.T / rows
    return ahead.astype(np.float32), back.astype(np.float32)


def states_kernel(p, hb, ha, u, filt, f1, we, wb, qkvg, e_out, a_out, xs):
    rows = p.shape[1]
    run = rows // SUB
    taps = filt.shape[1]
    poles = f1.shape[0]

    def tile(lt, carry):
        lanes = pl.ds(pl.multiple_of(lt * LANES, LANES), LANES)
        for j in range(3):
            xs[j, 0:SUB] = hb[j, :, lanes].astype(F32)
            xs[j, SUB : SUB + rows] = p[j, :, lanes].astype(F32)
            xs[j, SUB + rows :] = ha[j, :, lanes].astype(F32)
        xs[3, SUB : SUB + rows] = u[:, lanes].astype(F32)
        xs[3, SUB + rows :] = ha[3, :, lanes].astype(F32)
        for j in range(3):
            tap = [filt[j, i : i + 1, lanes] for i in range(taps)]
            view = [xs[j, pl.ds(SUB + a, SUB, stride=run), :] for a in range(1 - taps, run)]
            for a in range(run):
                total = tap[0] * view[a + taps - 1]
                for i in range(1, taps):
                    total = total + tap[i] * view[a + taps - 1 - i]
                qkvg[j, SUB * a : SUB * a + SUB, lanes] = total
            total = tap[0] * xs[j, SUB + rows : 2 * SUB + rows]
            for i in range(1, taps):
                total = total + tap[i] * xs[j, SUB + rows - i : 2 * SUB + rows - i]
            qkvg[j, rows : rows + SUB, lanes] = total
        for a in range(run):
            at = slice(SUB * a, SUB * a + SUB)
            qkvg[3, at, lanes] = xs[3, pl.ds(SUB + a, SUB, stride=run), :] * qkvg[0, at, lanes]
        at = slice(rows, rows + SUB)
        qkvg[3, at, lanes] = xs[3, SUB + rows :] * qkvg[0, at, lanes]
        decay = [jnp.broadcast_to(f1[n : n + 1, lanes], (SUB, LANES)) for n in range(poles)]
        for order, weight, out in ((range(run), we, e_out), (range(run - 1, -1, -1), wb, a_out)):
            state = None
            for a in order:
                at = slice(SUB * a, SUB * a + SUB)
                if out is e_out:
                    value = qkvg[1, at, lanes] * qkvg[2, at, lanes]
                else:
                    value = qkvg[3, at, lanes]
                if state is None:
                    state = [value] * poles
                else:
                    state = [decay[n] * state[n] + value for n in range(poles)]
            for n in range(poles):
                out[0, n : n + 1, lanes] = jnp.sum(
                    state[n] * weight[n, :, lanes], axis=0, keepdims=True
                )
        return carry

    lax.fori_loop(0, p.shape[2] // LANES, tile, 0)


def long_kernel(qkvg, lag, fwd, fwd_hi, inv_hi, inv_lo, conv, convg, spectrum):
    rows = conv.shape[0]

    def transform(value):
        high, low = split(value)
        both = jnp.concatenate([high, high], axis=0)
        return jnp.dot(fwd[...], both, preferred_element_type=F32) + jnp.dot(
            fwd_hi[...], low, preferred_element_type=F32
        )

    def inverse(real, imag):
        high, low = split(jnp.concatenate([real, imag], axis=0))
        return (
            jnp.dot(inv_hi[...], high, preferred_element_type=F32)
            + jnp.dot(inv_lo[...], high, preferred_element_type=F32)
            + jnp.dot(inv_hi[...], low, preferred_element_type=F32)
        )

    @pl.when(pl.program_id(0) == 0)
    def _():
        spectrum[...] = transform(lag[...])

    h_re = spectrum[0:rows]
    h_im = spectrum[rows:]
    x = transform(qkvg[1, 0:rows] * qkvg[2, 0:rows])
    x_re, x_im = x[0:rows], x[rows:]
    conv[...] = inverse(h_re * x_re - h_im * x_im, h_re * x_im + h_im * x_re)
    x = transform(qkvg[3, 0:rows])
    x_re, x_im = x[0:rows], x[rows:]
    convg[...] = inverse(h_re * x_re + h_im * x_im, h_re * x_im - h_im * x_re)


def final_kernel(
    p, hb, u, ha, qkvg, conv, convg, enter, arrive, ends, filt, skip, f1, f_all, cz, cy, ce, cb,
    near, output, grad_p, sums, ps, us, gs, os, es
):
    rows = p.shape[1]
    run = rows // SUB
    taps = filt.shape[1]
    poles = f1.shape[0]
    main = slice(0, rows)
    beyond = slice(rows, rows + SUB)

    def tile(lt, carry):
        lanes = pl.ds(pl.multiple_of(lt * LANES, LANES), LANES)
        for j in range(3):
            ps[j, 0:SUB] = hb[j, :, lanes].astype(F32)
            ps[j, SUB : SUB + rows] = p[j, :, lanes].astype(F32)
        us[...] = u[:, lanes].astype(F32)
        gain = skip[0:1, lanes]
        decay = [jnp.broadcast_to(f1[n : n + 1, lanes], (SUB, LANES)) for n in range(poles)]

        state = [cz[n, :, lanes] * enter[0, n : n + 1, lanes] for n in range(poles)]
        skip_sum = jnp.zeros((SUB, LANES), F32)
        for a in range(run):
            at = slice(SUB * a, SUB * a + SUB)
            gated = qkvg[1, at, lanes] * qkvg[2, at, lanes]
            skip_sum = skip_sum + gated * qkvg[3, at, lanes]
            filtered = conv[at, lanes] + gain * gated
            terms = list(state)
            while len(terms) > 1:
                terms = [sum(terms[k : k + 2][1:], terms[k]) for k in range(0, len(terms), 2)]
            filtered = filtered + terms[0]
            spread = pl.ds(a, SUB, stride=run)
            os[spread, :] = qkvg[0, at, lanes] * filtered
            gs[0, spread, :] = us[spread, :] * filtered
            if a + 1 < run:
                state = [state[n] * decay[n] for n in range(poles)]
        output[:, lanes] = os[...].astype(BF16)
        es[0:SUB] = jnp.zeros((SUB, LANES), F32)
        es[SUB:] = qkvg[1, beyond, lanes] * qkvg[2, beyond, lanes]
        total = (near[taps : taps + 1, lanes] + gain) * es[SUB:]
        for m in range(1, taps - 1):
            total = total + near[taps + m : taps + m + 1, lanes] * es[SUB - m : 2 * SUB - m]
        for n in range(poles):
            at_end = ends[0, n : n + 1, lanes] + f_all[n : n + 1, lanes] * enter[0, n : n + 1, lanes]
            total = total + ce[n, :, lanes] * at_end
        gs[0, beyond] = ha[3, :, lanes].astype(F32) * total

        state = [cy[n, :, lanes] * arrive[0, n : n + 1, lanes] for n in range(poles)]
        for a in range(run - 1, -1, -1):
            at = slice(SUB * a, SUB * a + SUB)
            terms = list(state)
            while len(terms) > 1:
                terms = [sum(terms[k : k + 2][1:], terms[k]) for k in range(0, len(terms), 2)]
            grad = convg[at, lanes] + gain * qkvg[3, at, lanes] + terms[0]
            spread = pl.ds(a, SUB, stride=run)
            gs[1, spread, :] = grad * qkvg[2, at, lanes]
            gs[2, spread, :] = grad * qkvg[1, at, lanes]
            if a:
                state = [state[n] * decay[n] for n in range(poles)]
        es[SUB:] = qkvg[3, beyond, lanes]
        total = gain * es[SUB:]
        for m in range(1, taps - 1):
            total = total - near[taps - m : taps - m + 1, lanes] * es[SUB - m : 2 * SUB - m]
        for n in range(poles):
            total = total + cb[n, :, lanes] * arrive[0, n : n + 1, lanes]
        gs[1, beyond] = total * qkvg[2, beyond, lanes]
        gs[2, beyond] = total * qkvg[1, beyond, lanes]

        for j in range(3):
            tap = [filt[j, i : i + 1, lanes] for i in range(taps)]
            grads = [gs[j, pl.ds(a, SUB, stride=run), :] for a in range(run + taps - 1)]
            views = [ps[j, pl.ds(SUB + a, SUB, stride=run), :] for a in range(1 - taps, run)]
            sums_of = [None] * taps
            for a in range(run):
                total = tap[0] * grads[a]
                for i in range(1, taps):
                    total = total + tap[i] * grads[a + i]
                os[pl.ds(a, SUB, stride=run), :] = total
                for i in range(taps):
                    term = grads[a] * views[a + taps - 1 - i]
                    sums_of[i] = term if a == 0 else sums_of[i] + term
            grad_p[j, :, lanes] = os[...].astype(BF16)
            for i in range(taps):
                at = j * taps + i
                sums[0, at : at + 1, lanes] = jnp.sum(sums_of[i], axis=0, keepdims=True)
        at = 3 * taps
        sums[0, at : at + 1, lanes] = jnp.sum(skip_sum, axis=0, keepdims=True)
        return carry

    lax.fori_loop(0, p.shape[2] // LANES, tile, 0)


def shifted(value, axis, steps):
    count = lax.axis_size(axis)
    first, last = (max(0, -steps), min(count, count - steps))
    return lax.ppermute(value, axis, [(source, source + steps) for source in range(first, last)])


def rotated(value, axis, steps):
    count = lax.axis_size(axis)
    return lax.ppermute(value, axis, [(s, (s + steps) % count) for s in range(count)])


def swapped(value):
    count = lax.axis_size("ctx")
    return lax.ppermute(value, "ctx", [(s, s ^ 1) for s in range(count)])


def exchange(ends, adjoints, f_all):
    chips = lax.axis_size("ctx") // 2
    core = lax.rem(lax.axis_index("ctx"), 2)
    half = ends.shape[0] // 2
    other_ends, other_adjoints = swapped(ends), swapped(adjoints)
    mine = lambda value: lax.dynamic_slice_in_dim(value, core * half, half, 0)
    first = core == 0
    my_e, my_a = mine(ends), mine(adjoints)
    their_e, their_a = mine(other_ends), mine(other_adjoints)
    chip_e = jnp.where(first, f_all * my_e + their_e, f_all * their_e + my_e)
    chip_a = jnp.where(first, my_a + f_all * their_a, their_a + f_all * my_a)
    f_chip = f_all * f_all
    before = after = None
    for hop in range(chips - 1):
        before = shifted(chip_e if hop == 0 else f_chip * before + chip_e, "ctx", 2)
        after = shifted(chip_a if hop == 0 else f_chip * after + chip_a, "ctx", -2)
    other_before, other_after = swapped(before), swapped(after)
    whole = lambda own, other: jnp.concatenate(
        [jnp.where(first, own, other), jnp.where(first, other, own)], axis=0
    )
    before, after = whole(before, other_before), whole(after, other_after)
    enter = jnp.where(first, before, f_all * before + other_ends)
    arrive = jnp.where(first, other_adjoints + f_all * after, after)
    return enter, arrive


def summed(value):
    index = lax.axis_index("ctx")
    core = lax.rem(index, 2)
    chip = index // 2
    chips = lax.axis_size("ctx") // 2
    dp = lax.axis_index("dp")
    parts = lax.axis_size("dp")
    half = value.shape[0] // 2
    keep = lax.dynamic_slice_in_dim(value, core * half, half, 0)
    give = lax.dynamic_slice_in_dim(value, (1 - core) * half, half, 0)
    value = keep + swapped(give)
    size = half // parts
    piece = lambda k: lax.dynamic_slice_in_dim(value, lax.rem(dp + k, parts) * size, size, 0)
    total = piece(0)
    for k in range(1, parts):
        total = total + rotated(piece(k), "dp", k)
    gathered = jnp.zeros((chips,) + total.shape, F32)
    put = lambda into, at, what: lax.dynamic_update_slice_in_dim(into, what[None], at, 0)
    gathered = put(gathered, chip, total)
    for k in range(1, chips):
        gathered = put(gathered, lax.rem(chip + chips - k, chips), rotated(total, "ctx", 2 * k))
    total = gathered[0]
    for k in range(1, chips):
        total = total + gathered[k]
    gathered = jnp.zeros((parts,) + total.shape, F32)
    gathered = put(gathered, dp, total)
    for k in range(1, parts):
        gathered = put(gathered, lax.rem(dp + parts - k, parts), rotated(total, "dp", k))
    mine = gathered.reshape((half,) + total.shape[1:])
    other = swapped(mine)
    first = core == 0
    return jnp.concatenate([jnp.where(first, mine, other), jnp.where(first, other, mine)], axis=0)


def local(projected, short_filter, residues, decay_rates, skip_gain, cotangent):
    rows = projected.shape[1]
    channels = projected.shape[3]
    taps = short_filter.shape[1]
    groups, poles = residues.shape
    width = channels // groups
    run = rows // SUB
    p = projected[0].transpose(1, 0, 2)
    u = cotangent[0]
    hb = shifted(p[:, rows - SUB :], "ctx", 1)
    ha = shifted(jnp.concatenate([p[:, :SUB], u[None, :SUB]], axis=0), "ctx", -1)

    rate = decay_rates.T
    weight = residues.T
    sub = np.arange(SUB)
    powers = np.stack(
        [run * (7 - sub), run * sub, 1 + run * sub, 1 + run * (7 - sub), 1 + sub, -sub]
    ).astype(np.float32)
    table = jnp.exp(-rate[None, :, None, :] * powers[:, None, :, None])
    we, wb = table[0], table[1]
    cz, cy, ce, cb = [weight[:, None, :] * table[k] for k in range(2, 6)]
    f1 = jnp.exp(-rate)
    f_all = jnp.exp(-rate * rows)
    row = np.arange(rows)
    lags = (run * (row % SUB) + row // SUB).astype(np.float32)
    lag = jnp.sum(weight[:, None, :] * jnp.exp(-rate[:, None, :] * lags[None, :, None]), axis=0)
    close = np.arange(-taps, 16 - taps).astype(np.float32)
    near = jnp.sum(weight[:, None, :] * jnp.exp(-rate[:, None, :] * close[None, :, None]), axis=0)
    ahead, back = fourier(rows)
    fwd_hi, fwd_lo = split(jnp.asarray(ahead))
    fwd = jnp.concatenate([fwd_hi, fwd_lo], axis=1)
    inv_hi, inv_lo = split(jnp.asarray(back))

    def by_w(*shape):
        axis = len(shape) - 1
        return pl.BlockSpec(shape, lambda w: (0,) * axis + (w,))

    def per_w(*shape):
        return pl.BlockSpec((1,) + shape, lambda w: (w,) + (0,) * len(shape))

    def fixed(value):
        return pl.BlockSpec(value.shape, lambda w: (0,) * value.ndim)

    params = pltpu.CompilerParams(vmem_limit_bytes=48 * 1024 * 1024)
    shape_of = jax.ShapeDtypeStruct
    qkvg, ends, adjoints = pl.pallas_call(
        states_kernel,
        grid=(width,),
        in_specs=[
            by_w(3, rows, groups), by_w(3, SUB, groups), by_w(4, SUB, groups), by_w(rows, groups),
            by_w(3, taps, groups), fixed(f1), fixed(we), fixed(wb),
        ],
        out_specs=[by_w(4, rows + SUB, groups), per_w(poles, groups), per_w(poles, groups)],
        out_shape=[
            shape_of((4, rows + SUB, channels), F32),
            shape_of((width, poles, groups), F32),
            shape_of((width, poles, groups), F32),
        ],
        scratch_shapes=[pltpu.VMEM((4, rows + 2 * SUB, LANES), F32)],
        compiler_params=params,
        name="states",
    )(p, hb, ha, u, short_filter, f1, we, wb)

    enter, arrive = exchange(ends, adjoints, f_all)

    conv, convg = pl.pallas_call(
        long_kernel,
        grid=(width,),
        in_specs=[
            by_w(4, rows + SUB, groups), fixed(lag), fixed(fwd), fixed(fwd_hi), fixed(inv_hi),
            fixed(inv_lo),
        ],
        out_specs=[by_w(rows, groups)] * 2,
        out_shape=[shape_of((rows, channels), F32)] * 2,
        scratch_shapes=[pltpu.VMEM((2 * rows, groups), F32)],
        compiler_params=params,
        cost_estimate=pl.CostEstimate(
            flops=2 * 2 * 6 * 256 * rows * channels, bytes_accessed=26 * 2**20, transcendentals=0
        ),
        name="long",
    )(qkvg, lag, fwd, fwd_hi, inv_hi, inv_lo)

    count = 3 * taps + 3
    output, grad_p, sums = pl.pallas_call(
        final_kernel,
        grid=(width,),
        in_specs=[
            by_w(3, rows, groups), by_w(3, SUB, groups), by_w(rows, groups), by_w(4, SUB, groups),
            by_w(4, rows + SUB, groups), by_w(rows, groups), by_w(rows, groups),
            per_w(poles, groups), per_w(poles, groups), per_w(poles, groups),
            by_w(3, taps, groups), by_w(1, groups), fixed(f1), fixed(f_all),
            fixed(cz), fixed(cy), fixed(ce), fixed(cb), fixed(near),
        ],
        out_specs=[by_w(rows, groups), by_w(3, rows, groups), per_w(count, groups)],
        out_shape=[
            shape_of((rows, channels), BF16),
            shape_of((3, rows, channels), BF16),
            shape_of((width, count, groups), F32),
        ],
        scratch_shapes=[
            pltpu.VMEM((3, rows + SUB, LANES), F32),
            pltpu.VMEM((rows, LANES), F32),
            pltpu.VMEM((3, rows + SUB, LANES), F32),
            pltpu.VMEM((rows, LANES), F32),
            pltpu.VMEM((2 * SUB, LANES), F32),
        ],
        compiler_params=params,
        name="final",
    )(
        p, hb, u, ha, qkvg, conv, convg, enter, arrive, ends, short_filter, skip_gain[None],
        f1, f_all, cz, cy, ce, cb, near,
    )

    total = summed(sums).transpose(1, 0, 2).reshape(count, channels)
    grad_short = total[: 3 * taps].reshape(3, taps, channels)
    grad_skip = total[3 * taps]
    return output[None], grad_p.transpose(1, 0, 2)[None], grad_short, grad_skip


def solution(mesh):
    placed = (P("dp", "ctx", None, None), P(), P(), P(), P(), P("dp", "ctx", None))
    return jax.shard_map(
        local,
        mesh=mesh,
        in_specs=placed,
        out_specs=(P("dp", "ctx", None), P("dp", "ctx", None, None), P(), P()),
        check_vma=False,
    )
```

```python
import functools

import jax
import jax.numpy as jnp
import numpy as np
from jax import lax
from jax.experimental import pallas as pl
from jax.experimental.pallas import tpu as pltpu
from jax.sharding import PartitionSpec as P

LANES = 128
SUB = 8
F32 = jnp.float32
BF16 = jnp.bfloat16


def spread(row):
    return jnp.broadcast_to(row, (SUB, LANES))


def added(terms):
    while len(terms) > 1:
        pairs = [terms[k] + terms[k + 1] for k in range(0, len(terms) - 1, 2)]
        terms = pairs + terms[len(terms) - len(terms) % 2 :]
    return terms[0]


def states_kernel(p, hb, ha, u, filt, f1, we, wb, qkvg, blocks_e, blocks_a, ends, xs):
    rows = p.shape[1]
    run = (rows + SUB) // SUB
    taps = filt.shape[1]
    poles = f1.shape[0]
    own = rows - run * (SUB - 1)

    def tile(lt, carry):
        lanes = pl.ds(pl.multiple_of(lt * LANES, LANES), LANES)
        inside = lax.broadcasted_iota(jnp.int32, (SUB, LANES), 0) < SUB - 1
        for j in range(3):
            xs[j, 0:SUB] = hb[j, :, lanes].astype(F32)
            xs[j, SUB : SUB + rows] = p[j, :, lanes].astype(F32)
            xs[j, SUB + rows :] = ha[j, :, lanes].astype(F32)
        xs[3, SUB : SUB + rows] = u[:, lanes].astype(F32)
        xs[3, SUB + rows :] = ha[3, :, lanes].astype(F32)
        for j in range(3):
            tap = [spread(filt[j, i : i + 1, lanes]) for i in range(taps)]
            view = [xs[j, pl.ds(SUB + a, SUB, stride=run), :] for a in range(1 - taps, run)]
            for a in range(run):
                total = added([tap[i] * view[a + taps - 1 - i] for i in range(taps)])
                qkvg[j, SUB * a : SUB * a + SUB, lanes] = total
        decay = [spread(f1[n : n + 1, lanes]) for n in range(poles)]
        state = None
        for a in range(run):
            at = slice(SUB * a, SUB * a + SUB)
            value = qkvg[1, at, lanes] * qkvg[2, at, lanes]
            if a >= own:
                value = jnp.where(inside, value, 0.0)
            state = [value] * poles if a == 0 else [decay[n] * state[n] + value for n in range(poles)]
        for n in range(poles):
            blocks_e[n, :, lanes] = state[n]
            ends[0, 0, n : n + 1, lanes] = jnp.sum(state[n] * we[n, :, lanes], axis=0, keepdims=True)
        state = None
        for a in range(run - 1, -1, -1):
            at = slice(SUB * a, SUB * a + SUB)
            value = xs[3, pl.ds(SUB + a, SUB, stride=run), :] * qkvg[0, at, lanes]
            qkvg[3, at, lanes] = value
            if a >= own:
                value = jnp.where(inside, value, 0.0)
            state = [value] * poles if a == run - 1 else [decay[n] * state[n] + value for n in range(poles)]
        for n in range(poles):
            blocks_a[n, :, lanes] = state[n]
            ends[1, 0, n : n + 1, lanes] = jnp.sum(state[n] * wb[n, :, lanes], axis=0, keepdims=True)
        return carry

    lax.fori_loop(0, p.shape[2] // LANES, tile, 0)


def blocks_kernel(kvg, blocks_e, blocks_a, near, skip, join_e, join_a, conv, convg, from_e, from_a):
    run = conv.shape[0] // SUB
    rows = conv.shape[0] - SUB
    taps = near.shape[0] - run
    poles = blocks_e.shape[0]
    own = rows - run * (SUB - 1)

    def tile(lt, carry):
        lanes = pl.ds(pl.multiple_of(lt * LANES, LANES), LANES)
        inside = lax.broadcasted_iota(jnp.int32, (SUB, LANES), 0) < SUB - 1
        gain = spread(skip[0:1, lanes])
        lag = [spread(near[taps + m : taps + m + 1, lanes]) for m in range(run)]
        lag[0] = lag[0] + gain
        x = [
            kvg[1, SUB * a : SUB * a + SUB, lanes] * kvg[2, SUB * a : SUB * a + SUB, lanes]
            for a in range(run)
        ]
        for a in range(run):
            conv[SUB * a : SUB * a + SUB, lanes] = added([lag[m] * x[a - m] for m in range(a + 1)])
        x = [kvg[3, SUB * a : SUB * a + SUB, lanes] for a in range(run)]
        masked = [x[a] if a < own else jnp.where(inside, x[a], 0.0) for a in range(run)]
        past = [jnp.where(inside, 0.0, gain)] + [
            jnp.where(inside, 0.0, -spread(near[taps - m : taps - m + 1, lanes]))
            for m in range(1, taps - 1)
        ]
        for a in range(run):
            terms = [lag[m] * masked[a + m] for m in range(run - a)]
            if own <= a < own + taps - 1:
                terms = terms + [past[m] * x[a - m] for m in range(a - own + 1)]
            convg[SUB * a : SUB * a + SUB, lanes] = added(terms)
        for n in range(poles):
            value = pltpu.roll(blocks_e[n, :, lanes], 1, 0) * join_e[0, n, :, lanes]
            for k, step in ((1, 1), (2, 2), (3, 4)):
                value = value + pltpu.roll(value, step, 0) * join_e[k, n, :, lanes]
            from_e[n, :, lanes] = value
            value = pltpu.roll(blocks_a[n, :, lanes], SUB - 1, 0) * join_a[0, n, :, lanes]
            for k, step in ((1, 1), (2, 2), (3, 4)):
                value = value + pltpu.roll(value, SUB - step, 0) * join_a[k, n, :, lanes]
            from_a[n, :, lanes] = value
        return carry

    lax.fori_loop(0, conv.shape[1] // LANES, tile, 0)


def final_kernel(
    p, hb, u, ha, qkvg, conv, convg, from_e, from_a, enter, arrive, filt, f1, cz, cy,
    output, grad_p, sums, ps, us, gs, os,
):
    rows = p.shape[1]
    run = (rows + SUB) // SUB
    taps = filt.shape[1]
    poles = f1.shape[0]
    own = rows - run * (SUB - 1)

    def tile(lt, carry):
        lanes = pl.ds(pl.multiple_of(lt * LANES, LANES), LANES)
        inside = lax.broadcasted_iota(jnp.int32, (SUB, LANES), 0) < SUB - 1
        for j in range(3):
            ps[j, 0:SUB] = hb[j, :, lanes].astype(F32)
            ps[j, SUB : SUB + rows] = p[j, :, lanes].astype(F32)
            ps[j, SUB + rows :] = ha[j, :, lanes].astype(F32)
        us[0:rows] = u[:, lanes].astype(F32)
        us[rows:] = ha[3, :, lanes].astype(F32)
        decay = [spread(f1[n : n + 1, lanes]) for n in range(poles)]

        state = [
            from_e[n, :, lanes] + cz[n, :, lanes] * spread(enter[0, n : n + 1, lanes])
            for n in range(poles)
        ]
        skip_sum = None
        for a in range(run):
            at = slice(SUB * a, SUB * a + SUB)
            term = qkvg[1, at, lanes] * qkvg[2, at, lanes] * qkvg[3, at, lanes]
            if a >= own:
                term = jnp.where(inside, term, 0.0)
            skip_sum = term if a == 0 else skip_sum + term
            filtered = conv[at, lanes] + added(list(state))
            os[pl.ds(a, SUB, stride=run), :] = qkvg[0, at, lanes] * filtered
            gs[0, pl.ds(a, SUB, stride=run), :] = us[pl.ds(a, SUB, stride=run), :] * filtered
            if a + 1 < run:
                state = [state[n] * decay[n] for n in range(poles)]
        output[:, lanes] = os[0:rows].astype(BF16)

        state = [
            from_a[n, :, lanes] + cy[n, :, lanes] * spread(arrive[0, n : n + 1, lanes])
            for n in range(poles)
        ]
        for a in range(run - 1, -1, -1):
            at = slice(SUB * a, SUB * a + SUB)
            grad = convg[at, lanes] + added(list(state))
            gs[1, pl.ds(a, SUB, stride=run), :] = grad * qkvg[2, at, lanes]
            gs[2, pl.ds(a, SUB, stride=run), :] = grad * qkvg[1, at, lanes]
            if a:
                state = [state[n] * decay[n] for n in range(poles)]

        for j in range(3):
            tap = [spread(filt[j, i : i + 1, lanes]) for i in range(taps)]
            grads = [gs[j, pl.ds(a, SUB, stride=run), :] for a in range(run + taps - 1)]
            views = [ps[j, pl.ds(SUB + a, SUB, stride=run), :] for a in range(1 - taps, run)]
            sums_of = [None] * taps
            for a in range(run):
                total = added([tap[i] * grads[a + i] for i in range(taps)])
                os[pl.ds(a, SUB, stride=run), :] = total
                grad = grads[a] if a < own else jnp.where(inside, grads[a], 0.0)
                for i in range(taps):
                    term = grad * views[a + taps - 1 - i]
                    sums_of[i] = term if a == 0 else sums_of[i] + term
            grad_p[j, :, lanes] = os[0:rows].astype(BF16)
            for i in range(taps):
                at = j * taps + i
                sums[0, at : at + 1, lanes] = jnp.sum(sums_of[i], axis=0, keepdims=True)
        at = 3 * taps
        sums[0, at : at + 1, lanes] = jnp.sum(skip_sum, axis=0, keepdims=True)
        return carry

    lax.fori_loop(0, p.shape[2] // LANES, tile, 0)


def shifted(value, axis, steps):
    count = lax.axis_size(axis)
    first, last = (max(0, -steps), min(count, count - steps))
    return lax.ppermute(value, axis, [(source, source + steps) for source in range(first, last)])


def rotated(value, axis, steps):
    count = lax.axis_size(axis)
    return lax.ppermute(value, axis, [(s, (s + steps) % count) for s in range(count)])


def swapped(value):
    count = lax.axis_size("ctx")
    return lax.ppermute(value, "ctx", [(s, s ^ 1) for s in range(count)])


def outward(ends, f_all):
    chips = lax.axis_size("ctx") // 2
    core = lax.rem(lax.axis_index("ctx"), 2)
    half = ends.shape[1] // 2
    other = swapped(ends)
    first = core == 0
    mine = lax.dynamic_slice_in_dim(ends, core * half, half, 1)
    theirs = lax.dynamic_slice_in_dim(other, core * half, half, 1)
    one, two = jnp.where(first, mine, theirs), jnp.where(first, theirs, mine)
    chip_e = f_all * one[0] + two[0]
    chip_a = one[1] + f_all * two[1]
    f_chip = f_all * f_all
    if chips <= 4:
        hops = range(1, chips)
        found = [(shifted(chip_e, "ctx", 2 * k), shifted(chip_a, "ctx", -2 * k)) for k in hops]
    else:
        before, after = shifted(chip_e, "ctx", 2), shifted(chip_a, "ctx", -2)
        for hop in range(2, chips):
            before = shifted(f_chip * before + chip_e, "ctx", 2)
            after = shifted(f_chip * after + chip_a, "ctx", -2)
        found = [(before, after)]
    return other, found, chip_e


def inward(other, found, f_all):
    first = lax.rem(lax.axis_index("ctx"), 2) == 0
    f_chip = f_all * f_all
    factor = f_chip
    before, after = found[0]
    for early, late in found[1:]:
        before = before + factor * early
        after = after + factor * late
        factor = factor * f_chip
    both = jnp.stack([before, after])
    found = swapped(both)
    both = jnp.concatenate([jnp.where(first, both, found), jnp.where(first, found, both)], axis=1)
    enter = jnp.where(first, both[0], f_all * both[0] + other[0])
    arrive = jnp.where(first, other[1] + f_all * both[1], both[1])
    return enter, arrive


def summed(value):
    index = lax.axis_index("ctx")
    core = lax.rem(index, 2)
    chip = index // 2
    chips = lax.axis_size("ctx") // 2
    dp = lax.axis_index("dp")
    parts = lax.axis_size("dp")
    half = value.shape[0] // 2
    keep = lax.dynamic_slice_in_dim(value, core * half, half, 0)
    give = lax.dynamic_slice_in_dim(value, (1 - core) * half, half, 0)
    value = keep + swapped(give)
    size = half // parts
    piece = lambda k: lax.dynamic_slice_in_dim(value, lax.rem(dp + k, parts) * size, size, 0)
    total = piece(0)
    for k in range(1, parts):
        total = total + rotated(piece(k), "dp", k)
    gathered = jnp.zeros((chips,) + total.shape, F32)
    put = lambda into, at, what: lax.dynamic_update_slice_in_dim(into, what[None], at, 0)
    gathered = put(gathered, chip, total)
    for k in range(1, chips):
        gathered = put(gathered, lax.rem(chip + chips - k, chips), rotated(total, "ctx", 2 * k))
    total = gathered[0]
    for k in range(1, chips):
        total = total + gathered[k]
    gathered = jnp.zeros((parts,) + total.shape, F32)
    gathered = put(gathered, dp, total)
    for k in range(1, parts):
        gathered = put(gathered, lax.rem(dp + parts - k, parts), rotated(total, "dp", k))
    mine = gathered.reshape((half,) + total.shape[1:])
    other = swapped(mine)
    first = core == 0
    return jnp.concatenate([jnp.where(first, mine, other), jnp.where(first, other, mine)], axis=0)


def local(projected, short_filter, residues, decay_rates, skip_gain, cotangent):
    rows = projected.shape[1]
    channels = projected.shape[3]
    taps = short_filter.shape[1]
    groups, poles = residues.shape
    width = channels // groups
    run = (rows + SUB) // SUB
    held = rows + SUB
    p = projected[0].transpose(1, 0, 2)
    u = cotangent[0]
    hb = shifted(p[:, rows - SUB :], "ctx", 1)
    ha = shifted(jnp.concatenate([p[:, :SUB], u[None, :SUB]], axis=0), "ctx", -1)

    rate = decay_rates.T
    weight = residues.T
    sub = np.arange(SUB)
    powers = np.stack([run * (7 - sub) - SUB, run * sub, 1 + run * sub, rows - run * (sub + 1) + 1])
    table = jnp.exp(-rate[None, :, None, :] * powers.astype(np.float32)[:, None, :, None])
    we, wb = table[0], table[1]
    cz, cy = weight[:, None, :] * table[2], weight[:, None, :] * table[3]
    f1 = jnp.exp(-rate)
    f_all = jnp.exp(-rate * rows)
    steps = np.array([1, run, 2 * run, 4 * run], np.float32)
    factor = jnp.exp(-rate[None] * steps[:, None, None])
    factor = jnp.concatenate([weight[None] * factor[:1], factor[1:]], axis=0)
    reach = np.array([1, 1, 2, 4])[:, None]
    down, up = sub[None] >= reach, sub[None] < SUB - reach
    join_e = jnp.where(down[:, None, :, None], factor[:, :, None, :], 0.0)
    join_a = jnp.where(up[:, None, :, None], factor[:, :, None, :], 0.0)
    close = np.arange(-taps, run).astype(np.float32)
    near = jnp.sum(weight[:, None, :] * jnp.exp(-rate[:, None, :] * close[None, :, None]), axis=0)

    def by_w(*shape):
        axis = len(shape) - 1
        return pl.BlockSpec(shape, lambda w: (0,) * axis + (w,))

    def per_w(*shape):
        return pl.BlockSpec((1,) + shape, lambda w: (w,) + (0,) * len(shape))

    def fixed(value):
        return pl.BlockSpec(value.shape, lambda w: (0,) * value.ndim)

    params = pltpu.CompilerParams(vmem_limit_bytes=48 * 1024 * 1024)
    shape_of = jax.ShapeDtypeStruct
    state_shape = shape_of((poles, SUB, channels), F32)
    qkvg, blocks_e, blocks_a, ends = pl.pallas_call(
        states_kernel,
        grid=(width,),
        in_specs=[
            by_w(3, rows, groups), by_w(3, SUB, groups), by_w(4, SUB, groups), by_w(rows, groups),
            by_w(3, taps, groups), fixed(f1), fixed(we), fixed(wb),
        ],
        out_specs=[
            by_w(4, held, groups), by_w(poles, SUB, groups), by_w(poles, SUB, groups),
            pl.BlockSpec((2, 1, poles, groups), lambda w: (0, w, 0, 0)),
        ],
        out_shape=[
            shape_of((4, held, channels), F32), state_shape, state_shape,
            shape_of((2, width, poles, groups), F32),
        ],
        scratch_shapes=[pltpu.VMEM((4, held + SUB, LANES), F32)],
        compiler_params=params,
        name="states",
    )(p, hb, ha, u, short_filter, f1, we, wb)

    other, found, chip_e = outward(ends, f_all)
    near, _ = lax.optimization_barrier((near, chip_e))

    conv, convg, from_e, from_a = pl.pallas_call(
        blocks_kernel,
        grid=(width,),
        in_specs=[
            by_w(4, held, groups), by_w(poles, SUB, groups), by_w(poles, SUB, groups), fixed(near),
            by_w(1, groups), fixed(join_e), fixed(join_a),
        ],
        out_specs=[by_w(held, groups)] * 2 + [by_w(poles, SUB, groups)] * 2,
        out_shape=[shape_of((held, channels), F32)] * 2 + [state_shape] * 2,
        compiler_params=params,
        cost_estimate=pl.CostEstimate(
            flops=60 * rows * channels, bytes_accessed=45 * 2**20, transcendentals=0
        ),
        name="blocks",
    )(qkvg, blocks_e, blocks_a, near, skip_gain[None], join_e, join_a)

    found, conv = lax.optimization_barrier((found, conv))
    enter, arrive = inward(other, found, f_all)

    count = 3 * taps + 3
    output, grad_p, sums = pl.pallas_call(
        final_kernel,
        grid=(width,),
        in_specs=[
            by_w(3, rows, groups), by_w(3, SUB, groups), by_w(rows, groups), by_w(4, SUB, groups),
            by_w(4, held, groups), by_w(held, groups), by_w(held, groups),
            by_w(poles, SUB, groups), by_w(poles, SUB, groups),
            per_w(poles, groups), per_w(poles, groups),
            by_w(3, taps, groups), fixed(f1), fixed(cz), fixed(cy),
        ],
        out_specs=[by_w(rows, groups), by_w(3, rows, groups), per_w(count, groups)],
        out_shape=[
            shape_of((rows, channels), BF16),
            shape_of((3, rows, channels), BF16),
            shape_of((width, count, groups), F32),
        ],
        scratch_shapes=[
            pltpu.VMEM((3, held + SUB, LANES), F32),
            pltpu.VMEM((held, LANES), F32),
            pltpu.VMEM((3, held + SUB, LANES), F32),
            pltpu.VMEM((held, LANES), F32),
        ],
        compiler_params=params,
        name="final",
    )(
        p, hb, u, ha, qkvg, conv, convg, from_e, from_a, enter, arrive, short_filter, f1, cz, cy,
    )

    total = summed(sums).transpose(1, 0, 2).reshape(count, channels)
    grad_short = total[: 3 * taps].reshape(3, taps, channels)
    grad_skip = total[3 * taps]
    return output[None], grad_p.transpose(1, 0, 2)[None], grad_short, grad_skip


def solution(mesh):
    placed = (P("dp", "ctx", None, None), P(), P(), P(), P(), P("dp", "ctx", None))
    return jax.shard_map(
        local,
        mesh=mesh,
        in_specs=placed,
        out_specs=(P("dp", "ctx", None), P("dp", "ctx", None, None), P(), P()),
        check_vma=False,
    )
```

```python
import functools

import jax
import jax.numpy as jnp
import numpy as np
from jax import lax
from jax.experimental import pallas as pl
from jax.experimental.pallas import tpu as pltpu
from jax.sharding import PartitionSpec as P

LANES = 128
SUB = 8
F32 = jnp.float32
BF16 = jnp.bfloat16


def spread(row):
    return jnp.broadcast_to(row, (SUB, LANES))


def added(terms):
    while len(terms) > 1:
        pairs = [terms[k] + terms[k + 1] for k in range(0, len(terms) - 1, 2)]
        terms = pairs + terms[len(terms) - len(terms) % 2 :]
    return terms[0]


def states_kernel(p, hb, ha, u, filt, f1, we, wb, xg, blocks_e, blocks_a, ends, xs):
    rows = p.shape[1]
    run = (rows + SUB) // SUB
    taps = filt.shape[1]
    poles, groups = f1.shape
    own = rows - run * (SUB - 1)
    tiles = groups // LANES

    def tile(lt, carry):
        lanes = pl.ds(pl.multiple_of(lt * LANES, LANES), LANES)
        part = pl.ds(pl.multiple_of(lax.rem(lt, tiles) * LANES, LANES), LANES)
        which = lt // tiles
        inside = lax.broadcasted_iota(jnp.int32, (SUB, LANES), 0) < SUB - 1
        for j in range(3):
            xs[j, 0:SUB] = hb[j, :, lanes].astype(F32)
            xs[j, SUB : SUB + rows] = p[j, :, lanes].astype(F32)
            xs[j, SUB + rows :] = ha[j, :, lanes].astype(F32)
        xs[3, SUB : SUB + rows] = u[:, lanes].astype(F32)
        xs[3, SUB + rows :] = ha[3, :, lanes].astype(F32)

        def mixed(j):
            tap = [spread(filt[j, i : i + 1, lanes]) for i in range(taps)]
            view = [xs[j, pl.ds(SUB + a, SUB, stride=run), :] for a in range(1 - taps, run)]
            return [
                added([tap[i] * view[a + taps - 1 - i] for i in range(taps)]) for a in range(run)
            ]

        decay = [spread(f1[n : n + 1, part]) for n in range(poles)]
        key, value = mixed(1), mixed(2)
        state = None
        for a in range(run):
            x = key[a] * value[a]
            xg[0, SUB * a : SUB * a + SUB, lanes] = x
            if a >= own:
                x = jnp.where(inside, x, 0.0)
            state = [x] * poles if a == 0 else [decay[n] * state[n] + x for n in range(poles)]
        for n in range(poles):
            blocks_e[n, :, lanes] = state[n]
            ends[0, which, n : n + 1, part] = jnp.sum(state[n] * we[n, :, part], axis=0, keepdims=True)
        query = mixed(0)
        state = None
        for a in range(run - 1, -1, -1):
            x = xs[3, pl.ds(SUB + a, SUB, stride=run), :] * query[a]
            xg[1, SUB * a : SUB * a + SUB, lanes] = x
            if a >= own:
                x = jnp.where(inside, x, 0.0)
            state = [x] * poles if a == run - 1 else [decay[n] * state[n] + x for n in range(poles)]
        for n in range(poles):
            blocks_a[n, :, lanes] = state[n]
            ends[1, which, n : n + 1, part] = jnp.sum(state[n] * wb[n, :, part], axis=0, keepdims=True)
        return carry

    lax.fori_loop(0, p.shape[2] // LANES, tile, 0)


def blocks_kernel(xg, blocks_e, blocks_a, near, skip, join_e, join_a, conv, from_e, from_a):
    run = xg.shape[1] // SUB
    rows = xg.shape[1] - SUB
    taps = near.shape[0] - run
    poles, groups = blocks_e.shape[0], near.shape[1]
    own = rows - run * (SUB - 1)
    tiles = groups // LANES

    def tile(lt, carry):
        lanes = pl.ds(pl.multiple_of(lt * LANES, LANES), LANES)
        part = pl.ds(pl.multiple_of(lax.rem(lt, tiles) * LANES, LANES), LANES)
        inside = lax.broadcasted_iota(jnp.int32, (SUB, LANES), 0) < SUB - 1
        gain = spread(skip[0:1, lanes])
        lag = [spread(near[taps + m : taps + m + 1, part]) for m in range(run)]
        lag[0] = lag[0] + gain
        x = [xg[0, SUB * a : SUB * a + SUB, lanes] for a in range(run)]
        for a in range(run):
            conv[0, SUB * a : SUB * a + SUB, lanes] = added([lag[m] * x[a - m] for m in range(a + 1)])
        x = [xg[1, SUB * a : SUB * a + SUB, lanes] for a in range(run)]
        masked = [x[a] if a < own else jnp.where(inside, x[a], 0.0) for a in range(run)]
        past = [jnp.where(inside, 0.0, gain)] + [
            jnp.where(inside, 0.0, -spread(near[taps - m : taps - m + 1, part]))
            for m in range(1, taps - 1)
        ]
        for a in range(run):
            terms = [lag[m] * masked[a + m] for m in range(run - a)]
            if own <= a < own + taps - 1:
                terms = terms + [past[m] * x[a - m] for m in range(a - own + 1)]
            conv[1, SUB * a : SUB * a + SUB, lanes] = added(terms)
        for n in range(poles):
            value = pltpu.roll(blocks_e[n, :, lanes], 1, 0) * join_e[0, n, :, part]
            for k, step in ((1, 1), (2, 2), (3, 4)):
                value = value + pltpu.roll(value, step, 0) * join_e[k, n, :, part]
            from_e[n, :, lanes] = value
            value = pltpu.roll(blocks_a[n, :, lanes], SUB - 1, 0) * join_a[0, n, :, part]
            for k, step in ((1, 1), (2, 2), (3, 4)):
                value = value + pltpu.roll(value, SUB - step, 0) * join_a[k, n, :, part]
            from_a[n, :, lanes] = value
        return carry

    lax.fori_loop(0, xg.shape[2] // LANES, tile, 0)


def final_kernel(
    p, hb, u, ha, conv, from_e, from_a, enter, arrive, filt, f1, cz, cy,
    output, grad_p, sums, ps, us, qs, gs, os,
):
    rows = p.shape[1]
    run = (rows + SUB) // SUB
    taps = filt.shape[1]
    poles, groups = f1.shape
    own = rows - run * (SUB - 1)
    tiles = groups // LANES

    def tile(lt, carry):
        lanes = pl.ds(pl.multiple_of(lt * LANES, LANES), LANES)
        part = pl.ds(pl.multiple_of(lax.rem(lt, tiles) * LANES, LANES), LANES)
        which = lt // tiles
        inside = lax.broadcasted_iota(jnp.int32, (SUB, LANES), 0) < SUB - 1
        for j in range(3):
            ps[j, 0:SUB] = hb[j, :, lanes].astype(F32)
            ps[j, SUB : SUB + rows] = p[j, :, lanes].astype(F32)
            ps[j, SUB + rows :] = ha[j, :, lanes].astype(F32)
        us[0:rows] = u[:, lanes].astype(F32)
        us[rows:] = ha[3, :, lanes].astype(F32)
        for j in range(3):
            tap = [spread(filt[j, i : i + 1, lanes]) for i in range(taps)]
            view = [ps[j, pl.ds(SUB + a, SUB, stride=run), :] for a in range(1 - taps, run)]
            for a in range(run):
                qs[j, SUB * a : SUB * a + SUB] = added(
                    [tap[i] * view[a + taps - 1 - i] for i in range(taps)]
                )
        decay = [spread(f1[n : n + 1, part]) for n in range(poles)]

        state = [
            from_e[n, :, lanes] + cz[n, :, part] * spread(enter[which, n : n + 1, part])
            for n in range(poles)
        ]
        skip_sum = None
        for a in range(run):
            at = slice(SUB * a, SUB * a + SUB)
            query, upstream = qs[0, at], us[pl.ds(a, SUB, stride=run), :]
            term = (qs[1, at] * qs[2, at]) * (query * upstream)
            if a >= own:
                term = jnp.where(inside, term, 0.0)
            skip_sum = term if a == 0 else skip_sum + term
            filtered = conv[0, at, lanes] + added(list(state))
            os[pl.ds(a, SUB, stride=run), :] = query * filtered
            gs[0, pl.ds(a, SUB, stride=run), :] = upstream * filtered
            if a + 1 < run:
                state = [state[n] * decay[n] for n in range(poles)]
        output[:, lanes] = os[0:rows].astype(BF16)

        state = [
            from_a[n, :, lanes] + cy[n, :, part] * spread(arrive[which, n : n + 1, part])
            for n in range(poles)
        ]
        for a in range(run - 1, -1, -1):
            at = slice(SUB * a, SUB * a + SUB)
            grad = conv[1, at, lanes] + added(list(state))
            gs[1, pl.ds(a, SUB, stride=run), :] = grad * qs[2, at]
            gs[2, pl.ds(a, SUB, stride=run), :] = grad * qs[1, at]
            if a:
                state = [state[n] * decay[n] for n in range(poles)]

        for j in range(3):
            tap = [spread(filt[j, i : i + 1, lanes]) for i in range(taps)]
            grads = [gs[j, pl.ds(a, SUB, stride=run), :] for a in range(run + taps - 1)]
            views = [ps[j, pl.ds(SUB + a, SUB, stride=run), :] for a in range(1 - taps, run)]
            sums_of = [None] * taps
            for a in range(run):
                total = added([tap[i] * grads[a + i] for i in range(taps)])
                os[pl.ds(a, SUB, stride=run), :] = total
                grad = grads[a] if a < own else jnp.where(inside, grads[a], 0.0)
                for i in range(taps):
                    term = grad * views[a + taps - 1 - i]
                    sums_of[i] = term if a == 0 else sums_of[i] + term
            grad_p[j, :, lanes] = os[0:rows].astype(BF16)
            for i in range(taps):
                at = j * taps + i
                sums[which, at : at + 1, part] = jnp.sum(sums_of[i], axis=0, keepdims=True)
        at = 3 * taps
        sums[which, at : at + 1, part] = jnp.sum(skip_sum, axis=0, keepdims=True)
        return carry

    lax.fori_loop(0, p.shape[2] // LANES, tile, 0)


def shifted(value, axis, steps):
    count = lax.axis_size(axis)
    first, last = (max(0, -steps), min(count, count - steps))
    return lax.ppermute(value, axis, [(source, source + steps) for source in range(first, last)])


def rotated(value, axis, steps):
    count = lax.axis_size(axis)
    return lax.ppermute(value, axis, [(s, (s + steps) % count) for s in range(count)])


def swapped(value):
    count = lax.axis_size("ctx")
    return lax.ppermute(value, "ctx", [(s, s ^ 1) for s in range(count)])


def joined(ends, f_all):
    core = lax.rem(lax.axis_index("ctx"), 2)
    half = ends.shape[1] // 2
    other = swapped(ends)
    first = core == 0
    mine = lax.dynamic_slice_in_dim(ends, core * half, half, 1)
    theirs = lax.dynamic_slice_in_dim(other, core * half, half, 1)
    one, two = jnp.where(first, mine, theirs), jnp.where(first, theirs, mine)
    return other, f_all * one[0] + two[0], one[1] + f_all * two[1]


def scanned(chip_e, chip_a, f_all, beside):
    chips = lax.axis_size("ctx") // 2
    f_chip = f_all * f_all
    before = after = None
    reach = 1
    kept = None
    while reach < chips:
        early, late = shifted(chip_e, "ctx", 2 * reach), shifted(chip_a, "ctx", -2 * reach)
        if 2 * reach >= chips:
            kept = beside(chip_e)
            (early, late), kept = lax.optimization_barrier(((early, late), kept))
        if before is None:
            before, after = early, late
        else:
            factor = f_chip ** (reach - 1)
            before, after = before + factor * early, after + factor * late
        factor = f_chip**reach
        chip_e, chip_a = chip_e + factor * early, chip_a + factor * late
        reach = 2 * reach
    return before, after, kept


def inward(other, before, after, f_all):
    first = lax.rem(lax.axis_index("ctx"), 2) == 0
    both = jnp.stack([before, after])
    found = swapped(both)
    both = jnp.concatenate([jnp.where(first, both, found), jnp.where(first, found, both)], axis=1)
    enter = jnp.where(first, both[0], f_all * both[0] + other[0])
    arrive = jnp.where(first, other[1] + f_all * both[1], both[1])
    return enter, arrive


def summed(value):
    index = lax.axis_index("ctx")
    core = lax.rem(index, 2)
    chip = index // 2
    chips = lax.axis_size("ctx") // 2
    dp = lax.axis_index("dp")
    parts = lax.axis_size("dp")
    half = value.shape[0] // 2
    keep = lax.dynamic_slice_in_dim(value, core * half, half, 0)
    give = lax.dynamic_slice_in_dim(value, (1 - core) * half, half, 0)
    value = keep + swapped(give)
    size = half // parts
    piece = lambda k: lax.dynamic_slice_in_dim(value, lax.rem(dp + k, parts) * size, size, 0)
    total = piece(0)
    for k in range(1, parts):
        total = total + rotated(piece(k), "dp", k)
    gathered = jnp.zeros((chips,) + total.shape, F32)
    put = lambda into, at, what: lax.dynamic_update_slice_in_dim(into, what[None], at, 0)
    gathered = put(gathered, chip, total)
    for k in range(1, chips):
        gathered = put(gathered, lax.rem(chip + chips - k, chips), rotated(total, "ctx", 2 * k))
    total = gathered[0]
    for k in range(1, chips):
        total = total + gathered[k]
    gathered = jnp.zeros((parts,) + total.shape, F32)
    gathered = put(gathered, dp, total)
    for k in range(1, parts):
        gathered = put(gathered, lax.rem(dp + parts - k, parts), rotated(total, "dp", k))
    mine = gathered.reshape((half,) + total.shape[1:])
    other = swapped(mine)
    first = core == 0
    return jnp.concatenate([jnp.where(first, mine, other), jnp.where(first, other, mine)], axis=0)


def local(projected, short_filter, residues, decay_rates, skip_gain, cotangent):
    rows = projected.shape[1]
    channels = projected.shape[3]
    taps = short_filter.shape[1]
    groups, poles = residues.shape
    width = channels // groups
    run = (rows + SUB) // SUB
    held = rows + SUB
    p = projected[0].transpose(1, 0, 2)
    u = cotangent[0]
    hb = shifted(p[:, rows - SUB :], "ctx", 1)
    ha = shifted(jnp.concatenate([p[:, :SUB], u[None, :SUB]], axis=0), "ctx", -1)

    rate = decay_rates.T
    weight = residues.T
    sub = np.arange(SUB)
    powers = np.stack([run * (7 - sub) - SUB, run * sub, 1 + run * sub, rows - run * (sub + 1) + 1])
    table = jnp.exp(-rate[None, :, None, :] * powers.astype(np.float32)[:, None, :, None])
    we, wb = table[0], table[1]
    cz, cy = weight[:, None, :] * table[2], weight[:, None, :] * table[3]
    f1 = jnp.exp(-rate)
    f_all = jnp.exp(-rate * rows)
    steps = np.array([1, run, 2 * run, 4 * run], np.float32)
    factor = jnp.exp(-rate[None] * steps[:, None, None])
    factor = jnp.concatenate([weight[None] * factor[:1], factor[1:]], axis=0)
    reach = np.array([1, 1, 2, 4])[:, None]
    down, up = sub[None] >= reach, sub[None] < SUB - reach
    join_e = jnp.where(down[:, None, :, None], factor[:, :, None, :], 0.0)
    join_a = jnp.where(up[:, None, :, None], factor[:, :, None, :], 0.0)
    close = np.arange(-taps, run).astype(np.float32)
    near = jnp.sum(weight[:, None, :] * jnp.exp(-rate[:, None, :] * close[None, :, None]), axis=0)

    each = 2 if width % 2 == 0 else 1

    def by_w(*shape):
        axis = len(shape)
        return pl.BlockSpec(shape + (each * groups,), lambda w: (0,) * axis + (w,))

    def per_w(*shape):
        return pl.BlockSpec((each,) + shape, lambda w: (w,) + (0,) * len(shape))

    def fixed(value):
        return pl.BlockSpec(
            value.shape, lambda w: (0,) * value.ndim, pipeline_mode=pl.Buffered(1)
        )

    params = pltpu.CompilerParams(vmem_limit_bytes=20 * 1024 * 1024)
    shape_of = jax.ShapeDtypeStruct
    state_shape = shape_of((poles, SUB, channels), F32)
    xg, blocks_e, blocks_a, ends = pl.pallas_call(
        states_kernel,
        grid=(width // each,),
        in_specs=[
            by_w(3, rows), by_w(3, SUB), by_w(4, SUB), by_w(rows), by_w(3, taps),
            fixed(f1), fixed(we), fixed(wb),
        ],
        out_specs=[
            by_w(2, held), by_w(poles, SUB), by_w(poles, SUB),
            pl.BlockSpec((2, each, poles, groups), lambda w: (0, w, 0, 0)),
        ],
        out_shape=[
            shape_of((2, held, channels), F32), state_shape, state_shape,
            shape_of((2, width, poles, groups), F32),
        ],
        scratch_shapes=[pltpu.VMEM((4, held + SUB, LANES), F32)],
        compiler_params=params,
        name="states",
    )(p, hb, ha, u, short_filter, f1, we, wb)

    def blocks(chip_e):
        close, _ = lax.optimization_barrier((near, chip_e))
        return pl.pallas_call(
            blocks_kernel,
            grid=(width // each,),
            in_specs=[
                by_w(2, held), by_w(poles, SUB), by_w(poles, SUB), fixed(near), by_w(1),
                fixed(join_e), fixed(join_a),
            ],
            out_specs=[by_w(2, held), by_w(poles, SUB), by_w(poles, SUB)],
            out_shape=[shape_of((2, held, channels), F32), state_shape, state_shape],
            input_output_aliases={0: 0, 1: 1, 2: 2},
            compiler_params=params,
            cost_estimate=pl.CostEstimate(
                flops=60 * rows * channels, bytes_accessed=35 * 2**20, transcendentals=0
            ),
            name="blocks",
        )(xg, blocks_e, blocks_a, close, skip_gain[None], join_e, join_a)

    other, chip_e, chip_a = joined(ends, f_all)
    before, after, (conv, from_e, from_a) = scanned(chip_e, chip_a, f_all, blocks)
    enter, arrive = inward(other, before, after, f_all)

    count = 3 * taps + 3
    scratch = [
        pltpu.VMEM((3, held + SUB, LANES), F32),
        pltpu.VMEM((held, LANES), F32),
        pltpu.VMEM((3, held, LANES), F32),
        pltpu.VMEM((3, held + SUB, LANES), F32),
        pltpu.VMEM((held, LANES), F32),
    ]
    output, grad_p, sums = pl.pallas_call(
        final_kernel,
        grid=(width // each,),
        in_specs=[
            by_w(3, rows), by_w(3, SUB), by_w(rows), by_w(4, SUB), by_w(2, held),
            by_w(poles, SUB), by_w(poles, SUB), per_w(poles, groups), per_w(poles, groups),
            by_w(3, taps), fixed(f1), fixed(cz), fixed(cy),
        ],
        out_specs=[by_w(rows), by_w(3, rows), per_w(count, groups)],
        out_shape=[
            shape_of((rows, channels), BF16),
            shape_of((3, rows, channels), BF16),
            shape_of((width, count, groups), F32),
        ],
        scratch_shapes=scratch,
        compiler_params=params,
        name="final",
    )(p, hb, u, ha, conv, from_e, from_a, enter, arrive, short_filter, f1, cz, cy)

    total = summed(sums).transpose(1, 0, 2).reshape(count, channels)
    grad_short = total[: 3 * taps].reshape(3, taps, channels)
    grad_skip = total[3 * taps]
    return output[None], grad_p.transpose(1, 0, 2)[None], grad_short, grad_skip


def solution(mesh):
    placed = (P("dp", "ctx", None, None), P(), P(), P(), P(), P("dp", "ctx", None))
    return jax.shard_map(
        local,
        mesh=mesh,
        in_specs=placed,
        out_specs=(P("dp", "ctx", None), P("dp", "ctx", None, None), P(), P()),
        check_vma=False,
    )
```

```python
import functools

import jax
import jax.numpy as jnp
import numpy as np
from jax import lax
from jax.experimental import pallas as pl
from jax.experimental.pallas import tpu as pltpu
from jax.sharding import PartitionSpec as P

LANES = 128
SUB = 8
F32 = jnp.float32
BF16 = jnp.bfloat16


def spread(row):
    return jnp.broadcast_to(row, (SUB, LANES))


def added(terms):
    while len(terms) > 1:
        pairs = [terms[k] + terms[k + 1] for k in range(0, len(terms) - 1, 2)]
        terms = pairs + terms[len(terms) - len(terms) % 2 :]
    return terms[0]


def folded(values):
    row = lax.broadcasted_iota(jnp.int32, (SUB, LANES), 0)
    upper = row < 4
    values = [
        jnp.where(upper, values[n], values[n + 4])
        + pltpu.roll(jnp.where(upper, values[n + 4], values[n]), 4, 0)
        for n in range(4)
    ]
    for step in (2, 1):
        even = (row // step) % 2 == 0
        values = [
            jnp.where(
                even,
                values[n] + pltpu.roll(values[n], SUB - step, 0),
                values[n + step] + pltpu.roll(values[n + step], step, 0),
            )
            for n in range(step)
        ]
    return values[0]


def states_kernel(p, hb, ha, u, filt, f1, we, wb, qkv, xg, blocks_e, blocks_a, ends, xs):
    rows = p.shape[1]
    run = (rows + SUB) // SUB
    taps = filt.shape[1]
    poles, groups = f1.shape
    own = rows - run * (SUB - 1)
    tiles = groups // LANES

    def tile(lt, carry):
        lanes = pl.ds(pl.multiple_of(lt * LANES, LANES), LANES)
        part = pl.ds(pl.multiple_of(lax.rem(lt, tiles) * LANES, LANES), LANES)
        which = lt // tiles
        inside = lax.broadcasted_iota(jnp.int32, (SUB, LANES), 0) < SUB - 1
        for j in range(3):
            xs[j, 0:SUB] = hb[j, :, lanes].astype(F32)
            xs[j, SUB : SUB + rows] = p[j, :, lanes].astype(F32)
            xs[j, SUB + rows :] = ha[j, :, lanes].astype(F32)
        xs[3, SUB : SUB + rows] = u[:, lanes].astype(F32)
        xs[3, SUB + rows :] = ha[3, :, lanes].astype(F32)

        def mixed(j):
            tap = [spread(filt[j, i : i + 1, lanes]) for i in range(taps)]
            view = [xs[j, pl.ds(SUB + a, SUB, stride=run), :] for a in range(1 - taps, run)]
            return [
                added([tap[i] * view[a + taps - 1 - i] for i in range(taps)]) for a in range(run)
            ]

        decay = [spread(f1[n : n + 1, part]) for n in range(poles)]
        for j in (1, 2, 0):
            for a, total in enumerate(mixed(j)):
                at = slice(SUB * a, SUB * a + SUB)
                qkv[j, at, lanes] = total
                if j == 2:
                    xg[0, at, lanes] = qkv[1, at, lanes] * total
                if j == 0:
                    xg[1, at, lanes] = xs[3, pl.ds(SUB + a, SUB, stride=run), :] * total
        for side, order, weight, blocks in (
            (0, range(run), we, blocks_e),
            (1, range(run - 1, -1, -1), wb, blocks_a),
        ):
            state = None
            for a in order:
                x = xg[side, SUB * a : SUB * a + SUB, lanes]
                if a >= own:
                    x = jnp.where(inside, x, 0.0)
                state = [x] * poles if state is None else [decay[n] * state[n] + x for n in range(poles)]
            for n in range(poles):
                blocks[n, :, lanes] = state[n]
            state = [state[n] * weight[n, :, part] for n in range(poles)]
            for n in range(0, poles, SUB):
                ends[side, which, n : n + SUB, part] = folded(state[n : n + SUB])
        return carry

    lax.fori_loop(0, p.shape[2] // LANES, tile, 0)


def blocks_kernel(xg, blocks_e, blocks_a, near, skip, join_e, join_a, conv, from_e, from_a):
    run = xg.shape[1] // SUB
    rows = xg.shape[1] - SUB
    taps = near.shape[0] - run
    poles, groups = blocks_e.shape[0], near.shape[1]
    own = rows - run * (SUB - 1)
    tiles = groups // LANES

    def tile(lt, carry):
        lanes = pl.ds(pl.multiple_of(lt * LANES, LANES), LANES)
        part = pl.ds(pl.multiple_of(lax.rem(lt, tiles) * LANES, LANES), LANES)
        inside = lax.broadcasted_iota(jnp.int32, (SUB, LANES), 0) < SUB - 1
        gain = spread(skip[0:1, lanes])
        lag = [spread(near[taps + m : taps + m + 1, part]) for m in range(run)]
        lag[0] = lag[0] + gain
        x = [xg[0, SUB * a : SUB * a + SUB, lanes] for a in range(run)]
        for a in range(run):
            conv[0, SUB * a : SUB * a + SUB, lanes] = added([lag[m] * x[a - m] for m in range(a + 1)])
        x = [xg[1, SUB * a : SUB * a + SUB, lanes] for a in range(run)]
        masked = [x[a] if a < own else jnp.where(inside, x[a], 0.0) for a in range(run)]
        past = [jnp.where(inside, 0.0, gain)] + [
            jnp.where(inside, 0.0, -spread(near[taps - m : taps - m + 1, part]))
            for m in range(1, taps - 1)
        ]
        for a in range(run):
            terms = [lag[m] * masked[a + m] for m in range(run - a)]
            if own <= a < own + taps - 1:
                terms = terms + [past[m] * x[a - m] for m in range(a - own + 1)]
            conv[1, SUB * a : SUB * a + SUB, lanes] = added(terms)
        for n in range(poles):
            value = pltpu.roll(blocks_e[n, :, lanes], 1, 0) * join_e[0, n, :, part]
            for k, step in ((1, 1), (2, 2), (3, 4)):
                value = value + pltpu.roll(value, step, 0) * join_e[k, n, :, part]
            from_e[n, :, lanes] = value
            value = pltpu.roll(blocks_a[n, :, lanes], SUB - 1, 0) * join_a[0, n, :, part]
            for k, step in ((1, 1), (2, 2), (3, 4)):
                value = value + pltpu.roll(value, SUB - step, 0) * join_a[k, n, :, part]
            from_a[n, :, lanes] = value
        return carry

    lax.fori_loop(0, xg.shape[2] // LANES, tile, 0)


def final_kernel(
    p, hb, u, ha, qkv, conv, from_e, from_a, enter, arrive, filt, f1, cz, cy,
    output, grad_p, sums, ps, us, gs, os,
):
    rows = p.shape[1]
    run = (rows + SUB) // SUB
    taps = filt.shape[1]
    poles, groups = f1.shape
    own = rows - run * (SUB - 1)
    tiles = groups // LANES

    def tile(lt, carry):
        lanes = pl.ds(pl.multiple_of(lt * LANES, LANES), LANES)
        part = pl.ds(pl.multiple_of(lax.rem(lt, tiles) * LANES, LANES), LANES)
        which = lt // tiles
        inside = lax.broadcasted_iota(jnp.int32, (SUB, LANES), 0) < SUB - 1
        for j in range(3):
            ps[j, 0:SUB] = hb[j, :, lanes].astype(F32)
            ps[j, SUB : SUB + rows] = p[j, :, lanes].astype(F32)
            ps[j, SUB + rows :] = ha[j, :, lanes].astype(F32)
        us[0:rows] = u[:, lanes].astype(F32)
        us[rows:] = ha[3, :, lanes].astype(F32)
        decay = [spread(f1[n : n + 1, part]) for n in range(poles)]

        state = [
            from_e[n, :, lanes] + cz[n, :, part] * spread(enter[which, n : n + 1, part])
            for n in range(poles)
        ]
        skip_sum = None
        for a in range(run):
            at = slice(SUB * a, SUB * a + SUB)
            query, upstream = qkv[0, at, lanes], us[pl.ds(a, SUB, stride=run), :]
            term = (qkv[1, at, lanes] * qkv[2, at, lanes]) * (query * upstream)
            if a >= own:
                term = jnp.where(inside, term, 0.0)
            skip_sum = term if a == 0 else skip_sum + term
            filtered = conv[0, at, lanes] + added(list(state))
            os[pl.ds(a, SUB, stride=run), :] = query * filtered
            gs[0, pl.ds(a, SUB, stride=run), :] = upstream * filtered
            if a + 1 < run:
                state = [state[n] * decay[n] for n in range(poles)]
        output[:, lanes] = os[0:rows].astype(BF16)

        state = [
            from_a[n, :, lanes] + cy[n, :, part] * spread(arrive[which, n : n + 1, part])
            for n in range(poles)
        ]
        for a in range(run - 1, -1, -1):
            at = slice(SUB * a, SUB * a + SUB)
            grad = conv[1, at, lanes] + added(list(state))
            gs[1, pl.ds(a, SUB, stride=run), :] = grad * qkv[2, at, lanes]
            gs[2, pl.ds(a, SUB, stride=run), :] = grad * qkv[1, at, lanes]
            if a:
                state = [state[n] * decay[n] for n in range(poles)]

        rest = []
        for j in range(3):
            tap = [spread(filt[j, i : i + 1, lanes]) for i in range(taps)]
            grads = [gs[j, pl.ds(a, SUB, stride=run), :] for a in range(run + taps - 1)]
            views = [ps[j, pl.ds(SUB + a, SUB, stride=run), :] for a in range(1 - taps, run)]
            sums_of = [None] * taps
            for a in range(run):
                total = added([tap[i] * grads[a + i] for i in range(taps)])
                os[pl.ds(a, SUB, stride=run), :] = total
                grad = grads[a] if a < own else jnp.where(inside, grads[a], 0.0)
                for i in range(taps):
                    term = grad * views[a + taps - 1 - i]
                    sums_of[i] = term if a == 0 else sums_of[i] + term
            grad_p[j, :, lanes] = os[0:rows].astype(BF16)
            rest = rest + sums_of
        rest = rest + [skip_sum] + [jnp.zeros((SUB, LANES), F32)] * (-(len(rest) + 1) % SUB)
        for n in range(0, len(rest), SUB):
            sums[which, n : n + SUB, part] = folded(rest[n : n + SUB])
        return carry

    lax.fori_loop(0, p.shape[2] // LANES, tile, 0)


def shifted(value, axis, steps):
    count = lax.axis_size(axis)
    first, last = (max(0, -steps), min(count, count - steps))
    return lax.ppermute(value, axis, [(source, source + steps) for source in range(first, last)])


def swapped(value):
    count = lax.axis_size("ctx")
    return lax.ppermute(value, "ctx", [(s, s ^ 1) for s in range(count)])


def joined(ends, f_all):
    core = lax.rem(lax.axis_index("ctx"), 2)
    half = ends.shape[1] // 2
    other = swapped(ends)
    first = core == 0
    mine = lax.dynamic_slice_in_dim(ends, core * half, half, 1)
    theirs = lax.dynamic_slice_in_dim(other, core * half, half, 1)
    one, two = jnp.where(first, mine, theirs), jnp.where(first, theirs, mine)
    return other, f_all * one[0] + two[0], one[1] + f_all * two[1]


def paired(value, axis, step, lines=None):
    count = lax.axis_size(axis)
    return lax.ppermute(value, axis, [(source, source ^ step) for source in lines or range(count)])


def scanned(chip_e, chip_a, f_all, beside):
    chips = lax.axis_size("ctx") // 2
    f_chip = f_all * f_all
    if chips == 4:
        odd = lax.rem(lax.axis_index("ctx") // 2, 2) == 1
        sent = jnp.where(odd, chip_a, chip_e)
        first = paired(sent, "ctx", 2)
        kept = beside[0](sent, None)
        first, kept = lax.optimization_barrier((first, kept))
        sent = jnp.where(odd, chip_e, chip_a) + f_chip * first
        near = lax.ppermute(sent, "ctx", [(2, 4), (3, 5), (4, 2), (5, 3)])
        far = lax.ppermute(sent, "ctx", [(2, 6), (3, 7), (4, 0), (5, 1)])
        kept = beside[1](sent, kept)
        near, far, kept = lax.optimization_barrier((near, far, kept))
        far = first + f_chip * far
        return jnp.where(odd, far, near), jnp.where(odd, near, far), kept
    kept = beside[1](chip_e, beside[0](chip_e, None))
    before, after = jnp.zeros_like(chip_e), jnp.zeros_like(chip_a)
    reach = 1
    while reach < chips:
        early, late = shifted(chip_e, "ctx", 2 * reach), shifted(chip_a, "ctx", -2 * reach)
        factor = f_chip ** (reach - 1)
        before, after = before + factor * early, after + factor * late
        factor = f_chip**reach
        chip_e, chip_a = chip_e + factor * early, chip_a + factor * late
        reach = 2 * reach
    return before, after, kept


def inward(other, before, after, f_all):
    first = lax.rem(lax.axis_index("ctx"), 2) == 0
    both = jnp.stack([before, after])
    found = swapped(both)
    both = jnp.concatenate([jnp.where(first, both, found), jnp.where(first, found, both)], axis=1)
    enter = jnp.where(first, both[0], f_all * both[0] + other[0])
    arrive = jnp.where(first, other[1] + f_all * both[1], both[1])
    return enter, arrive


def summed(value):
    index, dp = lax.axis_index("ctx"), lax.axis_index("dp")
    steps = [("ctx", 1, lax.rem(index, 2))]
    reach = 1
    while reach < lax.axis_size("dp"):
        steps.append(("dp", reach, lax.rem(dp // reach, 2)))
        reach = 2 * reach
    for axis, step, side in steps:
        half = value.shape[0] // 2
        keep = lax.dynamic_slice_in_dim(value, side * half, half, 0)
        give = lax.dynamic_slice_in_dim(value, (1 - side) * half, half, 0)
        value = keep + paired(give, axis, step)
    reach = 2
    while reach < lax.axis_size("ctx"):
        value = value + paired(value, "ctx", reach)
        reach = 2 * reach
    for axis, step, side in reversed(steps):
        other = paired(value, axis, step)
        low = side == 0
        value = jnp.concatenate([jnp.where(low, value, other), jnp.where(low, other, value)], axis=0)
    return value


def local(projected, short_filter, residues, decay_rates, skip_gain, cotangent):
    rows = projected.shape[1]
    channels = projected.shape[3]
    taps = short_filter.shape[1]
    groups, poles = residues.shape
    width = channels // groups
    run = (rows + SUB) // SUB
    held = rows + SUB
    p = projected[0].transpose(1, 0, 2)
    u = cotangent[0]
    hb = shifted(p[:, rows - SUB :], "ctx", 1)
    ha = shifted(jnp.concatenate([p[:, :SUB], u[None, :SUB]], axis=0), "ctx", -1)

    rate = decay_rates.T
    weight = residues.T
    sub = np.arange(SUB)
    powers = np.stack([run * (7 - sub) - SUB, run * sub, 1 + run * sub, rows - run * (sub + 1) + 1])
    table = jnp.exp(-rate[None, :, None, :] * powers.astype(np.float32)[:, None, :, None])
    we, wb = table[0], table[1]
    cz, cy = weight[:, None, :] * table[2], weight[:, None, :] * table[3]
    f1 = jnp.exp(-rate)
    f_all = jnp.exp(-rate * rows)
    steps = np.array([1, run, 2 * run, 4 * run], np.float32)
    factor = jnp.exp(-rate[None] * steps[:, None, None])
    factor = jnp.concatenate([weight[None] * factor[:1], factor[1:]], axis=0)
    reach = np.array([1, 1, 2, 4])[:, None]
    down, up = sub[None] >= reach, sub[None] < SUB - reach
    join_e = jnp.where(down[:, None, :, None], factor[:, :, None, :], 0.0)
    join_a = jnp.where(up[:, None, :, None], factor[:, :, None, :], 0.0)
    close = np.arange(-taps, run).astype(np.float32)
    near = jnp.sum(weight[:, None, :] * jnp.exp(-rate[:, None, :] * close[None, :, None]), axis=0)

    each = 2 if width % 2 == 0 else 1

    def by_w(*shape):
        axis = len(shape)
        return pl.BlockSpec(shape + (each * groups,), lambda w: (0,) * axis + (w,))

    def per_w(*shape):
        return pl.BlockSpec((each,) + shape, lambda w: (w,) + (0,) * len(shape))

    def fixed(value):
        return pl.BlockSpec(
            value.shape, lambda w: (0,) * value.ndim, pipeline_mode=pl.Buffered(1)
        )

    params = pltpu.CompilerParams(vmem_limit_bytes=48 * 1024 * 1024)
    shape_of = jax.ShapeDtypeStruct
    state_shape = shape_of((poles, SUB, channels), F32)
    qkv, xg, blocks_e, blocks_a, ends = pl.pallas_call(
        states_kernel,
        grid=(width // each,),
        in_specs=[
            by_w(3, rows), by_w(3, SUB), by_w(4, SUB), by_w(rows), by_w(3, taps),
            fixed(f1), fixed(we), fixed(wb),
        ],
        out_specs=[
            by_w(3, held), by_w(2, held), by_w(poles, SUB), by_w(poles, SUB),
            pl.BlockSpec((2, each, poles, groups), lambda w: (0, w, 0, 0)),
        ],
        out_shape=[
            shape_of((3, held, channels), F32), shape_of((2, held, channels), F32),
            state_shape, state_shape, shape_of((2, width, poles, groups), F32),
        ],
        scratch_shapes=[pltpu.VMEM((4, held + SUB, LANES), F32)],
        compiler_params=params,
        name="states",
    )(p, hb, ha, u, short_filter, f1, we, wb)

    def blocks(first, last):
        def at_w(*shape):
            axis = len(shape)
            return pl.BlockSpec(shape + (each * groups,), lambda w: (0,) * axis + (w + first,))

        def call(sent, kept):
            close, _ = lax.optimization_barrier((near, sent))
            return pl.pallas_call(
                blocks_kernel,
                grid=(last - first,),
                in_specs=[
                    at_w(2, held), at_w(poles, SUB), at_w(poles, SUB), fixed(near), at_w(1),
                    fixed(join_e), fixed(join_a),
                ],
                out_specs=[at_w(2, held), at_w(poles, SUB), at_w(poles, SUB)],
                out_shape=[shape_of((2, held, channels), F32), state_shape, state_shape],
                input_output_aliases={0: 0, 1: 1, 2: 2},
                compiler_params=params,
                cost_estimate=pl.CostEstimate(
                    flops=60 * rows * channels, bytes_accessed=35 * 2**20, transcendentals=0
                ),
                name="blocks",
            )(*(kept or (xg, blocks_e, blocks_a)), close, skip_gain[None], join_e, join_a)

        return call

    steps = width // each
    cut = (steps + 1) // 3
    other, chip_e, chip_a = joined(ends, f_all)
    before, after, (conv, from_e, from_a) = scanned(
        chip_e, chip_a, f_all, (blocks(0, cut), blocks(cut, steps))
    )
    enter, arrive = inward(other, before, after, f_all)

    count = 3 * taps + 3
    scratch = [
        pltpu.VMEM((3, held + SUB, LANES), F32),
        pltpu.VMEM((held, LANES), F32),
        pltpu.VMEM((3, held + SUB, LANES), F32),
        pltpu.VMEM((held, LANES), F32),
    ]
    output, grad_p, sums = pl.pallas_call(
        final_kernel,
        grid=(width // each,),
        in_specs=[
            by_w(3, rows), by_w(3, SUB), by_w(rows), by_w(4, SUB), by_w(3, held), by_w(2, held),
            by_w(poles, SUB), by_w(poles, SUB), per_w(poles, groups), per_w(poles, groups),
            by_w(3, taps), fixed(f1), fixed(cz), fixed(cy),
        ],
        out_specs=[by_w(rows), by_w(3, rows), per_w(count, groups)],
        out_shape=[
            shape_of((rows, channels), BF16),
            shape_of((3, rows, channels), BF16),
            shape_of((width, count, groups), F32),
        ],
        scratch_shapes=scratch,
        compiler_params=params,
        name="final",
    )(p, hb, u, ha, qkv, conv, from_e, from_a, enter, arrive, short_filter, f1, cz, cy)

    total = summed(sums).transpose(1, 0, 2).reshape(count, channels)
    grad_short = total[: 3 * taps].reshape(3, taps, channels)
    grad_skip = total[3 * taps]
    return output[None], grad_p.transpose(1, 0, 2)[None], grad_short, grad_skip


def solution(mesh):
    placed = (P("dp", "ctx", None, None), P(), P(), P(), P(), P("dp", "ctx", None))
    return jax.shard_map(
        local,
        mesh=mesh,
        in_specs=placed,
        out_specs=(P("dp", "ctx", None), P("dp", "ctx", None, None), P(), P()),
        check_vma=False,
    )
```

```python
import functools

import jax
import jax.numpy as jnp
import numpy as np
from jax import lax
from jax.experimental import pallas as pl
from jax.experimental.pallas import tpu as pltpu
from jax.sharding import PartitionSpec as P

LANES = 128
SUB = 8
F32 = jnp.float32
BF16 = jnp.bfloat16


def spread(row):
    return jnp.broadcast_to(row, (SUB, LANES))


def added(terms):
    while len(terms) > 1:
        pairs = [terms[k] + terms[k + 1] for k in range(0, len(terms) - 1, 2)]
        terms = pairs + terms[len(terms) - len(terms) % 2 :]
    return terms[0]


def folded(values):
    row = lax.broadcasted_iota(jnp.int32, (SUB, LANES), 0)
    upper = row < 4
    values = [
        jnp.where(upper, values[n], values[n + 4])
        + pltpu.roll(jnp.where(upper, values[n + 4], values[n]), 4, 0)
        for n in range(4)
    ]
    for step in (2, 1):
        even = (row // step) % 2 == 0
        values = [
            jnp.where(
                even,
                values[n] + pltpu.roll(values[n], SUB - step, 0),
                values[n + step] + pltpu.roll(values[n + step], step, 0),
            )
            for n in range(step)
        ]
    return values[0]


def states_kernel(p, hb, ha, u, filt, f1, we, wb, qkv, xg, blocks_e, blocks_a, ends, xs):
    rows = p.shape[1]
    run = (rows + SUB) // SUB
    taps = filt.shape[1]
    poles, groups = f1.shape
    own = rows - run * (SUB - 1)
    tiles = groups // LANES

    def tile(lt, carry):
        lanes = pl.ds(pl.multiple_of(lt * LANES, LANES), LANES)
        part = pl.ds(pl.multiple_of(lax.rem(lt, tiles) * LANES, LANES), LANES)
        which = lt // tiles
        inside = lax.broadcasted_iota(jnp.int32, (SUB, LANES), 0) < SUB - 1
        for j in range(3):
            xs[j, 0:SUB] = hb[j, :, lanes].astype(F32)
            xs[j, SUB : SUB + rows] = p[j, :, lanes].astype(F32)
            xs[j, SUB + rows :] = ha[j, :, lanes].astype(F32)
        xs[3, SUB : SUB + rows] = u[:, lanes].astype(F32)
        xs[3, SUB + rows :] = ha[3, :, lanes].astype(F32)

        def mixed(j):
            tap = [spread(filt[j, i : i + 1, lanes]) for i in range(taps)]
            view = [xs[j, pl.ds(SUB + a, SUB, stride=run), :] for a in range(1 - taps, run)]
            return [
                added([tap[i] * view[a + taps - 1 - i] for i in range(taps)]) for a in range(run)
            ]

        decay = [spread(f1[n : n + 1, part]) for n in range(poles)]
        for j in (1, 2, 0):
            for a, total in enumerate(mixed(j)):
                at = slice(SUB * a, SUB * a + SUB)
                qkv[j, at, lanes] = total
                if j == 2:
                    xg[0, at, lanes] = qkv[1, at, lanes] * total
                if j == 0:
                    xg[1, at, lanes] = xs[3, pl.ds(SUB + a, SUB, stride=run), :] * total
        for side, order, weight, blocks in (
            (0, range(run), we, blocks_e),
            (1, range(run - 1, -1, -1), wb, blocks_a),
        ):
            state = None
            for a in order:
                x = xg[side, SUB * a : SUB * a + SUB, lanes]
                if a >= own:
                    x = jnp.where(inside, x, 0.0)
                state = [x] * poles if state is None else [decay[n] * state[n] + x for n in range(poles)]
            for n in range(poles):
                blocks[n, :, lanes] = state[n]
            state = [state[n] * weight[n, :, part] for n in range(poles)]
            for n in range(0, poles, SUB):
                ends[side, which, n : n + SUB, part] = folded(state[n : n + SUB])
        return carry

    lax.fori_loop(0, p.shape[2] // LANES, tile, 0)


def blocks_kernel(xg, blocks_e, blocks_a, near, skip, join_e, join_a, conv, from_e, from_a):
    run = xg.shape[1] // SUB
    rows = xg.shape[1] - SUB
    taps = near.shape[0] - run
    poles, groups = blocks_e.shape[0], near.shape[1]
    own = rows - run * (SUB - 1)
    tiles = groups // LANES

    def tile(lt, carry):
        lanes = pl.ds(pl.multiple_of(lt * LANES, LANES), LANES)
        part = pl.ds(pl.multiple_of(lax.rem(lt, tiles) * LANES, LANES), LANES)
        inside = lax.broadcasted_iota(jnp.int32, (SUB, LANES), 0) < SUB - 1
        gain = spread(skip[0:1, lanes])
        lag = [spread(near[taps + m : taps + m + 1, part]) for m in range(run)]
        lag[0] = lag[0] + gain
        x = [xg[0, SUB * a : SUB * a + SUB, lanes] for a in range(run)]
        for a in range(run):
            conv[0, SUB * a : SUB * a + SUB, lanes] = added([lag[m] * x[a - m] for m in range(a + 1)])
        x = [xg[1, SUB * a : SUB * a + SUB, lanes] for a in range(run)]
        masked = [x[a] if a < own else jnp.where(inside, x[a], 0.0) for a in range(run)]
        past = [jnp.where(inside, 0.0, gain)] + [
            jnp.where(inside, 0.0, -spread(near[taps - m : taps - m + 1, part]))
            for m in range(1, taps - 1)
        ]
        for a in range(run):
            terms = [lag[m] * masked[a + m] for m in range(run - a)]
            if own <= a < own + taps - 1:
                terms = terms + [past[m] * x[a - m] for m in range(a - own + 1)]
            conv[1, SUB * a : SUB * a + SUB, lanes] = added(terms)
        for n in range(poles):
            value = pltpu.roll(blocks_e[n, :, lanes], 1, 0) * join_e[0, n, :, part]
            for k, step in ((1, 1), (2, 2), (3, 4)):
                value = value + pltpu.roll(value, step, 0) * join_e[k, n, :, part]
            from_e[n, :, lanes] = value
            value = pltpu.roll(blocks_a[n, :, lanes], SUB - 1, 0) * join_a[0, n, :, part]
            for k, step in ((1, 1), (2, 2), (3, 4)):
                value = value + pltpu.roll(value, SUB - step, 0) * join_a[k, n, :, part]
            from_a[n, :, lanes] = value
        return carry

    lax.fori_loop(0, xg.shape[2] // LANES, tile, 0)


def final_kernel(
    core, p, hb, u, ha, qkv, conv, from_e, from_a, both, found, other, filt, f1, f_all, cz, cy,
    output, grad_p, sums, ps, us, gs, os, es,
):
    rows = p.shape[1]
    run = (rows + SUB) // SUB
    taps = filt.shape[1]
    poles, groups = f1.shape
    own = rows - run * (SUB - 1)
    tiles = groups // LANES
    first = core[0] == 0
    halves = pl.num_programs(0) // 2
    kept = (pl.program_id(0) < halves) == first

    def tile(lt, carry):
        lanes = pl.ds(pl.multiple_of(lt * LANES, LANES), LANES)
        part = pl.ds(pl.multiple_of(lax.rem(lt, tiles) * LANES, LANES), LANES)
        which = lt // tiles
        inside = lax.broadcasted_iota(jnp.int32, (SUB, LANES), 0) < SUB - 1
        for side in range(2):
            far = jnp.where(kept, both[side, which, :, part], found[side, which, :, part])
            close = other[side, which, :, part] + f_all[:, part] * far
            es[side] = jnp.where(first == (side == 0), far, close)
        for j in range(3):
            ps[j, 0:SUB] = hb[j, :, lanes].astype(F32)
            ps[j, SUB : SUB + rows] = p[j, :, lanes].astype(F32)
            ps[j, SUB + rows :] = ha[j, :, lanes].astype(F32)
        us[0:rows] = u[:, lanes].astype(F32)
        us[rows:] = ha[3, :, lanes].astype(F32)
        decay = [spread(f1[n : n + 1, part]) for n in range(poles)]

        state = [
            from_e[n, :, lanes] + cz[n, :, part] * spread(es[0, n : n + 1])
            for n in range(poles)
        ]
        skip_sum = None
        for a in range(run):
            at = slice(SUB * a, SUB * a + SUB)
            query, upstream = qkv[0, at, lanes], us[pl.ds(a, SUB, stride=run), :]
            term = (qkv[1, at, lanes] * qkv[2, at, lanes]) * (query * upstream)
            if a >= own:
                term = jnp.where(inside, term, 0.0)
            skip_sum = term if a == 0 else skip_sum + term
            filtered = conv[0, at, lanes] + added(list(state))
            os[pl.ds(a, SUB, stride=run), :] = query * filtered
            gs[0, pl.ds(a, SUB, stride=run), :] = upstream * filtered
            if a + 1 < run:
                state = [state[n] * decay[n] for n in range(poles)]
        output[:, lanes] = os[0:rows].astype(BF16)

        state = [
            from_a[n, :, lanes] + cy[n, :, part] * spread(es[1, n : n + 1])
            for n in range(poles)
        ]
        for a in range(run - 1, -1, -1):
            at = slice(SUB * a, SUB * a + SUB)
            grad = conv[1, at, lanes] + added(list(state))
            gs[1, pl.ds(a, SUB, stride=run), :] = grad * qkv[2, at, lanes]
            gs[2, pl.ds(a, SUB, stride=run), :] = grad * qkv[1, at, lanes]
            if a:
                state = [state[n] * decay[n] for n in range(poles)]

        rest = []
        for j in range(3):
            tap = [spread(filt[j, i : i + 1, lanes]) for i in range(taps)]
            grads = [gs[j, pl.ds(a, SUB, stride=run), :] for a in range(run + taps - 1)]
            views = [ps[j, pl.ds(SUB + a, SUB, stride=run), :] for a in range(1 - taps, run)]
            sums_of = [None] * taps
            for a in range(run):
                total = added([tap[i] * grads[a + i] for i in range(taps)])
                os[pl.ds(a, SUB, stride=run), :] = total
                grad = grads[a] if a < own else jnp.where(inside, grads[a], 0.0)
                for i in range(taps):
                    term = grad * views[a + taps - 1 - i]
                    sums_of[i] = term if a == 0 else sums_of[i] + term
            grad_p[j, :, lanes] = os[0:rows].astype(BF16)
            rest = rest + sums_of
        rest = rest + [skip_sum] + [jnp.zeros((SUB, LANES), F32)] * (-(len(rest) + 1) % SUB)
        for n in range(0, len(rest), SUB):
            sums[which, n : n + SUB, part] = folded(rest[n : n + SUB])
        return carry

    lax.fori_loop(0, p.shape[2] // LANES, tile, 0)


def shifted(value, axis, steps):
    count = lax.axis_size(axis)
    first, last = (max(0, -steps), min(count, count - steps))
    return lax.ppermute(value, axis, [(source, source + steps) for source in range(first, last)])


def swapped(value):
    count = lax.axis_size("ctx")
    return lax.ppermute(value, "ctx", [(s, s ^ 1) for s in range(count)])


def joined(ends, f_all):
    core = lax.rem(lax.axis_index("ctx"), 2)
    half = ends.shape[1] // 2
    other = swapped(ends)
    first = core == 0
    mine = lax.dynamic_slice_in_dim(ends, core * half, half, 1)
    theirs = lax.dynamic_slice_in_dim(other, core * half, half, 1)
    one, two = jnp.where(first, mine, theirs), jnp.where(first, theirs, mine)
    return other, f_all * one[0] + two[0], one[1] + f_all * two[1]


def paired(value, axis, step, lines=None):
    count = lax.axis_size(axis)
    return lax.ppermute(value, axis, [(source, source ^ step) for source in lines or range(count)])


def scanned(chip_e, chip_a, f_all, beside):
    chips = lax.axis_size("ctx") // 2
    f_chip = f_all * f_all
    if chips == 4:
        odd = lax.rem(lax.axis_index("ctx") // 2, 2) == 1
        sent = jnp.where(odd, chip_a, chip_e)
        first = paired(sent, "ctx", 2)
        kept = beside[0](sent, None)
        first, kept = lax.optimization_barrier((first, kept))
        sent = jnp.where(odd, chip_e, chip_a) + f_chip * first
        near = lax.ppermute(sent, "ctx", [(2, 4), (3, 5), (4, 2), (5, 3)])
        far = lax.ppermute(sent, "ctx", [(2, 6), (3, 7), (4, 0), (5, 1)])
        kept = beside[1](sent, kept)
        near, far, kept = lax.optimization_barrier((near, far, kept))
        far = first + f_chip * far
        return jnp.where(odd, far, near), jnp.where(odd, near, far), kept
    kept = beside[1](chip_e, beside[0](chip_e, None))
    before, after = jnp.zeros_like(chip_e), jnp.zeros_like(chip_a)
    reach = 1
    while reach < chips:
        early, late = shifted(chip_e, "ctx", 2 * reach), shifted(chip_a, "ctx", -2 * reach)
        factor = f_chip ** (reach - 1)
        before, after = before + factor * early, after + factor * late
        factor = f_chip**reach
        chip_e, chip_a = chip_e + factor * early, chip_a + factor * late
        reach = 2 * reach
    return before, after, kept


def summed(value):
    parts = lax.axis_size("dp")
    side = lax.rem(lax.axis_index("ctx"), 2)
    half = value.shape[0] // 2
    keep = lax.dynamic_slice_in_dim(value, side * half, half, 0)
    give = lax.dynamic_slice_in_dim(value, (1 - side) * half, half, 0)
    value = keep + swapped(give)
    value = value.reshape((parts, half // parts) + value.shape[1:])
    value = jnp.sum(lax.all_to_all(value, "dp", 0, 0), axis=0)
    reach = 2
    while reach < lax.axis_size("ctx"):
        value = value + paired(value, "ctx", reach)
        reach = 2 * reach
    value = lax.all_to_all(jnp.broadcast_to(value, (parts,) + value.shape), "dp", 0, 0)
    value = value.reshape((half,) + value.shape[2:])
    other = swapped(value)
    low = side == 0
    return jnp.concatenate([jnp.where(low, value, other), jnp.where(low, other, value)], axis=0)


def local(projected, short_filter, residues, decay_rates, skip_gain, cotangent):
    rows = projected.shape[1]
    channels = projected.shape[3]
    taps = short_filter.shape[1]
    groups, poles = residues.shape
    width = channels // groups
    run = (rows + SUB) // SUB
    held = rows + SUB
    p = projected[0].transpose(1, 0, 2)
    u = cotangent[0]
    hb = shifted(p[:, rows - SUB :], "ctx", 1)
    ha = shifted(jnp.concatenate([p[:, :SUB], u[None, :SUB]], axis=0), "ctx", -1)

    rate = decay_rates.T
    weight = residues.T
    sub = np.arange(SUB)
    powers = np.stack([run * (7 - sub) - SUB, run * sub, 1 + run * sub, rows - run * (sub + 1) + 1])
    table = jnp.exp(-rate[None, :, None, :] * powers.astype(np.float32)[:, None, :, None])
    we, wb = table[0], table[1]
    cz, cy = weight[:, None, :] * table[2], weight[:, None, :] * table[3]
    f1 = jnp.exp(-rate)
    f_all = jnp.exp(-rate * rows)
    steps = np.array([1, run, 2 * run, 4 * run], np.float32)
    factor = jnp.exp(-rate[None] * steps[:, None, None])
    factor = jnp.concatenate([weight[None] * factor[:1], factor[1:]], axis=0)
    reach = np.array([1, 1, 2, 4])[:, None]
    down, up = sub[None] >= reach, sub[None] < SUB - reach
    join_e = jnp.where(down[:, None, :, None], factor[:, :, None, :], 0.0)
    join_a = jnp.where(up[:, None, :, None], factor[:, :, None, :], 0.0)
    close = np.arange(-taps, run).astype(np.float32)
    near = jnp.sum(weight[:, None, :] * jnp.exp(-rate[:, None, :] * close[None, :, None]), axis=0)

    each = 1

    def by_w(*shape):
        axis = len(shape)
        return pl.BlockSpec(shape + (each * groups,), lambda w: (0,) * axis + (w,))

    def per_w(*shape):
        return pl.BlockSpec((each,) + shape, lambda w: (w,) + (0,) * len(shape))

    def fixed(value):
        return pl.BlockSpec(
            value.shape, lambda w: (0,) * value.ndim, pipeline_mode=pl.Buffered(1)
        )

    params = pltpu.CompilerParams(vmem_limit_bytes=48 * 1024 * 1024)
    shape_of = jax.ShapeDtypeStruct
    ends_spec = pl.BlockSpec((2, each, poles, groups), lambda w: (0, w, 0, 0))
    halved = pl.BlockSpec(
        (2, each, poles, groups), lambda w: (0, lax.rem(w, width // each // 2), 0, 0)
    )
    state_shape = shape_of((poles, SUB, channels), F32)
    qkv, xg, blocks_e, blocks_a, ends = pl.pallas_call(
        states_kernel,
        grid=(width // each,),
        in_specs=[
            by_w(3, rows), by_w(3, SUB), by_w(4, SUB), by_w(rows), by_w(3, taps),
            fixed(f1), fixed(we), fixed(wb),
        ],
        out_specs=[
            by_w(3, held), by_w(2, held), by_w(poles, SUB), by_w(poles, SUB),
            ends_spec,
        ],
        out_shape=[
            shape_of((3, held, channels), F32), shape_of((2, held, channels), F32),
            state_shape, state_shape, shape_of((2, width, poles, groups), F32),
        ],
        scratch_shapes=[pltpu.VMEM((4, held + SUB, LANES), F32)],
        compiler_params=params,
        name="states",
    )(p, hb, ha, u, short_filter, f1, we, wb)

    def blocks(first, last):
        def at_w(*shape):
            axis = len(shape)
            return pl.BlockSpec(shape + (each * groups,), lambda w: (0,) * axis + (w + first,))

        def call(sent, kept):
            close, _ = lax.optimization_barrier((near, sent))
            return pl.pallas_call(
                blocks_kernel,
                grid=(last - first,),
                in_specs=[
                    at_w(2, held), at_w(poles, SUB), at_w(poles, SUB), fixed(near), at_w(1),
                    fixed(join_e), fixed(join_a),
                ],
                out_specs=[at_w(2, held), at_w(poles, SUB), at_w(poles, SUB)],
                out_shape=[shape_of((2, held, channels), F32), state_shape, state_shape],
                input_output_aliases={0: 0, 1: 1, 2: 2},
                compiler_params=params,
                cost_estimate=pl.CostEstimate(
                    flops=60 * rows * channels, bytes_accessed=35 * 2**20, transcendentals=0
                ),
                name="blocks",
            )(*(kept or (xg, blocks_e, blocks_a)), close, skip_gain[None], join_e, join_a)

        return call

    steps = width // each
    cut = (steps + 1) // 3
    other, chip_e, chip_a = joined(ends, f_all)
    before, after, (conv, from_e, from_a) = scanned(
        chip_e, chip_a, f_all, (blocks(0, cut), blocks(cut, steps))
    )
    both = jnp.stack([before, after])
    found = swapped(both)
    core = lax.rem(lax.axis_index("ctx"), 2)

    count = 3 * taps + 3
    scratch = [
        pltpu.VMEM((3, held + SUB, LANES), F32),
        pltpu.VMEM((held, LANES), F32),
        pltpu.VMEM((3, held + SUB, LANES), F32),
        pltpu.VMEM((held, LANES), F32),
        pltpu.VMEM((2, poles, LANES), F32),
    ]
    output, grad_p, sums = pl.pallas_call(
        final_kernel,
        grid=(width // each,),
        in_specs=[
            pl.BlockSpec(memory_space=pltpu.SMEM),
            by_w(3, rows), by_w(3, SUB), by_w(rows), by_w(4, SUB), by_w(3, held), by_w(2, held),
            by_w(poles, SUB), by_w(poles, SUB), halved, halved, ends_spec,
            by_w(3, taps), fixed(f1), fixed(f_all), fixed(cz), fixed(cy),
        ],
        out_specs=[by_w(rows), by_w(3, rows), per_w(count, groups)],
        out_shape=[
            shape_of((rows, channels), BF16),
            shape_of((3, rows, channels), BF16),
            shape_of((width, count, groups), F32),
        ],
        scratch_shapes=scratch,
        compiler_params=params,
        name="final",
    )(
        core[None], p, hb, u, ha, qkv, conv, from_e, from_a, both, found, other, short_filter,
        f1, f_all, cz, cy,
    )

    total = summed(sums).transpose(1, 0, 2).reshape(count, channels)
    grad_short = total[: 3 * taps].reshape(3, taps, channels)
    grad_skip = total[3 * taps]
    return output[None], grad_p.transpose(1, 0, 2)[None], grad_short, grad_skip


def solution(mesh):
    placed = (P("dp", "ctx", None, None), P(), P(), P(), P(), P("dp", "ctx", None))
    return jax.shard_map(
        local,
        mesh=mesh,
        in_specs=placed,
        out_specs=(P("dp", "ctx", None), P("dp", "ctx", None, None), P(), P()),
        check_vma=False,
    )
```

```python
import functools

import jax
import jax.numpy as jnp
import numpy as np
from jax import lax
from jax.experimental import pallas as pl
from jax.experimental.pallas import tpu as pltpu
from jax.sharding import PartitionSpec as P

LANES = 128
SUB = 8
F32 = jnp.float32
BF16 = jnp.bfloat16


def spread(row):
    return jnp.broadcast_to(row, (SUB, LANES))


def added(terms):
    while len(terms) > 1:
        pairs = [terms[k] + terms[k + 1] for k in range(0, len(terms) - 1, 2)]
        terms = pairs + terms[len(terms) - len(terms) % 2 :]
    return terms[0]


def folded(values):
    row = lax.broadcasted_iota(jnp.int32, (SUB, LANES), 0)
    upper = row < 4
    values = [
        jnp.where(upper, values[n], values[n + 4])
        + pltpu.roll(jnp.where(upper, values[n + 4], values[n]), 4, 0)
        for n in range(4)
    ]
    for step in (2, 1):
        even = (row // step) % 2 == 0
        values = [
            jnp.where(
                even,
                values[n] + pltpu.roll(values[n], SUB - step, 0),
                values[n + step] + pltpu.roll(values[n + step], step, 0),
            )
            for n in range(step)
        ]
    return values[0]


def states_kernel(core, p, hx, hi, u, filt, f1, we, wb, qkv, xg, blocks_e, blocks_a, ends, xs):
    rows = p.shape[1]
    run = (rows + SUB) // SUB
    taps = filt.shape[1]
    poles, groups = f1.shape
    own = rows - run * (SUB - 1)
    tiles = groups // LANES
    first = core[0] == 0

    def tile(lt, carry):
        lanes = pl.ds(pl.multiple_of(lt * LANES, LANES), LANES)
        part = pl.ds(pl.multiple_of(lax.rem(lt, tiles) * LANES, LANES), LANES)
        which = lt // tiles
        inside = lax.broadcasted_iota(jnp.int32, (SUB, LANES), 0) < SUB - 1
        for j in range(3):
            across, within = hx[j, :, lanes].astype(F32), hi[j, :, lanes].astype(F32)
            xs[j, 0:SUB] = jnp.where(first, across, within)
            xs[j, SUB : SUB + rows] = p[j, :, lanes].astype(F32)
            xs[j, SUB + rows :] = jnp.where(first, within, across)
        xs[3, SUB : SUB + rows] = u[:, lanes].astype(F32)
        across, within = hx[3, :, lanes].astype(F32), hi[3, :, lanes].astype(F32)
        xs[3, SUB + rows :] = jnp.where(first, within, across)

        def mixed(j):
            tap = [spread(filt[j, i : i + 1, lanes]) for i in range(taps)]
            view = [xs[j, pl.ds(SUB + a, SUB, stride=run), :] for a in range(1 - taps, run)]
            return [
                added([tap[i] * view[a + taps - 1 - i] for i in range(taps)]) for a in range(run)
            ]

        decay = [spread(f1[n : n + 1, part]) for n in range(poles)]
        for j in (1, 2, 0):
            for a, total in enumerate(mixed(j)):
                at = slice(SUB * a, SUB * a + SUB)
                qkv[j, at, lanes] = total
                if j == 2:
                    xg[0, at, lanes] = qkv[1, at, lanes] * total
                if j == 0:
                    xg[1, at, lanes] = xs[3, pl.ds(SUB + a, SUB, stride=run), :] * total
        for side, order, weight, blocks in (
            (0, range(run), we, blocks_e),
            (1, range(run - 1, -1, -1), wb, blocks_a),
        ):
            state = None
            for a in order:
                x = xg[side, SUB * a : SUB * a + SUB, lanes]
                if a >= own:
                    x = jnp.where(inside, x, 0.0)
                state = [x] * poles if state is None else [decay[n] * state[n] + x for n in range(poles)]
            for n in range(poles):
                blocks[n, :, lanes] = state[n]
            state = [state[n] * weight[n, :, part] for n in range(poles)]
            for n in range(0, poles, SUB):
                ends[side, which, n : n + SUB, part] = folded(state[n : n + SUB])
        return carry

    lax.fori_loop(0, p.shape[2] // LANES, tile, 0)


def blocks_kernel(xg, blocks_e, blocks_a, near, skip, join_e, join_a, conv, from_e, from_a):
    run = xg.shape[1] // SUB
    rows = xg.shape[1] - SUB
    taps = near.shape[0] - run
    poles, groups = blocks_e.shape[0], near.shape[1]
    own = rows - run * (SUB - 1)
    tiles = groups // LANES

    def tile(lt, carry):
        lanes = pl.ds(pl.multiple_of(lt * LANES, LANES), LANES)
        part = pl.ds(pl.multiple_of(lax.rem(lt, tiles) * LANES, LANES), LANES)
        inside = lax.broadcasted_iota(jnp.int32, (SUB, LANES), 0) < SUB - 1
        gain = spread(skip[0:1, lanes])
        lag = [spread(near[taps + m : taps + m + 1, part]) for m in range(run)]
        lag[0] = lag[0] + gain
        x = [xg[0, SUB * a : SUB * a + SUB, lanes] for a in range(run)]
        for a in range(run):
            conv[0, SUB * a : SUB * a + SUB, lanes] = added([lag[m] * x[a - m] for m in range(a + 1)])
        x = [xg[1, SUB * a : SUB * a + SUB, lanes] for a in range(run)]
        masked = [x[a] if a < own else jnp.where(inside, x[a], 0.0) for a in range(run)]
        past = [jnp.where(inside, 0.0, gain)] + [
            jnp.where(inside, 0.0, -spread(near[taps - m : taps - m + 1, part]))
            for m in range(1, taps - 1)
        ]
        for a in range(run):
            terms = [lag[m] * masked[a + m] for m in range(run - a)]
            if own <= a < own + taps - 1:
                terms = terms + [past[m] * x[a - m] for m in range(a - own + 1)]
            conv[1, SUB * a : SUB * a + SUB, lanes] = added(terms)
        for n in range(poles):
            value = pltpu.roll(blocks_e[n, :, lanes], 1, 0) * join_e[0, n, :, part]
            for k, step in ((1, 1), (2, 2), (3, 4)):
                value = value + pltpu.roll(value, step, 0) * join_e[k, n, :, part]
            from_e[n, :, lanes] = value
            value = pltpu.roll(blocks_a[n, :, lanes], SUB - 1, 0) * join_a[0, n, :, part]
            for k, step in ((1, 1), (2, 2), (3, 4)):
                value = value + pltpu.roll(value, SUB - step, 0) * join_a[k, n, :, part]
            from_a[n, :, lanes] = value
        return carry

    lax.fori_loop(0, xg.shape[2] // LANES, tile, 0)


def final_kernel(
    core, p, hx, hi, u, qkv, conv, from_e, from_a, both, found, other, filt, f1, f_all, cz, cy,
    output, grad_p, sums, ps, us, gs, os, es,
):
    rows = p.shape[1]
    run = (rows + SUB) // SUB
    taps = filt.shape[1]
    poles, groups = f1.shape
    own = rows - run * (SUB - 1)
    tiles = groups // LANES
    first = core[0] == 0
    halves = pl.num_programs(0) // 2
    kept = (pl.program_id(0) < halves) == first
    cut = sums.shape[2] // LANES

    def tile(lt, carry):
        lanes = pl.ds(pl.multiple_of(lt * LANES, LANES), LANES)
        part = pl.ds(pl.multiple_of(lax.rem(lt, tiles) * LANES, LANES), LANES)
        which = lt // tiles
        piece = lt // cut
        spot = pl.ds(pl.multiple_of(lax.rem(lt, cut) * LANES, LANES), LANES)
        inside = lax.broadcasted_iota(jnp.int32, (SUB, LANES), 0) < SUB - 1
        for side in range(2):
            far = jnp.where(kept, both[side, which, :, part], found[side, which, :, part])
            close = other[side, which, :, part] + f_all[:, part] * far
            es[side] = jnp.where(first == (side == 0), far, close)
        for j in range(3):
            across, within = hx[j, :, lanes].astype(F32), hi[j, :, lanes].astype(F32)
            ps[j, 0:SUB] = jnp.where(first, across, within)
            ps[j, SUB : SUB + rows] = p[j, :, lanes].astype(F32)
            ps[j, SUB + rows :] = jnp.where(first, within, across)
        us[0:rows] = u[:, lanes].astype(F32)
        across, within = hx[3, :, lanes].astype(F32), hi[3, :, lanes].astype(F32)
        us[rows:] = jnp.where(first, within, across)
        decay = [spread(f1[n : n + 1, part]) for n in range(poles)]

        state = [
            from_e[n, :, lanes] + cz[n, :, part] * spread(es[0, n : n + 1])
            for n in range(poles)
        ]
        skip_sum = None
        for a in range(run):
            at = slice(SUB * a, SUB * a + SUB)
            query, upstream = qkv[0, at, lanes], us[pl.ds(a, SUB, stride=run), :]
            term = (qkv[1, at, lanes] * qkv[2, at, lanes]) * (query * upstream)
            if a >= own:
                term = jnp.where(inside, term, 0.0)
            skip_sum = term if a == 0 else skip_sum + term
            filtered = conv[0, at, lanes] + added(list(state))
            os[pl.ds(a, SUB, stride=run), :] = query * filtered
            gs[0, pl.ds(a, SUB, stride=run), :] = upstream * filtered
            if a + 1 < run:
                state = [state[n] * decay[n] for n in range(poles)]
        output[:, lanes] = os[0:rows].astype(BF16)

        state = [
            from_a[n, :, lanes] + cy[n, :, part] * spread(es[1, n : n + 1])
            for n in range(poles)
        ]
        for a in range(run - 1, -1, -1):
            at = slice(SUB * a, SUB * a + SUB)
            grad = conv[1, at, lanes] + added(list(state))
            gs[1, pl.ds(a, SUB, stride=run), :] = grad * qkv[2, at, lanes]
            gs[2, pl.ds(a, SUB, stride=run), :] = grad * qkv[1, at, lanes]
            if a:
                state = [state[n] * decay[n] for n in range(poles)]

        rest = []
        for j in range(3):
            tap = [spread(filt[j, i : i + 1, lanes]) for i in range(taps)]
            grads = [gs[j, pl.ds(a, SUB, stride=run), :] for a in range(run + taps - 1)]
            views = [ps[j, pl.ds(SUB + a, SUB, stride=run), :] for a in range(1 - taps, run)]
            sums_of = [None] * taps
            for a in range(run):
                total = added([tap[i] * grads[a + i] for i in range(taps)])
                os[pl.ds(a, SUB, stride=run), :] = total
                grad = grads[a] if a < own else jnp.where(inside, grads[a], 0.0)
                for i in range(taps):
                    term = grad * views[a + taps - 1 - i]
                    sums_of[i] = term if a == 0 else sums_of[i] + term
            grad_p[j, :, lanes] = os[0:rows].astype(BF16)
            rest = rest + sums_of
        rest = rest + [skip_sum] + [jnp.zeros((SUB, LANES), F32)] * (-(len(rest) + 1) % SUB)
        for n in range(0, len(rest), SUB):
            sums[piece, n : n + SUB, spot] = folded(rest[n : n + SUB])
        return carry

    lax.fori_loop(0, p.shape[2] // LANES, tile, 0)


def shifted(value, axis, steps):
    count = lax.axis_size(axis)
    first, last = (max(0, -steps), min(count, count - steps))
    return lax.ppermute(value, axis, [(source, source + steps) for source in range(first, last)])


def swapped(value):
    count = lax.axis_size("ctx")
    return lax.ppermute(value, "ctx", [(s, s ^ 1) for s in range(count)])


def joined(ends, f_all):
    core = lax.rem(lax.axis_index("ctx"), 2)
    half = ends.shape[1] // 2
    other = swapped(ends)
    first = core == 0
    mine = lax.dynamic_slice_in_dim(ends, core * half, half, 1)
    theirs = lax.dynamic_slice_in_dim(other, core * half, half, 1)
    one, two = jnp.where(first, mine, theirs), jnp.where(first, theirs, mine)
    return other, f_all * one[0] + two[0], one[1] + f_all * two[1]


def paired(value, axis, step, lines=None):
    count = lax.axis_size(axis)
    return lax.ppermute(value, axis, [(source, source ^ step) for source in lines or range(count)])


def scanned(chip_e, chip_a, f_all, beside):
    chips = lax.axis_size("ctx") // 2
    f_chip = f_all * f_all
    if chips == 4:
        odd = lax.rem(lax.axis_index("ctx") // 2, 2) == 1
        sent = jnp.where(odd, chip_a, chip_e)
        first = paired(sent, "ctx", 2)
        kept = beside[0](sent, None)
        first, kept = lax.optimization_barrier((first, kept))
        sent = jnp.where(odd, chip_e, chip_a) + f_chip * first
        near = lax.ppermute(sent, "ctx", [(2, 4), (3, 5), (4, 2), (5, 3)])
        far = lax.ppermute(sent, "ctx", [(2, 6), (3, 7), (4, 0), (5, 1)])
        kept = beside[1](sent, kept)
        near, far, kept = lax.optimization_barrier((near, far, kept))
        far = first + f_chip * far
        return jnp.where(odd, far, near), jnp.where(odd, near, far), kept
    kept = beside[1](chip_e, beside[0](chip_e, None))
    before, after = jnp.zeros_like(chip_e), jnp.zeros_like(chip_a)
    reach = 1
    while reach < chips:
        early, late = shifted(chip_e, "ctx", 2 * reach), shifted(chip_a, "ctx", -2 * reach)
        factor = f_chip ** (reach - 1)
        before, after = before + factor * early, after + factor * late
        factor = f_chip**reach
        chip_e, chip_a = chip_e + factor * early, chip_a + factor * late
        reach = 2 * reach
    return before, after, kept


def summed(value):
    devices = lax.axis_size("ctx")
    total = lax.axis_size("dp") * devices
    sides = [[k for k in range(total) if k % 2 == side] for side in range(2)]
    parts = total // 2
    low = lax.rem(lax.axis_index("ctx"), 2) == 0
    half = value.shape[0] // 2
    left, right = value[:half], value[half:]
    value = jnp.where(low, left, right) + swapped(jnp.where(low, right, left))
    shape = value.shape

    def dealt(value):
        return lax.all_to_all(value, ("dp", "ctx"), 0, 0, axis_index_groups=sides)

    value = jnp.sum(dealt(value.reshape(parts, shape[1] * half // parts, shape[2])), axis=0)
    value = dealt(jnp.broadcast_to(value, (parts,) + value.shape)).reshape(shape)
    other = swapped(value)
    return jnp.concatenate([jnp.where(low, value, other), jnp.where(low, other, value)], axis=0)


def local(projected, short_filter, residues, decay_rates, skip_gain, cotangent):
    rows = projected.shape[1]
    channels = projected.shape[3]
    taps = short_filter.shape[1]
    groups, poles = residues.shape
    width = channels // groups
    run = (rows + SUB) // SUB
    held = rows + SUB
    p = projected[0].transpose(1, 0, 2)
    u = cotangent[0]
    core = lax.rem(lax.axis_index("ctx"), 2)
    head = jnp.concatenate([p[:, :SUB], u[None, :SUB]], axis=0)
    tail = jnp.concatenate([p[:, rows - SUB :], u[None, rows - SUB :]], axis=0)
    devices = lax.axis_size("ctx")
    across = [(k, k + 1) for k in range(1, devices - 1, 2)]
    across = across + [(target, source) for source, target in across]
    hx = lax.ppermute(jnp.where(core == 0, head, tail), "ctx", across)
    hi = swapped(jnp.where(core == 0, tail, head))

    rate = decay_rates.T
    weight = residues.T
    sub = np.arange(SUB)
    powers = np.stack([run * (7 - sub) - SUB, run * sub, 1 + run * sub, rows - run * (sub + 1) + 1])
    table = jnp.exp(-rate[None, :, None, :] * powers.astype(np.float32)[:, None, :, None])
    we, wb = table[0], table[1]
    cz, cy = weight[:, None, :] * table[2], weight[:, None, :] * table[3]
    f1 = jnp.exp(-rate)
    f_all = jnp.exp(-rate * rows)
    steps = np.array([1, run, 2 * run, 4 * run], np.float32)
    factor = jnp.exp(-rate[None] * steps[:, None, None])
    factor = jnp.concatenate([weight[None] * factor[:1], factor[1:]], axis=0)
    reach = np.array([1, 1, 2, 4])[:, None]
    down, up = sub[None] >= reach, sub[None] < SUB - reach
    join_e = jnp.where(down[:, None, :, None], factor[:, :, None, :], 0.0)
    join_a = jnp.where(up[:, None, :, None], factor[:, :, None, :], 0.0)
    close = np.arange(-taps, run).astype(np.float32)
    near = jnp.sum(weight[:, None, :] * jnp.exp(-rate[:, None, :] * close[None, :, None]), axis=0)

    each = 1

    def by_w(*shape):
        axis = len(shape)
        return pl.BlockSpec(shape + (each * groups,), lambda w: (0,) * axis + (w,))

    def fixed(value):
        return pl.BlockSpec(
            value.shape, lambda w: (0,) * value.ndim, pipeline_mode=pl.Buffered(1)
        )

    params = pltpu.CompilerParams(vmem_limit_bytes=48 * 1024 * 1024)
    shape_of = jax.ShapeDtypeStruct
    ends_spec = pl.BlockSpec((2, each, poles, groups), lambda w: (0, w, 0, 0))
    halved = pl.BlockSpec(
        (2, each, poles, groups), lambda w: (0, lax.rem(w, width // each // 2), 0, 0)
    )
    state_shape = shape_of((poles, SUB, channels), F32)
    qkv, xg, blocks_e, blocks_a, ends = pl.pallas_call(
        states_kernel,
        grid=(width // each,),
        in_specs=[
            pl.BlockSpec(memory_space=pltpu.SMEM),
            by_w(3, rows), by_w(4, SUB), by_w(4, SUB), by_w(rows), by_w(3, taps),
            fixed(f1), fixed(we), fixed(wb),
        ],
        out_specs=[
            by_w(3, held), by_w(2, held), by_w(poles, SUB), by_w(poles, SUB),
            ends_spec,
        ],
        out_shape=[
            shape_of((3, held, channels), F32), shape_of((2, held, channels), F32),
            state_shape, state_shape, shape_of((2, width, poles, groups), F32),
        ],
        scratch_shapes=[pltpu.VMEM((4, held + SUB, LANES), F32)],
        compiler_params=params,
        name="states",
    )(core[None], p, hx, hi, u, short_filter, f1, we, wb)

    many = 2 if width % 2 == 0 else 1

    def blocks(first, last):
        def at_w(*shape):
            axis = len(shape)
            return pl.BlockSpec(shape + (many * groups,), lambda w: (0,) * axis + (w + first,))

        def call(sent, kept):
            close, _ = lax.optimization_barrier((near, sent))
            return pl.pallas_call(
                blocks_kernel,
                grid=(last - first,),
                in_specs=[
                    at_w(2, held), at_w(poles, SUB), at_w(poles, SUB), fixed(near), at_w(1),
                    fixed(join_e), fixed(join_a),
                ],
                out_specs=[at_w(2, held), at_w(poles, SUB), at_w(poles, SUB)],
                out_shape=[shape_of((2, held, channels), F32), state_shape, state_shape],
                input_output_aliases={0: 0, 1: 1, 2: 2},
                compiler_params=params,
                cost_estimate=pl.CostEstimate(
                    flops=60 * rows * channels, bytes_accessed=35 * 2**20, transcendentals=0
                ),
                name="blocks",
            )(*(kept or (xg, blocks_e, blocks_a)), close, skip_gain[None], join_e, join_a)

        return call

    steps = width // many
    cut = (steps + 1) // 3
    other, chip_e, chip_a = joined(ends, f_all)
    before, after, (conv, from_e, from_a) = scanned(
        chip_e, chip_a, f_all, (blocks(0, cut), blocks(cut, steps))
    )
    both = jnp.stack([before, after])
    found = swapped(both)

    count = 3 * taps + 3
    split = 2 if groups % (2 * LANES) == 0 else 1
    scratch = [
        pltpu.VMEM((3, held + SUB, LANES), F32),
        pltpu.VMEM((held, LANES), F32),
        pltpu.VMEM((3, held + SUB, LANES), F32),
        pltpu.VMEM((held, LANES), F32),
        pltpu.VMEM((2, poles, LANES), F32),
    ]
    output, grad_p, sums = pl.pallas_call(
        final_kernel,
        grid=(width // each,),
        in_specs=[
            pl.BlockSpec(memory_space=pltpu.SMEM),
            by_w(3, rows), by_w(4, SUB), by_w(4, SUB), by_w(rows), by_w(3, held), by_w(2, held),
            by_w(poles, SUB), by_w(poles, SUB), halved, halved, ends_spec,
            by_w(3, taps), fixed(f1), fixed(f_all), fixed(cz), fixed(cy),
        ],
        out_specs=[
            by_w(rows), by_w(3, rows),
            pl.BlockSpec((each * split, count, groups // split), lambda w: (w, 0, 0)),
        ],
        out_shape=[
            shape_of((rows, channels), BF16),
            shape_of((3, rows, channels), BF16),
            shape_of((width * split, count, groups // split), F32),
        ],
        scratch_shapes=scratch,
        compiler_params=params,
        name="final",
    )(
        core[None], p, hx, hi, u, qkv, conv, from_e, from_a, both, found, other, short_filter,
        f1, f_all, cz, cy,
    )

    total = summed(sums).transpose(1, 0, 2).reshape(count, channels)
    grad_short = total[: 3 * taps].reshape(3, taps, channels)
    grad_skip = total[3 * taps]
    return output[None], grad_p.transpose(1, 0, 2)[None], grad_short, grad_skip


def solution(mesh):
    placed = (P("dp", "ctx", None, None), P(), P(), P(), P(), P("dp", "ctx", None))
    return jax.shard_map(
        local,
        mesh=mesh,
        in_specs=placed,
        out_specs=(P("dp", "ctx", None), P("dp", "ctx", None, None), P(), P()),
        check_vma=False,
    )
```

```python
import functools

import jax
import jax.numpy as jnp
import numpy as np
from jax import lax
from jax.experimental import pallas as pl
from jax.experimental.pallas import tpu as pltpu
from jax.sharding import PartitionSpec as P

LANES = 128
SUB = 8
F32 = jnp.float32
BF16 = jnp.bfloat16


def spread(row):
    return jnp.broadcast_to(row, (SUB, LANES))


def added(terms):
    while len(terms) > 1:
        pairs = [terms[k] + terms[k + 1] for k in range(0, len(terms) - 1, 2)]
        terms = pairs + terms[len(terms) - len(terms) % 2 :]
    return terms[0]


def folded(values):
    row = lax.broadcasted_iota(jnp.int32, (SUB, LANES), 0)
    upper = row < 4
    values = [
        jnp.where(upper, values[n], values[n + 4])
        + pltpu.roll(jnp.where(upper, values[n + 4], values[n]), 4, 0)
        for n in range(4)
    ]
    for step in (2, 1):
        even = (row // step) % 2 == 0
        values = [
            jnp.where(
                even,
                values[n] + pltpu.roll(values[n], SUB - step, 0),
                values[n + step] + pltpu.roll(values[n + step], step, 0),
            )
            for n in range(step)
        ]
    return values[0]


def states_kernel(core, p, hx_low, hx_high, hi, u, filt, f1, we, wb, qkv, xg, blocks_e, blocks_a, ends, xs):
    rows = p.shape[1]
    run = (rows + SUB) // SUB
    taps = filt.shape[1]
    poles, groups = f1.shape
    own = rows - run * (SUB - 1)
    tiles = groups // LANES
    first = core[0] == 0

    def tile(lt, carry):
        lanes = pl.ds(pl.multiple_of(lt * LANES, LANES), LANES)
        part = pl.ds(pl.multiple_of(lax.rem(lt, tiles) * LANES, LANES), LANES)
        which = lt // tiles
        inside = lax.broadcasted_iota(jnp.int32, (SUB, LANES), 0) < SUB - 1
        for j in range(3):
            across = (hx_low, hx_high)[j // 2][j % 2, :, lanes].astype(F32)
            within = hi[j, :, lanes].astype(F32)
            xs[j, 0:SUB] = jnp.where(first, across, within)
            xs[j, SUB : SUB + rows] = p[j, :, lanes].astype(F32)
            xs[j, SUB + rows :] = jnp.where(first, within, across)
        xs[3, SUB : SUB + rows] = u[:, lanes].astype(F32)
        across, within = hx_high[1, :, lanes].astype(F32), hi[3, :, lanes].astype(F32)
        xs[3, SUB + rows :] = jnp.where(first, within, across)

        def mixed(j):
            tap = [spread(filt[j, i : i + 1, lanes]) for i in range(taps)]
            view = [xs[j, pl.ds(SUB + a, SUB, stride=run), :] for a in range(1 - taps, 0)]
            for a in range(run):
                view = view[-(taps - 1) :] + [xs[j, pl.ds(SUB + a, SUB, stride=run), :]]
                yield added([tap[i] * view[-1 - i] for i in range(taps)])

        decay = [spread(f1[n : n + 1, part]) for n in range(poles)]
        for j in (1, 2, 0):
            for a, total in enumerate(mixed(j)):
                at = slice(SUB * a, SUB * a + SUB)
                qkv[j, at, lanes] = total
                if j == 2:
                    xg[0, at, lanes] = qkv[1, at, lanes] * total
                if j == 0:
                    xg[1, at, lanes] = xs[3, pl.ds(SUB + a, SUB, stride=run), :] * total
        for side, order, weight, blocks in (
            (0, range(run), we, blocks_e),
            (1, range(run - 1, -1, -1), wb, blocks_a),
        ):
            state = None
            for a in order:
                x = xg[side, SUB * a : SUB * a + SUB, lanes]
                if a >= own:
                    x = jnp.where(inside, x, 0.0)
                state = [x] * poles if state is None else [decay[n] * state[n] + x for n in range(poles)]
            for n in range(poles):
                blocks[n, :, lanes] = state[n]
            state = [state[n] * weight[n, :, part] for n in range(poles)]
            for n in range(0, poles, SUB):
                ends[side, which, n : n + SUB, part] = folded(state[n : n + SUB])
        return carry

    lax.fori_loop(0, p.shape[2] // LANES, tile, 0)


def blocks_kernel(xg, blocks_e, blocks_a, near, skip, join_e, join_a, conv, from_e, from_a):
    run = xg.shape[1] // SUB
    rows = xg.shape[1] - SUB
    taps = near.shape[0] - run
    poles, groups = blocks_e.shape[0], near.shape[1]
    own = rows - run * (SUB - 1)
    tiles = groups // LANES

    def tile(lt, carry):
        lanes = pl.ds(pl.multiple_of(lt * LANES, LANES), LANES)
        part = pl.ds(pl.multiple_of(lax.rem(lt, tiles) * LANES, LANES), LANES)
        inside = lax.broadcasted_iota(jnp.int32, (SUB, LANES), 0) < SUB - 1
        gain = spread(skip[0:1, lanes])
        lag = [spread(near[taps + m : taps + m + 1, part]) for m in range(run)]
        lag[0] = lag[0] + gain
        x = [xg[0, SUB * a : SUB * a + SUB, lanes] for a in range(run)]
        for a in range(run):
            conv[0, SUB * a : SUB * a + SUB, lanes] = added([lag[m] * x[a - m] for m in range(a + 1)])
        x = [xg[1, SUB * a : SUB * a + SUB, lanes] for a in range(run)]
        masked = [x[a] if a < own else jnp.where(inside, x[a], 0.0) for a in range(run)]
        past = [jnp.where(inside, 0.0, gain)] + [
            jnp.where(inside, 0.0, -spread(near[taps - m : taps - m + 1, part]))
            for m in range(1, taps - 1)
        ]
        for a in range(run):
            terms = [lag[m] * masked[a + m] for m in range(run - a)]
            if own <= a < own + taps - 1:
                terms = terms + [past[m] * x[a - m] for m in range(a - own + 1)]
            conv[1, SUB * a : SUB * a + SUB, lanes] = added(terms)
        for n in range(poles):
            value = pltpu.roll(blocks_e[n, :, lanes], 1, 0) * join_e[0, n, :, part]
            for k, step in ((1, 1), (2, 2), (3, 4)):
                value = value + pltpu.roll(value, step, 0) * join_e[k, n, :, part]
            from_e[n, :, lanes] = value
            value = pltpu.roll(blocks_a[n, :, lanes], SUB - 1, 0) * join_a[0, n, :, part]
            for k, step in ((1, 1), (2, 2), (3, 4)):
                value = value + pltpu.roll(value, SUB - step, 0) * join_a[k, n, :, part]
            from_a[n, :, lanes] = value
        return carry

    lax.fori_loop(0, xg.shape[2] // LANES, tile, 0)


def final_kernel(
    core, p, hx_low, hx_high, hi, u, qkv, conv, from_e, from_a, both, found, other, filt, f1, f_all, cz, cy,
    output, grad_p, sums, ps, us, gs, os, es,
):
    rows = p.shape[1]
    run = (rows + SUB) // SUB
    taps = filt.shape[1]
    poles, groups = f1.shape
    own = rows - run * (SUB - 1)
    tiles = groups // LANES
    first = core[0] == 0
    halves = pl.num_programs(0) // 2
    kept = (pl.program_id(0) < halves) == first
    cut = sums.shape[2] // LANES

    def tile(lt, carry):
        lanes = pl.ds(pl.multiple_of(lt * LANES, LANES), LANES)
        part = pl.ds(pl.multiple_of(lax.rem(lt, tiles) * LANES, LANES), LANES)
        which = lt // tiles
        piece = lt // cut
        spot = pl.ds(pl.multiple_of(lax.rem(lt, cut) * LANES, LANES), LANES)
        inside = lax.broadcasted_iota(jnp.int32, (SUB, LANES), 0) < SUB - 1
        for side in range(2):
            far = jnp.where(kept, both[side, which, :, part], found[side, which, :, part])
            close = other[side, which, :, part] + f_all[:, part] * far
            es[side] = jnp.where(first == (side == 0), far, close)
        for j in range(3):
            across = (hx_low, hx_high)[j // 2][j % 2, :, lanes].astype(F32)
            within = hi[j, :, lanes].astype(F32)
            ps[j, 0:SUB] = jnp.where(first, across, within)
            ps[j, SUB : SUB + rows] = p[j, :, lanes].astype(F32)
            ps[j, SUB + rows :] = jnp.where(first, within, across)
        us[0:rows] = u[:, lanes].astype(F32)
        across, within = hx_high[1, :, lanes].astype(F32), hi[3, :, lanes].astype(F32)
        us[rows:] = jnp.where(first, within, across)
        decay = [spread(f1[n : n + 1, part]) for n in range(poles)]

        state = [
            from_e[n, :, lanes] + cz[n, :, part] * spread(es[0, n : n + 1])
            for n in range(poles)
        ]
        skip_sum = None
        for a in range(run):
            at = slice(SUB * a, SUB * a + SUB)
            query, upstream = qkv[0, at, lanes], us[pl.ds(a, SUB, stride=run), :]
            term = (qkv[1, at, lanes] * qkv[2, at, lanes]) * (query * upstream)
            if a >= own:
                term = jnp.where(inside, term, 0.0)
            skip_sum = term if a == 0 else skip_sum + term
            filtered = conv[0, at, lanes] + added(list(state))
            os[pl.ds(a, SUB, stride=run), :] = query * filtered
            gs[0, pl.ds(a, SUB, stride=run), :] = upstream * filtered
            if a + 1 < run:
                state = [state[n] * decay[n] for n in range(poles)]
        output[:, lanes] = os[0:rows].astype(BF16)

        state = [
            from_a[n, :, lanes] + cy[n, :, part] * spread(es[1, n : n + 1])
            for n in range(poles)
        ]
        for a in range(run - 1, -1, -1):
            at = slice(SUB * a, SUB * a + SUB)
            grad = conv[1, at, lanes] + added(list(state))
            gs[1, pl.ds(a, SUB, stride=run), :] = grad * qkv[2, at, lanes]
            gs[2, pl.ds(a, SUB, stride=run), :] = grad * qkv[1, at, lanes]
            if a:
                state = [state[n] * decay[n] for n in range(poles)]

        rest = []
        for j in range(3):
            tap = [spread(filt[j, i : i + 1, lanes]) for i in range(taps)]
            grads = [gs[j, pl.ds(a, SUB, stride=run), :] for a in range(taps - 1)]
            views = [ps[j, pl.ds(SUB + a, SUB, stride=run), :] for a in range(1 - taps, 0)]
            sums_of = [None] * taps
            for a in range(run):
                grads = grads[-(taps - 1) :] + [gs[j, pl.ds(a + taps - 1, SUB, stride=run), :]]
                views = views[-(taps - 1) :] + [ps[j, pl.ds(SUB + a, SUB, stride=run), :]]
                total = added([tap[i] * grads[i] for i in range(taps)])
                os[pl.ds(a, SUB, stride=run), :] = total
                grad = grads[0] if a < own else jnp.where(inside, grads[0], 0.0)
                for i in range(taps):
                    term = grad * views[-1 - i]
                    sums_of[i] = term if a == 0 else sums_of[i] + term
            grad_p[j, :, lanes] = os[0:rows].astype(BF16)
            rest = rest + sums_of
        rest = rest + [skip_sum] + [jnp.zeros((SUB, LANES), F32)] * (-(len(rest) + 1) % SUB)
        for n in range(0, len(rest), SUB):
            sums[piece, n : n + SUB, spot] = folded(rest[n : n + SUB])
        return carry

    lax.fori_loop(0, p.shape[2] // LANES, tile, 0)


def shifted(value, axis, steps):
    count = lax.axis_size(axis)
    first, last = (max(0, -steps), min(count, count - steps))
    return lax.ppermute(value, axis, [(source, source + steps) for source in range(first, last)])


def swapped(value):
    count = lax.axis_size("ctx")
    return lax.ppermute(value, "ctx", [(s, s ^ 1) for s in range(count)])


def joined(ends, f_all):
    core = lax.rem(lax.axis_index("ctx"), 2)
    half = ends.shape[1] // 2
    other = swapped(ends)
    first = core == 0
    mine = lax.dynamic_slice_in_dim(ends, core * half, half, 1)
    theirs = lax.dynamic_slice_in_dim(other, core * half, half, 1)
    one, two = jnp.where(first, mine, theirs), jnp.where(first, theirs, mine)
    return other, f_all * one[0] + two[0], one[1] + f_all * two[1]


def paired(value, axis, step, lines=None):
    count = lax.axis_size(axis)
    return lax.ppermute(value, axis, [(source, source ^ step) for source in lines or range(count)])


def scanned(chip_e, chip_a, f_all, beside):
    chips = lax.axis_size("ctx") // 2
    f_chip = f_all * f_all
    if chips == 4:
        odd = lax.rem(lax.axis_index("ctx") // 2, 2) == 1
        sent = jnp.where(odd, chip_a, chip_e)
        first = paired(sent, "ctx", 2)
        kept = beside[0](sent, None)
        first, kept = lax.optimization_barrier((first, kept))
        sent = jnp.where(odd, chip_e, chip_a) + f_chip * first
        near = lax.ppermute(sent, "ctx", [(2, 4), (3, 5), (4, 2), (5, 3)])
        far = lax.ppermute(sent, "ctx", [(2, 6), (3, 7), (4, 0), (5, 1)])
        kept = beside[1](sent, kept)
        near, far, kept = lax.optimization_barrier((near, far, kept))
        far = first + f_chip * far
        return jnp.where(odd, far, near), jnp.where(odd, near, far), kept
    kept = beside[1](chip_e, beside[0](chip_e, None))
    before, after = jnp.zeros_like(chip_e), jnp.zeros_like(chip_a)
    reach = 1
    while reach < chips:
        early, late = shifted(chip_e, "ctx", 2 * reach), shifted(chip_a, "ctx", -2 * reach)
        factor = f_chip ** (reach - 1)
        before, after = before + factor * early, after + factor * late
        factor = f_chip**reach
        chip_e, chip_a = chip_e + factor * early, chip_a + factor * late
        reach = 2 * reach
    return before, after, kept


def chain(left, right, turn):
    index, dp = lax.axis_index("ctx"), lax.axis_index("dp")
    reaches = []
    while 2 ** len(reaches) < lax.axis_size("dp"):
        reaches.append(2 ** len(reaches))
    chips = []
    while 2 ** (len(chips) + 1) < lax.axis_size("ctx"):
        chips.append(2 ** (len(chips) + 1))
    steps = [("ctx", 1, lax.rem(index, 2) == 0)]
    steps = steps + [("dp", step, lax.rem(dp // step, 2) == 0) for step in reaches[::turn]]
    for axis, step, low in steps:
        value = jnp.where(low, left, right) + paired(jnp.where(low, right, left), axis, step)
        half = value.shape[0] // 2
        left, right = value[:half], value[half:]
    for step in chips[::turn]:
        value = value + paired(value, "ctx", step)
    for axis, step, low in reversed(steps):
        other = paired(value, axis, step)
        left, right = jnp.where(low, value, other), jnp.where(low, other, value)
        value = jnp.concatenate([left, right], axis=0)
    return left, right


def summed(value):
    quarter = value.shape[0] // 4
    parts = [value[k * quarter : (k + 1) * quarter] for k in range(4)]
    left, right = chain(parts[0], parts[2], 1)
    other_left, other_right = chain(parts[1], parts[3], -1)
    return jnp.concatenate([left, other_left, right, other_right], axis=0)


def local(projected, short_filter, residues, decay_rates, skip_gain, cotangent):
    rows = projected.shape[1]
    channels = projected.shape[3]
    taps = short_filter.shape[1]
    groups, poles = residues.shape
    width = channels // groups
    run = (rows + SUB) // SUB
    held = rows + SUB
    p = projected[0].transpose(1, 0, 2)
    u = cotangent[0]
    core = lax.rem(lax.axis_index("ctx"), 2)
    head = jnp.concatenate([p[:, :SUB], u[None, :SUB]], axis=0)
    tail = jnp.concatenate([p[:, rows - SUB :], u[None, rows - SUB :]], axis=0)
    devices = lax.axis_size("ctx")
    across = [(k, k + 1) for k in range(1, devices - 1, 2)]
    across = across + [(target, source) for source, target in across]
    sent = jnp.where(core == 0, head, tail)
    hx = [lax.ppermute(sent[2 * k : 2 * k + 2], "ctx", across) for k in range(2)]
    hi = swapped(jnp.where(core == 0, tail, head))

    rate = decay_rates.T
    weight = residues.T
    sub = np.arange(SUB)
    powers = np.stack([run * (7 - sub) - SUB, run * sub, 1 + run * sub, rows - run * (sub + 1) + 1])
    table = jnp.exp(-rate[None, :, None, :] * powers.astype(np.float32)[:, None, :, None])
    we, wb = table[0], table[1]
    cz, cy = weight[:, None, :] * table[2], weight[:, None, :] * table[3]
    f1 = jnp.exp(-rate)
    f_all = jnp.exp(-rate * rows)
    steps = np.array([1, run, 2 * run, 4 * run], np.float32)
    factor = jnp.exp(-rate[None] * steps[:, None, None])
    factor = jnp.concatenate([weight[None] * factor[:1], factor[1:]], axis=0)
    reach = np.array([1, 1, 2, 4])[:, None]
    down, up = sub[None] >= reach, sub[None] < SUB - reach
    join_e = jnp.where(down[:, None, :, None], factor[:, :, None, :], 0.0)
    join_a = jnp.where(up[:, None, :, None], factor[:, :, None, :], 0.0)
    close = np.arange(-taps, run).astype(np.float32)
    near = jnp.sum(weight[:, None, :] * jnp.exp(-rate[:, None, :] * close[None, :, None]), axis=0)

    each = 1

    def by_w(*shape):
        axis = len(shape)
        return pl.BlockSpec(shape + (each * groups,), lambda w: (0,) * axis + (w,))

    def fixed(value):
        return pl.BlockSpec(
            value.shape, lambda w: (0,) * value.ndim, pipeline_mode=pl.Buffered(1)
        )

    params = pltpu.CompilerParams(vmem_limit_bytes=48 * 1024 * 1024)
    shape_of = jax.ShapeDtypeStruct
    ends_spec = pl.BlockSpec((2, each, poles, groups), lambda w: (0, w, 0, 0))
    halved = pl.BlockSpec(
        (2, each, poles, groups), lambda w: (0, lax.rem(w, width // each // 2), 0, 0)
    )
    state_shape = shape_of((poles, SUB, channels), F32)
    qkv, xg, blocks_e, blocks_a, ends = pl.pallas_call(
        states_kernel,
        grid=(width // each,),
        in_specs=[
            pl.BlockSpec(memory_space=pltpu.SMEM),
            by_w(3, rows), by_w(2, SUB), by_w(2, SUB), by_w(4, SUB), by_w(rows), by_w(3, taps),
            fixed(f1), fixed(we), fixed(wb),
        ],
        out_specs=[
            by_w(3, held), by_w(2, held), by_w(poles, SUB), by_w(poles, SUB),
            ends_spec,
        ],
        out_shape=[
            shape_of((3, held, channels), F32), shape_of((2, held, channels), F32),
            state_shape, state_shape, shape_of((2, width, poles, groups), F32),
        ],
        scratch_shapes=[pltpu.VMEM((4, held + SUB, LANES), F32)],
        compiler_params=params,
        name="states",
    )(core[None], p, *hx, hi, u, short_filter, f1, we, wb)

    many = 2 if width % 2 == 0 else 1

    def blocks(first, last):
        def at_w(*shape):
            axis = len(shape)
            return pl.BlockSpec(shape + (many * groups,), lambda w: (0,) * axis + (w + first,))

        def call(sent, kept):
            close, _ = lax.optimization_barrier((near, sent))
            return pl.pallas_call(
                blocks_kernel,
                grid=(last - first,),
                in_specs=[
                    at_w(2, held), at_w(poles, SUB), at_w(poles, SUB), fixed(near), at_w(1),
                    fixed(join_e), fixed(join_a),
                ],
                out_specs=[at_w(2, held), at_w(poles, SUB), at_w(poles, SUB)],
                out_shape=[shape_of((2, held, channels), F32), state_shape, state_shape],
                input_output_aliases={0: 0, 1: 1, 2: 2},
                compiler_params=params,
                cost_estimate=pl.CostEstimate(
                    flops=60 * rows * channels, bytes_accessed=35 * 2**20, transcendentals=0
                ),
                name="blocks",
            )(*(kept or (xg, blocks_e, blocks_a)), close, skip_gain[None], join_e, join_a)

        return call

    steps = width // many
    cut = (steps + 1) // 3
    other, chip_e, chip_a = joined(ends, f_all)
    before, after, (conv, from_e, from_a) = scanned(
        chip_e, chip_a, f_all, (blocks(0, cut), blocks(cut, steps))
    )
    both = jnp.stack([before, after])
    found = swapped(both)

    count = 3 * taps + 3
    split = 2 if groups % (2 * LANES) == 0 else 1
    scratch = [
        pltpu.VMEM((3, held + SUB, LANES), F32),
        pltpu.VMEM((held, LANES), F32),
        pltpu.VMEM((3, held + SUB, LANES), F32),
        pltpu.VMEM((held, LANES), F32),
        pltpu.VMEM((2, poles, LANES), F32),
    ]
    output, grad_p, sums = pl.pallas_call(
        final_kernel,
        grid=(width // each,),
        in_specs=[
            pl.BlockSpec(memory_space=pltpu.SMEM),
            by_w(3, rows), by_w(2, SUB), by_w(2, SUB), by_w(4, SUB), by_w(rows), by_w(3, held), by_w(2, held),
            by_w(poles, SUB), by_w(poles, SUB), halved, halved, ends_spec,
            by_w(3, taps), fixed(f1), fixed(f_all), fixed(cz), fixed(cy),
        ],
        out_specs=[
            by_w(rows), by_w(3, rows),
            pl.BlockSpec((each * split, count, groups // split), lambda w: (w, 0, 0)),
        ],
        out_shape=[
            shape_of((rows, channels), BF16),
            shape_of((3, rows, channels), BF16),
            shape_of((width * split, count, groups // split), F32),
        ],
        scratch_shapes=scratch,
        compiler_params=params,
        name="final",
    )(
        core[None], p, *hx, hi, u, qkv, conv, from_e, from_a, both, found, other, short_filter,
        f1, f_all, cz, cy,
    )

    total = summed(sums).transpose(1, 0, 2).reshape(count, channels)
    grad_short = total[: 3 * taps].reshape(3, taps, channels)
    grad_skip = total[3 * taps]
    return output[None], grad_p.transpose(1, 0, 2)[None], grad_short, grad_skip


def solution(mesh):
    placed = (P("dp", "ctx", None, None), P(), P(), P(), P(), P("dp", "ctx", None))
    return jax.shard_map(
        local,
        mesh=mesh,
        in_specs=placed,
        out_specs=(P("dp", "ctx", None), P("dp", "ctx", None, None), P(), P()),
        check_vma=False,
    )
```

```python
import functools

import jax
import jax.numpy as jnp
import numpy as np
from jax import lax
from jax.experimental import pallas as pl
from jax.experimental.pallas import tpu as pltpu
from jax.sharding import PartitionSpec as P

LANES = 128
SUB = 8
F32 = jnp.float32
BF16 = jnp.bfloat16


def spread(row):
    return jnp.broadcast_to(row, (SUB, LANES))


def added(terms):
    while len(terms) > 1:
        pairs = [terms[k] + terms[k + 1] for k in range(0, len(terms) - 1, 2)]
        terms = pairs + terms[len(terms) - len(terms) % 2 :]
    return terms[0]


def folded(values):
    row = lax.broadcasted_iota(jnp.int32, (SUB, LANES), 0)
    upper = row < 4
    values = [
        jnp.where(upper, values[n], values[n + 4])
        + pltpu.roll(jnp.where(upper, values[n + 4], values[n]), 4, 0)
        for n in range(4)
    ]
    for step in (2, 1):
        even = (row // step) % 2 == 0
        values = [
            jnp.where(
                even,
                values[n] + pltpu.roll(values[n], SUB - step, 0),
                values[n + step] + pltpu.roll(values[n + step], step, 0),
            )
            for n in range(step)
        ]
    return values[0]


def states_kernel(core, p, hx_low, hx_high, hi, u, filt, f1, we, wb, qkv, xg, blocks_e, blocks_a, ends, xs):
    rows = p.shape[1]
    run = (rows + SUB) // SUB
    taps = filt.shape[1]
    poles, groups = f1.shape
    own = rows - run * (SUB - 1)
    tiles = groups // LANES
    first = core[0] == 0

    def tile(lt, carry):
        lanes = pl.ds(pl.multiple_of(lt * LANES, LANES), LANES)
        part = pl.ds(pl.multiple_of(lax.rem(lt, tiles) * LANES, LANES), LANES)
        which = lt // tiles
        inside = lax.broadcasted_iota(jnp.int32, (SUB, LANES), 0) < SUB - 1
        for j in range(3):
            across = (hx_low, hx_high)[j // 2][j % 2, :, lanes].astype(F32)
            within = hi[j, :, lanes].astype(F32)
            xs[j, 0:SUB] = jnp.where(first, across, within)
            xs[j, SUB : SUB + rows] = p[j, :, lanes].astype(F32)
            xs[j, SUB + rows :] = jnp.where(first, within, across)
        xs[3, SUB : SUB + rows] = u[:, lanes].astype(F32)
        across, within = hx_high[1, :, lanes].astype(F32), hi[3, :, lanes].astype(F32)
        xs[3, SUB + rows :] = jnp.where(first, within, across)

        def mixed(j):
            tap = [spread(filt[j, i : i + 1, lanes]) for i in range(taps)]
            view = [xs[j, pl.ds(SUB + a, SUB, stride=run), :] for a in range(1 - taps, 0)]
            for a in range(run):
                view = view[-(taps - 1) :] + [xs[j, pl.ds(SUB + a, SUB, stride=run), :]]
                yield added([tap[i] * view[-1 - i] for i in range(taps)])

        decay = [spread(f1[n : n + 1, part]) for n in range(poles)]
        for j in (1, 2, 0):
            for a, total in enumerate(mixed(j)):
                at = slice(SUB * a, SUB * a + SUB)
                qkv[which, j, at, part] = total
                if j == 2:
                    xg[which, 0, at, part] = qkv[which, 1, at, part] * total
                if j == 0:
                    xg[which, 1, at, part] = xs[3, pl.ds(SUB + a, SUB, stride=run), :] * total
        for side, order, weight, blocks in (
            (0, range(run), we, blocks_e),
            (1, range(run - 1, -1, -1), wb, blocks_a),
        ):
            state = None
            for a in order:
                x = xg[which, side, SUB * a : SUB * a + SUB, part]
                if a >= own:
                    x = jnp.where(inside, x, 0.0)
                state = [x] * poles if state is None else [decay[n] * state[n] + x for n in range(poles)]
            for n in range(poles):
                blocks[which, n, :, part] = state[n]
            state = [state[n] * weight[n, :, part] for n in range(poles)]
            for n in range(0, poles, SUB):
                ends[side, which, n : n + SUB, part] = folded(state[n : n + SUB])
        return carry

    lax.fori_loop(0, p.shape[2] // LANES, tile, 0)


def blocks_kernel(
    xg, blocks_e, blocks_a, near, skip, join_e, join_a, conv, from_e, from_a, skip_sum
):
    run = xg.shape[2] // SUB
    rows = xg.shape[2] - SUB
    taps = near.shape[0] - run
    poles, groups = blocks_e.shape[1], near.shape[1]
    own = rows - run * (SUB - 1)
    tiles = groups // LANES

    def tile(lt, carry):
        lanes = pl.ds(pl.multiple_of(lt * LANES, LANES), LANES)
        part = pl.ds(pl.multiple_of(lax.rem(lt, tiles) * LANES, LANES), LANES)
        which = lt // tiles
        inside = lax.broadcasted_iota(jnp.int32, (SUB, LANES), 0) < SUB - 1
        gain = spread(skip[0:1, lanes])
        lag = [spread(near[taps + m : taps + m + 1, part]) for m in range(run)]
        lag[0] = lag[0] + gain
        x = [xg[which, 0, SUB * a : SUB * a + SUB, part] for a in range(run)]
        for a in range(run):
            conv[which, 0, SUB * a : SUB * a + SUB, part] = added(
                [lag[m] * x[a - m] for m in range(a + 1)]
            )
        gated = x
        x = [xg[which, 1, SUB * a : SUB * a + SUB, part] for a in range(run)]
        masked = [x[a] if a < own else jnp.where(inside, x[a], 0.0) for a in range(run)]
        skip_sum[which, :, part] = added([masked[a] * gated[a] for a in range(run)])
        past = [jnp.where(inside, 0.0, gain)] + [
            jnp.where(inside, 0.0, -spread(near[taps - m : taps - m + 1, part]))
            for m in range(1, taps - 1)
        ]
        for a in range(run):
            terms = [lag[m] * masked[a + m] for m in range(run - a)]
            if own <= a < own + taps - 1:
                terms = terms + [past[m] * x[a - m] for m in range(a - own + 1)]
            conv[which, 1, SUB * a : SUB * a + SUB, part] = added(terms)
        for n in range(poles):
            value = pltpu.roll(blocks_e[which, n, :, part], 1, 0) * join_e[0, n, :, part]
            for k, step in ((1, 1), (2, 2), (3, 4)):
                value = value + pltpu.roll(value, step, 0) * join_e[k, n, :, part]
            from_e[which, n, :, part] = value
            value = pltpu.roll(blocks_a[which, n, :, part], SUB - 1, 0) * join_a[0, n, :, part]
            for k, step in ((1, 1), (2, 2), (3, 4)):
                value = value + pltpu.roll(value, SUB - step, 0) * join_a[k, n, :, part]
            from_a[which, n, :, part] = value
        return carry

    lax.fori_loop(0, xg.shape[0] * tiles, tile, 0)


def final_kernel(
    core, p, hx_low, hx_high, hi, u, qkv, conv, from_e, from_a, skip_sum, both, found, other, filt, f1, f_all, cz, cy,
    output, grad_p, sums, ps, us, gs, os, es,
):
    rows = p.shape[1]
    run = (rows + SUB) // SUB
    taps = filt.shape[1]
    poles, groups = f1.shape
    own = rows - run * (SUB - 1)
    tiles = groups // LANES
    first = core[0] == 0
    halves = pl.num_programs(0) // 2
    kept = (pl.program_id(0) < halves) == first
    cut = sums.shape[2] // LANES

    def tile(lt, carry):
        lanes = pl.ds(pl.multiple_of(lt * LANES, LANES), LANES)
        part = pl.ds(pl.multiple_of(lax.rem(lt, tiles) * LANES, LANES), LANES)
        which = lt // tiles
        piece = lt // cut
        spot = pl.ds(pl.multiple_of(lax.rem(lt, cut) * LANES, LANES), LANES)
        inside = lax.broadcasted_iota(jnp.int32, (SUB, LANES), 0) < SUB - 1
        for side in range(2):
            far = jnp.where(kept, both[side, which, :, part], found[side, which, :, part])
            close = other[side, which, :, part] + f_all[:, part] * far
            es[side] = jnp.where(first == (side == 0), far, close)
        for j in range(3):
            across = (hx_low, hx_high)[j // 2][j % 2, :, lanes].astype(F32)
            within = hi[j, :, lanes].astype(F32)
            ps[j, 0:SUB] = jnp.where(first, across, within)
            ps[j, SUB : SUB + rows] = p[j, :, lanes].astype(F32)
            ps[j, SUB + rows :] = jnp.where(first, within, across)
        us[0:rows] = u[:, lanes].astype(F32)
        across, within = hx_high[1, :, lanes].astype(F32), hi[3, :, lanes].astype(F32)
        us[rows:] = jnp.where(first, within, across)
        decay = [spread(f1[n : n + 1, part]) for n in range(poles)]

        state = [
            from_e[which, n, :, part] + cz[n, :, part] * spread(es[0, n : n + 1])
            for n in range(poles)
        ]
        for a in range(run):
            at = slice(SUB * a, SUB * a + SUB)
            query, upstream = qkv[which, 0, at, part], us[pl.ds(a, SUB, stride=run), :]
            filtered = conv[which, 0, at, part] + added(list(state))
            os[pl.ds(a, SUB, stride=run), :] = query * filtered
            gs[0, pl.ds(a, SUB, stride=run), :] = upstream * filtered
            if a + 1 < run:
                state = [state[n] * decay[n] for n in range(poles)]
        output[:, lanes] = os[0:rows].astype(BF16)

        state = [
            from_a[which, n, :, part] + cy[n, :, part] * spread(es[1, n : n + 1])
            for n in range(poles)
        ]
        for a in range(run - 1, -1, -1):
            at = slice(SUB * a, SUB * a + SUB)
            grad = conv[which, 1, at, part] + added(list(state))
            gs[1, pl.ds(a, SUB, stride=run), :] = grad * qkv[which, 2, at, part]
            gs[2, pl.ds(a, SUB, stride=run), :] = grad * qkv[which, 1, at, part]
            if a:
                state = [state[n] * decay[n] for n in range(poles)]

        for j in range(3):
            tap = [spread(filt[j, i : i + 1, lanes]) for i in range(taps)]
            grads = [gs[j, pl.ds(a, SUB, stride=run), :] for a in range(taps - 1)]
            views = [ps[j, pl.ds(SUB + a, SUB, stride=run), :] for a in range(1 - taps, 0)]
            sums_of = [None] * taps
            for a in range(run):
                grads = grads[-(taps - 1) :] + [gs[j, pl.ds(a + taps - 1, SUB, stride=run), :]]
                views = views[-(taps - 1) :] + [ps[j, pl.ds(SUB + a, SUB, stride=run), :]]
                total = added([tap[i] * grads[i] for i in range(taps)])
                os[pl.ds(a, SUB, stride=run), :] = total
                grad = grads[0] if a < own else jnp.where(inside, grads[0], 0.0)
                for i in range(taps):
                    term = grad * views[-1 - i]
                    sums_of[i] = term if a == 0 else sums_of[i] + term
            grad_p[j, :, lanes] = os[0:rows].astype(BF16)
            extra = [skip_sum[which, :, part]] + [jnp.zeros((SUB, LANES), F32)] * (SUB - taps)
            extra = extra[: SUB - taps] if j == 0 else extra[1 : SUB - taps + 1]
            sums[piece, j * SUB : j * SUB + SUB, spot] = folded(sums_of + extra)
        return carry

    lax.fori_loop(0, p.shape[2] // LANES, tile, 0)


def shifted(value, axis, steps):
    count = lax.axis_size(axis)
    first, last = (max(0, -steps), min(count, count - steps))
    return lax.ppermute(value, axis, [(source, source + steps) for source in range(first, last)])


def swapped(value):
    count = lax.axis_size("ctx")
    return lax.ppermute(value, "ctx", [(s, s ^ 1) for s in range(count)])


def joined(ends, f_all):
    core = lax.rem(lax.axis_index("ctx"), 2)
    half = ends.shape[1] // 2
    other = swapped(ends)
    first = core == 0
    mine = lax.dynamic_slice_in_dim(ends, core * half, half, 1)
    theirs = lax.dynamic_slice_in_dim(other, core * half, half, 1)
    one, two = jnp.where(first, mine, theirs), jnp.where(first, theirs, mine)
    return other, f_all * one[0] + two[0], one[1] + f_all * two[1]


def paired(value, axis, step, lines=None):
    count = lax.axis_size(axis)
    return lax.ppermute(value, axis, [(source, source ^ step) for source in lines or range(count)])


def scanned(chip_e, chip_a, f_all, beside):
    chips = lax.axis_size("ctx") // 2
    f_chip = f_all * f_all
    if chips == 4:
        odd = lax.rem(lax.axis_index("ctx") // 2, 2) == 1
        sent = jnp.where(odd, chip_a, chip_e)
        first = paired(sent, "ctx", 2)
        kept = beside[0](sent, None)
        first, kept = lax.optimization_barrier((first, kept))
        sent = jnp.where(odd, chip_e, chip_a) + f_chip * first
        near = lax.ppermute(sent, "ctx", [(2, 4), (3, 5), (4, 2), (5, 3)])
        far = lax.ppermute(sent, "ctx", [(2, 6), (3, 7), (4, 0), (5, 1)])
        kept = beside[1](sent, kept)
        near, far, kept = lax.optimization_barrier((near, far, kept))
        far = first + f_chip * far
        return jnp.where(odd, far, near), jnp.where(odd, near, far), kept
    kept = beside[1](chip_e, beside[0](chip_e, None))
    before, after = jnp.zeros_like(chip_e), jnp.zeros_like(chip_a)
    reach = 1
    while reach < chips:
        early, late = shifted(chip_e, "ctx", 2 * reach), shifted(chip_a, "ctx", -2 * reach)
        factor = f_chip ** (reach - 1)
        before, after = before + factor * early, after + factor * late
        factor = f_chip**reach
        chip_e, chip_a = chip_e + factor * early, chip_a + factor * late
        reach = 2 * reach
    return before, after, kept


def chain(left, right, turn):
    index, dp = lax.axis_index("ctx"), lax.axis_index("dp")
    reaches = []
    while 2 ** len(reaches) < lax.axis_size("dp"):
        reaches.append(2 ** len(reaches))
    chips = []
    while 2 ** (len(chips) + 1) < lax.axis_size("ctx"):
        chips.append(2 ** (len(chips) + 1))
    steps = [("ctx", 1, lax.rem(index, 2) == 0)]
    steps = steps + [("dp", step, lax.rem(dp // step, 2) == 0) for step in reaches[::turn]]
    for axis, step, low in steps:
        value = jnp.where(low, left, right) + paired(jnp.where(low, right, left), axis, step)
        half = value.shape[0] // 2
        left, right = value[:half], value[half:]
    for step in chips[::turn]:
        value = value + paired(value, "ctx", step)
    for axis, step, low in reversed(steps):
        other = paired(value, axis, step)
        left, right = jnp.where(low, value, other), jnp.where(low, other, value)
        value = jnp.concatenate([left, right], axis=0)
    return left, right


def summed(value):
    quarter = value.shape[0] // 4
    parts = [value[k * quarter : (k + 1) * quarter] for k in range(4)]
    left, right = chain(parts[0], parts[2], 1)
    other_left, other_right = chain(parts[1], parts[3], -1)
    return jnp.concatenate([left, other_left, right, other_right], axis=0)


def local(projected, short_filter, residues, decay_rates, skip_gain, cotangent):
    rows = projected.shape[1]
    channels = projected.shape[3]
    taps = short_filter.shape[1]
    groups, poles = residues.shape
    width = channels // groups
    run = (rows + SUB) // SUB
    held = rows + SUB
    p = projected[0].transpose(1, 0, 2)
    u = cotangent[0]
    core = lax.rem(lax.axis_index("ctx"), 2)
    head = jnp.concatenate([p[:, :SUB], u[None, :SUB]], axis=0)
    tail = jnp.concatenate([p[:, rows - SUB :], u[None, rows - SUB :]], axis=0)
    devices = lax.axis_size("ctx")
    across = [(k, k + 1) for k in range(1, devices - 1, 2)]
    across = across + [(target, source) for source, target in across]
    sent = jnp.where(core == 0, head, tail)
    hx = [lax.ppermute(sent[2 * k : 2 * k + 2], "ctx", across) for k in range(2)]
    hi = swapped(jnp.where(core == 0, tail, head))

    rate = decay_rates.T
    weight = residues.T
    sub = np.arange(SUB)
    powers = np.stack([run * (7 - sub) - SUB, run * sub, 1 + run * sub, rows - run * (sub + 1) + 1])
    table = jnp.exp(-rate[None, :, None, :] * powers.astype(np.float32)[:, None, :, None])
    we, wb = table[0], table[1]
    cz, cy = weight[:, None, :] * table[2], weight[:, None, :] * table[3]
    f1 = jnp.exp(-rate)
    f_all = jnp.exp(-rate * rows)
    steps = np.array([1, run, 2 * run, 4 * run], np.float32)
    factor = jnp.exp(-rate[None] * steps[:, None, None])
    factor = jnp.concatenate([weight[None] * factor[:1], factor[1:]], axis=0)
    reach = np.array([1, 1, 2, 4])[:, None]
    down, up = sub[None] >= reach, sub[None] < SUB - reach
    join_e = jnp.where(down[:, None, :, None], factor[:, :, None, :], 0.0)
    join_a = jnp.where(up[:, None, :, None], factor[:, :, None, :], 0.0)
    close = np.arange(-taps, run).astype(np.float32)
    near = jnp.sum(weight[:, None, :] * jnp.exp(-rate[:, None, :] * close[None, :, None]), axis=0)

    each = 1

    def by_w(*shape):
        axis = len(shape)
        return pl.BlockSpec(shape + (each * groups,), lambda w: (0,) * axis + (w,))

    def fixed(value):
        return pl.BlockSpec(
            value.shape, lambda w: (0,) * value.ndim, pipeline_mode=pl.Buffered(1)
        )

    params = pltpu.CompilerParams(vmem_limit_bytes=48 * 1024 * 1024)
    shape_of = jax.ShapeDtypeStruct
    ends_spec = pl.BlockSpec((2, each, poles, groups), lambda w: (0, w, 0, 0))
    halved = pl.BlockSpec(
        (2, each, poles, groups), lambda w: (0, lax.rem(w, width // each // 2), 0, 0)
    )
    state_shape = shape_of((width, poles, SUB, groups), F32)
    pair_shape = shape_of((width, 2, held, groups), F32)

    def by_block(*shape, count=each, first=0):
        return pl.BlockSpec((count,) + shape, lambda w: (w + first,) + (0,) * len(shape))

    state_spec = by_block(poles, SUB, groups)
    qkv, xg, blocks_e, blocks_a, ends = pl.pallas_call(
        states_kernel,
        grid=(width // each,),
        in_specs=[
            pl.BlockSpec(memory_space=pltpu.SMEM),
            by_w(3, rows), by_w(2, SUB), by_w(2, SUB), by_w(4, SUB), by_w(rows), by_w(3, taps),
            fixed(f1), fixed(we), fixed(wb),
        ],
        out_specs=[
            by_block(3, held, groups), by_block(2, held, groups), state_spec, state_spec,
            ends_spec,
        ],
        out_shape=[
            shape_of((width, 3, held, groups), F32), pair_shape,
            state_shape, state_shape, shape_of((2, width, poles, groups), F32),
        ],
        scratch_shapes=[pltpu.VMEM((4, held + SUB, LANES), F32)],
        compiler_params=params,
        name="states",
    )(core[None], p, *hx, hi, u, short_filter, f1, we, wb)

    many = 2 if width % 2 == 0 else 1

    def blocks(first, last):
        states = by_block(poles, SUB, groups, count=many, first=first)
        pairs = by_block(2, held, groups, count=many, first=first)

        def call(sent, kept):
            close, _ = lax.optimization_barrier((near, sent))
            held_before = kept or (xg, blocks_e, blocks_a)
            out = pl.pallas_call(
                blocks_kernel,
                grid=(last - first,),
                in_specs=[
                    pairs, states, states, fixed(near),
                    pl.BlockSpec((1, many * groups), lambda w: (0, w + first)),
                    fixed(join_e), fixed(join_a),
                ],
                out_specs=[pairs, states, states, by_block(SUB, groups, count=many)],
                out_shape=[
                    pair_shape, state_shape, state_shape,
                    shape_of(((last - first) * many, SUB, groups), F32),
                ],
                input_output_aliases={0: 0, 1: 1, 2: 2},
                compiler_params=params,
                cost_estimate=pl.CostEstimate(
                    flops=60 * rows * channels, bytes_accessed=35 * 2**20, transcendentals=0
                ),
                name="blocks",
            )(*held_before[:3], close, skip_gain[None], join_e, join_a)
            return [*out[:3], jnp.concatenate([*held_before[3:], out[3]], axis=0)]

        return call

    steps = width // many
    cut = (steps + 1) // 3
    other, chip_e, chip_a = joined(ends, f_all)
    before, after, (conv, from_e, from_a, skip_sum) = scanned(
        chip_e, chip_a, f_all, (blocks(0, cut), blocks(cut, steps))
    )
    both = jnp.stack([before, after])
    found = swapped(both)

    count = 3 * SUB
    split = 2 if groups % (2 * LANES) == 0 else 1
    scratch = [
        pltpu.VMEM((3, held + SUB, LANES), F32),
        pltpu.VMEM((held, LANES), F32),
        pltpu.VMEM((3, held + SUB, LANES), F32),
        pltpu.VMEM((held, LANES), F32),
        pltpu.VMEM((2, poles, LANES), F32),
    ]
    output, grad_p, sums = pl.pallas_call(
        final_kernel,
        grid=(width // each,),
        in_specs=[
            pl.BlockSpec(memory_space=pltpu.SMEM),
            by_w(3, rows), by_w(2, SUB), by_w(2, SUB), by_w(4, SUB), by_w(rows),
            by_block(3, held, groups), by_block(2, held, groups), state_spec, state_spec,
            by_block(SUB, groups), halved, halved, ends_spec,
            by_w(3, taps), fixed(f1), fixed(f_all), fixed(cz), fixed(cy),
        ],
        out_specs=[
            by_w(rows), by_w(3, rows),
            pl.BlockSpec((each * split, count, groups // split), lambda w: (w, 0, 0)),
        ],
        out_shape=[
            shape_of((rows, channels), BF16),
            shape_of((3, rows, channels), BF16),
            shape_of((width * split, count, groups // split), F32),
        ],
        scratch_shapes=scratch,
        compiler_params=params,
        name="final",
    )(
        core[None], p, *hx, hi, u, qkv, conv, from_e, from_a, skip_sum, both, found, other, short_filter,
        f1, f_all, cz, cy,
    )

    total = summed(sums).transpose(1, 0, 2).reshape(3, SUB, channels)
    grad_short, grad_skip = total[:, :taps], total[0, taps]
    return output[None], grad_p.transpose(1, 0, 2)[None], grad_short, grad_skip


def solution(mesh):
    placed = (P("dp", "ctx", None, None), P(), P(), P(), P(), P("dp", "ctx", None))
    return jax.shard_map(
        local,
        mesh=mesh,
        in_specs=placed,
        out_specs=(P("dp", "ctx", None), P("dp", "ctx", None, None), P(), P()),
        check_vma=False,
    )
```

```python
import functools

import jax
import jax.numpy as jnp
import numpy as np
from jax import lax
from jax.experimental import pallas as pl
from jax.experimental.pallas import tpu as pltpu
from jax.sharding import PartitionSpec as P

LANES = 128
SUB = 8
F32 = jnp.float32
BF16 = jnp.bfloat16


def spread(row):
    return jnp.broadcast_to(row, (SUB, LANES))


def added(terms):
    while len(terms) > 1:
        pairs = [terms[k] + terms[k + 1] for k in range(0, len(terms) - 1, 2)]
        terms = pairs + terms[len(terms) - len(terms) % 2 :]
    return terms[0]


def folded(values):
    row = lax.broadcasted_iota(jnp.int32, (SUB, LANES), 0)
    upper = row < 4
    values = [
        jnp.where(upper, values[n], values[n + 4])
        + pltpu.roll(jnp.where(upper, values[n + 4], values[n]), 4, 0)
        for n in range(4)
    ]
    for step in (2, 1):
        even = (row // step) % 2 == 0
        values = [
            jnp.where(
                even,
                values[n] + pltpu.roll(values[n], SUB - step, 0),
                values[n + step] + pltpu.roll(values[n + step], step, 0),
            )
            for n in range(step)
        ]
    return values[0]


def states_kernel(core, p, hx, hi, u, filt, f1, we, wb, *rest):
    qkv, xg, blocks_e, blocks_a, ends, xs = rest[-6:]
    rows = p.shape[1]
    run = (rows + SUB) // SUB
    taps = filt.shape[1]
    poles, groups = f1.shape
    own = rows - run * (SUB - 1)
    tiles = groups // LANES
    first = core[0] == 0

    def tile(lt, carry):
        lanes = pl.ds(pl.multiple_of(lt * LANES, LANES), LANES)
        part = pl.ds(pl.multiple_of(lax.rem(lt, tiles) * LANES, LANES), LANES)
        which = lt // tiles
        inside = lax.broadcasted_iota(jnp.int32, (SUB, LANES), 0) < SUB - 1
        for j in range(3):
            across, within = hx[j, :, lanes].astype(F32), hi[j, :, lanes].astype(F32)
            xs[j, 0:SUB] = jnp.where(first, across, within)
            xs[j, SUB : SUB + rows] = p[j, :, lanes].astype(F32)
            xs[j, SUB + rows :] = jnp.where(first, within, across)
        xs[3, SUB : SUB + rows] = u[:, lanes].astype(F32)
        across, within = hx[3, :, lanes].astype(F32), hi[3, :, lanes].astype(F32)
        xs[3, SUB + rows :] = jnp.where(first, within, across)

        def mixed(j):
            tap = [spread(filt[j, i : i + 1, lanes]) for i in range(taps)]
            view = [xs[j, pl.ds(SUB + a, SUB, stride=run), :] for a in range(1 - taps, 0)]
            for a in range(run):
                view = view[-(taps - 1) :] + [xs[j, pl.ds(SUB + a, SUB, stride=run), :]]
                yield added([tap[i] * view[-1 - i] for i in range(taps)])

        decay = [spread(f1[n : n + 1, part]) for n in range(poles)]
        for j in (1, 2, 0):
            for a, total in enumerate(mixed(j)):
                at = slice(SUB * a, SUB * a + SUB)
                qkv[which, j, at, part] = total
                if j == 2:
                    xg[which, 0, at, part] = qkv[which, 1, at, part] * total
                if j == 0:
                    xg[which, 1, at, part] = xs[3, pl.ds(SUB + a, SUB, stride=run), :] * total
        for side, order, weight, blocks in (
            (0, range(run), we, blocks_e),
            (1, range(run - 1, -1, -1), wb, blocks_a),
        ):
            state = None
            for a in order:
                x = xg[which, side, SUB * a : SUB * a + SUB, part]
                if a >= own:
                    x = jnp.where(inside, x, 0.0)
                state = [x] * poles if state is None else [decay[n] * state[n] + x for n in range(poles)]
            for n in range(poles):
                blocks[which, n, :, part] = state[n]
            state = [state[n] * weight[n, :, part] for n in range(poles)]
            for n in range(0, poles, SUB):
                ends[side, which, n : n + SUB, part] = folded(state[n : n + SUB])
        return carry

    lax.fori_loop(0, p.shape[2] // LANES, tile, 0)


def blocks_kernel(xg, near, skip, conv, skip_sum):
    run = xg.shape[2] // SUB
    rows = xg.shape[2] - SUB
    taps = near.shape[0] - run
    groups = near.shape[1]
    own = rows - run * (SUB - 1)
    tiles = groups // LANES

    def tile(lt, carry):
        lanes = pl.ds(pl.multiple_of(lt * LANES, LANES), LANES)
        part = pl.ds(pl.multiple_of(lax.rem(lt, tiles) * LANES, LANES), LANES)
        which = lt // tiles
        inside = lax.broadcasted_iota(jnp.int32, (SUB, LANES), 0) < SUB - 1
        gain = spread(skip[0:1, lanes])
        lag = [spread(near[taps + m : taps + m + 1, part]) for m in range(run)]
        lag[0] = lag[0] + gain
        x = [xg[which, 0, SUB * a : SUB * a + SUB, part] for a in range(run)]
        for a in range(run):
            conv[which, 0, SUB * a : SUB * a + SUB, part] = added(
                [lag[m] * x[a - m] for m in range(a + 1)]
            )
        gated = x
        x = [xg[which, 1, SUB * a : SUB * a + SUB, part] for a in range(run)]
        masked = [x[a] if a < own else jnp.where(inside, x[a], 0.0) for a in range(run)]
        skip_sum[which, :, part] = added([masked[a] * gated[a] for a in range(run)])
        past = [jnp.where(inside, 0.0, gain)] + [
            jnp.where(inside, 0.0, -spread(near[taps - m : taps - m + 1, part]))
            for m in range(1, taps - 1)
        ]
        for a in range(run):
            terms = [lag[m] * masked[a + m] for m in range(run - a)]
            if own <= a < own + taps - 1:
                terms = terms + [past[m] * x[a - m] for m in range(a - own + 1)]
            conv[which, 1, SUB * a : SUB * a + SUB, part] = added(terms)
        return carry

    lax.fori_loop(0, xg.shape[0] * tiles, tile, 0)


def entered(value, join, n, part, turn):
    value = pltpu.roll(value, turn % SUB, 0) * join[0, n, :, part]
    for k, step in ((1, 1), (2, 2), (3, 4)):
        value = value + pltpu.roll(value, (turn * step) % SUB, 0) * join[k, n, :, part]
    return value


def final_kernel(
    core, p, hx_low, hx_high, hi, u, qkv, conv, blocks_e, blocks_a, join_e, join_a, skip_sum, both, found, other, filt, f1, f_all, cz, cy,
    output, grad_p, sums, ps, us, gs, os, es,
):
    rows = p.shape[1]
    run = (rows + SUB) // SUB
    taps = filt.shape[1]
    poles, groups = f1.shape
    own = rows - run * (SUB - 1)
    tiles = groups // LANES
    first = core[0] == 0
    halves = pl.num_programs(0) // 2
    early = pl.program_id(0) < halves
    kept = early == first
    cut = sums.shape[2] // LANES

    def tile(lt, carry):
        lanes = pl.ds(pl.multiple_of(lt * LANES, LANES), LANES)
        part = pl.ds(pl.multiple_of(lax.rem(lt, tiles) * LANES, LANES), LANES)
        which = lt // tiles
        piece = lt // cut
        spot = pl.ds(pl.multiple_of(lax.rem(lt, cut) * LANES, LANES), LANES)
        inside = lax.broadcasted_iota(jnp.int32, (SUB, LANES), 0) < SUB - 1
        for side in range(2):
            far = jnp.where(kept, both[side, which, :, part], found[side, which, :, part])
            close = other[side, which, :, part] + f_all[:, part] * far
            es[side] = jnp.where(first == (side == 0), far, close)
        for j in range(3):
            across = jnp.where(early, hx_low[j, :, lanes].astype(F32), hx_high[j, :, lanes].astype(F32))
            within = hi[j, :, lanes].astype(F32)
            ps[j, 0:SUB] = jnp.where(first, across, within)
            ps[j, SUB : SUB + rows] = p[j, :, lanes].astype(F32)
            ps[j, SUB + rows :] = jnp.where(first, within, across)
        us[0:rows] = u[:, lanes].astype(F32)
        across = jnp.where(early, hx_low[3, :, lanes].astype(F32), hx_high[3, :, lanes].astype(F32))
        within = hi[3, :, lanes].astype(F32)
        us[rows:] = jnp.where(first, within, across)
        decay = [spread(f1[n : n + 1, part]) for n in range(poles)]

        state = [
            entered(blocks_e[which, n, :, part], join_e, n, part, 1)
            + cz[n, :, part] * spread(es[0, n : n + 1])
            for n in range(poles)
        ]
        for a in range(run):
            at = slice(SUB * a, SUB * a + SUB)
            query, upstream = qkv[which, 0, at, part], us[pl.ds(a, SUB, stride=run), :]
            filtered = conv[which, 0, at, part] + added(list(state))
            os[pl.ds(a, SUB, stride=run), :] = query * filtered
            gs[0, pl.ds(a, SUB, stride=run), :] = upstream * filtered
            if a + 1 < run:
                state = [state[n] * decay[n] for n in range(poles)]
        output[:, lanes] = os[0:rows].astype(BF16)

        state = [
            entered(blocks_a[which, n, :, part], join_a, n, part, -1)
            + cy[n, :, part] * spread(es[1, n : n + 1])
            for n in range(poles)
        ]
        for a in range(run - 1, -1, -1):
            at = slice(SUB * a, SUB * a + SUB)
            grad = conv[which, 1, at, part] + added(list(state))
            gs[1, pl.ds(a, SUB, stride=run), :] = grad * qkv[which, 2, at, part]
            gs[2, pl.ds(a, SUB, stride=run), :] = grad * qkv[which, 1, at, part]
            if a:
                state = [state[n] * decay[n] for n in range(poles)]

        for j in range(3):
            tap = [spread(filt[j, i : i + 1, lanes]) for i in range(taps)]
            grads = [gs[j, pl.ds(a, SUB, stride=run), :] for a in range(taps - 1)]
            views = [ps[j, pl.ds(SUB + a, SUB, stride=run), :] for a in range(1 - taps, 0)]
            sums_of = [None] * taps
            for a in range(run):
                grads = grads[-(taps - 1) :] + [gs[j, pl.ds(a + taps - 1, SUB, stride=run), :]]
                views = views[-(taps - 1) :] + [ps[j, pl.ds(SUB + a, SUB, stride=run), :]]
                total = added([tap[i] * grads[i] for i in range(taps)])
                os[pl.ds(a, SUB, stride=run), :] = total
                grad = grads[0] if a < own else jnp.where(inside, grads[0], 0.0)
                for i in range(taps):
                    term = grad * views[-1 - i]
                    sums_of[i] = term if a == 0 else sums_of[i] + term
            grad_p[j, :, lanes] = os[0:rows].astype(BF16)
            extra = [skip_sum[which, :, part]] + [jnp.zeros((SUB, LANES), F32)] * (SUB - taps)
            extra = extra[: SUB - taps] if j == 0 else extra[1 : SUB - taps + 1]
            sums[piece, j * SUB : j * SUB + SUB, spot] = folded(sums_of + extra)
        return carry

    lax.fori_loop(0, p.shape[2] // LANES, tile, 0)


def shifted(value, axis, steps):
    count = lax.axis_size(axis)
    first, last = (max(0, -steps), min(count, count - steps))
    return lax.ppermute(value, axis, [(source, source + steps) for source in range(first, last)])


def swapped(value):
    count = lax.axis_size("ctx")
    return lax.ppermute(value, "ctx", [(s, s ^ 1) for s in range(count)])


def joined(ends, f_all):
    core = lax.rem(lax.axis_index("ctx"), 2)
    half = ends.shape[1] // 2
    other = swapped(ends)
    first = core == 0
    mine = lax.dynamic_slice_in_dim(ends, core * half, half, 1)
    theirs = lax.dynamic_slice_in_dim(other, core * half, half, 1)
    one, two = jnp.where(first, mine, theirs), jnp.where(first, theirs, mine)
    return other, f_all * one[0] + two[0], one[1] + f_all * two[1]


def paired(value, axis, step, lines=None):
    count = lax.axis_size(axis)
    return lax.ppermute(value, axis, [(source, source ^ step) for source in lines or range(count)])


def scanned(chip_e, chip_a, f_all, beside):
    chips = lax.axis_size("ctx") // 2
    f_chip = f_all * f_all
    if chips == 4:
        odd = lax.rem(lax.axis_index("ctx") // 2, 2) == 1
        sent = jnp.where(odd, chip_a, chip_e)
        first = paired(sent, "ctx", 2)
        kept = beside[0](sent, None)
        first, kept = lax.optimization_barrier((first, kept))
        sent = jnp.where(odd, chip_e, chip_a) + f_chip * first
        near = lax.ppermute(sent, "ctx", [(2, 4), (3, 5), (4, 2), (5, 3)])
        far = lax.ppermute(sent, "ctx", [(2, 6), (3, 7), (4, 0), (5, 1)])
        kept = beside[1](sent, kept)
        near, far, kept = lax.optimization_barrier((near, far, kept))
        far = first + f_chip * far
        return jnp.where(odd, far, near), jnp.where(odd, near, far), kept
    kept = beside[1](chip_e, beside[0](chip_e, None))
    before, after = jnp.zeros_like(chip_e), jnp.zeros_like(chip_a)
    reach = 1
    while reach < chips:
        early, late = shifted(chip_e, "ctx", 2 * reach), shifted(chip_a, "ctx", -2 * reach)
        factor = f_chip ** (reach - 1)
        before, after = before + factor * early, after + factor * late
        factor = f_chip**reach
        chip_e, chip_a = chip_e + factor * early, chip_a + factor * late
        reach = 2 * reach
    return before, after, kept


def rotated(value, axis, steps):
    count = lax.axis_size(axis)
    return lax.ppermute(value, axis, [(s, (s + steps) % count) for s in range(count)])


def summed(value):
    dp, parts = lax.axis_index("dp"), lax.axis_size("dp")
    low = lax.rem(lax.axis_index("ctx"), 2) == 0
    half = value.shape[0] // 2
    left, right = value[:half], value[half:]
    value = jnp.where(low, left, right) + swapped(jnp.where(low, right, left))
    size = half // parts
    piece = lambda k: lax.dynamic_slice_in_dim(value, lax.rem(dp + k, parts) * size, size, 0)
    total = piece(0)
    for term in [rotated(piece(k), "dp", k) for k in range(1, parts)]:
        total = total + term
    reach = 2
    while reach < lax.axis_size("ctx"):
        total = total + paired(total, "ctx", reach)
        reach = 2 * reach
    value = jnp.zeros((half,) + value.shape[1:], F32)
    for k in range(parts):
        term = rotated(total, "dp", k) if k else total
        at = lax.rem(dp + parts - k, parts) * size
        value = lax.dynamic_update_slice_in_dim(value, term, at, 0)
    other = swapped(value)
    return jnp.concatenate([jnp.where(low, value, other), jnp.where(low, other, value)], axis=0)


def local(projected, short_filter, residues, decay_rates, skip_gain, cotangent):
    rows = projected.shape[1]
    channels = projected.shape[3]
    taps = short_filter.shape[1]
    groups, poles = residues.shape
    width = channels // groups
    run = (rows + SUB) // SUB
    held = rows + SUB
    p = projected[0].transpose(1, 0, 2)
    u = cotangent[0]
    core = lax.rem(lax.axis_index("ctx"), 2)
    head = jnp.concatenate([p[:, :SUB], u[None, :SUB]], axis=0)
    tail = jnp.concatenate([p[:, rows - SUB :], u[None, rows - SUB :]], axis=0)
    devices = lax.axis_size("ctx")
    across = [(k, k + 1) for k in range(1, devices - 1, 2)]
    across = across + [(target, source) for source, target in across]
    sent = jnp.where(core == 0, head, tail)
    middle = channels // 2
    hx = [lax.ppermute(part, "ctx", across) for part in (sent[..., :middle], sent[..., middle:])]
    hi = swapped(jnp.where(core == 0, tail, head))

    rate = decay_rates.T
    weight = residues.T
    sub = np.arange(SUB)
    powers = np.stack([run * (7 - sub) - SUB, run * sub, 1 + run * sub, rows - run * (sub + 1) + 1])
    table = jnp.exp(-rate[None, :, None, :] * powers.astype(np.float32)[:, None, :, None])
    we, wb = table[0], table[1]
    cz, cy = weight[:, None, :] * table[2], weight[:, None, :] * table[3]
    f1 = jnp.exp(-rate)
    f_all = jnp.exp(-rate * rows)
    steps = np.array([1, run, 2 * run, 4 * run], np.float32)
    factor = jnp.exp(-rate[None] * steps[:, None, None])
    factor = jnp.concatenate([weight[None] * factor[:1], factor[1:]], axis=0)
    reach = np.array([1, 1, 2, 4])[:, None]
    down, up = sub[None] >= reach, sub[None] < SUB - reach
    join_e = jnp.where(down[:, None, :, None], factor[:, :, None, :], 0.0)
    join_a = jnp.where(up[:, None, :, None], factor[:, :, None, :], 0.0)
    close = np.arange(-taps, run).astype(np.float32)
    near = jnp.sum(weight[:, None, :] * jnp.exp(-rate[:, None, :] * close[None, :, None]), axis=0)

    each = 1

    def by_w(*shape):
        axis = len(shape)
        return pl.BlockSpec(shape + (each * groups,), lambda w: (0,) * axis + (w,))

    def fixed(value):
        return pl.BlockSpec(
            value.shape, lambda w: (0,) * value.ndim, pipeline_mode=pl.Buffered(1)
        )

    params = pltpu.CompilerParams(vmem_limit_bytes=48 * 1024 * 1024)
    shape_of = jax.ShapeDtypeStruct
    ends_spec = pl.BlockSpec((2, each, poles, groups), lambda w: (0, w, 0, 0))
    halved = pl.BlockSpec(
        (2, each, poles, groups), lambda w: (0, lax.rem(w, width // each // 2), 0, 0)
    )
    state_shape = shape_of((width, poles, SUB, groups), F32)
    pair_shape = shape_of((width, 2, held, groups), F32)

    def by_block(*shape, count=each, first=0):
        return pl.BlockSpec((count,) + shape, lambda w: (w + first,) + (0,) * len(shape))

    state_spec = by_block(poles, SUB, groups)
    half = width // 2

    def states(k, filled):
        def at_w(*shape):
            axis = len(shape)
            return pl.BlockSpec(shape + (groups,), lambda w: (0,) * axis + (w + k * half,))

        block = functools.partial(by_block, first=k * half)
        return pl.pallas_call(
            states_kernel,
            grid=(half,),
            in_specs=[
                pl.BlockSpec(memory_space=pltpu.SMEM),
                at_w(3, rows), by_w(4, SUB), at_w(4, SUB), at_w(rows), at_w(3, taps),
                fixed(f1), fixed(we), fixed(wb),
            ] + [pl.BlockSpec(memory_space=pl.ANY)] * len(filled),
            out_specs=[
                block(3, held, groups), block(2, held, groups), block(poles, SUB, groups),
                block(poles, SUB, groups),
                pl.BlockSpec((2, each, poles, groups), lambda w: (0, w + k * half, 0, 0)),
            ],
            out_shape=[
                shape_of((width, 3, held, groups), F32), pair_shape,
                state_shape, state_shape, shape_of((2, width, poles, groups), F32),
            ],
            input_output_aliases={9 + side: side for side in range(len(filled))},
            scratch_shapes=[pltpu.VMEM((4, held + SUB, LANES), F32)],
            compiler_params=params,
            name="states",
        )(core[None], p, hx[k], hi, u, short_filter, f1, we, wb, *filled)

    qkv, xg, blocks_e, blocks_a, ends = states(1, states(0, ()))

    many = 2 if width % 2 == 0 else 1

    def blocks(first, last):
        pairs = by_block(2, held, groups, count=many, first=first)

        def call(sent, kept):
            close, _ = lax.optimization_barrier((near, sent))
            pair, *sums = kept or (xg,)
            pair, skip = pl.pallas_call(
                blocks_kernel,
                grid=(last - first,),
                in_specs=[
                    pairs, fixed(near), pl.BlockSpec((1, many * groups), lambda w: (0, w + first)),
                ],
                out_specs=[pairs, by_block(SUB, groups, count=many)],
                out_shape=[pair_shape, shape_of(((last - first) * many, SUB, groups), F32)],
                input_output_aliases={0: 0},
                compiler_params=params,
                cost_estimate=pl.CostEstimate(
                    flops=60 * rows * channels, bytes_accessed=18 * 2**20, transcendentals=0
                ),
                name="blocks",
            )(pair, close, skip_gain[None])
            return [pair, jnp.concatenate([*sums, skip], axis=0)]

        return call

    steps = width // many
    cut = (steps + 1) // 3
    other, chip_e, chip_a = joined(ends, f_all)
    before, after, (conv, skip_sum) = scanned(
        chip_e, chip_a, f_all, (blocks(0, cut), blocks(cut, steps))
    )
    both = jnp.stack([before, after])
    found = swapped(both)

    count = 3 * SUB
    low = pl.BlockSpec((4, SUB, groups), lambda w: (0, 0, jnp.minimum(w, half - 1)))
    high = pl.BlockSpec((4, SUB, groups), lambda w: (0, 0, jnp.maximum(w - half, 0)))
    split = 2 if groups % (2 * LANES) == 0 else 1
    scratch = [
        pltpu.VMEM((3, held + SUB, LANES), F32),
        pltpu.VMEM((held, LANES), F32),
        pltpu.VMEM((3, held + SUB, LANES), F32),
        pltpu.VMEM((held, LANES), F32),
        pltpu.VMEM((2, poles, LANES), F32),
    ]
    output, grad_p, sums = pl.pallas_call(
        final_kernel,
        grid=(width // each,),
        in_specs=[
            pl.BlockSpec(memory_space=pltpu.SMEM),
            by_w(3, rows), low, high, by_w(4, SUB), by_w(rows),
            by_block(3, held, groups), by_block(2, held, groups), state_spec, state_spec,
            fixed(join_e), fixed(join_a), by_block(SUB, groups), halved, halved, ends_spec,
            by_w(3, taps), fixed(f1), fixed(f_all), fixed(cz), fixed(cy),
        ],
        out_specs=[
            by_w(rows), by_w(3, rows),
            pl.BlockSpec((each * split, count, groups // split), lambda w: (w, 0, 0)),
        ],
        out_shape=[
            shape_of((rows, channels), BF16),
            shape_of((3, rows, channels), BF16),
            shape_of((width * split, count, groups // split), F32),
        ],
        scratch_shapes=scratch,
        compiler_params=params,
        name="final",
    )(
        core[None], p, *hx, hi, u, qkv, conv, blocks_e, blocks_a, join_e, join_a, skip_sum, both, found, other, short_filter,
        f1, f_all, cz, cy,
    )

    total = summed(sums).transpose(1, 0, 2).reshape(3, SUB, channels)
    grad_short, grad_skip = total[:, :taps], total[0, taps]
    return output[None], grad_p.transpose(1, 0, 2)[None], grad_short, grad_skip


def solution(mesh):
    placed = (P("dp", "ctx", None, None), P(), P(), P(), P(), P("dp", "ctx", None))
    return jax.shard_map(
        local,
        mesh=mesh,
        in_specs=placed,
        out_specs=(P("dp", "ctx", None), P("dp", "ctx", None, None), P(), P()),
        check_vma=False,
    )
```

```python
import functools

import jax
import jax.numpy as jnp
import numpy as np
from jax import lax
from jax.experimental import pallas as pl
from jax.experimental.pallas import tpu as pltpu
from jax.sharding import PartitionSpec as P

LANES = 128
SUB = 8
F32 = jnp.float32
BF16 = jnp.bfloat16


def spread(row):
    return jnp.broadcast_to(row, (SUB, LANES))


def added(terms):
    while len(terms) > 1:
        pairs = [terms[k] + terms[k + 1] for k in range(0, len(terms) - 1, 2)]
        terms = pairs + terms[len(terms) - len(terms) % 2 :]
    return terms[0]


def folded(values):
    row = lax.broadcasted_iota(jnp.int32, (SUB, LANES), 0)
    upper = row < 4
    values = [
        jnp.where(upper, values[n], values[n + 4])
        + pltpu.roll(jnp.where(upper, values[n + 4], values[n]), 4, 0)
        for n in range(4)
    ]
    for step in (2, 1):
        even = (row // step) % 2 == 0
        values = [
            jnp.where(
                even,
                values[n] + pltpu.roll(values[n], SUB - step, 0),
                values[n + step] + pltpu.roll(values[n + step], step, 0),
            )
            for n in range(step)
        ]
    return values[0]


def states_kernel(core, p, hx_low, hx_high, hi, u, filt, f1, we, wb, qkv, xg, blocks_e, blocks_a, ends, xs):
    rows = p.shape[1]
    run = (rows + SUB) // SUB
    taps = filt.shape[1]
    poles, groups = f1.shape
    own = rows - run * (SUB - 1)
    tiles = groups // LANES
    first = core[0] == 0

    def tile(lt, carry):
        lanes = pl.ds(pl.multiple_of(lt * LANES, LANES), LANES)
        part = pl.ds(pl.multiple_of(lax.rem(lt, tiles) * LANES, LANES), LANES)
        which = lt // tiles
        inside = lax.broadcasted_iota(jnp.int32, (SUB, LANES), 0) < SUB - 1
        for j in range(3):
            across = (hx_low, hx_high)[j // 2][j % 2, :, lanes].astype(F32)
            within = hi[j, :, lanes].astype(F32)
            xs[j, 0:SUB] = jnp.where(first, across, within)
            xs[j, SUB : SUB + rows] = p[j, :, lanes].astype(F32)
            xs[j, SUB + rows :] = jnp.where(first, within, across)
        xs[3, SUB : SUB + rows] = u[:, lanes].astype(F32)
        across, within = hx_high[1, :, lanes].astype(F32), hi[3, :, lanes].astype(F32)
        xs[3, SUB + rows :] = jnp.where(first, within, across)

        def mixed(j):
            tap = [spread(filt[j, i : i + 1, lanes]) for i in range(taps)]
            view = [xs[j, pl.ds(SUB + a, SUB, stride=run), :] for a in range(1 - taps, 0)]
            for a in range(run):
                view = view[-(taps - 1) :] + [xs[j, pl.ds(SUB + a, SUB, stride=run), :]]
                yield added([tap[i] * view[-1 - i] for i in range(taps)])

        decay = [spread(f1[n : n + 1, part]) for n in range(poles)]
        for j in (1, 2, 0):
            for a, total in enumerate(mixed(j)):
                at = slice(SUB * a, SUB * a + SUB)
                qkv[which, j, at, part] = total
                if j == 2:
                    xg[which, 0, at, part] = qkv[which, 1, at, part] * total
                if j == 0:
                    xg[which, 1, at, part] = xs[3, pl.ds(SUB + a, SUB, stride=run), :] * total
        for side, order, weight, blocks in (
            (0, range(run), we, blocks_e),
            (1, range(run - 1, -1, -1), wb, blocks_a),
        ):
            state = None
            for a in order:
                x = xg[which, side, SUB * a : SUB * a + SUB, part]
                if a >= own:
                    x = jnp.where(inside, x, 0.0)
                state = [x] * poles if state is None else [decay[n] * state[n] + x for n in range(poles)]
            for n in range(poles):
                blocks[which, n, :, part] = state[n]
            state = [state[n] * weight[n, :, part] for n in range(poles)]
            for n in range(0, poles, SUB):
                ends[side, which, n : n + SUB, part] = folded(state[n : n + SUB])
        return carry

    lax.fori_loop(0, p.shape[2] // LANES, tile, 0)


def blocks_kernel(
    xg, blocks_e, blocks_a, near, skip, join_e, join_a, conv, from_e, from_a, skip_sum
):
    run = xg.shape[2] // SUB
    rows = xg.shape[2] - SUB
    taps = near.shape[0] - run
    poles, groups = blocks_e.shape[1], near.shape[1]
    own = rows - run * (SUB - 1)
    tiles = groups // LANES

    def tile(lt, carry):
        lanes = pl.ds(pl.multiple_of(lt * LANES, LANES), LANES)
        part = pl.ds(pl.multiple_of(lax.rem(lt, tiles) * LANES, LANES), LANES)
        which = lt // tiles
        inside = lax.broadcasted_iota(jnp.int32, (SUB, LANES), 0) < SUB - 1
        gain = spread(skip[0:1, lanes])
        lag = [spread(near[taps + m : taps + m + 1, part]) for m in range(run)]
        lag[0] = lag[0] + gain
        x = [xg[which, 0, SUB * a : SUB * a + SUB, part] for a in range(run)]
        for a in range(run):
            conv[which, 0, SUB * a : SUB * a + SUB, part] = added(
                [lag[m] * x[a - m] for m in range(a + 1)]
            )
        gated = x
        x = [xg[which, 1, SUB * a : SUB * a + SUB, part] for a in range(run)]
        masked = [x[a] if a < own else jnp.where(inside, x[a], 0.0) for a in range(run)]
        skip_sum[which, :, part] = added([masked[a] * gated[a] for a in range(run)])
        past = [jnp.where(inside, 0.0, gain)] + [
            jnp.where(inside, 0.0, -spread(near[taps - m : taps - m + 1, part]))
            for m in range(1, taps - 1)
        ]
        for a in range(run):
            terms = [lag[m] * masked[a + m] for m in range(run - a)]
            if own <= a < own + taps - 1:
                terms = terms + [past[m] * x[a - m] for m in range(a - own + 1)]
            conv[which, 1, SUB * a : SUB * a + SUB, part] = added(terms)
        for n in range(poles):
            value = pltpu.roll(blocks_e[which, n, :, part], 1, 0) * join_e[0, n, :, part]
            for k, step in ((1, 1), (2, 2), (3, 4)):
                value = value + pltpu.roll(value, step, 0) * join_e[k, n, :, part]
            from_e[which, n, :, part] = value
            value = pltpu.roll(blocks_a[which, n, :, part], SUB - 1, 0) * join_a[0, n, :, part]
            for k, step in ((1, 1), (2, 2), (3, 4)):
                value = value + pltpu.roll(value, SUB - step, 0) * join_a[k, n, :, part]
            from_a[which, n, :, part] = value
        return carry

    lax.fori_loop(0, xg.shape[0] * tiles, tile, 0)


def final_kernel(
    core, p, hx_low, hx_high, hi, u, qkv, conv, from_e, from_a, skip_sum, both, found, other, filt, f1, f_all, cz, cy,
    output, grad_p, sums, ps, us, gs, os, es,
):
    rows = p.shape[1]
    run = (rows + SUB) // SUB
    taps = filt.shape[1]
    poles, groups = f1.shape
    own = rows - run * (SUB - 1)
    tiles = groups // LANES
    first = core[0] == 0
    halves = pl.num_programs(0) // 2
    kept = (pl.program_id(0) < halves) == first
    cut = sums.shape[2] // LANES

    def tile(lt, carry):
        lanes = pl.ds(pl.multiple_of(lt * LANES, LANES), LANES)
        part = pl.ds(pl.multiple_of(lax.rem(lt, tiles) * LANES, LANES), LANES)
        which = lt // tiles
        piece = lt // cut
        spot = pl.ds(pl.multiple_of(lax.rem(lt, cut) * LANES, LANES), LANES)
        inside = lax.broadcasted_iota(jnp.int32, (SUB, LANES), 0) < SUB - 1
        for side in range(2):
            far = jnp.where(kept, both[side, which, :, part], found[side, which, :, part])
            close = other[side, which, :, part] + f_all[:, part] * far
            es[side] = jnp.where(first == (side == 0), far, close)
        for j in range(3):
            across = (hx_low, hx_high)[j // 2][j % 2, :, lanes].astype(F32)
            within = hi[j, :, lanes].astype(F32)
            ps[j, 0:SUB] = jnp.where(first, across, within)
            ps[j, SUB : SUB + rows] = p[j, :, lanes].astype(F32)
            ps[j, SUB + rows :] = jnp.where(first, within, across)
        us[0:rows] = u[:, lanes].astype(F32)
        across, within = hx_high[1, :, lanes].astype(F32), hi[3, :, lanes].astype(F32)
        us[rows:] = jnp.where(first, within, across)
        decay = [spread(f1[n : n + 1, part]) for n in range(poles)]

        state = [
            from_e[which, n, :, part] + cz[n, :, part] * spread(es[0, n : n + 1])
            for n in range(poles)
        ]
        for a in range(run):
            at = slice(SUB * a, SUB * a + SUB)
            query, upstream = qkv[which, 0, at, part], us[pl.ds(a, SUB, stride=run), :]
            filtered = conv[which, 0, at, part] + added(list(state))
            os[pl.ds(a, SUB, stride=run), :] = query * filtered
            gs[0, at] = upstream * filtered
            if a + 1 < run:
                state = [state[n] * decay[n] for n in range(poles)]
        output[:, lanes] = os[0:rows].astype(BF16)

        state = [
            from_a[which, n, :, part] + cy[n, :, part] * spread(es[1, n : n + 1])
            for n in range(poles)
        ]
        for a in range(run - 1, -1, -1):
            at = slice(SUB * a, SUB * a + SUB)
            grad = conv[which, 1, at, part] + added(list(state))
            gs[1, at] = grad * qkv[which, 2, at, part]
            gs[2, at] = grad * qkv[which, 1, at, part]
            if a:
                state = [state[n] * decay[n] for n in range(poles)]

        for j in range(3):
            tap = [spread(filt[j, i : i + 1, lanes]) for i in range(taps)]
            grads = [gs[j, SUB * a : SUB * a + SUB] for a in range(taps - 1)]
            beyond = [pltpu.roll(value, SUB - 1, 0) for value in grads]
            views = [ps[j, pl.ds(SUB + a, SUB, stride=run), :] for a in range(1 - taps, 0)]
            sums_of = [None] * taps
            for a in range(run):
                ahead = a + taps - 1
                ahead = gs[j, SUB * ahead : SUB * ahead + SUB] if ahead < run else beyond[ahead - run]
                grads = grads[-(taps - 1) :] + [ahead]
                views = views[-(taps - 1) :] + [ps[j, pl.ds(SUB + a, SUB, stride=run), :]]
                total = added([tap[i] * grads[i] for i in range(taps)])
                os[pl.ds(a, SUB, stride=run), :] = total
                grad = grads[0] if a < own else jnp.where(inside, grads[0], 0.0)
                for i in range(taps):
                    term = grad * views[-1 - i]
                    sums_of[i] = term if a == 0 else sums_of[i] + term
            grad_p[j, :, lanes] = os[0:rows].astype(BF16)
            extra = [skip_sum[which, :, part]] + [jnp.zeros((SUB, LANES), F32)] * (SUB - taps)
            extra = extra[: SUB - taps] if j == 0 else extra[1 : SUB - taps + 1]
            sums[piece, j * SUB : j * SUB + SUB, spot] = folded(sums_of + extra)
        return carry

    lax.fori_loop(0, p.shape[2] // LANES, tile, 0)


def shifted(value, axis, steps):
    count = lax.axis_size(axis)
    first, last = (max(0, -steps), min(count, count - steps))
    return lax.ppermute(value, axis, [(source, source + steps) for source in range(first, last)])


def swapped(value):
    count = lax.axis_size("ctx")
    return lax.ppermute(value, "ctx", [(s, s ^ 1) for s in range(count)])


def joined(ends, f_all):
    core = lax.rem(lax.axis_index("ctx"), 2)
    half = ends.shape[1] // 2
    other = swapped(ends)
    first = core == 0
    mine = lax.dynamic_slice_in_dim(ends, core * half, half, 1)
    theirs = lax.dynamic_slice_in_dim(other, core * half, half, 1)
    one, two = jnp.where(first, mine, theirs), jnp.where(first, theirs, mine)
    return other, f_all * one[0] + two[0], one[1] + f_all * two[1]


def paired(value, axis, step, lines=None):
    count = lax.axis_size(axis)
    return lax.ppermute(value, axis, [(source, source ^ step) for source in lines or range(count)])


def scanned(chip_e, chip_a, f_all, beside):
    chips = lax.axis_size("ctx") // 2
    f_chip = f_all * f_all
    if chips == 4:
        odd = lax.rem(lax.axis_index("ctx") // 2, 2) == 1
        sent = jnp.where(odd, chip_a, chip_e)
        first = paired(sent, "ctx", 2)
        kept = beside[0](sent, None)
        first, kept = lax.optimization_barrier((first, kept))
        sent = jnp.where(odd, chip_e, chip_a) + f_chip * first
        near = lax.ppermute(sent, "ctx", [(2, 4), (3, 5), (4, 2), (5, 3)])
        kept = beside[1](sent, kept)
        near, kept = lax.optimization_barrier((near, kept))
        far = lax.ppermute(near, "ctx", [(4, 6), (5, 7), (2, 0), (3, 1)])
        kept = beside[2](near, kept)
        far, kept = lax.optimization_barrier((far, kept))
        far = first + f_chip * far
        return jnp.where(odd, far, near), jnp.where(odd, near, far), kept
    kept = beside[2](chip_e, beside[1](chip_e, beside[0](chip_e, None)))
    before, after = jnp.zeros_like(chip_e), jnp.zeros_like(chip_a)
    reach = 1
    while reach < chips:
        early, late = shifted(chip_e, "ctx", 2 * reach), shifted(chip_a, "ctx", -2 * reach)
        factor = f_chip ** (reach - 1)
        before, after = before + factor * early, after + factor * late
        factor = f_chip**reach
        chip_e, chip_a = chip_e + factor * early, chip_a + factor * late
        reach = 2 * reach
    return before, after, kept


def rotated(value, axis, steps):
    count = lax.axis_size(axis)
    return lax.ppermute(value, axis, [(s, (s + steps) % count) for s in range(count)])


def summed(value):
    dp, parts = lax.axis_index("dp"), lax.axis_size("dp")
    low = lax.rem(lax.axis_index("ctx"), 2) == 0
    half = value.shape[0] // 2
    left, right = value[:half], value[half:]
    value = jnp.where(low, left, right) + swapped(jnp.where(low, right, left))
    size = half // parts
    piece = lambda k: lax.dynamic_slice_in_dim(value, lax.rem(dp + k, parts) * size, size, 0)
    total = piece(0)
    for term in [rotated(piece(k), "dp", k) for k in range(1, parts)]:
        total = total + term
    reach = 2
    while reach < lax.axis_size("ctx"):
        total = total + paired(total, "ctx", reach)
        reach = 2 * reach
    value = jnp.zeros((half,) + value.shape[1:], F32)
    for k in range(parts):
        term = rotated(total, "dp", k) if k else total
        at = lax.rem(dp + parts - k, parts) * size
        value = lax.dynamic_update_slice_in_dim(value, term, at, 0)
    other = swapped(value)
    return jnp.concatenate([jnp.where(low, value, other), jnp.where(low, other, value)], axis=0)


def local(projected, short_filter, residues, decay_rates, skip_gain, cotangent):
    rows = projected.shape[1]
    channels = projected.shape[3]
    taps = short_filter.shape[1]
    groups, poles = residues.shape
    width = channels // groups
    run = (rows + SUB) // SUB
    held = rows + SUB
    p = projected[0].transpose(1, 0, 2)
    u = cotangent[0]
    core = lax.rem(lax.axis_index("ctx"), 2)
    head = jnp.concatenate([p[:, :SUB], u[None, :SUB]], axis=0)
    tail = jnp.concatenate([p[:, rows - SUB :], u[None, rows - SUB :]], axis=0)
    devices = lax.axis_size("ctx")
    across = [(k, k + 1) for k in range(1, devices - 1, 2)]
    across = across + [(target, source) for source, target in across]
    sent = jnp.where(core == 0, head, tail)
    hx = [lax.ppermute(sent[2 * k : 2 * k + 2], "ctx", across) for k in range(2)]
    hi = swapped(jnp.where(core == 0, tail, head))

    rate = decay_rates.T
    weight = residues.T
    sub = np.arange(SUB)
    powers = np.stack([run * (7 - sub) - SUB, run * sub, 1 + run * sub, rows - run * (sub + 1) + 1])
    table = jnp.exp(-rate[None, :, None, :] * powers.astype(np.float32)[:, None, :, None])
    we, wb = table[0], table[1]
    cz, cy = weight[:, None, :] * table[2], weight[:, None, :] * table[3]
    f1 = jnp.exp(-rate)
    f_all = jnp.exp(-rate * rows)
    steps = np.array([1, run, 2 * run, 4 * run], np.float32)
    factor = jnp.exp(-rate[None] * steps[:, None, None])
    factor = jnp.concatenate([weight[None] * factor[:1], factor[1:]], axis=0)
    reach = np.array([1, 1, 2, 4])[:, None]
    down, up = sub[None] >= reach, sub[None] < SUB - reach
    join_e = jnp.where(down[:, None, :, None], factor[:, :, None, :], 0.0)
    join_a = jnp.where(up[:, None, :, None], factor[:, :, None, :], 0.0)
    close = np.arange(-taps, run).astype(np.float32)
    near = jnp.sum(weight[:, None, :] * jnp.exp(-rate[:, None, :] * close[None, :, None]), axis=0)

    each = 1

    def by_w(*shape):
        axis = len(shape)
        return pl.BlockSpec(shape + (each * groups,), lambda w: (0,) * axis + (w,))

    def fixed(value):
        return pl.BlockSpec(
            value.shape, lambda w: (0,) * value.ndim, pipeline_mode=pl.Buffered(1)
        )

    params = pltpu.CompilerParams(vmem_limit_bytes=48 * 1024 * 1024)
    shape_of = jax.ShapeDtypeStruct
    ends_spec = pl.BlockSpec((2, each, poles, groups), lambda w: (0, w, 0, 0))
    halved = pl.BlockSpec(
        (2, each, poles, groups), lambda w: (0, lax.rem(w, width // each // 2), 0, 0)
    )
    state_shape = shape_of((width, poles, SUB, groups), F32)
    pair_shape = shape_of((width, 2, held, groups), F32)

    def by_block(*shape, count=each, first=0):
        return pl.BlockSpec((count,) + shape, lambda w: (w + first,) + (0,) * len(shape))

    state_spec = by_block(poles, SUB, groups)
    qkv, xg, blocks_e, blocks_a, ends = pl.pallas_call(
        states_kernel,
        grid=(width // each,),
        in_specs=[
            pl.BlockSpec(memory_space=pltpu.SMEM),
            by_w(3, rows), by_w(2, SUB), by_w(2, SUB), by_w(4, SUB), by_w(rows), by_w(3, taps),
            fixed(f1), fixed(we), fixed(wb),
        ],
        out_specs=[
            by_block(3, held, groups), by_block(2, held, groups), state_spec, state_spec,
            ends_spec,
        ],
        out_shape=[
            shape_of((width, 3, held, groups), F32), pair_shape,
            state_shape, state_shape, shape_of((2, width, poles, groups), F32),
        ],
        scratch_shapes=[pltpu.VMEM((4, held + SUB, LANES), F32)],
        compiler_params=params,
        name="states",
    )(core[None], p, *hx, hi, u, short_filter, f1, we, wb)

    many = 2 if width % 2 == 0 else 1

    def blocks(first, last):
        states = by_block(poles, SUB, groups, count=many, first=first)
        pairs = by_block(2, held, groups, count=many, first=first)

        def call(sent, kept):
            close, _ = lax.optimization_barrier((near, sent))
            held_before = kept or (xg, blocks_e, blocks_a)
            out = pl.pallas_call(
                blocks_kernel,
                grid=(last - first,),
                in_specs=[
                    pairs, states, states, fixed(near),
                    pl.BlockSpec((1, many * groups), lambda w: (0, w + first)),
                    fixed(join_e), fixed(join_a),
                ],
                out_specs=[pairs, states, states, by_block(SUB, groups, count=many)],
                out_shape=[
                    pair_shape, state_shape, state_shape,
                    shape_of(((last - first) * many, SUB, groups), F32),
                ],
                input_output_aliases={0: 0, 1: 1, 2: 2},
                compiler_params=params,
                cost_estimate=pl.CostEstimate(
                    flops=60 * rows * channels, bytes_accessed=35 * 2**20, transcendentals=0
                ),
                name="blocks",
            )(*held_before[:3], close, skip_gain[None], join_e, join_a)
            return [*out[:3], jnp.concatenate([*held_before[3:], out[3]], axis=0)]

        return call

    steps = width // many
    cuts = (0, steps // 4, (5 * steps) // 8, steps)
    other, chip_e, chip_a = joined(ends, f_all)
    before, after, (conv, from_e, from_a, skip_sum) = scanned(
        chip_e, chip_a, f_all, [blocks(cuts[k], cuts[k + 1]) for k in range(3)]
    )
    both = jnp.stack([before, after])
    found = swapped(both)

    count = 3 * SUB
    split = 2 if groups % (2 * LANES) == 0 else 1
    scratch = [
        pltpu.VMEM((3, held + SUB, LANES), F32),
        pltpu.VMEM((held, LANES), F32),
        pltpu.VMEM((3, held, LANES), F32),
        pltpu.VMEM((held, LANES), F32),
        pltpu.VMEM((2, poles, LANES), F32),
    ]
    output, grad_p, sums = pl.pallas_call(
        final_kernel,
        grid=(width // each,),
        in_specs=[
            pl.BlockSpec(memory_space=pltpu.SMEM),
            by_w(3, rows), by_w(2, SUB), by_w(2, SUB), by_w(4, SUB), by_w(rows),
            by_block(3, held, groups), by_block(2, held, groups), state_spec, state_spec,
            by_block(SUB, groups), halved, halved, ends_spec,
            by_w(3, taps), fixed(f1), fixed(f_all), fixed(cz), fixed(cy),
        ],
        out_specs=[
            by_w(rows), by_w(3, rows),
            pl.BlockSpec((each * split, count, groups // split), lambda w: (w, 0, 0)),
        ],
        out_shape=[
            shape_of((rows, channels), BF16),
            shape_of((3, rows, channels), BF16),
            shape_of((width * split, count, groups // split), F32),
        ],
        scratch_shapes=scratch,
        compiler_params=params,
        name="final",
    )(
        core[None], p, *hx, hi, u, qkv, conv, from_e, from_a, skip_sum, both, found, other, short_filter,
        f1, f_all, cz, cy,
    )

    total = summed(sums).transpose(1, 0, 2).reshape(3, SUB, channels)
    grad_short, grad_skip = total[:, :taps], total[0, taps]
    return output[None], grad_p.transpose(1, 0, 2)[None], grad_short, grad_skip


def solution(mesh):
    placed = (P("dp", "ctx", None, None), P(), P(), P(), P(), P("dp", "ctx", None))
    return jax.shard_map(
        local,
        mesh=mesh,
        in_specs=placed,
        out_specs=(P("dp", "ctx", None), P("dp", "ctx", None, None), P(), P()),
        check_vma=False,
    )
```

```python
import functools

import jax
import jax.numpy as jnp
import numpy as np
from jax import lax
from jax.experimental import pallas as pl
from jax.experimental.pallas import tpu as pltpu
from jax.sharding import PartitionSpec as P

LANES = 128
SUB = 8
F32 = jnp.float32
BF16 = jnp.bfloat16


def spread(row):
    return jnp.broadcast_to(row, (SUB, LANES))


def added(terms):
    while len(terms) > 1:
        pairs = [terms[k] + terms[k + 1] for k in range(0, len(terms) - 1, 2)]
        terms = pairs + terms[len(terms) - len(terms) % 2 :]
    return terms[0]


def folded(values):
    row = lax.broadcasted_iota(jnp.int32, (SUB, LANES), 0)
    upper = row < 4
    values = [
        jnp.where(upper, values[n], values[n + 4])
        + pltpu.roll(jnp.where(upper, values[n + 4], values[n]), 4, 0)
        for n in range(4)
    ]
    for step in (2, 1):
        even = (row // step) % 2 == 0
        values = [
            jnp.where(
                even,
                values[n] + pltpu.roll(values[n], SUB - step, 0),
                values[n + step] + pltpu.roll(values[n + step], step, 0),
            )
            for n in range(step)
        ]
    return values[0]


def states_kernel(core, p, hx, hi, u, filt, f1, we, wb, qkv, xg, blocks_e, blocks_a, ends, xs):
    rows = p.shape[1]
    run = (rows + SUB) // SUB
    taps = filt.shape[1]
    poles, groups = f1.shape
    own = rows - run * (SUB - 1)
    tiles = groups // LANES
    first = core[0] == 0

    def tile(lt, carry):
        lanes = pl.ds(pl.multiple_of(lt * LANES, LANES), LANES)
        part = pl.ds(pl.multiple_of(lax.rem(lt, tiles) * LANES, LANES), LANES)
        which = lt // tiles
        inside = lax.broadcasted_iota(jnp.int32, (SUB, LANES), 0) < SUB - 1
        for j in range(3):
            across, within = hx[j, :, lanes].astype(F32), hi[j, :, lanes].astype(F32)
            xs[j, 0:SUB] = jnp.where(first, across, within)
            xs[j, SUB : SUB + rows] = p[j, :, lanes].astype(F32)
            xs[j, SUB + rows :] = jnp.where(first, within, across)
        xs[3, SUB : SUB + rows] = u[:, lanes].astype(F32)
        across, within = hx[3, :, lanes].astype(F32), hi[3, :, lanes].astype(F32)
        xs[3, SUB + rows :] = jnp.where(first, within, across)

        def mixed(j):
            tap = [spread(filt[j, i : i + 1, lanes]) for i in range(taps)]
            view = [xs[j, pl.ds(SUB + a, SUB, stride=run), :] for a in range(1 - taps, 0)]
            for a in range(run):
                view = view[-(taps - 1) :] + [xs[j, pl.ds(SUB + a, SUB, stride=run), :]]
                yield added([tap[i] * view[-1 - i] for i in range(taps)])

        decay = [spread(f1[n : n + 1, part]) for n in range(poles)]
        for j in (1, 2, 0):
            for a, total in enumerate(mixed(j)):
                at = slice(SUB * a, SUB * a + SUB)
                qkv[which, j, at, part] = total
                if j == 2:
                    xg[which, 0, at, part] = qkv[which, 1, at, part] * total
                if j == 0:
                    xg[which, 1, at, part] = xs[3, pl.ds(SUB + a, SUB, stride=run), :] * total
        for side, order, weight, blocks in (
            (0, range(run), we, blocks_e),
            (1, range(run - 1, -1, -1), wb, blocks_a),
        ):
            state = None
            for a in order:
                x = xg[which, side, SUB * a : SUB * a + SUB, part]
                if a >= own:
                    x = jnp.where(inside, x, 0.0)
                state = [x] * poles if state is None else [decay[n] * state[n] + x for n in range(poles)]
            for n in range(poles):
                blocks[which, n, :, part] = state[n]
            state = [state[n] * weight[n, :, part] for n in range(poles)]
            for n in range(0, poles, SUB):
                ends[side, which, n : n + SUB, part] = folded(state[n : n + SUB])
        return carry

    lax.fori_loop(0, p.shape[2] // LANES, tile, 0)


def blocks_kernel(
    xg, blocks_e, blocks_a, near, skip, join_e, join_a, conv, from_e, from_a, skip_sum
):
    run = xg.shape[2] // SUB
    rows = xg.shape[2] - SUB
    taps = near.shape[0] - run
    poles, groups = blocks_e.shape[1], near.shape[1]
    own = rows - run * (SUB - 1)
    tiles = groups // LANES

    def tile(lt, carry):
        lanes = pl.ds(pl.multiple_of(lt * LANES, LANES), LANES)
        part = pl.ds(pl.multiple_of(lax.rem(lt, tiles) * LANES, LANES), LANES)
        which = lt // tiles
        inside = lax.broadcasted_iota(jnp.int32, (SUB, LANES), 0) < SUB - 1
        gain = spread(skip[0:1, lanes])
        lag = [spread(near[taps + m : taps + m + 1, part]) for m in range(run)]
        lag[0] = lag[0] + gain
        x = [xg[which, 0, SUB * a : SUB * a + SUB, part] for a in range(run)]
        for a in range(run):
            conv[which, 0, SUB * a : SUB * a + SUB, part] = added(
                [lag[m] * x[a - m] for m in range(a + 1)]
            )
        gated = x
        x = [xg[which, 1, SUB * a : SUB * a + SUB, part] for a in range(run)]
        masked = [x[a] if a < own else jnp.where(inside, x[a], 0.0) for a in range(run)]
        skip_sum[which, :, part] = added([masked[a] * gated[a] for a in range(run)])
        past = [jnp.where(inside, 0.0, gain)] + [
            jnp.where(inside, 0.0, -spread(near[taps - m : taps - m + 1, part]))
            for m in range(1, taps - 1)
        ]
        for a in range(run):
            terms = [lag[m] * masked[a + m] for m in range(run - a)]
            if own <= a < own + taps - 1:
                terms = terms + [past[m] * x[a - m] for m in range(a - own + 1)]
            conv[which, 1, SUB * a : SUB * a + SUB, part] = added(terms)
        for n in range(poles):
            value = pltpu.roll(blocks_e[which, n, :, part], 1, 0) * join_e[0, n, :, part]
            for k, step in ((1, 1), (2, 2), (3, 4)):
                value = value + pltpu.roll(value, step, 0) * join_e[k, n, :, part]
            from_e[which, n, :, part] = value
            value = pltpu.roll(blocks_a[which, n, :, part], SUB - 1, 0) * join_a[0, n, :, part]
            for k, step in ((1, 1), (2, 2), (3, 4)):
                value = value + pltpu.roll(value, SUB - step, 0) * join_a[k, n, :, part]
            from_a[which, n, :, part] = value
        return carry

    lax.fori_loop(0, xg.shape[0] * tiles, tile, 0)


def final_kernel(
    core, p, hx, hi, u, qkv, conv, from_e, from_a, skip_sum, both, found, other, filt, f1, f_all, cz, cy,
    output, grad_p, sums, ps, us, gs, os, es,
):
    rows = p.shape[1]
    run = (rows + SUB) // SUB
    taps = filt.shape[1]
    poles, groups = f1.shape
    own = rows - run * (SUB - 1)
    tiles = groups // LANES
    first = core[0] == 0
    halves = pl.num_programs(0) // 2
    kept = (pl.program_id(0) < halves) == first
    cut = sums.shape[2] // LANES

    def tile(lt, carry):
        lanes = pl.ds(pl.multiple_of(lt * LANES, LANES), LANES)
        part = pl.ds(pl.multiple_of(lax.rem(lt, tiles) * LANES, LANES), LANES)
        which = lt // tiles
        piece = lt // cut
        spot = pl.ds(pl.multiple_of(lax.rem(lt, cut) * LANES, LANES), LANES)
        inside = lax.broadcasted_iota(jnp.int32, (SUB, LANES), 0) < SUB - 1
        for side in range(2):
            far = jnp.where(kept, both[side, which, :, part], found[side, which, :, part])
            close = other[side, which, :, part] + f_all[:, part] * far
            es[side] = jnp.where(first == (side == 0), far, close)
        for j in range(3):
            across, within = hx[j, :, lanes].astype(F32), hi[j, :, lanes].astype(F32)
            ps[j, 0:SUB] = jnp.where(first, across, within)
            ps[j, SUB : SUB + rows] = p[j, :, lanes].astype(F32)
            ps[j, SUB + rows :] = jnp.where(first, within, across)
        us[0:rows] = u[:, lanes].astype(F32)
        across, within = hx[3, :, lanes].astype(F32), hi[3, :, lanes].astype(F32)
        us[rows:] = jnp.where(first, within, across)
        decay = [spread(f1[n : n + 1, part]) for n in range(poles)]

        state = [
            from_e[which, n, :, part] + cz[n, :, part] * spread(es[0, n : n + 1])
            for n in range(poles)
        ]
        for a in range(run):
            at = slice(SUB * a, SUB * a + SUB)
            query, upstream = qkv[which, 0, at, part], us[pl.ds(a, SUB, stride=run), :]
            filtered = conv[which, 0, at, part] + added(list(state))
            os[pl.ds(a, SUB, stride=run), :] = query * filtered
            gs[0, at] = upstream * filtered
            if a + 1 < run:
                state = [state[n] * decay[n] for n in range(poles)]
        output[:, lanes] = os[0:rows].astype(BF16)

        state = [
            from_a[which, n, :, part] + cy[n, :, part] * spread(es[1, n : n + 1])
            for n in range(poles)
        ]
        for a in range(run - 1, -1, -1):
            at = slice(SUB * a, SUB * a + SUB)
            grad = conv[which, 1, at, part] + added(list(state))
            gs[1, at] = grad * qkv[which, 2, at, part]
            gs[2, at] = grad * qkv[which, 1, at, part]
            if a:
                state = [state[n] * decay[n] for n in range(poles)]

        for j in range(3):
            tap = [spread(filt[j, i : i + 1, lanes]) for i in range(taps)]
            grads = [gs[j, SUB * a : SUB * a + SUB] for a in range(taps - 1)]
            beyond = [pltpu.roll(value, SUB - 1, 0) for value in grads]
            views = [ps[j, pl.ds(SUB + a, SUB, stride=run), :] for a in range(1 - taps, 0)]
            sums_of = [None] * taps
            for a in range(run):
                ahead = a + taps - 1
                ahead = gs[j, SUB * ahead : SUB * ahead + SUB] if ahead < run else beyond[ahead - run]
                grads = grads[-(taps - 1) :] + [ahead]
                views = views[-(taps - 1) :] + [ps[j, pl.ds(SUB + a, SUB, stride=run), :]]
                total = added([tap[i] * grads[i] for i in range(taps)])
                os[pl.ds(a, SUB, stride=run), :] = total
                grad = grads[0] if a < own else jnp.where(inside, grads[0], 0.0)
                for i in range(taps):
                    term = grad * views[-1 - i]
                    sums_of[i] = term if a == 0 else sums_of[i] + term
            grad_p[j, :, lanes] = os[0:rows].astype(BF16)
            extra = [skip_sum[which, :, part]] + [jnp.zeros((SUB, LANES), F32)] * (SUB - taps)
            extra = extra[: SUB - taps] if j == 0 else extra[1 : SUB - taps + 1]
            sums[piece, j * SUB : j * SUB + SUB, spot] = folded(sums_of + extra)
        return carry

    lax.fori_loop(0, p.shape[2] // LANES, tile, 0)


def shifted(value, axis, steps):
    count = lax.axis_size(axis)
    first, last = (max(0, -steps), min(count, count - steps))
    return lax.ppermute(value, axis, [(source, source + steps) for source in range(first, last)])


def swapped(value):
    count = lax.axis_size("ctx")
    return lax.ppermute(value, "ctx", [(s, s ^ 1) for s in range(count)])


def joined(ends, f_all):
    core = lax.rem(lax.axis_index("ctx"), 2)
    half = ends.shape[1] // 2
    other = swapped(ends)
    first = core == 0
    mine = lax.dynamic_slice_in_dim(ends, core * half, half, 1)
    theirs = lax.dynamic_slice_in_dim(other, core * half, half, 1)
    one, two = jnp.where(first, mine, theirs), jnp.where(first, theirs, mine)
    return other, f_all * one[0] + two[0], one[1] + f_all * two[1]


def paired(value, axis, step, lines=None):
    count = lax.axis_size(axis)
    return lax.ppermute(value, axis, [(source, source ^ step) for source in lines or range(count)])


def scanned(chip_e, chip_a, f_all, beside):
    chips = lax.axis_size("ctx") // 2
    f_chip = f_all * f_all
    if chips == 4:
        odd = lax.rem(lax.axis_index("ctx") // 2, 2) == 1
        sent = jnp.where(odd, chip_a, chip_e)
        first = paired(sent, "ctx", 2)
        kept = beside[0](sent, None)
        first, kept = lax.optimization_barrier((first, kept))
        sent = jnp.where(odd, chip_e, chip_a) + f_chip * first
        near = lax.ppermute(sent, "ctx", [(2, 4), (3, 5), (4, 2), (5, 3)])
        kept = beside[1](sent, kept)
        near, kept = lax.optimization_barrier((near, kept))
        far = lax.ppermute(near, "ctx", [(4, 6), (5, 7), (2, 0), (3, 1)])
        kept = beside[2](near, kept)
        far, kept = lax.optimization_barrier((far, kept))
        far = first + f_chip * far
        return jnp.where(odd, far, near), jnp.where(odd, near, far), kept
    kept = beside[2](chip_e, beside[1](chip_e, beside[0](chip_e, None)))
    before, after = jnp.zeros_like(chip_e), jnp.zeros_like(chip_a)
    reach = 1
    while reach < chips:
        early, late = shifted(chip_e, "ctx", 2 * reach), shifted(chip_a, "ctx", -2 * reach)
        factor = f_chip ** (reach - 1)
        before, after = before + factor * early, after + factor * late
        factor = f_chip**reach
        chip_e, chip_a = chip_e + factor * early, chip_a + factor * late
        reach = 2 * reach
    return before, after, kept


def rotated(value, axis, steps):
    count = lax.axis_size(axis)
    return lax.ppermute(value, axis, [(s, (s + steps) % count) for s in range(count)])


def summed(value):
    dp, parts = lax.axis_index("dp"), lax.axis_size("dp")
    low = lax.rem(lax.axis_index("ctx"), 2) == 0
    half = value.shape[0] // 2
    left, right = value[:half], value[half:]
    value = jnp.where(low, left, right) + swapped(jnp.where(low, right, left))
    size = half // parts
    piece = lambda k: lax.dynamic_slice_in_dim(value, lax.rem(dp + k, parts) * size, size, 0)
    total = piece(0)
    for term in [rotated(piece(k), "dp", k) for k in range(1, parts)]:
        total = total + term
    reach = 2
    while reach < lax.axis_size("ctx"):
        total = total + paired(total, "ctx", reach)
        reach = 2 * reach
    value = jnp.zeros((half,) + value.shape[1:], F32)
    for k in range(parts):
        term = rotated(total, "dp", k) if k else total
        at = lax.rem(dp + parts - k, parts) * size
        value = lax.dynamic_update_slice_in_dim(value, term, at, 0)
    other = swapped(value)
    return jnp.concatenate([jnp.where(low, value, other), jnp.where(low, other, value)], axis=0)


def local(projected, short_filter, residues, decay_rates, skip_gain, cotangent):
    rows = projected.shape[1]
    channels = projected.shape[3]
    taps = short_filter.shape[1]
    groups, poles = residues.shape
    width = channels // groups
    run = (rows + SUB) // SUB
    held = rows + SUB
    p = projected[0].transpose(1, 0, 2)
    u = cotangent[0]
    core = lax.rem(lax.axis_index("ctx"), 2)

    def edge(last):
        start = jnp.where(last, rows - SUB, 0)
        cut = lambda value, axis: lax.dynamic_slice_in_dim(value, start, SUB, axis)
        return jnp.concatenate([cut(p, 1), cut(u, 0)[None]], axis=0)

    devices = lax.axis_size("ctx")
    across = [(k, k + 1) for k in range(1, devices - 1, 2)]
    across = across + [(target, source) for source, target in across]
    hx = lax.ppermute(edge(core == 1), "ctx", across)
    hi = swapped(edge(core == 0))

    rate = decay_rates.T
    weight = residues.T
    sub = np.arange(SUB)
    powers = np.stack([run * (7 - sub) - SUB, run * sub, 1 + run * sub, rows - run * (sub + 1) + 1])
    table = jnp.exp(-rate[None, :, None, :] * powers.astype(np.float32)[:, None, :, None])
    we, wb = table[0], table[1]
    cz, cy = weight[:, None, :] * table[2], weight[:, None, :] * table[3]
    f1 = jnp.exp(-rate)
    f_all = jnp.exp(-rate * rows)
    steps = np.array([1, run, 2 * run, 4 * run], np.float32)
    factor = jnp.exp(-rate[None] * steps[:, None, None])
    factor = jnp.concatenate([weight[None] * factor[:1], factor[1:]], axis=0)
    reach = np.array([1, 1, 2, 4])[:, None]
    down, up = sub[None] >= reach, sub[None] < SUB - reach
    join_e = jnp.where(down[:, None, :, None], factor[:, :, None, :], 0.0)
    join_a = jnp.where(up[:, None, :, None], factor[:, :, None, :], 0.0)
    close = np.arange(-taps, run).astype(np.float32)
    near = jnp.sum(weight[:, None, :] * jnp.exp(-rate[:, None, :] * close[None, :, None]), axis=0)

    each = 1

    def by_w(*shape):
        axis = len(shape)
        return pl.BlockSpec(shape + (each * groups,), lambda w: (0,) * axis + (w,))

    def fixed(value):
        return pl.BlockSpec(
            value.shape, lambda w: (0,) * value.ndim, pipeline_mode=pl.Buffered(1)
        )

    params = pltpu.CompilerParams(vmem_limit_bytes=48 * 1024 * 1024)
    shape_of = jax.ShapeDtypeStruct
    ends_spec = pl.BlockSpec((2, each, poles, groups), lambda w: (0, w, 0, 0))
    halved = pl.BlockSpec(
        (2, each, poles, groups), lambda w: (0, lax.rem(w, width // each // 2), 0, 0)
    )
    state_shape = shape_of((width, poles, SUB, groups), F32)
    pair_shape = shape_of((width, 2, held, groups), F32)

    def by_block(*shape, count=each, first=0):
        return pl.BlockSpec((count,) + shape, lambda w: (w + first,) + (0,) * len(shape))

    state_spec = by_block(poles, SUB, groups)
    qkv, xg, blocks_e, blocks_a, ends = pl.pallas_call(
        states_kernel,
        grid=(width // each,),
        in_specs=[
            pl.BlockSpec(memory_space=pltpu.SMEM),
            by_w(3, rows), by_w(4, SUB), by_w(4, SUB), by_w(rows), by_w(3, taps),
            fixed(f1), fixed(we), fixed(wb),
        ],
        out_specs=[
            by_block(3, held, groups), by_block(2, held, groups), state_spec, state_spec,
            ends_spec,
        ],
        out_shape=[
            shape_of((width, 3, held, groups), F32), pair_shape,
            state_shape, state_shape, shape_of((2, width, poles, groups), F32),
        ],
        scratch_shapes=[pltpu.VMEM((4, held + SUB, LANES), F32)],
        compiler_params=params,
        name="states",
    )(core[None], p, hx, hi, u, short_filter, f1, we, wb)

    many = 2 if width % 2 == 0 else 1

    def blocks(first, last):
        place = {"count": many, "first": first}
        states, pairs = by_block(poles, SUB, groups, **place), by_block(2, held, groups, **place)

        def call(sent, kept):
            close, _ = lax.optimization_barrier((near, sent))
            held_before = kept or (xg, blocks_e, blocks_a)
            out = pl.pallas_call(
                blocks_kernel,
                grid=(last - first,),
                in_specs=[
                    pairs, states, states, fixed(near),
                    pl.BlockSpec((1, many * groups), lambda w: (0, w + first)),
                    fixed(join_e), fixed(join_a),
                ],
                out_specs=[pairs, states, states, by_block(SUB, groups, count=many)],
                out_shape=[
                    pair_shape, state_shape, state_shape,
                    shape_of(((last - first) * many, SUB, groups), F32),
                ],
                input_output_aliases={0: 0, 1: 1, 2: 2},
                compiler_params=params,
                cost_estimate=pl.CostEstimate(
                    flops=60 * rows * channels, bytes_accessed=35 * 2**20, transcendentals=0
                ),
                name="blocks",
            )(*held_before[:3], close, skip_gain[None], join_e, join_a)
            return [*out[:3], jnp.concatenate([*held_before[3:], out[3]], axis=0)]

        return call

    steps = width // many
    cuts = (0, (3 * steps) // 8, (5 * steps) // 8, steps)
    other, chip_e, chip_a = joined(ends, f_all)
    before, after, (conv, from_e, from_a, skip_sum) = scanned(
        chip_e, chip_a, f_all, [blocks(cuts[k], cuts[k + 1]) for k in range(3)]
    )
    both = jnp.stack([before, after])
    found = swapped(both)

    count = 3 * SUB
    split = 2 if groups % (2 * LANES) == 0 else 1
    scratch = [
        pltpu.VMEM((3, held + SUB, LANES), F32),
        pltpu.VMEM((held, LANES), F32),
        pltpu.VMEM((3, held, LANES), F32),
        pltpu.VMEM((held, LANES), F32),
        pltpu.VMEM((2, poles, LANES), F32),
    ]
    output, grad_p, sums = pl.pallas_call(
        final_kernel,
        grid=(width // each,),
        in_specs=[
            pl.BlockSpec(memory_space=pltpu.SMEM),
            by_w(3, rows), by_w(4, SUB), by_w(4, SUB), by_w(rows),
            by_block(3, held, groups), by_block(2, held, groups), state_spec, state_spec,
            by_block(SUB, groups), halved, halved, ends_spec,
            by_w(3, taps), fixed(f1), fixed(f_all), fixed(cz), fixed(cy),
        ],
        out_specs=[
            by_w(rows), by_w(3, rows),
            pl.BlockSpec((each * split, count, groups // split), lambda w: (w, 0, 0)),
        ],
        out_shape=[
            shape_of((rows, channels), BF16),
            shape_of((3, rows, channels), BF16),
            shape_of((width * split, count, groups // split), F32),
        ],
        scratch_shapes=scratch,
        compiler_params=params,
        name="final",
    )(
        core[None], p, hx, hi, u, qkv, conv, from_e, from_a, skip_sum, both, found, other, short_filter,
        f1, f_all, cz, cy,
    )

    total = summed(sums).transpose(1, 0, 2).reshape(3, SUB, channels)
    grad_short, grad_skip = total[:, :taps], total[0, taps]
    return output[None], grad_p.transpose(1, 0, 2)[None], grad_short, grad_skip


def solution(mesh):
    placed = (P("dp", "ctx", None, None), P(), P(), P(), P(), P("dp", "ctx", None))
    return jax.shard_map(
        local,
        mesh=mesh,
        in_specs=placed,
        out_specs=(P("dp", "ctx", None), P("dp", "ctx", None, None), P(), P()),
        check_vma=False,
    )
```

```python
import functools

import jax
import jax.numpy as jnp
import numpy as np
from jax import lax
from jax.experimental import pallas as pl
from jax.experimental.pallas import tpu as pltpu
from jax.sharding import PartitionSpec as P

LANES = 128
SUB = 8
F32 = jnp.float32
BF16 = jnp.bfloat16


def spread(row):
    return jnp.broadcast_to(row, (SUB, LANES))


def added(terms):
    while len(terms) > 1:
        pairs = [terms[k] + terms[k + 1] for k in range(0, len(terms) - 1, 2)]
        terms = pairs + terms[len(terms) - len(terms) % 2 :]
    return terms[0]


def folded(values):
    row = lax.broadcasted_iota(jnp.int32, (SUB, LANES), 0)
    upper = row < 4
    values = [
        jnp.where(upper, values[n], values[n + 4])
        + pltpu.roll(jnp.where(upper, values[n + 4], values[n]), 4, 0)
        for n in range(4)
    ]
    for step in (2, 1):
        even = (row // step) % 2 == 0
        values = [
            jnp.where(
                even,
                values[n] + pltpu.roll(values[n], SUB - step, 0),
                values[n + step] + pltpu.roll(values[n + step], step, 0),
            )
            for n in range(step)
        ]
    return values[0]


def states_kernel(core, p, hx, hi, u, filt, f1, we, wb, qkv, xg, blocks_e, blocks_a, ends, xs):
    rows = p.shape[1]
    run = (rows + SUB) // SUB
    taps = filt.shape[1]
    poles, groups = f1.shape
    own = rows - run * (SUB - 1)
    tiles = groups // LANES
    first = core[0] == 0

    def tile(lt, carry):
        lanes = pl.ds(pl.multiple_of(lt * LANES, LANES), LANES)
        part = pl.ds(pl.multiple_of(lax.rem(lt, tiles) * LANES, LANES), LANES)
        which = lt // tiles
        inside = lax.broadcasted_iota(jnp.int32, (SUB, LANES), 0) < SUB - 1
        for j in range(3):
            across, within = hx[j, :, lanes].astype(F32), hi[j, :, lanes].astype(F32)
            xs[j, 0:SUB] = jnp.where(first, across, within)
            xs[j, SUB : SUB + rows] = p[j, :, lanes].astype(F32)
            xs[j, SUB + rows :] = jnp.where(first, within, across)
        xs[3, SUB : SUB + rows] = u[:, lanes].astype(F32)
        xs[3, SUB + rows :] = jnp.ones((SUB, LANES), F32)

        def mixed(j):
            tap = [spread(filt[j, i : i + 1, lanes]) for i in range(taps)]
            view = [xs[j, pl.ds(SUB + a, SUB, stride=run), :] for a in range(1 - taps, 0)]
            for a in range(run):
                view = view[-(taps - 1) :] + [xs[j, pl.ds(SUB + a, SUB, stride=run), :]]
                yield added([tap[i] * view[-1 - i] for i in range(taps)])

        decay = [spread(f1[n : n + 1, part]) for n in range(poles)]
        for j in (1, 2, 0):
            for a, total in enumerate(mixed(j)):
                at = slice(SUB * a, SUB * a + SUB)
                qkv[which, j, at, part] = total
                if j == 2:
                    xg[which, 0, at, part] = qkv[which, 1, at, part] * total
                if j == 0:
                    xg[which, 1, at, part] = xs[3, pl.ds(SUB + a, SUB, stride=run), :] * total
        for side, order, weight, blocks in (
            (0, range(run), we, blocks_e),
            (1, range(run - 1, -1, -1), wb, blocks_a),
        ):
            state = None
            for a in order:
                x = xg[which, side, SUB * a : SUB * a + SUB, part]
                if a >= own:
                    x = jnp.where(inside, x, 0.0)
                state = [x] * poles if state is None else [decay[n] * state[n] + x for n in range(poles)]
            for n in range(poles):
                blocks[which, n, :, part] = state[n]
            state = [state[n] * weight[n, :, part] for n in range(poles)]
            for n in range(0, poles, SUB):
                ends[side, which, n : n + SUB, part] = folded(state[n : n + SUB])
        return carry

    lax.fori_loop(0, p.shape[2] // LANES, tile, 0)


def blocks_kernel(
    xg, blocks_e, blocks_a, hu, near, skip, join_e, join_a, conv, from_e, from_a, skip_sum, es
):
    run = xg.shape[2] // SUB
    rows = xg.shape[2] - SUB
    taps = near.shape[0] - run
    poles, groups = blocks_e.shape[1], near.shape[1]
    own = rows - run * (SUB - 1)
    tiles = groups // LANES

    def tile(lt, carry):
        lanes = pl.ds(pl.multiple_of(lt * LANES, LANES), LANES)
        part = pl.ds(pl.multiple_of(lax.rem(lt, tiles) * LANES, LANES), LANES)
        which = lt // tiles
        inside = lax.broadcasted_iota(jnp.int32, (SUB, LANES), 0) < SUB - 1
        gain = spread(skip[0:1, lanes])
        lag = [spread(near[taps + m : taps + m + 1, part]) for m in range(run)]
        lag[0] = lag[0] + gain
        x = [xg[which, 0, SUB * a : SUB * a + SUB, part] for a in range(run)]
        for a in range(run):
            conv[which, 0, SUB * a : SUB * a + SUB, part] = added(
                [lag[m] * x[a - m] for m in range(a + 1)]
            )
        gated = x
        x = [xg[which, 1, SUB * a : SUB * a + SUB, part] for a in range(run)]
        es[...] = hu[:, lanes].astype(F32)
        for a in range(own, run):
            x[a] = x[a] * jnp.where(inside, 1.0, spread(es[a - own : a - own + 1]))
        masked = [x[a] if a < own else jnp.where(inside, x[a], 0.0) for a in range(run)]
        skip_sum[which, :, part] = added([masked[a] * gated[a] for a in range(run)])
        past = [jnp.where(inside, 0.0, gain)] + [
            jnp.where(inside, 0.0, -spread(near[taps - m : taps - m + 1, part]))
            for m in range(1, taps - 1)
        ]
        for a in range(run):
            terms = [lag[m] * masked[a + m] for m in range(run - a)]
            if own <= a < own + taps - 1:
                terms = terms + [past[m] * x[a - m] for m in range(a - own + 1)]
            conv[which, 1, SUB * a : SUB * a + SUB, part] = added(terms)
        for n in range(poles):
            value = pltpu.roll(blocks_e[which, n, :, part], 1, 0) * join_e[0, n, :, part]
            for k, step in ((1, 1), (2, 2), (3, 4)):
                value = value + pltpu.roll(value, step, 0) * join_e[k, n, :, part]
            from_e[which, n, :, part] = value
            value = pltpu.roll(blocks_a[which, n, :, part], SUB - 1, 0) * join_a[0, n, :, part]
            for k, step in ((1, 1), (2, 2), (3, 4)):
                value = value + pltpu.roll(value, SUB - step, 0) * join_a[k, n, :, part]
            from_a[which, n, :, part] = value
        return carry

    lax.fori_loop(0, xg.shape[0] * tiles, tile, 0)


def final_kernel(
    core, p, hx, hi, hu, u, qkv, conv, from_e, from_a, skip_sum, both, found, other, filt, f1, f_all, cz, cy,
    output, grad_p, sums, ps, us, gs, os, es,
):
    rows = p.shape[1]
    run = (rows + SUB) // SUB
    taps = filt.shape[1]
    poles, groups = f1.shape
    own = rows - run * (SUB - 1)
    tiles = groups // LANES
    first = core[0] == 0
    halves = pl.num_programs(0) // 2
    kept = (pl.program_id(0) < halves) == first
    cut = sums.shape[2] // LANES

    def tile(lt, carry):
        lanes = pl.ds(pl.multiple_of(lt * LANES, LANES), LANES)
        part = pl.ds(pl.multiple_of(lax.rem(lt, tiles) * LANES, LANES), LANES)
        which = lt // tiles
        piece = lt // cut
        spot = pl.ds(pl.multiple_of(lax.rem(lt, cut) * LANES, LANES), LANES)
        inside = lax.broadcasted_iota(jnp.int32, (SUB, LANES), 0) < SUB - 1
        for side in range(2):
            far = jnp.where(kept, both[side, which, :, part], found[side, which, :, part])
            close = other[side, which, :, part] + f_all[:, part] * far
            es[side] = jnp.where(first == (side == 0), far, close)
        for j in range(3):
            across, within = hx[j, :, lanes].astype(F32), hi[j, :, lanes].astype(F32)
            ps[j, 0:SUB] = jnp.where(first, across, within)
            ps[j, SUB : SUB + rows] = p[j, :, lanes].astype(F32)
            ps[j, SUB + rows :] = jnp.where(first, within, across)
        us[0:rows] = u[:, lanes].astype(F32)
        us[rows:] = hu[:, lanes].astype(F32)
        decay = [spread(f1[n : n + 1, part]) for n in range(poles)]

        state = [
            from_e[which, n, :, part] + cz[n, :, part] * spread(es[0, n : n + 1])
            for n in range(poles)
        ]
        for a in range(run):
            at = slice(SUB * a, SUB * a + SUB)
            query, upstream = qkv[which, 0, at, part], us[pl.ds(a, SUB, stride=run), :]
            filtered = conv[which, 0, at, part] + added(list(state))
            os[pl.ds(a, SUB, stride=run), :] = query * filtered
            gs[0, at] = upstream * filtered
            if a + 1 < run:
                state = [state[n] * decay[n] for n in range(poles)]
        output[:, lanes] = os[0:rows].astype(BF16)

        state = [
            from_a[which, n, :, part] + cy[n, :, part] * spread(es[1, n : n + 1])
            for n in range(poles)
        ]
        for a in range(run - 1, -1, -1):
            at = slice(SUB * a, SUB * a + SUB)
            grad = conv[which, 1, at, part] + added(list(state))
            gs[1, at] = grad * qkv[which, 2, at, part]
            gs[2, at] = grad * qkv[which, 1, at, part]
            if a:
                state = [state[n] * decay[n] for n in range(poles)]

        for j in range(3):
            tap = [spread(filt[j, i : i + 1, lanes]) for i in range(taps)]
            grads = [gs[j, SUB * a : SUB * a + SUB] for a in range(taps - 1)]
            beyond = [pltpu.roll(value, SUB - 1, 0) for value in grads]
            views = [ps[j, pl.ds(SUB + a, SUB, stride=run), :] for a in range(1 - taps, 0)]
            sums_of = [None] * taps
            for a in range(run):
                ahead = a + taps - 1
                ahead = gs[j, SUB * ahead : SUB * ahead + SUB] if ahead < run else beyond[ahead - run]
                grads = grads[-(taps - 1) :] + [ahead]
                views = views[-(taps - 1) :] + [ps[j, pl.ds(SUB + a, SUB, stride=run), :]]
                total = added([tap[i] * grads[i] for i in range(taps)])
                os[pl.ds(a, SUB, stride=run), :] = total
                grad = grads[0] if a < own else jnp.where(inside, grads[0], 0.0)
                for i in range(taps):
                    term = grad * views[-1 - i]
                    sums_of[i] = term if a == 0 else sums_of[i] + term
            grad_p[j, :, lanes] = os[0:rows].astype(BF16)
            extra = [skip_sum[which, :, part]] + [jnp.zeros((SUB, LANES), F32)] * (SUB - taps)
            extra = extra[: SUB - taps] if j == 0 else extra[1 : SUB - taps + 1]
            sums[piece, j * SUB : j * SUB + SUB, spot] = folded(sums_of + extra)
        return carry

    lax.fori_loop(0, p.shape[2] // LANES, tile, 0)


def shifted(value, axis, steps):
    count = lax.axis_size(axis)
    first, last = (max(0, -steps), min(count, count - steps))
    return lax.ppermute(value, axis, [(source, source + steps) for source in range(first, last)])


def swapped(value):
    count = lax.axis_size("ctx")
    return lax.ppermute(value, "ctx", [(s, s ^ 1) for s in range(count)])


def joined(ends, f_all):
    core = lax.rem(lax.axis_index("ctx"), 2)
    half = ends.shape[1] // 2
    other = swapped(ends)
    first = core == 0
    mine = lax.dynamic_slice_in_dim(ends, core * half, half, 1)
    theirs = lax.dynamic_slice_in_dim(other, core * half, half, 1)
    one, two = jnp.where(first, mine, theirs), jnp.where(first, theirs, mine)
    return other, f_all * one[0] + two[0], one[1] + f_all * two[1]


def paired(value, axis, step, lines=None):
    count = lax.axis_size(axis)
    return lax.ppermute(value, axis, [(source, source ^ step) for source in lines or range(count)])


def scanned(chip_e, chip_a, f_all, beside):
    chips = lax.axis_size("ctx") // 2
    f_chip = f_all * f_all
    if chips == 4:
        odd = lax.rem(lax.axis_index("ctx") // 2, 2) == 1
        sent = jnp.where(odd, chip_a, chip_e)
        first = paired(sent, "ctx", 2)
        kept = beside[0](sent, None)
        first, kept = lax.optimization_barrier((first, kept))
        sent = jnp.where(odd, chip_e, chip_a) + f_chip * first
        near = lax.ppermute(sent, "ctx", [(2, 4), (3, 5), (4, 2), (5, 3)])
        kept = beside[1](sent, kept)
        near, kept = lax.optimization_barrier((near, kept))
        far = lax.ppermute(near, "ctx", [(4, 6), (5, 7), (2, 0), (3, 1)])
        kept = beside[2](near, kept)
        far, kept = lax.optimization_barrier((far, kept))
        far = first + f_chip * far
        return jnp.where(odd, far, near), jnp.where(odd, near, far), kept
    kept = beside[2](chip_e, beside[1](chip_e, beside[0](chip_e, None)))
    before, after = jnp.zeros_like(chip_e), jnp.zeros_like(chip_a)
    reach = 1
    while reach < chips:
        early, late = shifted(chip_e, "ctx", 2 * reach), shifted(chip_a, "ctx", -2 * reach)
        factor = f_chip ** (reach - 1)
        before, after = before + factor * early, after + factor * late
        factor = f_chip**reach
        chip_e, chip_a = chip_e + factor * early, chip_a + factor * late
        reach = 2 * reach
    return before, after, kept


def rotated(value, axis, steps):
    count = lax.axis_size(axis)
    return lax.ppermute(value, axis, [(s, (s + steps) % count) for s in range(count)])


def summed(value):
    dp, parts = lax.axis_index("dp"), lax.axis_size("dp")
    low = lax.rem(lax.axis_index("ctx"), 2) == 0
    half = value.shape[0] // 2
    left, right = value[:half], value[half:]
    value = jnp.where(low, left, right) + swapped(jnp.where(low, right, left))
    size = half // parts
    piece = lambda k: lax.dynamic_slice_in_dim(value, lax.rem(dp + k, parts) * size, size, 0)
    total = piece(0)
    for term in [rotated(piece(k), "dp", k) for k in range(1, parts)]:
        total = total + term
    reach = 2
    while reach < lax.axis_size("ctx"):
        total = total + paired(total, "ctx", reach)
        reach = 2 * reach
    value = jnp.zeros((half,) + value.shape[1:], F32)
    for k in range(parts):
        term = rotated(total, "dp", k) if k else total
        at = lax.rem(dp + parts - k, parts) * size
        value = lax.dynamic_update_slice_in_dim(value, term, at, 0)
    other = swapped(value)
    return jnp.concatenate([jnp.where(low, value, other), jnp.where(low, other, value)], axis=0)


def local(projected, short_filter, residues, decay_rates, skip_gain, cotangent):
    rows = projected.shape[1]
    channels = projected.shape[3]
    taps = short_filter.shape[1]
    groups, poles = residues.shape
    width = channels // groups
    run = (rows + SUB) // SUB
    held = rows + SUB
    p = projected[0].transpose(1, 0, 2)
    u = cotangent[0]
    core = lax.rem(lax.axis_index("ctx"), 2)

    def edge(last):
        return lax.dynamic_slice_in_dim(p, jnp.where(last, rows - SUB, 0), SUB, 1)

    devices = lax.axis_size("ctx")
    across = [(k, k + 1) for k in range(1, devices - 1, 2)]
    across = across + [(target, source) for source, target in across]
    hx = lax.ppermute(edge(core == 1), "ctx", across)
    hi = swapped(edge(core == 0))
    hu = shifted(u[:SUB], "ctx", -1)

    rate = decay_rates.T
    weight = residues.T
    sub = np.arange(SUB)
    powers = np.stack([run * (7 - sub) - SUB, run * sub, 1 + run * sub, rows - run * (sub + 1) + 1])
    table = jnp.exp(-rate[None, :, None, :] * powers.astype(np.float32)[:, None, :, None])
    we, wb = table[0], table[1]
    cz, cy = weight[:, None, :] * table[2], weight[:, None, :] * table[3]
    f1 = jnp.exp(-rate)
    f_all = jnp.exp(-rate * rows)
    steps = np.array([1, run, 2 * run, 4 * run], np.float32)
    factor = jnp.exp(-rate[None] * steps[:, None, None])
    factor = jnp.concatenate([weight[None] * factor[:1], factor[1:]], axis=0)
    reach = np.array([1, 1, 2, 4])[:, None]
    down, up = sub[None] >= reach, sub[None] < SUB - reach
    join_e = jnp.where(down[:, None, :, None], factor[:, :, None, :], 0.0)
    join_a = jnp.where(up[:, None, :, None], factor[:, :, None, :], 0.0)
    close = np.arange(-taps, run).astype(np.float32)
    near = jnp.sum(weight[:, None, :] * jnp.exp(-rate[:, None, :] * close[None, :, None]), axis=0)

    each = 1

    def by_w(*shape):
        axis = len(shape)
        return pl.BlockSpec(shape + (each * groups,), lambda w: (0,) * axis + (w,))

    def fixed(value):
        return pl.BlockSpec(
            value.shape, lambda w: (0,) * value.ndim, pipeline_mode=pl.Buffered(1)
        )

    params = pltpu.CompilerParams(vmem_limit_bytes=48 * 1024 * 1024)
    shape_of = jax.ShapeDtypeStruct
    ends_spec = pl.BlockSpec((2, each, poles, groups), lambda w: (0, w, 0, 0))
    halved = pl.BlockSpec(
        (2, each, poles, groups), lambda w: (0, lax.rem(w, width // each // 2), 0, 0)
    )
    state_shape = shape_of((width, poles, SUB, groups), F32)
    pair_shape = shape_of((width, 2, held, groups), F32)

    def by_block(*shape, count=each, first=0):
        return pl.BlockSpec((count,) + shape, lambda w: (w + first,) + (0,) * len(shape))

    state_spec = by_block(poles, SUB, groups)
    qkv, xg, blocks_e, blocks_a, ends = pl.pallas_call(
        states_kernel,
        grid=(width // each,),
        in_specs=[
            pl.BlockSpec(memory_space=pltpu.SMEM),
            by_w(3, rows), by_w(3, SUB), by_w(3, SUB), by_w(rows), by_w(3, taps),
            fixed(f1), fixed(we), fixed(wb),
        ],
        out_specs=[
            by_block(3, held, groups), by_block(2, held, groups), state_spec, state_spec,
            ends_spec,
        ],
        out_shape=[
            shape_of((width, 3, held, groups), F32), pair_shape,
            state_shape, state_shape, shape_of((2, width, poles, groups), F32),
        ],
        scratch_shapes=[pltpu.VMEM((4, held + SUB, LANES), F32)],
        compiler_params=params,
        name="states",
    )(core[None], p, hx, hi, u, short_filter, f1, we, wb)

    many = 2 if width % 2 == 0 else 1

    def blocks(first, last):
        place = {"count": many, "first": first}
        states, pairs = by_block(poles, SUB, groups, **place), by_block(2, held, groups, **place)

        def call(sent, kept):
            close, _ = lax.optimization_barrier((near, sent))
            held_before = kept or (xg, blocks_e, blocks_a)
            out = pl.pallas_call(
                blocks_kernel,
                grid=(last - first,),
                in_specs=[
                    pairs, states, states,
                    pl.BlockSpec((SUB, many * groups), lambda w: (0, w + first)), fixed(near),
                    pl.BlockSpec((1, many * groups), lambda w: (0, w + first)),
                    fixed(join_e), fixed(join_a),
                ],
                out_specs=[pairs, states, states, by_block(SUB, groups, count=many)],
                out_shape=[
                    pair_shape, state_shape, state_shape,
                    shape_of(((last - first) * many, SUB, groups), F32),
                ],
                input_output_aliases={0: 0, 1: 1, 2: 2},
                scratch_shapes=[pltpu.VMEM((SUB, LANES), F32)],
                compiler_params=params,
                cost_estimate=pl.CostEstimate(
                    flops=60 * rows * channels, bytes_accessed=35 * 2**20, transcendentals=0
                ),
                name="blocks",
            )(*held_before[:3], hu, close, skip_gain[None], join_e, join_a)
            return [*out[:3], jnp.concatenate([*held_before[3:], out[3]], axis=0)]

        return call

    steps = width // many
    cuts = (0, (3 * steps) // 8, (5 * steps) // 8, steps)
    other, chip_e, chip_a = joined(ends, f_all)
    before, after, (conv, from_e, from_a, skip_sum) = scanned(
        chip_e, chip_a, f_all, [blocks(cuts[k], cuts[k + 1]) for k in range(3)]
    )
    both = jnp.stack([before, after])
    found = swapped(both)

    count = 3 * SUB
    split = 2 if groups % (2 * LANES) == 0 else 1
    scratch = [
        pltpu.VMEM((3, held + SUB, LANES), F32),
        pltpu.VMEM((held, LANES), F32),
        pltpu.VMEM((3, held, LANES), F32),
        pltpu.VMEM((held, LANES), F32),
        pltpu.VMEM((2, poles, LANES), F32),
    ]
    output, grad_p, sums = pl.pallas_call(
        final_kernel,
        grid=(width // each,),
        in_specs=[
            pl.BlockSpec(memory_space=pltpu.SMEM),
            by_w(3, rows), by_w(3, SUB), by_w(3, SUB), by_w(SUB), by_w(rows),
            by_block(3, held, groups), by_block(2, held, groups), state_spec, state_spec,
            by_block(SUB, groups), halved, halved, ends_spec,
            by_w(3, taps), fixed(f1), fixed(f_all), fixed(cz), fixed(cy),
        ],
        out_specs=[
            by_w(rows), by_w(3, rows),
            pl.BlockSpec((each * split, count, groups // split), lambda w: (w, 0, 0)),
        ],
        out_shape=[
            shape_of((rows, channels), BF16),
            shape_of((3, rows, channels), BF16),
            shape_of((width * split, count, groups // split), F32),
        ],
        scratch_shapes=scratch,
        compiler_params=params,
        name="final",
    )(
        core[None], p, hx, hi, hu, u, qkv, conv, from_e, from_a, skip_sum, both, found, other, short_filter,
        f1, f_all, cz, cy,
    )

    total = summed(sums).transpose(1, 0, 2).reshape(3, SUB, channels)
    grad_short, grad_skip = total[:, :taps], total[0, taps]
    return output[None], grad_p.transpose(1, 0, 2)[None], grad_short, grad_skip


def solution(mesh):
    placed = (P("dp", "ctx", None, None), P(), P(), P(), P(), P("dp", "ctx", None))
    return jax.shard_map(
        local,
        mesh=mesh,
        in_specs=placed,
        out_specs=(P("dp", "ctx", None), P("dp", "ctx", None, None), P(), P()),
        check_vma=False,
    )
```

```python
import functools

import jax
import jax.numpy as jnp
import numpy as np
from jax import lax
from jax.experimental import pallas as pl
from jax.experimental.pallas import tpu as pltpu
from jax.sharding import PartitionSpec as P

LANES = 128
SUB = 8
F32 = jnp.float32
BF16 = jnp.bfloat16


def spread(row):
    return jnp.broadcast_to(row, (SUB, LANES))


def added(terms):
    while len(terms) > 1:
        pairs = [terms[k] + terms[k + 1] for k in range(0, len(terms) - 1, 2)]
        terms = pairs + terms[len(terms) - len(terms) % 2 :]
    return terms[0]


def folded(values):
    row = lax.broadcasted_iota(jnp.int32, (SUB, LANES), 0)
    upper = row < 4
    values = [
        jnp.where(upper, values[n], values[n + 4])
        + pltpu.roll(jnp.where(upper, values[n + 4], values[n]), 4, 0)
        for n in range(4)
    ]
    for step in (2, 1):
        even = (row // step) % 2 == 0
        values = [
            jnp.where(
                even,
                values[n] + pltpu.roll(values[n], SUB - step, 0),
                values[n + step] + pltpu.roll(values[n + step], step, 0),
            )
            for n in range(step)
        ]
    return values[0]


def phases(tap):
    even, odd = tap[0::2], tap[1::2]
    both = [even[k] + odd[k] if k < len(odd) else even[k] for k in range(len(even))]
    return even, odd, both


def weighted(tap, values):
    return added([tap[k] * values[k] for k in range(len(tap))])


def states_kernel(core, p, hx, hi, u, filt, f1, we, wb, qkv, xg, blocks_e, blocks_a, ends, xs):
    rows = p.shape[1]
    run = (rows + SUB) // SUB
    taps = filt.shape[1]
    poles, groups = f1.shape
    own = rows - run * (SUB - 1)
    tiles = groups // LANES
    first = core[0] == 0

    def tile(lt, carry):
        lanes = pl.ds(pl.multiple_of(lt * LANES, LANES), LANES)
        part = pl.ds(pl.multiple_of(lax.rem(lt, tiles) * LANES, LANES), LANES)
        which = lt // tiles
        inside = lax.broadcasted_iota(jnp.int32, (SUB, LANES), 0) < SUB - 1
        for j in range(3):
            across, within = hx[j, :, lanes].astype(F32), hi[j, :, lanes].astype(F32)
            xs[j, 0:SUB] = jnp.where(first, across, within)
            xs[j, SUB : SUB + rows] = p[j, :, lanes].astype(F32)
            xs[j, SUB + rows :] = jnp.where(first, within, across)
        xs[3, SUB : SUB + rows] = u[:, lanes].astype(F32)
        xs[3, SUB + rows :] = jnp.ones((SUB, LANES), F32)

        def mixed(j):
            even, odd, both = phases([spread(filt[j, i : i + 1, lanes]) for i in range(taps)])
            row = lambda a: xs[j, pl.ds(SUB + a, SUB, stride=run), :]
            reach = len(even)
            evens = [row(-2 * k) for k in range(1, reach)]
            odds = [row(1 - 2 * k) for k in range(1, reach)]
            pairs = [evens[k] + odds[k] for k in range(reach - 1)]
            before = weighted(odd, odds)
            for a in range(0, run, 2):
                evens = [row(a)] + evens[: reach - 1]
                first = weighted(even, evens)
                yield first + before
                if a + 1 < run:
                    odds = [row(a + 1)] + odds[: reach - 1]
                    pairs = [evens[0] + odds[0]] + pairs[: reach - 1]
                    before = weighted(odd, odds)
                    yield weighted(both, pairs) - first - before

        decay = [spread(f1[n : n + 1, part]) for n in range(poles)]
        for j in (1, 2, 0):
            for a, total in enumerate(mixed(j)):
                at = slice(SUB * a, SUB * a + SUB)
                qkv[which, j, at, part] = total
                if j == 2:
                    xg[which, 0, at, part] = qkv[which, 1, at, part] * total
                if j == 0:
                    xg[which, 1, at, part] = xs[3, pl.ds(SUB + a, SUB, stride=run), :] * total
        for side, order, weight, blocks in (
            (0, range(run), we, blocks_e),
            (1, range(run - 1, -1, -1), wb, blocks_a),
        ):
            state = None
            for a in order:
                x = xg[which, side, SUB * a : SUB * a + SUB, part]
                if a >= own:
                    x = jnp.where(inside, x, 0.0)
                state = [x] * poles if state is None else [decay[n] * state[n] + x for n in range(poles)]
            for n in range(poles):
                blocks[which, n, :, part] = state[n]
            state = [state[n] * weight[n, :, part] for n in range(poles)]
            for n in range(0, poles, SUB):
                ends[side, which, n : n + SUB, part] = folded(state[n : n + SUB])
        return carry

    lax.fori_loop(0, p.shape[2] // LANES, tile, 0)


def blocks_kernel(
    xg, blocks_e, blocks_a, hu, near, skip, join_e, join_a, conv, from_e, from_a, skip_sum, es
):
    run = xg.shape[2] // SUB
    rows = xg.shape[2] - SUB
    taps = near.shape[0] - run
    poles, groups = blocks_e.shape[1], near.shape[1]
    own = rows - run * (SUB - 1)
    tiles = groups // LANES

    def tile(lt, carry):
        lanes = pl.ds(pl.multiple_of(lt * LANES, LANES), LANES)
        part = pl.ds(pl.multiple_of(lax.rem(lt, tiles) * LANES, LANES), LANES)
        which = lt // tiles
        inside = lax.broadcasted_iota(jnp.int32, (SUB, LANES), 0) < SUB - 1
        gain = spread(skip[0:1, lanes])
        lag = [spread(near[taps + m : taps + m + 1, part]) for m in range(run)]
        lag[0] = lag[0] + gain
        x = [xg[which, 0, SUB * a : SUB * a + SUB, part] for a in range(run)]
        for a in range(run):
            conv[which, 0, SUB * a : SUB * a + SUB, part] = added(
                [lag[m] * x[a - m] for m in range(a + 1)]
            )
        gated = x
        x = [xg[which, 1, SUB * a : SUB * a + SUB, part] for a in range(run)]
        es[...] = hu[:, lanes].astype(F32)
        for a in range(own, run):
            x[a] = x[a] * jnp.where(inside, 1.0, spread(es[a - own : a - own + 1]))
        masked = [x[a] if a < own else jnp.where(inside, x[a], 0.0) for a in range(run)]
        skip_sum[which, :, part] = added([masked[a] * gated[a] for a in range(run)])
        past = [jnp.where(inside, 0.0, gain)] + [
            jnp.where(inside, 0.0, -spread(near[taps - m : taps - m + 1, part]))
            for m in range(1, taps - 1)
        ]
        for a in range(run):
            terms = [lag[m] * masked[a + m] for m in range(run - a)]
            if own <= a < own + taps - 1:
                terms = terms + [past[m] * x[a - m] for m in range(a - own + 1)]
            conv[which, 1, SUB * a : SUB * a + SUB, part] = added(terms)
        for n in range(poles):
            value = pltpu.roll(blocks_e[which, n, :, part], 1, 0) * join_e[0, n, :, part]
            for k, step in ((1, 1), (2, 2), (3, 4)):
                value = value + pltpu.roll(value, step, 0) * join_e[k, n, :, part]
            from_e[which, n, :, part] = value
            value = pltpu.roll(blocks_a[which, n, :, part], SUB - 1, 0) * join_a[0, n, :, part]
            for k, step in ((1, 1), (2, 2), (3, 4)):
                value = value + pltpu.roll(value, SUB - step, 0) * join_a[k, n, :, part]
            from_a[which, n, :, part] = value
        return carry

    lax.fori_loop(0, xg.shape[0] * tiles, tile, 0)


def final_kernel(
    core, p, hx, hi, hu, u, qkv, conv, from_e, from_a, skip_sum, both, found, other, filt, f1, f_all, cz, cy,
    output, grad_p, sums, ps, us, gs, os, es,
):
    rows = p.shape[1]
    run = (rows + SUB) // SUB
    taps = filt.shape[1]
    poles, groups = f1.shape
    own = rows - run * (SUB - 1)
    tiles = groups // LANES
    first = core[0] == 0
    halves = pl.num_programs(0) // 2
    kept = (pl.program_id(0) < halves) == first
    cut = sums.shape[2] // LANES

    def tile(lt, carry):
        lanes = pl.ds(pl.multiple_of(lt * LANES, LANES), LANES)
        part = pl.ds(pl.multiple_of(lax.rem(lt, tiles) * LANES, LANES), LANES)
        which = lt // tiles
        piece = lt // cut
        spot = pl.ds(pl.multiple_of(lax.rem(lt, cut) * LANES, LANES), LANES)
        inside = lax.broadcasted_iota(jnp.int32, (SUB, LANES), 0) < SUB - 1
        for side in range(2):
            far = jnp.where(kept, both[side, which, :, part], found[side, which, :, part])
            close = other[side, which, :, part] + f_all[:, part] * far
            es[side] = jnp.where(first == (side == 0), far, close)
        for j in range(3):
            across, within = hx[j, :, lanes].astype(F32), hi[j, :, lanes].astype(F32)
            ps[j, 0:SUB] = jnp.where(first, across, within)
            ps[j, SUB : SUB + rows] = p[j, :, lanes].astype(F32)
            ps[j, SUB + rows :] = jnp.where(first, within, across)
        us[0:rows] = u[:, lanes].astype(F32)
        us[rows:] = hu[:, lanes].astype(F32)
        decay = [spread(f1[n : n + 1, part]) for n in range(poles)]

        state = [
            from_e[which, n, :, part] + cz[n, :, part] * spread(es[0, n : n + 1])
            for n in range(poles)
        ]
        for a in range(run):
            at = slice(SUB * a, SUB * a + SUB)
            query, upstream = qkv[which, 0, at, part], us[pl.ds(a, SUB, stride=run), :]
            filtered = conv[which, 0, at, part] + added(list(state))
            os[pl.ds(a, SUB, stride=run), :] = query * filtered
            gs[0, at] = upstream * filtered
            if a + 1 < run:
                state = [state[n] * decay[n] for n in range(poles)]
        output[:, lanes] = os[0:rows].astype(BF16)

        state = [
            from_a[which, n, :, part] + cy[n, :, part] * spread(es[1, n : n + 1])
            for n in range(poles)
        ]
        for a in range(run - 1, -1, -1):
            at = slice(SUB * a, SUB * a + SUB)
            grad = conv[which, 1, at, part] + added(list(state))
            gs[1, at] = grad * qkv[which, 2, at, part]
            gs[2, at] = grad * qkv[which, 1, at, part]
            if a:
                state = [state[n] * decay[n] for n in range(poles)]

        for j in range(3):
            even, odd, paired_taps = phases([spread(filt[j, i : i + 1, lanes]) for i in range(taps)])
            reach = len(even)
            grads = [gs[j, SUB * a : SUB * a + SUB] for a in range(taps - 1)]
            beyond = [pltpu.roll(value, SUB - 1, 0) for value in grads]

            def ahead(a):
                return gs[j, SUB * a : SUB * a + SUB] if a < run else beyond[a - run]

            def behind(a):
                return ps[j, pl.ds(SUB + a, SUB, stride=run), :]

            def own_rows(a):
                return grads[a] if a < own else jnp.where(inside, grads[a], 0.0)

            grads = {a: grads[a] for a in range(taps - 1)}
            joint = {k: grads[2 * k + 1] + grads[2 * k + 2] for k in range((taps - 3) // 2)}
            leading = weighted(even, [grads[2 * k] if 2 * k in grads else ahead(2 * k) for k in range(reach)])
            evens = [behind(-2 * k) for k in range(1, reach)]
            odds = [behind(1 - 2 * k) for k in range(1, reach)]
            pairs = [evens[k] + odds[k] for k in range(reach - 1)]
            sums_of = [[None] * reach for _ in range(3)]

            def collect(kind, grad, values, count):
                for k in range(count):
                    term = grad * values[k]
                    so_far = sums_of[kind][k]
                    sums_of[kind][k] = term if so_far is None else so_far + term

            previous = None
            for a in range(0, run, 2):
                for c in range(a, a + 2 * reach + 1):
                    if c not in grads and c < run + taps - 1:
                        grads[c] = ahead(c)
                here = own_rows(a)
                collect(1, here if previous is None else here - previous, odds, len(odd))
                second = weighted(odd, [grads[a + 2 * k + 1] for k in range(len(odd))])
                os[pl.ds(a, SUB, stride=run), :] = leading + second
                evens = [behind(a)] + evens[: reach - 1]
                if a + 1 < run:
                    previous = own_rows(a + 1)
                    for k in range(a // 2, a // 2 + reach):
                        if k not in joint:
                            joint[k] = grads[2 * k + 1] + grads[2 * k + 2]
                    following = weighted(even, [grads[a + 2 + 2 * k] for k in range(reach)])
                    total = weighted(paired_taps, [joint[a // 2 + k] for k in range(reach)])
                    os[pl.ds(a + 1, SUB, stride=run), :] = total - following - second
                    leading = following
                    odds = [behind(a + 1)] + odds[: reach - 1]
                    pairs = [evens[0] + odds[0]] + pairs[: reach - 1]
                    collect(0, here - previous, evens, reach)
                    collect(2, previous, pairs, reach)
                else:
                    collect(0, here, evens, reach)
            sums_of = [sums_of[i % 2][i // 2] + sums_of[2][i // 2] for i in range(taps)]
            grad_p[j, :, lanes] = os[0:rows].astype(BF16)
            extra = [skip_sum[which, :, part]] + [jnp.zeros((SUB, LANES), F32)] * (SUB - taps)
            extra = extra[: SUB - taps] if j == 0 else extra[1 : SUB - taps + 1]
            sums[piece, j * SUB : j * SUB + SUB, spot] = folded(sums_of + extra)
        return carry

    lax.fori_loop(0, p.shape[2] // LANES, tile, 0)


def shifted(value, axis, steps):
    count = lax.axis_size(axis)
    first, last = (max(0, -steps), min(count, count - steps))
    return lax.ppermute(value, axis, [(source, source + steps) for source in range(first, last)])


def swapped(value):
    count = lax.axis_size("ctx")
    return lax.ppermute(value, "ctx", [(s, s ^ 1) for s in range(count)])


def joined(ends, hu, f_all):
    core = lax.rem(lax.axis_index("ctx"), 2)
    half = ends.shape[1] // 2
    other, hu = lax.optimization_barrier((swapped(ends), hu))
    first = core == 0
    mine = lax.dynamic_slice_in_dim(ends, core * half, half, 1)
    theirs = lax.dynamic_slice_in_dim(other, core * half, half, 1)
    one, two = jnp.where(first, mine, theirs), jnp.where(first, theirs, mine)
    return other, hu, f_all * one[0] + two[0], one[1] + f_all * two[1]


def paired(value, axis, step, lines=None):
    count = lax.axis_size(axis)
    return lax.ppermute(value, axis, [(source, source ^ step) for source in lines or range(count)])


def scanned(chip_e, chip_a, f_all, beside):
    chips = lax.axis_size("ctx") // 2
    f_chip = f_all * f_all
    if chips == 4:
        odd = lax.rem(lax.axis_index("ctx") // 2, 2) == 1
        sent = jnp.where(odd, chip_a, chip_e)
        first = paired(sent, "ctx", 2)
        kept = beside[0](sent, None)
        first, kept = lax.optimization_barrier((first, kept))
        sent = jnp.where(odd, chip_e, chip_a) + f_chip * first
        near = lax.ppermute(sent, "ctx", [(2, 4), (3, 5), (4, 2), (5, 3)])
        kept = beside[1](sent, kept)
        near, kept = lax.optimization_barrier((near, kept))
        far = lax.ppermute(near, "ctx", [(4, 6), (5, 7), (2, 0), (3, 1)])
        kept = beside[2](near, kept)
        far, kept = lax.optimization_barrier((far, kept))
        far = first + f_chip * far
        return jnp.where(odd, far, near), jnp.where(odd, near, far), kept
    kept = beside[2](chip_e, beside[1](chip_e, beside[0](chip_e, None)))
    before, after = jnp.zeros_like(chip_e), jnp.zeros_like(chip_a)
    reach = 1
    while reach < chips:
        early, late = shifted(chip_e, "ctx", 2 * reach), shifted(chip_a, "ctx", -2 * reach)
        factor = f_chip ** (reach - 1)
        before, after = before + factor * early, after + factor * late
        factor = f_chip**reach
        chip_e, chip_a = chip_e + factor * early, chip_a + factor * late
        reach = 2 * reach
    return before, after, kept


def rotated(value, axis, steps):
    count = lax.axis_size(axis)
    return lax.ppermute(value, axis, [(s, (s + steps) % count) for s in range(count)])


def summed(value):
    dp, parts = lax.axis_index("dp"), lax.axis_size("dp")
    low = lax.rem(lax.axis_index("ctx"), 2) == 0
    half = value.shape[0] // 2
    left, right = value[:half], value[half:]
    value = jnp.where(low, left, right) + swapped(jnp.where(low, right, left))
    size = half // parts
    piece = lambda k: lax.dynamic_slice_in_dim(value, lax.rem(dp + k, parts) * size, size, 0)
    total = piece(0)
    for term in [rotated(piece(k), "dp", k) for k in range(1, parts)]:
        total = total + term
    reach = 2
    while reach < lax.axis_size("ctx"):
        total = total + paired(total, "ctx", reach)
        reach = 2 * reach
    value = jnp.zeros((half,) + value.shape[1:], F32)
    for k in range(parts):
        term = rotated(total, "dp", k) if k else total
        at = lax.rem(dp + parts - k, parts) * size
        value = lax.dynamic_update_slice_in_dim(value, term, at, 0)
    other = swapped(value)
    return jnp.concatenate([jnp.where(low, value, other), jnp.where(low, other, value)], axis=0)


def local(projected, short_filter, residues, decay_rates, skip_gain, cotangent):
    rows = projected.shape[1]
    channels = projected.shape[3]
    taps = short_filter.shape[1]
    groups, poles = residues.shape
    width = channels // groups
    run = (rows + SUB) // SUB
    held = rows + SUB
    p = projected[0].transpose(1, 0, 2)
    u = cotangent[0]
    core = lax.rem(lax.axis_index("ctx"), 2)

    def edge(last):
        return lax.dynamic_slice_in_dim(p, jnp.where(last, rows - SUB, 0), SUB, 1)

    devices = lax.axis_size("ctx")
    across = [(k, k + 1) for k in range(1, devices - 1, 2)]
    across = across + [(target, source) for source, target in across]
    hx = lax.ppermute(edge(core == 1), "ctx", across)
    hi = swapped(edge(core == 0))

    rate = decay_rates.T
    weight = residues.T
    sub = np.arange(SUB)
    powers = np.stack([run * (7 - sub) - SUB, run * sub, 1 + run * sub, rows - run * (sub + 1) + 1])
    table = jnp.exp(-rate[None, :, None, :] * powers.astype(np.float32)[:, None, :, None])
    we, wb = table[0], table[1]
    cz, cy = weight[:, None, :] * table[2], weight[:, None, :] * table[3]
    f1 = jnp.exp(-rate)
    f_all = jnp.exp(-rate * rows)
    steps = np.array([1, run, 2 * run, 4 * run], np.float32)
    factor = jnp.exp(-rate[None] * steps[:, None, None])
    factor = jnp.concatenate([weight[None] * factor[:1], factor[1:]], axis=0)
    reach = np.array([1, 1, 2, 4])[:, None]
    down, up = sub[None] >= reach, sub[None] < SUB - reach
    join_e = jnp.where(down[:, None, :, None], factor[:, :, None, :], 0.0)
    join_a = jnp.where(up[:, None, :, None], factor[:, :, None, :], 0.0)
    close = np.arange(-taps, run).astype(np.float32)
    near = jnp.sum(weight[:, None, :] * jnp.exp(-rate[:, None, :] * close[None, :, None]), axis=0)

    each = 1

    def by_w(*shape):
        axis = len(shape)
        return pl.BlockSpec(shape + (each * groups,), lambda w: (0,) * axis + (w,))

    def fixed(value):
        return pl.BlockSpec(
            value.shape, lambda w: (0,) * value.ndim, pipeline_mode=pl.Buffered(1)
        )

    params = pltpu.CompilerParams(vmem_limit_bytes=48 * 1024 * 1024)
    shape_of = jax.ShapeDtypeStruct
    ends_spec = pl.BlockSpec((2, each, poles, groups), lambda w: (0, w, 0, 0))
    halved = pl.BlockSpec(
        (2, each, poles, groups), lambda w: (0, lax.rem(w, width // each // 2), 0, 0)
    )
    early = (hx, near, join_e, join_a, cz, cy, f_all, u[:SUB])
    hx, near, join_e, join_a, cz, cy, f_all, u_head = lax.optimization_barrier(early)
    hu = shifted(u_head, "ctx", -1)
    state_shape = shape_of((width, poles, SUB, groups), F32)
    pair_shape = shape_of((width, 2, held, groups), F32)

    def by_block(*shape, count=each, first=0):
        return pl.BlockSpec((count,) + shape, lambda w: (w + first,) + (0,) * len(shape))

    state_spec = by_block(poles, SUB, groups)
    qkv, xg, blocks_e, blocks_a, ends = pl.pallas_call(
        states_kernel,
        grid=(width // each,),
        in_specs=[
            pl.BlockSpec(memory_space=pltpu.SMEM),
            by_w(3, rows), by_w(3, SUB), by_w(3, SUB), by_w(rows), by_w(3, taps),
            fixed(f1), fixed(we), fixed(wb),
        ],
        out_specs=[
            by_block(3, held, groups), by_block(2, held, groups), state_spec, state_spec,
            ends_spec,
        ],
        out_shape=[
            shape_of((width, 3, held, groups), F32), pair_shape,
            state_shape, state_shape, shape_of((2, width, poles, groups), F32),
        ],
        scratch_shapes=[pltpu.VMEM((4, held + SUB, LANES), F32)],
        compiler_params=params,
        name="states",
    )(core[None], p, hx, hi, u, short_filter, f1, we, wb)

    many = 2 if width % 2 == 0 else 1

    def blocks(first, last):
        place = {"count": many, "first": first}
        states, pairs = by_block(poles, SUB, groups, **place), by_block(2, held, groups, **place)

        def call(sent, kept):
            close, _ = lax.optimization_barrier((near, sent))
            held_before = kept or (xg, blocks_e, blocks_a)
            out = pl.pallas_call(
                blocks_kernel,
                grid=(last - first,),
                in_specs=[
                    pairs, states, states,
                    pl.BlockSpec((SUB, many * groups), lambda w: (0, w + first)), fixed(near),
                    pl.BlockSpec((1, many * groups), lambda w: (0, w + first)),
                    fixed(join_e), fixed(join_a),
                ],
                out_specs=[pairs, states, states, by_block(SUB, groups, count=many)],
                out_shape=[
                    pair_shape, state_shape, state_shape,
                    shape_of(((last - first) * many, SUB, groups), F32),
                ],
                input_output_aliases={0: 0, 1: 1, 2: 2},
                scratch_shapes=[pltpu.VMEM((SUB, LANES), F32)],
                compiler_params=params,
                cost_estimate=pl.CostEstimate(
                    flops=60 * rows * channels, bytes_accessed=35 * 2**20, transcendentals=0
                ),
                name="blocks",
            )(*held_before[:3], hu, close, skip_gain[None], join_e, join_a)
            return [*out[:3], jnp.concatenate([*held_before[3:], out[3]], axis=0)]

        return call

    steps = width // many
    cuts = (0, (3 * steps) // 8, (5 * steps) // 8, steps)
    other, hu, chip_e, chip_a = joined(ends, hu, f_all)
    before, after, (conv, from_e, from_a, skip_sum) = scanned(
        chip_e, chip_a, f_all, [blocks(cuts[k], cuts[k + 1]) for k in range(3)]
    )
    both = jnp.stack([before, after])
    found = swapped(both)

    count = 3 * SUB
    split = 2 if groups % (2 * LANES) == 0 else 1
    scratch = [
        pltpu.VMEM((3, held + SUB, LANES), F32),
        pltpu.VMEM((held, LANES), F32),
        pltpu.VMEM((3, held, LANES), F32),
        pltpu.VMEM((held, LANES), F32),
        pltpu.VMEM((2, poles, LANES), F32),
    ]
    output, grad_p, sums = pl.pallas_call(
        final_kernel,
        grid=(width // each,),
        in_specs=[
            pl.BlockSpec(memory_space=pltpu.SMEM),
            by_w(3, rows), by_w(3, SUB), by_w(3, SUB), by_w(SUB), by_w(rows),
            by_block(3, held, groups), by_block(2, held, groups), state_spec, state_spec,
            by_block(SUB, groups), halved, halved, ends_spec,
            by_w(3, taps), fixed(f1), fixed(f_all), fixed(cz), fixed(cy),
        ],
        out_specs=[
            by_w(rows), by_w(3, rows),
            pl.BlockSpec((each * split, count, groups // split), lambda w: (w, 0, 0)),
        ],
        out_shape=[
            shape_of((rows, channels), BF16),
            shape_of((3, rows, channels), BF16),
            shape_of((width * split, count, groups // split), F32),
        ],
        scratch_shapes=scratch,
        compiler_params=params,
        name="final",
    )(
        core[None], p, hx, hi, hu, u, qkv, conv, from_e, from_a, skip_sum, both, found, other, short_filter,
        f1, f_all, cz, cy,
    )

    total = summed(sums).transpose(1, 0, 2).reshape(3, SUB, channels)
    grad_short, grad_skip = total[:, :taps], total[0, taps]
    return output[None], grad_p.transpose(1, 0, 2)[None], grad_short, grad_skip


def solution(mesh):
    placed = (P("dp", "ctx", None, None), P(), P(), P(), P(), P("dp", "ctx", None))
    return jax.shard_map(
        local,
        mesh=mesh,
        in_specs=placed,
        out_specs=(P("dp", "ctx", None), P("dp", "ctx", None, None), P(), P()),
        check_vma=False,
    )
```

```python
import functools

import jax
import jax.numpy as jnp
import numpy as np
from jax import lax
from jax.experimental import pallas as pl
from jax.experimental.pallas import tpu as pltpu
from jax.sharding import PartitionSpec as P

LANES = 128
SUB = 8
F32 = jnp.float32
BF16 = jnp.bfloat16


def spread(row):
    return jnp.broadcast_to(row, (SUB, LANES))


def added(terms):
    while len(terms) > 1:
        pairs = [terms[k] + terms[k + 1] for k in range(0, len(terms) - 1, 2)]
        terms = pairs + terms[len(terms) - len(terms) % 2 :]
    return terms[0]


def folded(values):
    row = lax.broadcasted_iota(jnp.int32, (SUB, LANES), 0)
    upper = row < 4
    values = [
        jnp.where(upper, values[n], values[n + 4])
        + pltpu.roll(jnp.where(upper, values[n + 4], values[n]), 4, 0)
        for n in range(4)
    ]
    for step in (2, 1):
        even = (row // step) % 2 == 0
        values = [
            jnp.where(
                even,
                values[n] + pltpu.roll(values[n], SUB - step, 0),
                values[n + step] + pltpu.roll(values[n + step], step, 0),
            )
            for n in range(step)
        ]
    return values[0]


def phases(tap):
    even, odd = tap[0::2], tap[1::2]
    both = [even[k] + odd[k] if k < len(odd) else even[k] for k in range(len(even))]
    return even, odd, both


def weighted(tap, values):
    return added([tap[k] * values[k] for k in range(len(tap))])


def states_kernel(core, p, hx, hi, u, filt, f1, we, wb, qkv, xg, blocks_e, blocks_a, ends, xs):
    rows = p.shape[1]
    run = (rows + SUB) // SUB
    taps = filt.shape[1]
    poles, groups = f1.shape
    own = rows - run * (SUB - 1)
    tiles = groups // LANES
    first = core[0] == 0

    def tile(lt, carry):
        lanes = pl.ds(pl.multiple_of(lt * LANES, LANES), LANES)
        part = pl.ds(pl.multiple_of(lax.rem(lt, tiles) * LANES, LANES), LANES)
        which = lt // tiles
        inside = lax.broadcasted_iota(jnp.int32, (SUB, LANES), 0) < SUB - 1
        for j in range(3):
            across, within = hx[j, :, lanes].astype(F32), hi[j, :, lanes].astype(F32)
            xs[j, 0:SUB] = jnp.where(first, across, within)
            xs[j, SUB : SUB + rows] = p[j, :, lanes].astype(F32)
            xs[j, SUB + rows :] = jnp.where(first, within, across)
        xs[3, SUB : SUB + rows] = u[:, lanes].astype(F32)
        across, within = hx[3, :, lanes].astype(F32), hi[3, :, lanes].astype(F32)
        xs[3, SUB + rows :] = jnp.where(first, within, across)

        def mixed(j):
            even, odd, both = phases([spread(filt[j, i : i + 1, lanes]) for i in range(taps)])
            row = lambda a: xs[j, pl.ds(SUB + a, SUB, stride=run), :]
            reach = len(even)
            evens = [row(-2 * k) for k in range(1, reach)]
            odds = [row(1 - 2 * k) for k in range(1, reach)]
            pairs = [evens[k] + odds[k] for k in range(reach - 1)]
            before = weighted(odd, odds)
            for a in range(0, run, 2):
                evens = [row(a)] + evens[: reach - 1]
                first = weighted(even, evens)
                yield first + before
                if a + 1 < run:
                    odds = [row(a + 1)] + odds[: reach - 1]
                    pairs = [evens[0] + odds[0]] + pairs[: reach - 1]
                    before = weighted(odd, odds)
                    yield weighted(both, pairs) - first - before

        decay = [spread(f1[n : n + 1, part]) for n in range(poles)]
        for j in (1, 2, 0):
            for a, total in enumerate(mixed(j)):
                at = slice(SUB * a, SUB * a + SUB)
                qkv[which, j, at, part] = total
                if j == 2:
                    xg[which, 0, at, part] = qkv[which, 1, at, part] * total
                if j == 0:
                    xg[which, 1, at, part] = xs[3, pl.ds(SUB + a, SUB, stride=run), :] * total
        for side, order, weight, blocks in (
            (0, range(run), we, blocks_e),
            (1, range(run - 1, -1, -1), wb, blocks_a),
        ):
            state = None
            for a in order:
                x = xg[which, side, SUB * a : SUB * a + SUB, part]
                if a >= own:
                    x = jnp.where(inside, x, 0.0)
                state = [x] * poles if state is None else [decay[n] * state[n] + x for n in range(poles)]
            for n in range(poles):
                blocks[which, n, :, part] = state[n]
            state = [state[n] * weight[n, :, part] for n in range(poles)]
            for n in range(0, poles, SUB):
                ends[side, which, n : n + SUB, part] = folded(state[n : n + SUB])
        return carry

    lax.fori_loop(0, p.shape[2] // LANES, tile, 0)


def blocks_kernel(
    xg, blocks_e, blocks_a, near, skip, join_e, join_a, conv, from_e, from_a, skip_sum
):
    run = xg.shape[2] // SUB
    rows = xg.shape[2] - SUB
    taps = near.shape[0] - run
    poles, groups = blocks_e.shape[1], near.shape[1]
    own = rows - run * (SUB - 1)
    tiles = groups // LANES

    def tile(lt, carry):
        lanes = pl.ds(pl.multiple_of(lt * LANES, LANES), LANES)
        part = pl.ds(pl.multiple_of(lax.rem(lt, tiles) * LANES, LANES), LANES)
        which = lt // tiles
        inside = lax.broadcasted_iota(jnp.int32, (SUB, LANES), 0) < SUB - 1
        gain = spread(skip[0:1, lanes])
        lag = [spread(near[taps + m : taps + m + 1, part]) for m in range(run)]
        lag[0] = lag[0] + gain
        x = [xg[which, 0, SUB * a : SUB * a + SUB, part] for a in range(run)]
        for a in range(run):
            conv[which, 0, SUB * a : SUB * a + SUB, part] = added(
                [lag[m] * x[a - m] for m in range(a + 1)]
            )
        gated = x
        x = [xg[which, 1, SUB * a : SUB * a + SUB, part] for a in range(run)]
        masked = [x[a] if a < own else jnp.where(inside, x[a], 0.0) for a in range(run)]
        skip_sum[which, :, part] = added([masked[a] * gated[a] for a in range(run)])
        past = [jnp.where(inside, 0.0, gain)] + [
            jnp.where(inside, 0.0, -spread(near[taps - m : taps - m + 1, part]))
            for m in range(1, taps - 1)
        ]
        for a in range(run):
            terms = [lag[m] * masked[a + m] for m in range(run - a)]
            if own <= a < own + taps - 1:
                terms = terms + [past[m] * x[a - m] for m in range(a - own + 1)]
            conv[which, 1, SUB * a : SUB * a + SUB, part] = added(terms)
        for n in range(poles):
            value = pltpu.roll(blocks_e[which, n, :, part], 1, 0) * join_e[0, n, :, part]
            for k, step in ((1, 1), (2, 2), (3, 4)):
                value = value + pltpu.roll(value, step, 0) * join_e[k, n, :, part]
            from_e[which, n, :, part] = value
            value = pltpu.roll(blocks_a[which, n, :, part], SUB - 1, 0) * join_a[0, n, :, part]
            for k, step in ((1, 1), (2, 2), (3, 4)):
                value = value + pltpu.roll(value, SUB - step, 0) * join_a[k, n, :, part]
            from_a[which, n, :, part] = value
        return carry

    lax.fori_loop(0, xg.shape[0] * tiles, tile, 0)


def final_kernel(
    core, p, hx, hi, u, qkv, conv, from_e, from_a, skip_sum, both, found, other, filt, f1, f_all, cz, cy,
    output, grad_p, sums, ps, us, gs, os, es,
):
    rows = p.shape[1]
    run = (rows + SUB) // SUB
    taps = filt.shape[1]
    poles, groups = f1.shape
    own = rows - run * (SUB - 1)
    tiles = groups // LANES
    first = core[0] == 0
    halves = pl.num_programs(0) // 2
    kept = (pl.program_id(0) < halves) == first
    cut = sums.shape[2] // LANES

    def tile(lt, carry):
        lanes = pl.ds(pl.multiple_of(lt * LANES, LANES), LANES)
        part = pl.ds(pl.multiple_of(lax.rem(lt, tiles) * LANES, LANES), LANES)
        which = lt // tiles
        piece = lt // cut
        spot = pl.ds(pl.multiple_of(lax.rem(lt, cut) * LANES, LANES), LANES)
        inside = lax.broadcasted_iota(jnp.int32, (SUB, LANES), 0) < SUB - 1
        for side in range(2):
            far = jnp.where(kept, both[side, which, :, part], found[side, which, :, part])
            close = other[side, which, :, part] + f_all[:, part] * far
            es[side] = jnp.where(first == (side == 0), far, close)
        for j in range(3):
            across, within = hx[j, :, lanes].astype(F32), hi[j, :, lanes].astype(F32)
            ps[j, 0:SUB] = jnp.where(first, across, within)
            ps[j, SUB : SUB + rows] = p[j, :, lanes].astype(F32)
            ps[j, SUB + rows :] = jnp.where(first, within, across)
        us[0:rows] = u[:, lanes].astype(F32)
        across, within = hx[3, :, lanes].astype(F32), hi[3, :, lanes].astype(F32)
        us[rows:] = jnp.where(first, within, across)
        decay = [spread(f1[n : n + 1, part]) for n in range(poles)]

        state = [
            from_e[which, n, :, part] + cz[n, :, part] * spread(es[0, n : n + 1])
            for n in range(poles)
        ]
        for a in range(run):
            at = slice(SUB * a, SUB * a + SUB)
            query, upstream = qkv[which, 0, at, part], us[pl.ds(a, SUB, stride=run), :]
            filtered = conv[which, 0, at, part] + added(list(state))
            os[pl.ds(a, SUB, stride=run), :] = query * filtered
            gs[0, at] = upstream * filtered
            if a + 1 < run:
                state = [state[n] * decay[n] for n in range(poles)]
        output[:, lanes] = os[0:rows].astype(BF16)

        state = [
            from_a[which, n, :, part] + cy[n, :, part] * spread(es[1, n : n + 1])
            for n in range(poles)
        ]
        for a in range(run - 1, -1, -1):
            at = slice(SUB * a, SUB * a + SUB)
            grad = conv[which, 1, at, part] + added(list(state))
            gs[1, at] = grad * qkv[which, 2, at, part]
            gs[2, at] = grad * qkv[which, 1, at, part]
            if a:
                state = [state[n] * decay[n] for n in range(poles)]

        for j in range(3):
            even, odd, paired_taps = phases([spread(filt[j, i : i + 1, lanes]) for i in range(taps)])
            reach = len(even)
            grads = [gs[j, SUB * a : SUB * a + SUB] for a in range(taps - 1)]
            beyond = [pltpu.roll(value, SUB - 1, 0) for value in grads]

            def ahead(a):
                return gs[j, SUB * a : SUB * a + SUB] if a < run else beyond[a - run]

            def behind(a):
                return ps[j, pl.ds(SUB + a, SUB, stride=run), :]

            def own_rows(a):
                return grads[a] if a < own else jnp.where(inside, grads[a], 0.0)

            grads = {a: grads[a] for a in range(taps - 1)}
            joint = {k: grads[2 * k + 1] + grads[2 * k + 2] for k in range((taps - 3) // 2)}
            leading = weighted(even, [grads[2 * k] if 2 * k in grads else ahead(2 * k) for k in range(reach)])
            evens = [behind(-2 * k) for k in range(1, reach)]
            odds = [behind(1 - 2 * k) for k in range(1, reach)]
            pairs = [evens[k] + odds[k] for k in range(reach - 1)]
            sums_of = [[None] * reach for _ in range(3)]

            def collect(kind, grad, values, count):
                for k in range(count):
                    term = grad * values[k]
                    so_far = sums_of[kind][k]
                    sums_of[kind][k] = term if so_far is None else so_far + term

            previous = None
            for a in range(0, run, 2):
                for c in range(a, a + 2 * reach + 1):
                    if c not in grads and c < run + taps - 1:
                        grads[c] = ahead(c)
                here = own_rows(a)
                collect(1, here if previous is None else here - previous, odds, len(odd))
                second = weighted(odd, [grads[a + 2 * k + 1] for k in range(len(odd))])
                os[pl.ds(a, SUB, stride=run), :] = leading + second
                evens = [behind(a)] + evens[: reach - 1]
                if a + 1 < run:
                    previous = own_rows(a + 1)
                    for k in range(a // 2, a // 2 + reach):
                        if k not in joint:
                            joint[k] = grads[2 * k + 1] + grads[2 * k + 2]
                    following = weighted(even, [grads[a + 2 + 2 * k] for k in range(reach)])
                    total = weighted(paired_taps, [joint[a // 2 + k] for k in range(reach)])
                    os[pl.ds(a + 1, SUB, stride=run), :] = total - following - second
                    leading = following
                    odds = [behind(a + 1)] + odds[: reach - 1]
                    pairs = [evens[0] + odds[0]] + pairs[: reach - 1]
                    collect(0, here - previous, evens, reach)
                    collect(2, previous, pairs, reach)
                else:
                    collect(0, here, evens, reach)
            sums_of = [sums_of[i % 2][i // 2] + sums_of[2][i // 2] for i in range(taps)]
            grad_p[j, :, lanes] = os[0:rows].astype(BF16)
            extra = [skip_sum[which, :, part]] + [jnp.zeros((SUB, LANES), F32)] * (SUB - taps)
            extra = extra[: SUB - taps] if j == 0 else extra[1 : SUB - taps + 1]
            sums[piece, j * SUB : j * SUB + SUB, spot] = folded(sums_of + extra)
        return carry

    lax.fori_loop(0, p.shape[2] // LANES, tile, 0)


def shifted(value, axis, steps):
    count = lax.axis_size(axis)
    first, last = (max(0, -steps), min(count, count - steps))
    return lax.ppermute(value, axis, [(source, source + steps) for source in range(first, last)])


def swapped(value):
    count = lax.axis_size("ctx")
    return lax.ppermute(value, "ctx", [(s, s ^ 1) for s in range(count)])


def joined(ends, f_all):
    core = lax.rem(lax.axis_index("ctx"), 2)
    half = ends.shape[1] // 2
    other = swapped(ends)
    first = core == 0
    mine = lax.dynamic_slice_in_dim(ends, core * half, half, 1)
    theirs = lax.dynamic_slice_in_dim(other, core * half, half, 1)
    one, two = jnp.where(first, mine, theirs), jnp.where(first, theirs, mine)
    return other, f_all * one[0] + two[0], one[1] + f_all * two[1]


def paired(value, axis, step, lines=None):
    count = lax.axis_size(axis)
    return lax.ppermute(value, axis, [(source, source ^ step) for source in lines or range(count)])


def scanned(chip_e, chip_a, f_all, beside):
    chips = lax.axis_size("ctx") // 2
    f_chip = f_all * f_all
    if chips == 4:
        odd = lax.rem(lax.axis_index("ctx") // 2, 2) == 1
        sent = jnp.where(odd, chip_a, chip_e)
        first = paired(sent, "ctx", 2)
        kept = beside[0](sent, None)
        first, kept = lax.optimization_barrier((first, kept))
        sent = jnp.where(odd, chip_e, chip_a) + f_chip * first
        near = lax.ppermute(sent, "ctx", [(2, 4), (3, 5), (4, 2), (5, 3)])
        kept = beside[1](sent, kept)
        near, kept = lax.optimization_barrier((near, kept))
        far = lax.ppermute(near, "ctx", [(4, 6), (5, 7), (2, 0), (3, 1)])
        kept = beside[2](near, kept)
        far, kept = lax.optimization_barrier((far, kept))
        far = first + f_chip * far
        return jnp.where(odd, far, near), jnp.where(odd, near, far), kept
    kept = beside[2](chip_e, beside[1](chip_e, beside[0](chip_e, None)))
    before, after = jnp.zeros_like(chip_e), jnp.zeros_like(chip_a)
    reach = 1
    while reach < chips:
        early, late = shifted(chip_e, "ctx", 2 * reach), shifted(chip_a, "ctx", -2 * reach)
        factor = f_chip ** (reach - 1)
        before, after = before + factor * early, after + factor * late
        factor = f_chip**reach
        chip_e, chip_a = chip_e + factor * early, chip_a + factor * late
        reach = 2 * reach
    return before, after, kept


def rotated(value, axis, steps):
    count = lax.axis_size(axis)
    return lax.ppermute(value, axis, [(s, (s + steps) % count) for s in range(count)])


def summed(value):
    dp, parts = lax.axis_index("dp"), lax.axis_size("dp")
    low = lax.rem(lax.axis_index("ctx"), 2) == 0
    half = value.shape[0] // 2
    left, right = value[:half], value[half:]
    value = jnp.where(low, left, right) + swapped(jnp.where(low, right, left))
    size = half // parts
    piece = lambda k: lax.dynamic_slice_in_dim(value, lax.rem(dp + k, parts) * size, size, 0)
    total = piece(0)
    for term in [rotated(piece(k), "dp", k) for k in range(1, parts)]:
        total = total + term
    reach = 2
    while reach < lax.axis_size("ctx"):
        total = total + paired(total, "ctx", reach)
        reach = 2 * reach
    value = jnp.zeros((half,) + value.shape[1:], F32)
    for k in range(parts):
        term = rotated(total, "dp", k) if k else total
        at = lax.rem(dp + parts - k, parts) * size
        value = lax.dynamic_update_slice_in_dim(value, term, at, 0)
    other = swapped(value)
    return jnp.concatenate([jnp.where(low, value, other), jnp.where(low, other, value)], axis=0)


def local(projected, short_filter, residues, decay_rates, skip_gain, cotangent):
    rows = projected.shape[1]
    channels = projected.shape[3]
    taps = short_filter.shape[1]
    groups, poles = residues.shape
    width = channels // groups
    run = (rows + SUB) // SUB
    held = rows + SUB
    p = projected[0].transpose(1, 0, 2)
    u = cotangent[0]
    core = lax.rem(lax.axis_index("ctx"), 2)

    def edge(last):
        start = jnp.where(last, rows - SUB, 0)
        cut = lambda value, axis: lax.dynamic_slice_in_dim(value, start, SUB, axis)
        return jnp.concatenate([cut(p, 1), cut(u, 0)[None]], axis=0)

    devices = lax.axis_size("ctx")
    across = [(k, k + 1) for k in range(1, devices - 1, 2)]
    across = across + [(target, source) for source, target in across]
    hx = lax.ppermute(edge(core == 1), "ctx", across)
    hi = swapped(edge(core == 0))

    rate = decay_rates.T
    weight = residues.T
    sub = np.arange(SUB)
    powers = np.stack([run * (7 - sub) - SUB, run * sub, 1 + run * sub, rows - run * (sub + 1) + 1])
    table = jnp.exp(-rate[None, :, None, :] * powers.astype(np.float32)[:, None, :, None])
    we, wb = table[0], table[1]
    cz, cy = weight[:, None, :] * table[2], weight[:, None, :] * table[3]
    f1 = jnp.exp(-rate)
    f_all = jnp.exp(-rate * rows)
    steps = np.array([1, run, 2 * run, 4 * run], np.float32)
    factor = jnp.exp(-rate[None] * steps[:, None, None])
    factor = jnp.concatenate([weight[None] * factor[:1], factor[1:]], axis=0)
    reach = np.array([1, 1, 2, 4])[:, None]
    down, up = sub[None] >= reach, sub[None] < SUB - reach
    join_e = jnp.where(down[:, None, :, None], factor[:, :, None, :], 0.0)
    join_a = jnp.where(up[:, None, :, None], factor[:, :, None, :], 0.0)
    close = np.arange(-taps, run).astype(np.float32)
    near = jnp.sum(weight[:, None, :] * jnp.exp(-rate[:, None, :] * close[None, :, None]), axis=0)

    each = 1

    def by_w(*shape):
        axis = len(shape)
        return pl.BlockSpec(shape + (each * groups,), lambda w: (0,) * axis + (w,))

    def fixed(value):
        return pl.BlockSpec(
            value.shape, lambda w: (0,) * value.ndim, pipeline_mode=pl.Buffered(1)
        )

    params = pltpu.CompilerParams(vmem_limit_bytes=48 * 1024 * 1024)
    shape_of = jax.ShapeDtypeStruct
    ends_spec = pl.BlockSpec((2, each, poles, groups), lambda w: (0, w, 0, 0))
    halved = pl.BlockSpec(
        (2, each, poles, groups), lambda w: (0, lax.rem(w, width // each // 2), 0, 0)
    )
    early = (hx, near, join_e, join_a, cz, cy, f_all)
    hx, near, join_e, join_a, cz, cy, f_all = lax.optimization_barrier(early)
    state_shape = shape_of((width, poles, SUB, groups), F32)
    pair_shape = shape_of((width, 2, held, groups), F32)

    def by_block(*shape, count=each, first=0):
        return pl.BlockSpec((count,) + shape, lambda w: (w + first,) + (0,) * len(shape))

    state_spec = by_block(poles, SUB, groups)
    qkv, xg, blocks_e, blocks_a, ends = pl.pallas_call(
        states_kernel,
        grid=(width // each,),
        in_specs=[
            pl.BlockSpec(memory_space=pltpu.SMEM),
            by_w(3, rows), by_w(4, SUB), by_w(4, SUB), by_w(rows), by_w(3, taps),
            fixed(f1), fixed(we), fixed(wb),
        ],
        out_specs=[
            by_block(3, held, groups), by_block(2, held, groups), state_spec, state_spec,
            ends_spec,
        ],
        out_shape=[
            shape_of((width, 3, held, groups), F32), pair_shape,
            state_shape, state_shape, shape_of((2, width, poles, groups), F32),
        ],
        scratch_shapes=[pltpu.VMEM((4, held + SUB, LANES), F32)],
        compiler_params=params,
        name="states",
    )(core[None], p, hx, hi, u, short_filter, f1, we, wb)

    many = 2 if width % 2 == 0 else 1

    def blocks(first, last):
        place = {"count": many, "first": first}
        states, pairs = by_block(poles, SUB, groups, **place), by_block(2, held, groups, **place)

        def call(sent, kept):
            close, _ = lax.optimization_barrier((near, sent))
            held_before = kept or (xg, blocks_e, blocks_a)
            out = pl.pallas_call(
                blocks_kernel,
                grid=(last - first,),
                in_specs=[
                    pairs, states, states, fixed(near),
                    pl.BlockSpec((1, many * groups), lambda w: (0, w + first)),
                    fixed(join_e), fixed(join_a),
                ],
                out_specs=[pairs, states, states, by_block(SUB, groups, count=many)],
                out_shape=[
                    pair_shape, state_shape, state_shape,
                    shape_of(((last - first) * many, SUB, groups), F32),
                ],
                input_output_aliases={0: 0, 1: 1, 2: 2},
                compiler_params=params,
                cost_estimate=pl.CostEstimate(
                    flops=60 * rows * channels, bytes_accessed=35 * 2**20, transcendentals=0
                ),
                name="blocks",
            )(*held_before[:3], close, skip_gain[None], join_e, join_a)
            return [*out[:3], jnp.concatenate([*held_before[3:], out[3]], axis=0)]

        return call

    steps = width // many
    cuts = (0, (3 * steps) // 8, (5 * steps) // 8, steps)
    other, chip_e, chip_a = joined(ends, f_all)
    before, after, (conv, from_e, from_a, skip_sum) = scanned(
        chip_e, chip_a, f_all, [blocks(cuts[k], cuts[k + 1]) for k in range(3)]
    )
    both = jnp.stack([before, after])
    found = swapped(both)

    count = 3 * SUB
    split = 2 if groups % (2 * LANES) == 0 else 1
    scratch = [
        pltpu.VMEM((3, held + SUB, LANES), F32),
        pltpu.VMEM((held, LANES), F32),
        pltpu.VMEM((3, held, LANES), F32),
        pltpu.VMEM((held, LANES), F32),
        pltpu.VMEM((2, poles, LANES), F32),
    ]
    output, grad_p, sums = pl.pallas_call(
        final_kernel,
        grid=(width // each,),
        in_specs=[
            pl.BlockSpec(memory_space=pltpu.SMEM),
            by_w(3, rows), by_w(4, SUB), by_w(4, SUB), by_w(rows),
            by_block(3, held, groups), by_block(2, held, groups), state_spec, state_spec,
            by_block(SUB, groups), halved, halved, ends_spec,
            by_w(3, taps), fixed(f1), fixed(f_all), fixed(cz), fixed(cy),
        ],
        out_specs=[
            by_w(rows), by_w(3, rows),
            pl.BlockSpec((each * split, count, groups // split), lambda w: (w, 0, 0)),
        ],
        out_shape=[
            shape_of((rows, channels), BF16),
            shape_of((3, rows, channels), BF16),
            shape_of((width * split, count, groups // split), F32),
        ],
        scratch_shapes=scratch,
        compiler_params=params,
        name="final",
    )(
        core[None], p, hx, hi, u, qkv, conv, from_e, from_a, skip_sum, both, found, other, short_filter,
        f1, f_all, cz, cy,
    )

    total = summed(sums).transpose(1, 0, 2).reshape(3, SUB, channels)
    grad_short, grad_skip = total[:, :taps], total[0, taps]
    return output[None], grad_p.transpose(1, 0, 2)[None], grad_short, grad_skip


def solution(mesh):
    placed = (P("dp", "ctx", None, None), P(), P(), P(), P(), P("dp", "ctx", None))
    return jax.shard_map(
        local,
        mesh=mesh,
        in_specs=placed,
        out_specs=(P("dp", "ctx", None), P("dp", "ctx", None, None), P(), P()),
        check_vma=False,
    )
```

```python
import functools

import jax
import jax.numpy as jnp
import numpy as np
from jax import lax
from jax.experimental import pallas as pl
from jax.experimental.pallas import tpu as pltpu
from jax.sharding import PartitionSpec as P

LANES = 128
SUB = 8
F32 = jnp.float32
BF16 = jnp.bfloat16


def spread(row):
    return jnp.broadcast_to(row, (SUB, LANES))


def added(terms):
    while len(terms) > 1:
        pairs = [terms[k] + terms[k + 1] for k in range(0, len(terms) - 1, 2)]
        terms = pairs + terms[len(terms) - len(terms) % 2 :]
    return terms[0]


def folded(values):
    row = lax.broadcasted_iota(jnp.int32, (SUB, LANES), 0)
    upper = row < 4
    values = [
        jnp.where(upper, values[n], values[n + 4])
        + pltpu.roll(jnp.where(upper, values[n + 4], values[n]), 4, 0)
        for n in range(4)
    ]
    for step in (2, 1):
        even = (row // step) % 2 == 0
        values = [
            jnp.where(
                even,
                values[n] + pltpu.roll(values[n], SUB - step, 0),
                values[n + step] + pltpu.roll(values[n + step], step, 0),
            )
            for n in range(step)
        ]
    return values[0]


def phases(tap):
    even, odd = tap[0::2], tap[1::2]
    both = [even[k] + odd[k] if k < len(odd) else even[k] for k in range(len(even))]
    return even, odd, both


def weighted(tap, values):
    return added([tap[k] * values[k] for k in range(len(tap))])


def states_kernel(core, p, hx, hi, u, filt, f1, we, wb, qkv, xg, blocks_e, blocks_a, ends, xs):
    rows = p.shape[1]
    run = (rows + SUB) // SUB
    taps = filt.shape[1]
    poles, groups = f1.shape
    own = rows - run * (SUB - 1)
    tiles = groups // LANES
    first = core[0] == 0

    def tile(lt, carry):
        lanes = pl.ds(pl.multiple_of(lt * LANES, LANES), LANES)
        part = pl.ds(pl.multiple_of(lax.rem(lt, tiles) * LANES, LANES), LANES)
        which = lt // tiles
        inside = lax.broadcasted_iota(jnp.int32, (SUB, LANES), 0) < SUB - 1
        for j in range(3):
            across, within = hx[j, :, lanes].astype(F32), hi[j, :, lanes].astype(F32)
            xs[j, 0:SUB] = jnp.where(first, across, within)
            xs[j, SUB : SUB + rows] = p[j, :, lanes].astype(F32)
            xs[j, SUB + rows :] = jnp.where(first, within, across)
        xs[3, SUB : SUB + rows] = u[:, lanes].astype(F32)
        across, within = hx[3, :, lanes].astype(F32), hi[3, :, lanes].astype(F32)
        xs[3, SUB + rows :] = jnp.where(first, within, across)

        def mixed(j):
            even, odd, both = phases([spread(filt[j, i : i + 1, lanes]) for i in range(taps)])
            row = lambda a: xs[j, pl.ds(SUB + a, SUB, stride=run), :]
            reach = len(even)
            evens = [row(-2 * k) for k in range(1, reach)]
            odds = [row(1 - 2 * k) for k in range(1, reach)]
            pairs = [evens[k] + odds[k] for k in range(reach - 1)]
            before = weighted(odd, odds)
            for a in range(0, run, 2):
                evens = [row(a)] + evens[: reach - 1]
                first = weighted(even, evens)
                yield first + before
                if a + 1 < run:
                    odds = [row(a + 1)] + odds[: reach - 1]
                    pairs = [evens[0] + odds[0]] + pairs[: reach - 1]
                    before = weighted(odd, odds)
                    yield weighted(both, pairs) - first - before

        decay = [spread(f1[n : n + 1, part]) for n in range(poles)]
        for j in (1, 2, 0):
            for a, total in enumerate(mixed(j)):
                at = slice(SUB * a, SUB * a + SUB)
                qkv[which, j, at, part] = total
                if j == 2:
                    xg[which, 0, at, part] = qkv[which, 1, at, part] * total
                if j == 0:
                    xg[which, 1, at, part] = xs[3, pl.ds(SUB + a, SUB, stride=run), :] * total
        for side, order, weight, blocks in (
            (0, range(run), we, blocks_e),
            (1, range(run - 1, -1, -1), wb, blocks_a),
        ):
            state = None
            for a in order:
                x = xg[which, side, SUB * a : SUB * a + SUB, part]
                if a >= own:
                    x = jnp.where(inside, x, 0.0)
                state = [x] * poles if state is None else [decay[n] * state[n] + x for n in range(poles)]
            for n in range(poles):
                blocks[which, n, :, part] = state[n]
            state = [state[n] * weight[n, :, part] for n in range(poles)]
            for n in range(0, poles, SUB):
                ends[side, which, n : n + SUB, part] = folded(state[n : n + SUB])
        return carry

    lax.fori_loop(0, p.shape[2] // LANES, tile, 0)


def blocks_kernel(
    xg, blocks_e, blocks_a, near, skip, join_e, join_a, conv, from_e, from_a, skip_sum
):
    run = xg.shape[2] // SUB
    rows = xg.shape[2] - SUB
    taps = near.shape[0] - run
    poles, groups = blocks_e.shape[1], near.shape[1]
    own = rows - run * (SUB - 1)
    tiles = groups // LANES

    def tile(lt, carry):
        lanes = pl.ds(pl.multiple_of(lt * LANES, LANES), LANES)
        part = pl.ds(pl.multiple_of(lax.rem(lt, tiles) * LANES, LANES), LANES)
        which = lt // tiles
        inside = lax.broadcasted_iota(jnp.int32, (SUB, LANES), 0) < SUB - 1
        gain = spread(skip[0:1, lanes])
        lag = [spread(near[taps + m : taps + m + 1, part]) for m in range(run)]
        lag[0] = lag[0] + gain
        x = [xg[which, 0, SUB * a : SUB * a + SUB, part] for a in range(run)]
        for a in range(run):
            conv[which, 0, SUB * a : SUB * a + SUB, part] = added(
                [lag[m] * x[a - m] for m in range(a + 1)]
            )
        gated = x
        x = [xg[which, 1, SUB * a : SUB * a + SUB, part] for a in range(run)]
        masked = [x[a] if a < own else jnp.where(inside, x[a], 0.0) for a in range(run)]
        skip_sum[which, :, part] = added([masked[a] * gated[a] for a in range(run)])
        past = [jnp.where(inside, 0.0, gain)] + [
            jnp.where(inside, 0.0, -spread(near[taps - m : taps - m + 1, part]))
            for m in range(1, taps - 1)
        ]
        for a in range(run):
            terms = [lag[m] * masked[a + m] for m in range(run - a)]
            if own <= a < own + taps - 1:
                terms = terms + [past[m] * x[a - m] for m in range(a - own + 1)]
            conv[which, 1, SUB * a : SUB * a + SUB, part] = added(terms)
        for n in range(poles):
            value = pltpu.roll(blocks_e[which, n, :, part], 1, 0) * join_e[0, n, :, part]
            for k, step in ((1, 1), (2, 2), (3, 4)):
                value = value + pltpu.roll(value, step, 0) * join_e[k, n, :, part]
            from_e[which, n, :, part] = value
            value = pltpu.roll(blocks_a[which, n, :, part], SUB - 1, 0) * join_a[0, n, :, part]
            for k, step in ((1, 1), (2, 2), (3, 4)):
                value = value + pltpu.roll(value, SUB - step, 0) * join_a[k, n, :, part]
            from_a[which, n, :, part] = value
        return carry

    lax.fori_loop(0, xg.shape[0] * tiles, tile, 0)


def final_kernel(
    core, p, hx, hi, u, qkv, conv, from_e, from_a, skip_sum, both, found, other, filt, f1, f_all, cz, cy,
    output, grad_p, sums, ps, us, gs, os, es,
):
    rows = p.shape[1]
    run = (rows + SUB) // SUB
    taps = filt.shape[1]
    poles, groups = f1.shape
    own = rows - run * (SUB - 1)
    tiles = groups // LANES
    first = core[0] == 0
    halves = pl.num_programs(0) // 2
    kept = (pl.program_id(0) < halves) == first
    cut = sums.shape[2] // LANES

    def tile(lt, carry):
        lanes = pl.ds(pl.multiple_of(lt * LANES, LANES), LANES)
        part = pl.ds(pl.multiple_of(lax.rem(lt, tiles) * LANES, LANES), LANES)
        which = lt // tiles
        piece = lt // cut
        spot = pl.ds(pl.multiple_of(lax.rem(lt, cut) * LANES, LANES), LANES)
        inside = lax.broadcasted_iota(jnp.int32, (SUB, LANES), 0) < SUB - 1
        for side in range(2):
            far = jnp.where(kept, both[side, which, :, part], found[side, which, :, part])
            close = other[side, which, :, part] + f_all[:, part] * far
            es[side] = jnp.where(first == (side == 0), far, close)
        for j in range(3):
            across, within = hx[j, :, lanes].astype(F32), hi[j, :, lanes].astype(F32)
            ps[j, 0:SUB] = jnp.where(first, across, within)
            ps[j, SUB : SUB + rows] = p[j, :, lanes].astype(F32)
            ps[j, SUB + rows :] = jnp.where(first, within, across)
        us[0:rows] = u[:, lanes].astype(F32)
        across, within = hx[3, :, lanes].astype(F32), hi[3, :, lanes].astype(F32)
        us[rows:] = jnp.where(first, within, across)
        decay = [spread(f1[n : n + 1, part]) for n in range(poles)]

        state = [
            from_e[which, n, :, part] + cz[n, :, part] * spread(es[0, n : n + 1])
            for n in range(poles)
        ]
        for a in range(run):
            at = slice(SUB * a, SUB * a + SUB)
            query, upstream = qkv[which, 0, at, part], us[pl.ds(a, SUB, stride=run), :]
            filtered = conv[which, 0, at, part] + added(list(state))
            os[pl.ds(a, SUB, stride=run), :] = query * filtered
            gs[0, at] = upstream * filtered
            if a + 1 < run:
                state = [state[n] * decay[n] for n in range(poles)]
        output[:, lanes] = os[0:rows].astype(BF16)

        state = [
            from_a[which, n, :, part] + cy[n, :, part] * spread(es[1, n : n + 1])
            for n in range(poles)
        ]
        for a in range(run - 1, -1, -1):
            at = slice(SUB * a, SUB * a + SUB)
            grad = conv[which, 1, at, part] + added(list(state))
            gs[1, at] = grad * qkv[which, 2, at, part]
            gs[2, at] = grad * qkv[which, 1, at, part]
            if a:
                state = [state[n] * decay[n] for n in range(poles)]

        for j in range(3):
            even, odd, paired_taps = phases([spread(filt[j, i : i + 1, lanes]) for i in range(taps)])
            reach = len(even)
            grads = [gs[j, SUB * a : SUB * a + SUB] for a in range(taps - 1)]
            beyond = [pltpu.roll(value, SUB - 1, 0) for value in grads]

            def ahead(a):
                return gs[j, SUB * a : SUB * a + SUB] if a < run else beyond[a - run]

            def behind(a):
                return ps[j, pl.ds(SUB + a, SUB, stride=run), :]

            def own_rows(a):
                return grads[a] if a < own else jnp.where(inside, grads[a], 0.0)

            grads = {a: grads[a] for a in range(taps - 1)}
            joint = {k: grads[2 * k + 1] + grads[2 * k + 2] for k in range((taps - 3) // 2)}
            leading = weighted(even, [grads[2 * k] if 2 * k in grads else ahead(2 * k) for k in range(reach)])
            evens = [behind(-2 * k) for k in range(1, reach)]
            odds = [behind(1 - 2 * k) for k in range(1, reach)]
            pairs = [evens[k] + odds[k] for k in range(reach - 1)]
            sums_of = [[None] * reach for _ in range(3)]

            def collect(kind, grad, values, count):
                for k in range(count):
                    term = grad * values[k]
                    so_far = sums_of[kind][k]
                    sums_of[kind][k] = term if so_far is None else so_far + term

            previous = None
            for a in range(0, run, 2):
                for c in range(a, a + 2 * reach + 1):
                    if c not in grads and c < run + taps - 1:
                        grads[c] = ahead(c)
                here = own_rows(a)
                collect(1, here if previous is None else here - previous, odds, len(odd))
                second = weighted(odd, [grads[a + 2 * k + 1] for k in range(len(odd))])
                os[pl.ds(a, SUB, stride=run), :] = leading + second
                evens = [behind(a)] + evens[: reach - 1]
                if a + 1 < run:
                    previous = own_rows(a + 1)
                    for k in range(a // 2, a // 2 + reach):
                        if k not in joint:
                            joint[k] = grads[2 * k + 1] + grads[2 * k + 2]
                    following = weighted(even, [grads[a + 2 + 2 * k] for k in range(reach)])
                    total = weighted(paired_taps, [joint[a // 2 + k] for k in range(reach)])
                    os[pl.ds(a + 1, SUB, stride=run), :] = total - following - second
                    leading = following
                    odds = [behind(a + 1)] + odds[: reach - 1]
                    pairs = [evens[0] + odds[0]] + pairs[: reach - 1]
                    collect(0, here - previous, evens, reach)
                    collect(2, previous, pairs, reach)
                else:
                    collect(0, here, evens, reach)
            sums_of = [sums_of[i % 2][i // 2] + sums_of[2][i // 2] for i in range(taps)]
            grad_p[j, :, lanes] = os[0:rows].astype(BF16)
            extra = [skip_sum[which, :, part]] + [jnp.zeros((SUB, LANES), F32)] * (SUB - taps)
            extra = extra[: SUB - taps] if j == 0 else extra[1 : SUB - taps + 1]
            sums[piece, j * SUB : j * SUB + SUB, spot] = folded(sums_of + extra)
        return carry

    lax.fori_loop(0, p.shape[2] // LANES, tile, 0)


def shifted(value, axis, steps):
    count = lax.axis_size(axis)
    first, last = (max(0, -steps), min(count, count - steps))
    return lax.ppermute(value, axis, [(source, source + steps) for source in range(first, last)])


def swapped(value):
    count = lax.axis_size("ctx")
    return lax.ppermute(value, "ctx", [(s, s ^ 1) for s in range(count)])


def joined(ends, f_all):
    core = lax.rem(lax.axis_index("ctx"), 2)
    half = ends.shape[1] // 2
    other = swapped(ends)
    first = core == 0
    mine = lax.dynamic_slice_in_dim(ends, core * half, half, 1)
    theirs = lax.dynamic_slice_in_dim(other, core * half, half, 1)
    one, two = jnp.where(first, mine, theirs), jnp.where(first, theirs, mine)
    return other, f_all * one[0] + two[0], one[1] + f_all * two[1]


def paired(value, axis, step, lines=None):
    count = lax.axis_size(axis)
    return lax.ppermute(value, axis, [(source, source ^ step) for source in lines or range(count)])


def scanned(chip_e, chip_a, f_all, beside):
    chips = lax.axis_size("ctx") // 2
    f_chip = f_all * f_all
    if chips == 4:
        odd = lax.rem(lax.axis_index("ctx") // 2, 2) == 1
        sent = jnp.where(odd, chip_a, chip_e)
        first = paired(sent, "ctx", 2)
        kept = beside[0](sent, None)
        first, kept = lax.optimization_barrier((first, kept))
        sent = jnp.where(odd, chip_e, chip_a) + f_chip * first
        near = lax.ppermute(sent, "ctx", [(2, 4), (3, 5), (4, 2), (5, 3)])
        kept = beside[1](sent, kept)
        near, kept = lax.optimization_barrier((near, kept))
        far = lax.ppermute(near, "ctx", [(4, 6), (5, 7), (2, 0), (3, 1)])
        kept = beside[2](near, kept)
        far, kept = lax.optimization_barrier((far, kept))
        far = first + f_chip * far
        return jnp.where(odd, far, near), jnp.where(odd, near, far), kept
    kept = beside[2](chip_e, beside[1](chip_e, beside[0](chip_e, None)))
    before, after = jnp.zeros_like(chip_e), jnp.zeros_like(chip_a)
    reach = 1
    while reach < chips:
        early, late = shifted(chip_e, "ctx", 2 * reach), shifted(chip_a, "ctx", -2 * reach)
        factor = f_chip ** (reach - 1)
        before, after = before + factor * early, after + factor * late
        factor = f_chip**reach
        chip_e, chip_a = chip_e + factor * early, chip_a + factor * late
        reach = 2 * reach
    return before, after, kept


def summed(value):
    dp, parts = lax.axis_index("dp"), lax.axis_size("dp")
    low = lax.rem(lax.axis_index("ctx"), 2) == 0
    half = value.shape[0] // 2
    left, right = value[:half], value[half:]
    value = jnp.where(low, left, right) + swapped(jnp.where(low, right, left))
    size = half // parts
    piece = lambda k: lax.dynamic_slice_in_dim(value, jnp.bitwise_xor(dp, k) * size, size, 0)
    total = piece(0)
    for term in [paired(piece(k), "dp", k) for k in range(1, parts)]:
        total = total + term
    count = lax.axis_size("ctx")
    reaches = [2 << k for k in range((count // 2).bit_length() - 1)]
    for near, far in zip(reaches, reversed(reaches)):
        pairs = [(s, s ^ (far if s % 2 else near)) for s in range(count)]
        total = total + lax.ppermute(total, "ctx", pairs)
    value = jnp.zeros((half,) + value.shape[1:], F32)
    for k in range(parts):
        term = paired(total, "dp", k) if k else total
        value = lax.dynamic_update_slice_in_dim(value, term, jnp.bitwise_xor(dp, k) * size, 0)
    other = swapped(value)
    return jnp.concatenate([jnp.where(low, value, other), jnp.where(low, other, value)], axis=0)


def local(projected, short_filter, residues, decay_rates, skip_gain, cotangent):
    rows = projected.shape[1]
    channels = projected.shape[3]
    taps = short_filter.shape[1]
    groups, poles = residues.shape
    width = channels // groups
    run = (rows + SUB) // SUB
    held = rows + SUB
    p = projected[0].transpose(1, 0, 2)
    u = cotangent[0]
    core = lax.rem(lax.axis_index("ctx"), 2)

    def edge(last):
        start = jnp.where(last, rows - SUB, 0)
        cut = lambda value, axis: lax.dynamic_slice_in_dim(value, start, SUB, axis)
        return jnp.concatenate([cut(p, 1), cut(u, 0)[None]], axis=0)

    devices = lax.axis_size("ctx")
    across = [(k, k + 1) for k in range(1, devices - 1, 2)]
    across = across + [(target, source) for source, target in across]
    hx = lax.ppermute(edge(core == 1), "ctx", across)
    hi = swapped(edge(core == 0))

    rate = decay_rates.T
    weight = residues.T
    sub = np.arange(SUB)
    powers = np.stack([run * (7 - sub) - SUB, run * sub, 1 + run * sub, rows - run * (sub + 1) + 1])
    table = jnp.exp(-rate[None, :, None, :] * powers.astype(np.float32)[:, None, :, None])
    we, wb = table[0], table[1]
    cz, cy = weight[:, None, :] * table[2], weight[:, None, :] * table[3]
    f1 = jnp.exp(-rate)
    f_all = jnp.exp(-rate * rows)
    steps = np.array([1, run, 2 * run, 4 * run], np.float32)
    factor = jnp.exp(-rate[None] * steps[:, None, None])
    factor = jnp.concatenate([weight[None] * factor[:1], factor[1:]], axis=0)
    reach = np.array([1, 1, 2, 4])[:, None]
    down, up = sub[None] >= reach, sub[None] < SUB - reach
    join_e = jnp.where(down[:, None, :, None], factor[:, :, None, :], 0.0)
    join_a = jnp.where(up[:, None, :, None], factor[:, :, None, :], 0.0)
    close = np.arange(-taps, run).astype(np.float32)
    near = jnp.sum(weight[:, None, :] * jnp.exp(-rate[:, None, :] * close[None, :, None]), axis=0)

    each = 1

    def by_w(*shape):
        axis = len(shape)
        return pl.BlockSpec(shape + (each * groups,), lambda w: (0,) * axis + (w,))

    def fixed(value):
        return pl.BlockSpec(
            value.shape, lambda w: (0,) * value.ndim, pipeline_mode=pl.Buffered(1)
        )

    params = pltpu.CompilerParams(vmem_limit_bytes=48 * 1024 * 1024)
    shape_of = jax.ShapeDtypeStruct
    ends_spec = pl.BlockSpec((2, each, poles, groups), lambda w: (0, w, 0, 0))
    halved = pl.BlockSpec(
        (2, each, poles, groups), lambda w: (0, lax.rem(w, width // each // 2), 0, 0)
    )
    early = (hx, near, join_e, join_a, cz, cy, f_all)
    hx, near, join_e, join_a, cz, cy, f_all = lax.optimization_barrier(early)
    state_shape = shape_of((width, poles, SUB, groups), F32)
    pair_shape = shape_of((width, 2, held, groups), F32)

    def by_block(*shape, count=each, first=0):
        return pl.BlockSpec((count,) + shape, lambda w: (w + first,) + (0,) * len(shape))

    state_spec = by_block(poles, SUB, groups)
    qkv, xg, blocks_e, blocks_a, ends = pl.pallas_call(
        states_kernel,
        grid=(width // each,),
        in_specs=[
            pl.BlockSpec(memory_space=pltpu.SMEM),
            by_w(3, rows), by_w(4, SUB), by_w(4, SUB), by_w(rows), by_w(3, taps),
            fixed(f1), fixed(we), fixed(wb),
        ],
        out_specs=[
            by_block(3, held, groups), by_block(2, held, groups), state_spec, state_spec,
            ends_spec,
        ],
        out_shape=[
            shape_of((width, 3, held, groups), F32), pair_shape,
            state_shape, state_shape, shape_of((2, width, poles, groups), F32),
        ],
        scratch_shapes=[pltpu.VMEM((4, held + SUB, LANES), F32)],
        compiler_params=params,
        name="states",
    )(core[None], p, hx, hi, u, short_filter, f1, we, wb)

    many = 2 if width % 2 == 0 else 1

    def blocks(first, last):
        place = {"count": many, "first": first}
        states, pairs = by_block(poles, SUB, groups, **place), by_block(2, held, groups, **place)

        def call(sent, kept):
            close, _ = lax.optimization_barrier((near, sent))
            held_before = kept or (xg, blocks_e, blocks_a)
            out = pl.pallas_call(
                blocks_kernel,
                grid=(last - first,),
                in_specs=[
                    pairs, states, states, fixed(near),
                    pl.BlockSpec((1, many * groups), lambda w: (0, w + first)),
                    fixed(join_e), fixed(join_a),
                ],
                out_specs=[pairs, states, states, by_block(SUB, groups, count=many)],
                out_shape=[
                    pair_shape, state_shape, state_shape,
                    shape_of(((last - first) * many, SUB, groups), F32),
                ],
                input_output_aliases={0: 0, 1: 1, 2: 2},
                compiler_params=params,
                cost_estimate=pl.CostEstimate(
                    flops=60 * rows * channels, bytes_accessed=35 * 2**20, transcendentals=0
                ),
                name="blocks",
            )(*held_before[:3], close, skip_gain[None], join_e, join_a)
            return [*out[:3], jnp.concatenate([*held_before[3:], out[3]], axis=0)]

        return call

    steps = width // many
    cuts = (0, (3 * steps) // 8, (5 * steps) // 8, steps)
    other, chip_e, chip_a = joined(ends, f_all)
    before, after, (conv, from_e, from_a, skip_sum) = scanned(
        chip_e, chip_a, f_all, [blocks(cuts[k], cuts[k + 1]) for k in range(3)]
    )
    both = jnp.stack([before, after])
    found = swapped(both)

    count = 3 * SUB
    split = 2 if groups % (2 * LANES) == 0 else 1
    scratch = [
        pltpu.VMEM((3, held + SUB, LANES), F32),
        pltpu.VMEM((held, LANES), F32),
        pltpu.VMEM((3, held, LANES), F32),
        pltpu.VMEM((held, LANES), F32),
        pltpu.VMEM((2, poles, LANES), F32),
    ]
    output, grad_p, sums = pl.pallas_call(
        final_kernel,
        grid=(width // each,),
        in_specs=[
            pl.BlockSpec(memory_space=pltpu.SMEM),
            by_w(3, rows), by_w(4, SUB), by_w(4, SUB), by_w(rows),
            by_block(3, held, groups), by_block(2, held, groups), state_spec, state_spec,
            by_block(SUB, groups), halved, halved, ends_spec,
            by_w(3, taps), fixed(f1), fixed(f_all), fixed(cz), fixed(cy),
        ],
        out_specs=[
            by_w(rows), by_w(3, rows),
            pl.BlockSpec((each * split, count, groups // split), lambda w: (w, 0, 0)),
        ],
        out_shape=[
            shape_of((rows, channels), BF16),
            shape_of((3, rows, channels), BF16),
            shape_of((width * split, count, groups // split), F32),
        ],
        scratch_shapes=scratch,
        compiler_params=params,
        name="final",
    )(
        core[None], p, hx, hi, u, qkv, conv, from_e, from_a, skip_sum, both, found, other, short_filter,
        f1, f_all, cz, cy,
    )

    total = summed(sums).transpose(1, 0, 2).reshape(3, SUB, channels)
    grad_short, grad_skip = total[:, :taps], total[0, taps]
    return output[None], grad_p.transpose(1, 0, 2)[None], grad_short, grad_skip


def solution(mesh):
    placed = (P("dp", "ctx", None, None), P(), P(), P(), P(), P("dp", "ctx", None))
    return jax.shard_map(
        local,
        mesh=mesh,
        in_specs=placed,
        out_specs=(P("dp", "ctx", None), P("dp", "ctx", None, None), P(), P()),
        check_vma=False,
    )
```

```python
import functools

import jax
import jax.numpy as jnp
import numpy as np
from jax import lax
from jax.experimental import pallas as pl
from jax.experimental.pallas import tpu as pltpu
from jax.sharding import PartitionSpec as P

LANES = 128
SUB = 8
F32 = jnp.float32
BF16 = jnp.bfloat16


def spread(row):
    return jnp.broadcast_to(row, (SUB, LANES))


def added(terms):
    while len(terms) > 1:
        pairs = [terms[k] + terms[k + 1] for k in range(0, len(terms) - 1, 2)]
        terms = pairs + terms[len(terms) - len(terms) % 2 :]
    return terms[0]


def folded(values):
    row = lax.broadcasted_iota(jnp.int32, (SUB, LANES), 0)
    upper = row < 4
    values = [
        jnp.where(upper, values[n], values[n + 4])
        + pltpu.roll(jnp.where(upper, values[n + 4], values[n]), 4, 0)
        for n in range(4)
    ]
    for step in (2, 1):
        even = (row // step) % 2 == 0
        values = [
            jnp.where(
                even,
                values[n] + pltpu.roll(values[n], SUB - step, 0),
                values[n + step] + pltpu.roll(values[n + step], step, 0),
            )
            for n in range(step)
        ]
    return values[0]


def phases(tap):
    even, odd = tap[0::2], tap[1::2]
    both = [even[k] + odd[k] if k < len(odd) else even[k] for k in range(len(even))]
    return even, odd, both


def weighted(tap, values):
    return added([tap[k] * values[k] for k in range(len(tap))])


def edges_kernel(core, p_head, p_tail, u_head, u_tail, across, within, heads, tails):
    first = core[0] == 0
    reach = across.shape[0] // 4
    for j in range(4):
        head = (p_head[j] if j < 3 else u_head[...]).astype(F32)
        tail = (p_tail[j] if j < 3 else u_tail[...]).astype(F32)
        heads[reach * j : reach * j + reach] = head[:reach]
        tails[reach * j : reach * j + reach] = tail[tail.shape[0] - reach :]
    head, tail = heads[...], tails[...]
    across[...] = jnp.where(first, head, tail).astype(BF16)
    within[...] = jnp.where(first, tail, head).astype(BF16)


def place_edges(first, hx, hi, lanes, edges, streams, rows):
    across, within = hx[:, lanes].astype(F32), hi[:, lanes].astype(F32)
    edges[0], edges[1] = jnp.where(first, across, within), jnp.where(first, within, across)
    reach = across.shape[0] // 4
    for j in range(len(streams)):
        if j < 3:
            streams[j][SUB - reach : SUB] = edges[0, reach * j : reach * j + reach]
        streams[j][SUB + rows :] = jnp.zeros((SUB, LANES), F32)
        streams[j][SUB + rows : SUB + rows + reach] = edges[1, reach * j : reach * j + reach]


def states_kernel(core, p, hx, hi, u, filt, f1, we, wb, qkv, xg, blocks_e, blocks_a, ends, xs, edges):
    rows = p.shape[1]
    run = (rows + SUB) // SUB
    taps = filt.shape[1]
    poles, groups = f1.shape
    own = rows - run * (SUB - 1)
    tiles = groups // LANES
    first = core[0] == 0

    def tile(lt, carry):
        lanes = pl.ds(pl.multiple_of(lt * LANES, LANES), LANES)
        part = pl.ds(pl.multiple_of(lax.rem(lt, tiles) * LANES, LANES), LANES)
        which = lt // tiles
        inside = lax.broadcasted_iota(jnp.int32, (SUB, LANES), 0) < SUB - 1
        for j in range(3):
            xs[j, SUB : SUB + rows] = p[j, :, lanes].astype(F32)
        xs[3, SUB : SUB + rows] = u[:, lanes].astype(F32)
        place_edges(first, hx, hi, lanes, edges, [xs.at[j] for j in range(4)], rows)

        def mixed(j):
            even, odd, both = phases([spread(filt[j, i : i + 1, lanes]) for i in range(taps)])
            row = lambda a: xs[j, pl.ds(SUB + a, SUB, stride=run), :]
            reach = len(even)
            evens = [row(-2 * k) for k in range(1, reach)]
            odds = [row(1 - 2 * k) for k in range(1, reach)]
            pairs = [evens[k] + odds[k] for k in range(reach - 1)]
            before = weighted(odd, odds)
            for a in range(0, run, 2):
                evens = [row(a)] + evens[: reach - 1]
                first = weighted(even, evens)
                yield first + before
                if a + 1 < run:
                    odds = [row(a + 1)] + odds[: reach - 1]
                    pairs = [evens[0] + odds[0]] + pairs[: reach - 1]
                    before = weighted(odd, odds)
                    yield weighted(both, pairs) - first - before

        decay = [spread(f1[n : n + 1, part]) for n in range(poles)]
        for j in (1, 2, 0):
            for a, total in enumerate(mixed(j)):
                at = slice(SUB * a, SUB * a + SUB)
                qkv[which, j, at, part] = total
                if j == 2:
                    xg[which, 0, at, part] = qkv[which, 1, at, part] * total
                if j == 0:
                    xg[which, 1, at, part] = xs[3, pl.ds(SUB + a, SUB, stride=run), :] * total
        for side, order, weight, blocks in (
            (0, range(run), we, blocks_e),
            (1, range(run - 1, -1, -1), wb, blocks_a),
        ):
            state = None
            for a in order:
                x = xg[which, side, SUB * a : SUB * a + SUB, part]
                if a >= own:
                    x = jnp.where(inside, x, 0.0)
                state = [x] * poles if state is None else [decay[n] * state[n] + x for n in range(poles)]
            for n in range(poles):
                blocks[which, n, :, part] = state[n]
            state = [state[n] * weight[n, :, part] for n in range(poles)]
            for n in range(0, poles, SUB):
                ends[side, which, n : n + SUB, part] = folded(state[n : n + SUB])
        return carry

    lax.fori_loop(0, p.shape[2] // LANES, tile, 0)


def blocks_kernel(
    xg, blocks_e, blocks_a, near, skip, join_e, join_a, conv, from_e, from_a, skip_sum
):
    run = xg.shape[2] // SUB
    rows = xg.shape[2] - SUB
    taps = near.shape[0] - run
    poles, groups = blocks_e.shape[1], near.shape[1]
    own = rows - run * (SUB - 1)
    tiles = groups // LANES

    def tile(lt, carry):
        lanes = pl.ds(pl.multiple_of(lt * LANES, LANES), LANES)
        part = pl.ds(pl.multiple_of(lax.rem(lt, tiles) * LANES, LANES), LANES)
        which = lt // tiles
        inside = lax.broadcasted_iota(jnp.int32, (SUB, LANES), 0) < SUB - 1
        gain = spread(skip[0:1, lanes])
        lag = [spread(near[taps + m : taps + m + 1, part]) for m in range(run)]
        lag[0] = lag[0] + gain
        x = [xg[which, 0, SUB * a : SUB * a + SUB, part] for a in range(run)]
        for a in range(run):
            conv[which, 0, SUB * a : SUB * a + SUB, part] = added(
                [lag[m] * x[a - m] for m in range(a + 1)]
            )
        gated = x
        x = [xg[which, 1, SUB * a : SUB * a + SUB, part] for a in range(run)]
        masked = [x[a] if a < own else jnp.where(inside, x[a], 0.0) for a in range(run)]
        skip_sum[which, :, part] = added([masked[a] * gated[a] for a in range(run)])
        past = [jnp.where(inside, 0.0, gain)] + [
            jnp.where(inside, 0.0, -spread(near[taps - m : taps - m + 1, part]))
            for m in range(1, taps - 1)
        ]
        for a in range(run):
            terms = [lag[m] * masked[a + m] for m in range(run - a)]
            if own <= a < own + taps - 1:
                terms = terms + [past[m] * x[a - m] for m in range(a - own + 1)]
            conv[which, 1, SUB * a : SUB * a + SUB, part] = added(terms)
        for n in range(poles):
            value = pltpu.roll(blocks_e[which, n, :, part], 1, 0) * join_e[0, n, :, part]
            for k, step in ((1, 1), (2, 2), (3, 4)):
                value = value + pltpu.roll(value, step, 0) * join_e[k, n, :, part]
            from_e[which, n, :, part] = value
            value = pltpu.roll(blocks_a[which, n, :, part], SUB - 1, 0) * join_a[0, n, :, part]
            for k, step in ((1, 1), (2, 2), (3, 4)):
                value = value + pltpu.roll(value, SUB - step, 0) * join_a[k, n, :, part]
            from_a[which, n, :, part] = value
        return carry

    lax.fori_loop(0, xg.shape[0] * tiles, tile, 0)


def final_kernel(
    core, p, hx, hi, u, qkv, conv, from_e, from_a, skip_sum, both, found, other, filt, f1, f_all, cz, cy,
    output, grad_p, sums, ps, gs, os, es, edges,
):
    rows = p.shape[1]
    run = (rows + SUB) // SUB
    taps = filt.shape[1]
    poles, groups = f1.shape
    own = rows - run * (SUB - 1)
    tiles = groups // LANES
    first = core[0] == 0
    halves = pl.num_programs(0) // 2
    kept = (pl.program_id(0) < halves) == first
    cut = sums.shape[2] // LANES

    def tile(lt, carry):
        lanes = pl.ds(pl.multiple_of(lt * LANES, LANES), LANES)
        part = pl.ds(pl.multiple_of(lax.rem(lt, tiles) * LANES, LANES), LANES)
        which = lt // tiles
        piece = lt // cut
        spot = pl.ds(pl.multiple_of(lax.rem(lt, cut) * LANES, LANES), LANES)
        inside = lax.broadcasted_iota(jnp.int32, (SUB, LANES), 0) < SUB - 1
        for side in range(2):
            far = jnp.where(kept, both[side, which, :, part], found[side, which, :, part])
            close = other[side, which, :, part] + f_all[:, part] * far
            es[side] = jnp.where(first == (side == 0), far, close)
        for j in range(3):
            ps[j, SUB : SUB + rows] = p[j, :, lanes].astype(F32)
        ps[3, SUB : SUB + rows] = u[:, lanes].astype(F32)
        place_edges(first, hx, hi, lanes, edges, [ps.at[j] for j in range(4)], rows)
        decay = [spread(f1[n : n + 1, part]) for n in range(poles)]

        state = [
            from_e[which, n, :, part] + cz[n, :, part] * spread(es[0, n : n + 1])
            for n in range(poles)
        ]
        for a in range(run):
            at = slice(SUB * a, SUB * a + SUB)
            query, upstream = qkv[which, 0, at, part], ps[3, pl.ds(SUB + a, SUB, stride=run), :]
            filtered = conv[which, 0, at, part] + added(list(state))
            os[pl.ds(a, SUB, stride=run), :] = query * filtered
            gs[0, at] = upstream * filtered
            if a + 1 < run:
                state = [state[n] * decay[n] for n in range(poles)]
        output[:, lanes] = os[0:rows].astype(BF16)

        state = [
            from_a[which, n, :, part] + cy[n, :, part] * spread(es[1, n : n + 1])
            for n in range(poles)
        ]
        for a in range(run - 1, -1, -1):
            at = slice(SUB * a, SUB * a + SUB)
            grad = conv[which, 1, at, part] + added(list(state))
            gs[1, at] = grad * qkv[which, 2, at, part]
            gs[2, at] = grad * qkv[which, 1, at, part]
            if a:
                state = [state[n] * decay[n] for n in range(poles)]

        for j in range(3):
            even, odd, paired_taps = phases([spread(filt[j, i : i + 1, lanes]) for i in range(taps)])
            reach = len(even)
            grads = [gs[j, SUB * a : SUB * a + SUB] for a in range(taps - 1)]
            beyond = [pltpu.roll(value, SUB - 1, 0) for value in grads]

            def ahead(a):
                return gs[j, SUB * a : SUB * a + SUB] if a < run else beyond[a - run]

            def behind(a):
                return ps[j, pl.ds(SUB + a, SUB, stride=run), :]

            def own_rows(a):
                return grads[a] if a < own else jnp.where(inside, grads[a], 0.0)

            grads = {a: grads[a] for a in range(taps - 1)}
            joint = {k: grads[2 * k + 1] + grads[2 * k + 2] for k in range((taps - 3) // 2)}
            leading = weighted(even, [grads[2 * k] if 2 * k in grads else ahead(2 * k) for k in range(reach)])
            evens = [behind(-2 * k) for k in range(1, reach)]
            odds = [behind(1 - 2 * k) for k in range(1, reach)]
            pairs = [evens[k] + odds[k] for k in range(reach - 1)]
            sums_of = [[None] * reach for _ in range(3)]

            def collect(kind, grad, values, count):
                for k in range(count):
                    term = grad * values[k]
                    so_far = sums_of[kind][k]
                    sums_of[kind][k] = term if so_far is None else so_far + term

            previous = None
            for a in range(0, run, 2):
                for c in range(a, a + 2 * reach + 1):
                    if c not in grads and c < run + taps - 1:
                        grads[c] = ahead(c)
                here = own_rows(a)
                collect(1, here if previous is None else here - previous, odds, len(odd))
                second = weighted(odd, [grads[a + 2 * k + 1] for k in range(len(odd))])
                os[pl.ds(a, SUB, stride=run), :] = leading + second
                evens = [behind(a)] + evens[: reach - 1]
                if a + 1 < run:
                    previous = own_rows(a + 1)
                    for k in range(a // 2, a // 2 + reach):
                        if k not in joint:
                            joint[k] = grads[2 * k + 1] + grads[2 * k + 2]
                    following = weighted(even, [grads[a + 2 + 2 * k] for k in range(reach)])
                    total = weighted(paired_taps, [joint[a // 2 + k] for k in range(reach)])
                    os[pl.ds(a + 1, SUB, stride=run), :] = total - following - second
                    leading = following
                    odds = [behind(a + 1)] + odds[: reach - 1]
                    pairs = [evens[0] + odds[0]] + pairs[: reach - 1]
                    collect(0, here - previous, evens, reach)
                    collect(2, previous, pairs, reach)
                else:
                    collect(0, here, evens, reach)
            sums_of = [sums_of[i % 2][i // 2] + sums_of[2][i // 2] for i in range(taps)]
            grad_p[j, :, lanes] = os[0:rows].astype(BF16)
            extra = [skip_sum[which, :, part]] + [jnp.zeros((SUB, LANES), F32)] * (SUB - taps)
            extra = extra[: SUB - taps] if j == 0 else extra[1 : SUB - taps + 1]
            sums[piece, j * SUB : j * SUB + SUB, spot] = folded(sums_of + extra)
        return carry

    lax.fori_loop(0, p.shape[2] // LANES, tile, 0)


def shifted(value, axis, steps):
    count = lax.axis_size(axis)
    first, last = (max(0, -steps), min(count, count - steps))
    return lax.ppermute(value, axis, [(source, source + steps) for source in range(first, last)])


def swapped(value):
    count = lax.axis_size("ctx")
    return lax.ppermute(value, "ctx", [(s, s ^ 1) for s in range(count)])


def joined(ends, f_all):
    core = lax.rem(lax.axis_index("ctx"), 2)
    half = ends.shape[1] // 2
    other = swapped(ends)
    first = core == 0
    mine = lax.dynamic_slice_in_dim(ends, core * half, half, 1)
    theirs = lax.dynamic_slice_in_dim(other, core * half, half, 1)
    one, two = jnp.where(first, mine, theirs), jnp.where(first, theirs, mine)
    return other, f_all * one[0] + two[0], one[1] + f_all * two[1]


def paired(value, axis, step, lines=None):
    count = lax.axis_size(axis)
    return lax.ppermute(value, axis, [(source, source ^ step) for source in lines or range(count)])


def scanned(chip_e, chip_a, f_all, beside):
    chips = lax.axis_size("ctx") // 2
    f_chip = f_all * f_all
    if chips == 4:
        odd = lax.rem(lax.axis_index("ctx") // 2, 2) == 1
        sent = jnp.where(odd, chip_a, chip_e)
        first = paired(sent, "ctx", 2)
        kept = beside[0](sent, None)
        first, kept = lax.optimization_barrier((first, kept))
        sent = jnp.where(odd, chip_e, chip_a) + f_chip * first
        near = lax.ppermute(sent, "ctx", [(2, 4), (3, 5), (4, 2), (5, 3)])
        kept = beside[1](sent, kept)
        near, kept = lax.optimization_barrier((near, kept))
        far = lax.ppermute(near, "ctx", [(4, 6), (5, 7), (2, 0), (3, 1)])
        kept = beside[2](near, kept)
        far, kept = lax.optimization_barrier((far, kept))
        far = first + f_chip * far
        return jnp.where(odd, far, near), jnp.where(odd, near, far), kept
    kept = beside[2](chip_e, beside[1](chip_e, beside[0](chip_e, None)))
    before, after = jnp.zeros_like(chip_e), jnp.zeros_like(chip_a)
    reach = 1
    while reach < chips:
        early, late = shifted(chip_e, "ctx", 2 * reach), shifted(chip_a, "ctx", -2 * reach)
        factor = f_chip ** (reach - 1)
        before, after = before + factor * early, after + factor * late
        factor = f_chip**reach
        chip_e, chip_a = chip_e + factor * early, chip_a + factor * late
        reach = 2 * reach
    return before, after, kept


def summed(value):
    dp, parts = lax.axis_index("dp"), lax.axis_size("dp")
    low = lax.rem(lax.axis_index("ctx"), 2) == 0
    half = value.shape[0] // 2
    left, right = value[:half], value[half:]
    value = jnp.where(low, left, right) + swapped(jnp.where(low, right, left))
    size = half // parts
    piece = lambda k: lax.dynamic_slice_in_dim(value, jnp.bitwise_xor(dp, k) * size, size, 0)
    total = piece(0)
    for term in [paired(piece(k), "dp", k) for k in range(1, parts)]:
        total = total + term
    reach = 2
    while reach < lax.axis_size("ctx"):
        total = total + paired(total, "ctx", reach)
        reach = 2 * reach
    value = jnp.zeros((half,) + value.shape[1:], F32)
    for k in range(parts):
        term = paired(total, "dp", k) if k else total
        value = lax.dynamic_update_slice_in_dim(value, term, jnp.bitwise_xor(dp, k) * size, 0)
    other = swapped(value)
    return jnp.concatenate([jnp.where(low, value, other), jnp.where(low, other, value)], axis=0)


def local(projected, short_filter, residues, decay_rates, skip_gain, cotangent):
    rows = projected.shape[1]
    channels = projected.shape[3]
    taps = short_filter.shape[1]
    groups, poles = residues.shape
    width = channels // groups
    run = (rows + SUB) // SUB
    held = rows + SUB
    p = projected[0].transpose(1, 0, 2)
    u = cotangent[0]
    core = lax.rem(lax.axis_index("ctx"), 2)
    params = pltpu.CompilerParams(vmem_limit_bytes=48 * 1024 * 1024)
    shape_of = jax.ShapeDtypeStruct
    span, tail, chunk = taps - 1, 2 * SUB, channels // 4
    packed = pl.BlockSpec((4 * span, chunk), lambda w: (0, w))
    to_across, to_within = pl.pallas_call(
        edges_kernel,
        grid=(4,),
        in_specs=[
            pl.BlockSpec(memory_space=pltpu.SMEM),
            pl.BlockSpec((3, tail, chunk), lambda w: (0, 0, w)),
            pl.BlockSpec((3, tail, chunk), lambda w: (0, rows // tail - 1, w)),
            pl.BlockSpec((tail, chunk), lambda w: (0, w)),
            pl.BlockSpec((tail, chunk), lambda w: (rows // tail - 1, w)),
        ],
        out_specs=[packed, packed],
        out_shape=[shape_of((4 * span, channels), BF16)] * 2,
        scratch_shapes=[pltpu.VMEM((4 * span, chunk), F32)] * 2,
        compiler_params=params,
        name="edges",
    )(core[None], p, p, u, u)
    devices = lax.axis_size("ctx")
    across = [(k, k + 1) for k in range(1, devices - 1, 2)]
    across = across + [(target, source) for source, target in across]
    hx = lax.ppermute(to_across, "ctx", across)
    hi = swapped(to_within)

    rate = decay_rates.T
    weight = residues.T
    sub = np.arange(SUB)
    powers = np.stack([run * (7 - sub) - SUB, run * sub, 1 + run * sub, rows - run * (sub + 1) + 1])
    table = jnp.exp(-rate[None, :, None, :] * powers.astype(np.float32)[:, None, :, None])
    we, wb = table[0], table[1]
    cz, cy = weight[:, None, :] * table[2], weight[:, None, :] * table[3]
    f1 = jnp.exp(-rate)
    f_all = jnp.exp(-rate * rows)
    steps = np.array([1, run, 2 * run, 4 * run], np.float32)
    factor = jnp.exp(-rate[None] * steps[:, None, None])
    factor = jnp.concatenate([weight[None] * factor[:1], factor[1:]], axis=0)
    reach = np.array([1, 1, 2, 4])[:, None]
    down, up = sub[None] >= reach, sub[None] < SUB - reach
    join_e = jnp.where(down[:, None, :, None], factor[:, :, None, :], 0.0)
    join_a = jnp.where(up[:, None, :, None], factor[:, :, None, :], 0.0)
    close = np.arange(-taps, run).astype(np.float32)
    near = jnp.sum(weight[:, None, :] * jnp.exp(-rate[:, None, :] * close[None, :, None]), axis=0)

    each = 1

    def by_w(*shape):
        axis = len(shape)
        return pl.BlockSpec(shape + (each * groups,), lambda w: (0,) * axis + (w,))

    def fixed(value):
        return pl.BlockSpec(
            value.shape, lambda w: (0,) * value.ndim, pipeline_mode=pl.Buffered(1)
        )

    ends_spec = pl.BlockSpec((2, each, poles, groups), lambda w: (0, w, 0, 0))
    halved = pl.BlockSpec(
        (2, each, poles, groups), lambda w: (0, lax.rem(w, width // each // 2), 0, 0)
    )
    early = (hx, near, join_e, join_a, cz, cy, f_all)
    hx, near, join_e, join_a, cz, cy, f_all = lax.optimization_barrier(early)
    state_shape = shape_of((width, poles, SUB, groups), F32)
    pair_shape = shape_of((width, 2, held, groups), F32)

    def by_block(*shape, count=each, first=0):
        return pl.BlockSpec((count,) + shape, lambda w: (w + first,) + (0,) * len(shape))

    state_spec = by_block(poles, SUB, groups)
    qkv, xg, blocks_e, blocks_a, ends = pl.pallas_call(
        states_kernel,
        grid=(width // each,),
        in_specs=[
            pl.BlockSpec(memory_space=pltpu.SMEM),
            by_w(3, rows), by_w(4 * span), by_w(4 * span), by_w(rows), by_w(3, taps),
            fixed(f1), fixed(we), fixed(wb),
        ],
        out_specs=[
            by_block(3, held, groups), by_block(2, held, groups), state_spec, state_spec,
            ends_spec,
        ],
        out_shape=[
            shape_of((width, 3, held, groups), F32), pair_shape,
            state_shape, state_shape, shape_of((2, width, poles, groups), F32),
        ],
        scratch_shapes=[
            pltpu.VMEM((4, held + SUB, LANES), F32), pltpu.VMEM((2, 4 * span, LANES), F32),
        ],
        compiler_params=params,
        name="states",
    )(core[None], p, hx, hi, u, short_filter, f1, we, wb)

    many = 2 if width % 2 == 0 else 1

    def blocks(first, last):
        place = {"count": many, "first": first}
        states, pairs = by_block(poles, SUB, groups, **place), by_block(2, held, groups, **place)

        def call(sent, kept):
            close, _ = lax.optimization_barrier((near, sent))
            held_before = kept or (xg, blocks_e, blocks_a)
            out = pl.pallas_call(
                blocks_kernel,
                grid=(last - first,),
                in_specs=[
                    pairs, states, states, fixed(near),
                    pl.BlockSpec((1, many * groups), lambda w: (0, w + first)),
                    fixed(join_e), fixed(join_a),
                ],
                out_specs=[pairs, states, states, by_block(SUB, groups, count=many)],
                out_shape=[
                    pair_shape, state_shape, state_shape,
                    shape_of(((last - first) * many, SUB, groups), F32),
                ],
                input_output_aliases={0: 0, 1: 1, 2: 2},
                compiler_params=params,
                cost_estimate=pl.CostEstimate(
                    flops=60 * rows * channels, bytes_accessed=35 * 2**20, transcendentals=0
                ),
                name="blocks",
            )(*held_before[:3], close, skip_gain[None], join_e, join_a)
            return [*out[:3], jnp.concatenate([*held_before[3:], out[3]], axis=0)]

        return call

    steps = width // many
    cuts = (0, (3 * steps) // 8, (5 * steps) // 8, steps)
    other, chip_e, chip_a = joined(ends, f_all)
    before, after, (conv, from_e, from_a, skip_sum) = scanned(
        chip_e, chip_a, f_all, [blocks(cuts[k], cuts[k + 1]) for k in range(3)]
    )
    both = jnp.stack([before, after])
    found = swapped(both)

    count = 3 * SUB
    split = 2 if groups % (2 * LANES) == 0 else 1
    scratch = [
        pltpu.VMEM((4, held + SUB, LANES), F32),
        pltpu.VMEM((3, held, LANES), F32),
        pltpu.VMEM((held, LANES), F32),
        pltpu.VMEM((2, poles, LANES), F32),
        pltpu.VMEM((2, 4 * span, LANES), F32),
    ]
    output, grad_p, sums = pl.pallas_call(
        final_kernel,
        grid=(width // each,),
        in_specs=[
            pl.BlockSpec(memory_space=pltpu.SMEM),
            by_w(3, rows), by_w(4 * span), by_w(4 * span), by_w(rows),
            by_block(3, held, groups), by_block(2, held, groups), state_spec, state_spec,
            by_block(SUB, groups), halved, halved, ends_spec,
            by_w(3, taps), fixed(f1), fixed(f_all), fixed(cz), fixed(cy),
        ],
        out_specs=[
            by_w(rows), by_w(3, rows),
            pl.BlockSpec((each * split, count, groups // split), lambda w: (w, 0, 0)),
        ],
        out_shape=[
            shape_of((rows, channels), BF16),
            shape_of((3, rows, channels), BF16),
            shape_of((width * split, count, groups // split), F32),
        ],
        scratch_shapes=scratch,
        compiler_params=params,
        name="final",
    )(
        core[None], p, hx, hi, u, qkv, conv, from_e, from_a, skip_sum, both, found, other, short_filter,
        f1, f_all, cz, cy,
    )

    total = summed(sums).transpose(1, 0, 2).reshape(3, SUB, channels)
    grad_short, grad_skip = total[:, :taps], total[0, taps]
    return output[None], grad_p.transpose(1, 0, 2)[None], grad_short, grad_skip


def solution(mesh):
    placed = (P("dp", "ctx", None, None), P(), P(), P(), P(), P("dp", "ctx", None))
    return jax.shard_map(
        local,
        mesh=mesh,
        in_specs=placed,
        out_specs=(P("dp", "ctx", None), P("dp", "ctx", None, None), P(), P()),
        check_vma=False,
    )
```

```python
import functools

import jax
import jax.numpy as jnp
import numpy as np
from jax import lax
from jax.experimental import pallas as pl
from jax.experimental.pallas import tpu as pltpu
from jax.sharding import PartitionSpec as P

LANES = 128
SUB = 8
F32 = jnp.float32
BF16 = jnp.bfloat16


def spread(row):
    return jnp.broadcast_to(row, (SUB, LANES))


def added(terms):
    while len(terms) > 1:
        pairs = [terms[k] + terms[k + 1] for k in range(0, len(terms) - 1, 2)]
        terms = pairs + terms[len(terms) - len(terms) % 2 :]
    return terms[0]


def folded(values):
    row = lax.broadcasted_iota(jnp.int32, (SUB, LANES), 0)
    upper = row < 4
    values = [
        jnp.where(upper, values[n], values[n + 4])
        + pltpu.roll(jnp.where(upper, values[n + 4], values[n]), 4, 0)
        for n in range(4)
    ]
    for step in (2, 1):
        even = (row // step) % 2 == 0
        values = [
            jnp.where(
                even,
                values[n] + pltpu.roll(values[n], SUB - step, 0),
                values[n + step] + pltpu.roll(values[n + step], step, 0),
            )
            for n in range(step)
        ]
    return values[0]


def phases(tap):
    even, odd = tap[0::2], tap[1::2]
    both = [even[k] + odd[k] if k < len(odd) else even[k] for k in range(len(even))]
    return even, odd, both


def weighted(tap, values):
    return added([tap[k] * values[k] for k in range(len(tap))])


def states_kernel(core, p, hx, hi, u, filt, f1, we, wb, qkv, xg, blocks_e, blocks_a, ends, xs):
    rows = p.shape[1]
    run = (rows + SUB) // SUB
    taps = filt.shape[1]
    poles, groups = f1.shape
    own = rows - run * (SUB - 1)
    tiles = groups // LANES
    first = core[0] == 0

    def tile(lt, carry):
        lanes = pl.ds(pl.multiple_of(lt * LANES, LANES), LANES)
        part = pl.ds(pl.multiple_of(lax.rem(lt, tiles) * LANES, LANES), LANES)
        which = lt // tiles
        inside = lax.broadcasted_iota(jnp.int32, (SUB, LANES), 0) < SUB - 1
        for j in range(3):
            across, within = hx[j, :, lanes].astype(F32), hi[j, :, lanes].astype(F32)
            xs[j, 0:SUB] = jnp.where(first, across, within)
            xs[j, SUB : SUB + rows] = p[j, :, lanes].astype(F32)
            xs[j, SUB + rows :] = jnp.where(first, within, across)
        xs[3, SUB : SUB + rows] = u[:, lanes].astype(F32)
        across, within = hx[3, :, lanes].astype(F32), hi[3, :, lanes].astype(F32)
        xs[3, SUB + rows :] = jnp.where(first, within, across)

        def mixed(j):
            even, odd, both = phases([spread(filt[j, i : i + 1, lanes]) for i in range(taps)])
            row = lambda a: xs[j, pl.ds(SUB + a, SUB, stride=run), :]
            reach = len(even)
            evens = [row(-2 * k) for k in range(1, reach)]
            odds = [row(1 - 2 * k) for k in range(1, reach)]
            pairs = [evens[k] + odds[k] for k in range(reach - 1)]
            before = weighted(odd, odds)
            for a in range(0, run, 2):
                evens = [row(a)] + evens[: reach - 1]
                first = weighted(even, evens)
                yield first + before
                if a + 1 < run:
                    odds = [row(a + 1)] + odds[: reach - 1]
                    pairs = [evens[0] + odds[0]] + pairs[: reach - 1]
                    before = weighted(odd, odds)
                    yield weighted(both, pairs) - first - before

        decay = [spread(f1[n : n + 1, part]) for n in range(poles)]
        for j in (1, 2, 0):
            for a, total in enumerate(mixed(j)):
                at = slice(SUB * a, SUB * a + SUB)
                qkv[which, j, at, part] = total
                if j == 2:
                    xg[which, 0, at, part] = qkv[which, 1, at, part] * total
                if j == 0:
                    xg[which, 1, at, part] = xs[3, pl.ds(SUB + a, SUB, stride=run), :] * total
        for side, order, weight, blocks in (
            (0, range(run), we, blocks_e),
            (1, range(run - 1, -1, -1), wb, blocks_a),
        ):
            state = None
            for a in order:
                x = xg[which, side, SUB * a : SUB * a + SUB, part]
                if a >= own:
                    x = jnp.where(inside, x, 0.0)
                state = [x] * poles if state is None else [decay[n] * state[n] + x for n in range(poles)]
            for n in range(poles):
                blocks[which, n, :, part] = state[n]
            state = [state[n] * weight[n, :, part] for n in range(poles)]
            for n in range(0, poles, SUB):
                ends[side, which, n : n + SUB, part] = folded(state[n : n + SUB])
        return carry

    lax.fori_loop(0, p.shape[2] // LANES, tile, 0)


def blocks_kernel(
    xg, blocks_e, blocks_a, near, skip, join_e, join_a, conv, from_e, from_a, skip_sum
):
    run = xg.shape[2] // SUB
    rows = xg.shape[2] - SUB
    taps = near.shape[0] - run
    poles, groups = blocks_e.shape[1], near.shape[1]
    own = rows - run * (SUB - 1)
    tiles = groups // LANES

    def tile(lt, carry):
        lanes = pl.ds(pl.multiple_of(lt * LANES, LANES), LANES)
        part = pl.ds(pl.multiple_of(lax.rem(lt, tiles) * LANES, LANES), LANES)
        which = lt // tiles
        inside = lax.broadcasted_iota(jnp.int32, (SUB, LANES), 0) < SUB - 1
        gain = spread(skip[0:1, lanes])
        lag = [spread(near[taps + m : taps + m + 1, part]) for m in range(run)]
        lag[0] = lag[0] + gain
        x = [xg[which, 0, SUB * a : SUB * a + SUB, part] for a in range(run)]
        for a in range(run):
            conv[which, 0, SUB * a : SUB * a + SUB, part] = added(
                [lag[m] * x[a - m] for m in range(a + 1)]
            )
        gated = x
        x = [xg[which, 1, SUB * a : SUB * a + SUB, part] for a in range(run)]
        masked = [x[a] if a < own else jnp.where(inside, x[a], 0.0) for a in range(run)]
        skip_sum[which, :, part] = added([masked[a] * gated[a] for a in range(run)])
        past = [jnp.where(inside, 0.0, gain)] + [
            jnp.where(inside, 0.0, -spread(near[taps - m : taps - m + 1, part]))
            for m in range(1, taps - 1)
        ]
        for a in range(run):
            terms = [lag[m] * masked[a + m] for m in range(run - a)]
            if own <= a < own + taps - 1:
                terms = terms + [past[m] * x[a - m] for m in range(a - own + 1)]
            conv[which, 1, SUB * a : SUB * a + SUB, part] = added(terms)
        for n in range(poles):
            value = pltpu.roll(blocks_e[which, n, :, part], 1, 0) * join_e[0, n, :, part]
            for k, step in ((1, 1), (2, 2), (3, 4)):
                value = value + pltpu.roll(value, step, 0) * join_e[k, n, :, part]
            from_e[which, n, :, part] = value
            value = pltpu.roll(blocks_a[which, n, :, part], SUB - 1, 0) * join_a[0, n, :, part]
            for k, step in ((1, 1), (2, 2), (3, 4)):
                value = value + pltpu.roll(value, SUB - step, 0) * join_a[k, n, :, part]
            from_a[which, n, :, part] = value
        return carry

    lax.fori_loop(0, xg.shape[0] * tiles, tile, 0)


def back_conv(row, tap, run, os):
    even, odd, both = phases(tap)
    reach = len(even)
    known, joint = {}, {}

    def get(a):
        if a not in known:
            known[a] = row(a) if a < run else pltpu.roll(row(a - run), SUB - 1, 0)
        return known[a]

    def pair(k):
        if k not in joint:
            joint[k] = get(2 * k + 1) + get(2 * k + 2)
        return joint[k]

    leading = weighted(even, [get(2 * k) for k in range(reach)])
    for a in range(0, run, 2):
        second = weighted(odd, [get(a + 2 * k + 1) for k in range(len(odd))])
        os[pl.ds(a, SUB, stride=run), :] = leading + second
        if a + 1 < run:
            following = weighted(even, [get(a + 2 + 2 * k) for k in range(reach)])
            total = weighted(both, [pair(a // 2 + k) for k in range(reach)])
            os[pl.ds(a + 1, SUB, stride=run), :] = total - following - second
            leading = following


def later_kernel(later, filt, filled, grad_p, os):
    rows = grad_p.shape[1]
    run = (rows + SUB) // SUB

    def tile(lt, carry):
        lanes = pl.ds(pl.multiple_of(lt * LANES, LANES), LANES)
        for j in range(3):
            tap = [spread(filt[j, i : i + 1, lanes]) for i in range(filt.shape[1])]
            back_conv(lambda a: later[0, j, SUB * a : SUB * a + SUB, lanes], tap, run, os)
            grad_p[j, :, lanes] = os[0:rows].astype(BF16)
        return carry

    lax.fori_loop(0, grad_p.shape[2] // LANES, tile, 0)


def final_kernel(
    here, core, p, hx, hi, u, qkv, conv, from_e, from_a, skip_sum, both, found, other, filt, f1, f_all, cz, cy,
    output, grad_p, sums, later, ps, us, gs, os, es,
):
    rows = p.shape[1]
    run = (rows + SUB) // SUB
    taps = filt.shape[1]
    poles, groups = f1.shape
    own = rows - run * (SUB - 1)
    tiles = groups // LANES
    first = core[0] == 0
    halves = pl.num_programs(0) // 2
    kept = (pl.program_id(0) < halves) == first
    cut = sums.shape[2] // LANES

    def tile(lt, carry):
        lanes = pl.ds(pl.multiple_of(lt * LANES, LANES), LANES)
        part = pl.ds(pl.multiple_of(lax.rem(lt, tiles) * LANES, LANES), LANES)
        which = lt // tiles
        piece = lt // cut
        spot = pl.ds(pl.multiple_of(lax.rem(lt, cut) * LANES, LANES), LANES)
        inside = lax.broadcasted_iota(jnp.int32, (SUB, LANES), 0) < SUB - 1
        for side in range(2):
            far = jnp.where(kept, both[side, which, :, part], found[side, which, :, part])
            close = other[side, which, :, part] + f_all[:, part] * far
            es[side] = jnp.where(first == (side == 0), far, close)
        for j in range(3):
            across, within = hx[j, :, lanes].astype(F32), hi[j, :, lanes].astype(F32)
            ps[j, 0:SUB] = jnp.where(first, across, within)
            ps[j, SUB : SUB + rows] = p[j, :, lanes].astype(F32)
            ps[j, SUB + rows :] = jnp.where(first, within, across)
        us[0:rows] = u[:, lanes].astype(F32)
        across, within = hx[3, :, lanes].astype(F32), hi[3, :, lanes].astype(F32)
        us[rows:] = jnp.where(first, within, across)
        decay = [spread(f1[n : n + 1, part]) for n in range(poles)]

        state = [
            from_e[which, n, :, part] + cz[n, :, part] * spread(es[0, n : n + 1])
            for n in range(poles)
        ]
        for a in range(run):
            at = slice(SUB * a, SUB * a + SUB)
            query, upstream = qkv[which, 0, at, part], us[pl.ds(a, SUB, stride=run), :]
            filtered = conv[which, 0, at, part] + added(list(state))
            os[pl.ds(a, SUB, stride=run), :] = query * filtered
            gs[0, at] = upstream * filtered
            if a + 1 < run:
                state = [state[n] * decay[n] for n in range(poles)]
        output[:, lanes] = os[0:rows].astype(BF16)

        state = [
            from_a[which, n, :, part] + cy[n, :, part] * spread(es[1, n : n + 1])
            for n in range(poles)
        ]
        for a in range(run - 1, -1, -1):
            at = slice(SUB * a, SUB * a + SUB)
            grad = conv[which, 1, at, part] + added(list(state))
            gs[1, at] = grad * qkv[which, 2, at, part]
            gs[2, at] = grad * qkv[which, 1, at, part]
            if a:
                state = [state[n] * decay[n] for n in range(poles)]

        for j in range(3):
            reach = (taps + 1) // 2
            odd_count = taps // 2

            def behind(a):
                return ps[j, pl.ds(SUB + a, SUB, stride=run), :]

            def own_rows(a):
                value = gs[j, SUB * a : SUB * a + SUB]
                return value if a < own else jnp.where(inside, value, 0.0)

            evens = [behind(-2 * k) for k in range(1, reach)]
            odds = [behind(1 - 2 * k) for k in range(1, reach)]
            pairs = [evens[k] + odds[k] for k in range(reach - 1)]
            sums_of = [[None] * reach for _ in range(3)]

            def collect(kind, grad, values, count):
                for k in range(count):
                    term = grad * values[k]
                    so_far = sums_of[kind][k]
                    sums_of[kind][k] = term if so_far is None else so_far + term

            previous = None
            for a in range(0, run, 2):
                current = own_rows(a)
                collect(1, current if previous is None else current - previous, odds, odd_count)
                evens = [behind(a)] + evens[: reach - 1]
                if a + 1 < run:
                    previous = own_rows(a + 1)
                    odds = [behind(a + 1)] + odds[: reach - 1]
                    pairs = [evens[0] + odds[0]] + pairs[: reach - 1]
                    collect(0, current - previous, evens, reach)
                    collect(2, previous, pairs, reach)
                else:
                    collect(0, current, evens, reach)
            sums_of = [sums_of[i % 2][i // 2] + sums_of[2][i // 2] for i in range(taps)]
            extra = [skip_sum[which, :, part]] + [jnp.zeros((SUB, LANES), F32)] * (SUB - taps)
            extra = extra[: SUB - taps] if j == 0 else extra[1 : SUB - taps + 1]
            sums[piece, j * SUB : j * SUB + SUB, spot] = folded(sums_of + extra)

        @pl.when(pl.program_id(0) < here)
        def _():
            for j in range(3):
                tap = [spread(filt[j, i : i + 1, lanes]) for i in range(taps)]
                back_conv(lambda a: gs[j, SUB * a : SUB * a + SUB], tap, run, os)
                grad_p[j, :, lanes] = os[0:rows].astype(BF16)

        @pl.when(pl.program_id(0) >= here)
        def _():
            for j in range(3):
                later[which, j, :, part] = gs[j]

        return carry

    lax.fori_loop(0, p.shape[2] // LANES, tile, 0)


def shifted(value, axis, steps):
    count = lax.axis_size(axis)
    first, last = (max(0, -steps), min(count, count - steps))
    return lax.ppermute(value, axis, [(source, source + steps) for source in range(first, last)])


def swapped(value):
    count = lax.axis_size("ctx")
    return lax.ppermute(value, "ctx", [(s, s ^ 1) for s in range(count)])


def joined(ends, f_all):
    core = lax.rem(lax.axis_index("ctx"), 2)
    half = ends.shape[1] // 2
    other = swapped(ends)
    first = core == 0
    mine = lax.dynamic_slice_in_dim(ends, core * half, half, 1)
    theirs = lax.dynamic_slice_in_dim(other, core * half, half, 1)
    one, two = jnp.where(first, mine, theirs), jnp.where(first, theirs, mine)
    return other, f_all * one[0] + two[0], one[1] + f_all * two[1]


def paired(value, axis, step, lines=None):
    count = lax.axis_size(axis)
    return lax.ppermute(value, axis, [(source, source ^ step) for source in lines or range(count)])


def scanned(chip_e, chip_a, f_all, beside):
    chips = lax.axis_size("ctx") // 2
    f_chip = f_all * f_all
    if chips == 4:
        odd = lax.rem(lax.axis_index("ctx") // 2, 2) == 1
        sent = jnp.where(odd, chip_a, chip_e)
        first = paired(sent, "ctx", 2)
        kept = beside[0](sent, None)
        first, kept = lax.optimization_barrier((first, kept))
        sent = jnp.where(odd, chip_e, chip_a) + f_chip * first
        near = lax.ppermute(sent, "ctx", [(2, 4), (3, 5), (4, 2), (5, 3)])
        kept = beside[1](sent, kept)
        near, kept = lax.optimization_barrier((near, kept))
        far = lax.ppermute(near, "ctx", [(4, 6), (5, 7), (2, 0), (3, 1)])
        kept = beside[2](near, kept)
        far, kept = lax.optimization_barrier((far, kept))
        far = first + f_chip * far
        return jnp.where(odd, far, near), jnp.where(odd, near, far), kept
    kept = beside[2](chip_e, beside[1](chip_e, beside[0](chip_e, None)))
    before, after = jnp.zeros_like(chip_e), jnp.zeros_like(chip_a)
    reach = 1
    while reach < chips:
        early, late = shifted(chip_e, "ctx", 2 * reach), shifted(chip_a, "ctx", -2 * reach)
        factor = f_chip ** (reach - 1)
        before, after = before + factor * early, after + factor * late
        factor = f_chip**reach
        chip_e, chip_a = chip_e + factor * early, chip_a + factor * late
        reach = 2 * reach
    return before, after, kept


def summed(value, beside, kept):
    dp, parts = lax.axis_index("dp"), lax.axis_size("dp")
    low = lax.rem(lax.axis_index("ctx"), 2) == 0
    half = value.shape[0] // 2
    left, right = value[:half], value[half:]
    value = jnp.where(low, left, right) + swapped(jnp.where(low, right, left))
    size = half // parts
    piece = lambda k: lax.dynamic_slice_in_dim(value, jnp.bitwise_xor(dp, k) * size, size, 0)
    total = piece(0)
    for term in [paired(piece(k), "dp", k) for k in range(1, parts)]:
        total = total + term
    reach = 2
    beside = list(beside)
    while reach < lax.axis_size("ctx"):
        found = paired(total, "ctx", reach)
        if beside:
            kept = beside.pop(0)(total, kept)
            found, kept = lax.optimization_barrier((found, kept))
        total = total + found
        reach = 2 * reach
    for rest in beside:
        kept = rest(total, kept)
    value = jnp.zeros((half,) + value.shape[1:], F32)
    for k in range(parts):
        term = paired(total, "dp", k) if k else total
        value = lax.dynamic_update_slice_in_dim(value, term, jnp.bitwise_xor(dp, k) * size, 0)
    other = swapped(value)
    value = jnp.concatenate([jnp.where(low, value, other), jnp.where(low, other, value)], axis=0)
    return value, kept


def local(projected, short_filter, residues, decay_rates, skip_gain, cotangent):
    rows = projected.shape[1]
    channels = projected.shape[3]
    taps = short_filter.shape[1]
    groups, poles = residues.shape
    width = channels // groups
    run = (rows + SUB) // SUB
    held = rows + SUB
    p = projected[0].transpose(1, 0, 2)
    u = cotangent[0]
    core = lax.rem(lax.axis_index("ctx"), 2)

    def edge(last):
        start = jnp.where(last, rows - SUB, 0)
        cut = lambda value, axis: lax.dynamic_slice_in_dim(value, start, SUB, axis)
        return jnp.concatenate([cut(p, 1), cut(u, 0)[None]], axis=0)

    devices = lax.axis_size("ctx")
    across = [(k, k + 1) for k in range(1, devices - 1, 2)]
    across = across + [(target, source) for source, target in across]
    hx = lax.ppermute(edge(core == 1), "ctx", across)
    hi = swapped(edge(core == 0))

    rate = decay_rates.T
    weight = residues.T
    sub = np.arange(SUB)
    powers = np.stack([run * (7 - sub) - SUB, run * sub, 1 + run * sub, rows - run * (sub + 1) + 1])
    table = jnp.exp(-rate[None, :, None, :] * powers.astype(np.float32)[:, None, :, None])
    we, wb = table[0], table[1]
    cz, cy = weight[:, None, :] * table[2], weight[:, None, :] * table[3]
    f1 = jnp.exp(-rate)
    f_all = jnp.exp(-rate * rows)
    steps = np.array([1, run, 2 * run, 4 * run], np.float32)
    factor = jnp.exp(-rate[None] * steps[:, None, None])
    factor = jnp.concatenate([weight[None] * factor[:1], factor[1:]], axis=0)
    reach = np.array([1, 1, 2, 4])[:, None]
    down, up = sub[None] >= reach, sub[None] < SUB - reach
    join_e = jnp.where(down[:, None, :, None], factor[:, :, None, :], 0.0)
    join_a = jnp.where(up[:, None, :, None], factor[:, :, None, :], 0.0)
    close = np.arange(-taps, run).astype(np.float32)
    near = jnp.sum(weight[:, None, :] * jnp.exp(-rate[:, None, :] * close[None, :, None]), axis=0)

    each = 1

    def by_w(*shape):
        axis = len(shape)
        return pl.BlockSpec(shape + (each * groups,), lambda w: (0,) * axis + (w,))

    def fixed(value):
        return pl.BlockSpec(
            value.shape, lambda w: (0,) * value.ndim, pipeline_mode=pl.Buffered(1)
        )

    params = pltpu.CompilerParams(vmem_limit_bytes=48 * 1024 * 1024)
    shape_of = jax.ShapeDtypeStruct
    ends_spec = pl.BlockSpec((2, each, poles, groups), lambda w: (0, w, 0, 0))
    halved = pl.BlockSpec(
        (2, each, poles, groups), lambda w: (0, lax.rem(w, width // each // 2), 0, 0)
    )
    early = (hx, near, join_e, join_a, cz, cy, f_all)
    hx, near, join_e, join_a, cz, cy, f_all = lax.optimization_barrier(early)
    state_shape = shape_of((width, poles, SUB, groups), F32)
    pair_shape = shape_of((width, 2, held, groups), F32)

    def by_block(*shape, count=each, first=0):
        return pl.BlockSpec((count,) + shape, lambda w: (w + first,) + (0,) * len(shape))

    state_spec = by_block(poles, SUB, groups)
    qkv, xg, blocks_e, blocks_a, ends = pl.pallas_call(
        states_kernel,
        grid=(width // each,),
        in_specs=[
            pl.BlockSpec(memory_space=pltpu.SMEM),
            by_w(3, rows), by_w(4, SUB), by_w(4, SUB), by_w(rows), by_w(3, taps),
            fixed(f1), fixed(we), fixed(wb),
        ],
        out_specs=[
            by_block(3, held, groups), by_block(2, held, groups), state_spec, state_spec,
            ends_spec,
        ],
        out_shape=[
            shape_of((width, 3, held, groups), F32), pair_shape,
            state_shape, state_shape, shape_of((2, width, poles, groups), F32),
        ],
        scratch_shapes=[pltpu.VMEM((4, held + SUB, LANES), F32)],
        compiler_params=params,
        name="states",
    )(core[None], p, hx, hi, u, short_filter, f1, we, wb)

    many = 2 if width % 2 == 0 else 1

    def blocks(first, last):
        place = {"count": many, "first": first}
        states, pairs = by_block(poles, SUB, groups, **place), by_block(2, held, groups, **place)

        def call(sent, kept):
            close, _ = lax.optimization_barrier((near, sent))
            held_before = kept or (xg, blocks_e, blocks_a)
            out = pl.pallas_call(
                blocks_kernel,
                grid=(last - first,),
                in_specs=[
                    pairs, states, states, fixed(near),
                    pl.BlockSpec((1, many * groups), lambda w: (0, w + first)),
                    fixed(join_e), fixed(join_a),
                ],
                out_specs=[pairs, states, states, by_block(SUB, groups, count=many)],
                out_shape=[
                    pair_shape, state_shape, state_shape,
                    shape_of(((last - first) * many, SUB, groups), F32),
                ],
                input_output_aliases={0: 0, 1: 1, 2: 2},
                compiler_params=params,
                cost_estimate=pl.CostEstimate(
                    flops=60 * rows * channels, bytes_accessed=35 * 2**20, transcendentals=0
                ),
                name="blocks",
            )(*held_before[:3], close, skip_gain[None], join_e, join_a)
            return [*out[:3], jnp.concatenate([*held_before[3:], out[3]], axis=0)]

        return call

    steps = width // many
    cuts = (0, (3 * steps) // 8, (5 * steps) // 8, steps)
    other, chip_e, chip_a = joined(ends, f_all)
    before, after, (conv, from_e, from_a, skip_sum) = scanned(
        chip_e, chip_a, f_all, [blocks(cuts[k], cuts[k + 1]) for k in range(3)]
    )
    both = jnp.stack([before, after])
    found = swapped(both)

    count = 3 * SUB
    split = 2 if groups % (2 * LANES) == 0 else 1
    scratch = [
        pltpu.VMEM((3, held + SUB, LANES), F32),
        pltpu.VMEM((held, LANES), F32),
        pltpu.VMEM((3, held, LANES), F32),
        pltpu.VMEM((held, LANES), F32),
        pltpu.VMEM((2, poles, LANES), F32),
    ]
    here = width // 2
    output, grad_p, sums, later = pl.pallas_call(
        functools.partial(final_kernel, here),
        grid=(width // each,),
        in_specs=[
            pl.BlockSpec(memory_space=pltpu.SMEM),
            by_w(3, rows), by_w(4, SUB), by_w(4, SUB), by_w(rows),
            by_block(3, held, groups), by_block(2, held, groups), state_spec, state_spec,
            by_block(SUB, groups), halved, halved, ends_spec,
            by_w(3, taps), fixed(f1), fixed(f_all), fixed(cz), fixed(cy),
        ],
        out_specs=[
            by_w(rows),
            pl.BlockSpec((3, rows, groups), lambda w: (0, 0, jnp.minimum(w, here - 1))),
            pl.BlockSpec((each * split, count, groups // split), lambda w: (w, 0, 0)),
            pl.BlockSpec((1, 3, held, groups), lambda w: (jnp.maximum(w - here, 0), 0, 0, 0)),
        ],
        out_shape=[
            shape_of((rows, channels), BF16),
            shape_of((3, rows, channels), BF16),
            shape_of((width * split, count, groups // split), F32),
            shape_of((width - here, 3, held, groups), F32),
        ],
        scratch_shapes=scratch,
        compiler_params=params,
        name="final",
    )(
        core[None], p, hx, hi, u, qkv, conv, from_e, from_a, skip_sum, both, found, other, short_filter,
        f1, f_all, cz, cy,
    )

    def rest(first, last):
        def call(sent, filled):
            tap, _ = lax.optimization_barrier((short_filter, sent))
            return pl.pallas_call(
                later_kernel,
                grid=(last - first,),
                in_specs=[
                    pl.BlockSpec((1, 3, held, groups), lambda w: (w + first, 0, 0, 0)),
                    pl.BlockSpec((3, taps, groups), lambda w: (0, 0, w + first + here)),
                    pl.BlockSpec(memory_space=pl.ANY),
                ],
                out_specs=pl.BlockSpec((3, rows, groups), lambda w: (0, 0, w + first + here)),
                out_shape=shape_of((3, rows, channels), BF16),
                input_output_aliases={2: 0},
                scratch_shapes=[pltpu.VMEM((held, LANES), F32)],
                compiler_params=params,
                cost_estimate=pl.CostEstimate(
                    flops=40 * rows * channels // 4, bytes_accessed=5 * 2**20, transcendentals=0
                ),
                name="later",
            )(later, tap, filled)

        return call

    middle = (width - here) // 2
    total, grad_p = summed(sums, (rest(0, middle), rest(middle, width - here)), grad_p)
    total = total.transpose(1, 0, 2).reshape(3, SUB, channels)
    grad_short, grad_skip = total[:, :taps], total[0, taps]
    return output[None], grad_p.transpose(1, 0, 2)[None], grad_short, grad_skip


def solution(mesh):
    placed = (P("dp", "ctx", None, None), P(), P(), P(), P(), P("dp", "ctx", None))
    return jax.shard_map(
        local,
        mesh=mesh,
        in_specs=placed,
        out_specs=(P("dp", "ctx", None), P("dp", "ctx", None, None), P(), P()),
        check_vma=False,
    )
```

```python
import functools

import jax
import jax.numpy as jnp
import numpy as np
from jax import lax
from jax.experimental import pallas as pl
from jax.experimental.pallas import tpu as pltpu
from jax.sharding import PartitionSpec as P

LANES = 128
SUB = 8
F32 = jnp.float32
BF16 = jnp.bfloat16


def spread(row):
    return jnp.broadcast_to(row, (SUB, LANES))


def added(terms):
    while len(terms) > 1:
        pairs = [terms[k] + terms[k + 1] for k in range(0, len(terms) - 1, 2)]
        terms = pairs + terms[len(terms) - len(terms) % 2 :]
    return terms[0]


def folded(values):
    row = lax.broadcasted_iota(jnp.int32, (SUB, LANES), 0)
    upper = row < 4
    values = [
        jnp.where(upper, values[n], values[n + 4])
        + pltpu.roll(jnp.where(upper, values[n + 4], values[n]), 4, 0)
        for n in range(4)
    ]
    for step in (2, 1):
        even = (row // step) % 2 == 0
        values = [
            jnp.where(
                even,
                values[n] + pltpu.roll(values[n], SUB - step, 0),
                values[n + step] + pltpu.roll(values[n + step], step, 0),
            )
            for n in range(step)
        ]
    return values[0]


def phases(tap):
    even, odd = tap[0::2], tap[1::2]
    both = [even[k] + odd[k] if k < len(odd) else even[k] for k in range(len(even))]
    return even, odd, both


def weighted(tap, values):
    return added([tap[k] * values[k] for k in range(len(tap))])


def tap_sums(row, tap, run):
    even, odd, both = phases(tap)
    reach = len(even)
    evens = [row(-2 * k) for k in range(1, reach)]
    odds = [row(1 - 2 * k) for k in range(1, reach)]
    pairs = [evens[k] + odds[k] for k in range(reach - 1)]
    before = weighted(odd, odds)
    for a in range(0, run, 2):
        evens = [row(a)] + evens[: reach - 1]
        first = weighted(even, evens)
        yield first + before
        if a + 1 < run:
            odds = [row(a + 1)] + odds[: reach - 1]
            pairs = [evens[0] + odds[0]] + pairs[: reach - 1]
            before = weighted(odd, odds)
            yield weighted(both, pairs) - first - before


def states_kernel(core, p, hx, hi, u, filt, f1, we, wb, kv, xg, blocks_e, blocks_a, ends, xs):
    rows = p.shape[1]
    run = (rows + SUB) // SUB
    taps = filt.shape[1]
    poles, groups = f1.shape
    own = rows - run * (SUB - 1)
    tiles = groups // LANES
    first = core[0] == 0

    def tile(lt, carry):
        lanes = pl.ds(pl.multiple_of(lt * LANES, LANES), LANES)
        part = pl.ds(pl.multiple_of(lax.rem(lt, tiles) * LANES, LANES), LANES)
        which = lt // tiles
        inside = lax.broadcasted_iota(jnp.int32, (SUB, LANES), 0) < SUB - 1
        for j in range(3):
            across, within = hx[j, :, lanes].astype(F32), hi[j, :, lanes].astype(F32)
            xs[j, 0:SUB] = jnp.where(first, across, within)
            xs[j, SUB : SUB + rows] = p[j, :, lanes].astype(F32)
            xs[j, SUB + rows :] = jnp.where(first, within, across)
        xs[3, SUB : SUB + rows] = u[:, lanes].astype(F32)
        across, within = hx[3, :, lanes].astype(F32), hi[3, :, lanes].astype(F32)
        xs[3, SUB + rows :] = jnp.where(first, within, across)

        def mixed(j):
            tap = [spread(filt[j, i : i + 1, lanes]) for i in range(taps)]
            return tap_sums(lambda a: xs[j, pl.ds(SUB + a, SUB, stride=run), :], tap, run)

        decay = [spread(f1[n : n + 1, part]) for n in range(poles)]
        for j in (1, 2, 0):
            for a, total in enumerate(mixed(j)):
                at = slice(SUB * a, SUB * a + SUB)
                if j > 0:
                    kv[which, j - 1, at, part] = total
                if j == 2:
                    xg[which, 0, at, part] = kv[which, 0, at, part] * total
                if j == 0:
                    xg[which, 1, at, part] = xs[3, pl.ds(SUB + a, SUB, stride=run), :] * total
        for side, order, weight, blocks in (
            (0, range(run), we, blocks_e),
            (1, range(run - 1, -1, -1), wb, blocks_a),
        ):
            state = None
            for a in order:
                x = xg[which, side, SUB * a : SUB * a + SUB, part]
                if a >= own:
                    x = jnp.where(inside, x, 0.0)
                state = [x] * poles if state is None else [decay[n] * state[n] + x for n in range(poles)]
            for n in range(poles):
                blocks[which, n, :, part] = state[n]
            state = [state[n] * weight[n, :, part] for n in range(poles)]
            for n in range(0, poles, SUB):
                ends[side, which, n : n + SUB, part] = folded(state[n : n + SUB])
        return carry

    lax.fori_loop(0, p.shape[2] // LANES, tile, 0)


def blocks_kernel(
    xg, blocks_e, blocks_a, near, skip, join_e, join_a, conv, from_e, from_a, skip_sum
):
    run = xg.shape[2] // SUB
    rows = xg.shape[2] - SUB
    taps = near.shape[0] - run
    poles, groups = blocks_e.shape[1], near.shape[1]
    own = rows - run * (SUB - 1)
    tiles = groups // LANES

    def tile(lt, carry):
        lanes = pl.ds(pl.multiple_of(lt * LANES, LANES), LANES)
        part = pl.ds(pl.multiple_of(lax.rem(lt, tiles) * LANES, LANES), LANES)
        which = lt // tiles
        inside = lax.broadcasted_iota(jnp.int32, (SUB, LANES), 0) < SUB - 1
        gain = spread(skip[0:1, lanes])
        lag = [spread(near[taps + m : taps + m + 1, part]) for m in range(run)]
        lag[0] = lag[0] + gain
        x = [xg[which, 0, SUB * a : SUB * a + SUB, part] for a in range(run)]
        for a in range(run):
            conv[which, 0, SUB * a : SUB * a + SUB, part] = added(
                [lag[m] * x[a - m] for m in range(a + 1)]
            )
        gated = x
        x = [xg[which, 1, SUB * a : SUB * a + SUB, part] for a in range(run)]
        masked = [x[a] if a < own else jnp.where(inside, x[a], 0.0) for a in range(run)]
        skip_sum[which, :, part] = added([masked[a] * gated[a] for a in range(run)])
        past = [jnp.where(inside, 0.0, gain)] + [
            jnp.where(inside, 0.0, -spread(near[taps - m : taps - m + 1, part]))
            for m in range(1, taps - 1)
        ]
        for a in range(run):
            terms = [lag[m] * masked[a + m] for m in range(run - a)]
            if own <= a < own + taps - 1:
                terms = terms + [past[m] * x[a - m] for m in range(a - own + 1)]
            conv[which, 1, SUB * a : SUB * a + SUB, part] = added(terms)
        for n in range(poles):
            value = pltpu.roll(blocks_e[which, n, :, part], 1, 0) * join_e[0, n, :, part]
            for k, step in ((1, 1), (2, 2), (3, 4)):
                value = value + pltpu.roll(value, step, 0) * join_e[k, n, :, part]
            from_e[which, n, :, part] = value
            value = pltpu.roll(blocks_a[which, n, :, part], SUB - 1, 0) * join_a[0, n, :, part]
            for k, step in ((1, 1), (2, 2), (3, 4)):
                value = value + pltpu.roll(value, SUB - step, 0) * join_a[k, n, :, part]
            from_a[which, n, :, part] = value
        return carry

    lax.fori_loop(0, xg.shape[0] * tiles, tile, 0)


def final_kernel(
    core, p, hx, hi, u, kv, conv, from_e, from_a, skip_sum, both, found, other, filt, f1, f_all, cz, cy,
    output, grad_p, sums, ps, us, gs, os, es,
):
    rows = p.shape[1]
    run = (rows + SUB) // SUB
    taps = filt.shape[1]
    poles, groups = f1.shape
    own = rows - run * (SUB - 1)
    tiles = groups // LANES
    first = core[0] == 0
    halves = pl.num_programs(0) // 2
    kept = (pl.program_id(0) < halves) == first
    cut = sums.shape[2] // LANES

    def tile(lt, carry):
        lanes = pl.ds(pl.multiple_of(lt * LANES, LANES), LANES)
        part = pl.ds(pl.multiple_of(lax.rem(lt, tiles) * LANES, LANES), LANES)
        which = lt // tiles
        piece = lt // cut
        spot = pl.ds(pl.multiple_of(lax.rem(lt, cut) * LANES, LANES), LANES)
        inside = lax.broadcasted_iota(jnp.int32, (SUB, LANES), 0) < SUB - 1
        for side in range(2):
            far = jnp.where(kept, both[side, which, :, part], found[side, which, :, part])
            close = other[side, which, :, part] + f_all[:, part] * far
            es[side] = jnp.where(first == (side == 0), far, close)
        for j in range(3):
            across, within = hx[j, :, lanes].astype(F32), hi[j, :, lanes].astype(F32)
            ps[j, 0:SUB] = jnp.where(first, across, within)
            ps[j, SUB : SUB + rows] = p[j, :, lanes].astype(F32)
            ps[j, SUB + rows :] = jnp.where(first, within, across)
        us[0:rows] = u[:, lanes].astype(F32)
        across, within = hx[3, :, lanes].astype(F32), hi[3, :, lanes].astype(F32)
        us[rows:] = jnp.where(first, within, across)
        decay = [spread(f1[n : n + 1, part]) for n in range(poles)]

        state = [
            from_e[which, n, :, part] + cz[n, :, part] * spread(es[0, n : n + 1])
            for n in range(poles)
        ]
        tap = [spread(filt[0, i : i + 1, lanes]) for i in range(taps)]
        queries = tap_sums(lambda a: ps[0, pl.ds(SUB + a, SUB, stride=run), :], tap, run)
        for a in range(run):
            at = slice(SUB * a, SUB * a + SUB)
            query, upstream = next(queries), us[pl.ds(a, SUB, stride=run), :]
            filtered = conv[which, 0, at, part] + added(list(state))
            os[pl.ds(a, SUB, stride=run), :] = query * filtered
            gs[0, at] = upstream * filtered
            if a + 1 < run:
                state = [state[n] * decay[n] for n in range(poles)]
        output[:, lanes] = os[0:rows].astype(BF16)

        state = [
            from_a[which, n, :, part] + cy[n, :, part] * spread(es[1, n : n + 1])
            for n in range(poles)
        ]
        for a in range(run - 1, -1, -1):
            at = slice(SUB * a, SUB * a + SUB)
            grad = conv[which, 1, at, part] + added(list(state))
            gs[1, at] = grad * kv[which, 1, at, part]
            gs[2, at] = grad * kv[which, 0, at, part]
            if a:
                state = [state[n] * decay[n] for n in range(poles)]

        for j in range(3):
            even, odd, paired_taps = phases([spread(filt[j, i : i + 1, lanes]) for i in range(taps)])
            reach = len(even)
            grads = [gs[j, SUB * a : SUB * a + SUB] for a in range(taps - 1)]
            beyond = [pltpu.roll(value, SUB - 1, 0) for value in grads]

            def ahead(a):
                return gs[j, SUB * a : SUB * a + SUB] if a < run else beyond[a - run]

            def behind(a):
                return ps[j, pl.ds(SUB + a, SUB, stride=run), :]

            def own_rows(a):
                return grads[a] if a < own else jnp.where(inside, grads[a], 0.0)

            grads = {a: grads[a] for a in range(taps - 1)}
            joint = {k: grads[2 * k + 1] + grads[2 * k + 2] for k in range((taps - 3) // 2)}
            leading = weighted(even, [grads[2 * k] if 2 * k in grads else ahead(2 * k) for k in range(reach)])
            evens = [behind(-2 * k) for k in range(1, reach)]
            odds = [behind(1 - 2 * k) for k in range(1, reach)]
            pairs = [evens[k] + odds[k] for k in range(reach - 1)]
            sums_of = [[None] * reach for _ in range(3)]

            def collect(kind, grad, values, count):
                for k in range(count):
                    term = grad * values[k]
                    so_far = sums_of[kind][k]
                    sums_of[kind][k] = term if so_far is None else so_far + term

            previous = None
            for a in range(0, run, 2):
                for c in range(a, a + 2 * reach + 1):
                    if c not in grads and c < run + taps - 1:
                        grads[c] = ahead(c)
                here = own_rows(a)
                collect(1, here if previous is None else here - previous, odds, len(odd))
                second = weighted(odd, [grads[a + 2 * k + 1] for k in range(len(odd))])
                os[pl.ds(a, SUB, stride=run), :] = leading + second
                evens = [behind(a)] + evens[: reach - 1]
                if a + 1 < run:
                    previous = own_rows(a + 1)
                    for k in range(a // 2, a // 2 + reach):
                        if k not in joint:
                            joint[k] = grads[2 * k + 1] + grads[2 * k + 2]
                    following = weighted(even, [grads[a + 2 + 2 * k] for k in range(reach)])
                    total = weighted(paired_taps, [joint[a // 2 + k] for k in range(reach)])
                    os[pl.ds(a + 1, SUB, stride=run), :] = total - following - second
                    leading = following
                    odds = [behind(a + 1)] + odds[: reach - 1]
                    pairs = [evens[0] + odds[0]] + pairs[: reach - 1]
                    collect(0, here - previous, evens, reach)
                    collect(2, previous, pairs, reach)
                else:
                    collect(0, here, evens, reach)
            sums_of = [sums_of[i % 2][i // 2] + sums_of[2][i // 2] for i in range(taps)]
            grad_p[j, :, lanes] = os[0:rows].astype(BF16)
            extra = [skip_sum[which, :, part]] + [jnp.zeros((SUB, LANES), F32)] * (SUB - taps)
            extra = extra[: SUB - taps] if j == 0 else extra[1 : SUB - taps + 1]
            sums[piece, j * SUB : j * SUB + SUB, spot] = folded(sums_of + extra)
        return carry

    lax.fori_loop(0, p.shape[2] // LANES, tile, 0)


def shifted(value, axis, steps):
    count = lax.axis_size(axis)
    first, last = (max(0, -steps), min(count, count - steps))
    return lax.ppermute(value, axis, [(source, source + steps) for source in range(first, last)])


def swapped(value):
    count = lax.axis_size("ctx")
    return lax.ppermute(value, "ctx", [(s, s ^ 1) for s in range(count)])


def joined(ends, f_all):
    core = lax.rem(lax.axis_index("ctx"), 2)
    half = ends.shape[1] // 2
    other = swapped(ends)
    first = core == 0
    mine = lax.dynamic_slice_in_dim(ends, core * half, half, 1)
    theirs = lax.dynamic_slice_in_dim(other, core * half, half, 1)
    one, two = jnp.where(first, mine, theirs), jnp.where(first, theirs, mine)
    return other, f_all * one[0] + two[0], one[1] + f_all * two[1]


def paired(value, axis, step, lines=None):
    count = lax.axis_size(axis)
    return lax.ppermute(value, axis, [(source, source ^ step) for source in lines or range(count)])


def scanned(chip_e, chip_a, f_all, beside):
    chips = lax.axis_size("ctx") // 2
    f_chip = f_all * f_all
    if chips == 4:
        odd = lax.rem(lax.axis_index("ctx") // 2, 2) == 1
        sent = jnp.where(odd, chip_a, chip_e)
        first = paired(sent, "ctx", 2)
        kept = beside[0](sent, None)
        first, kept = lax.optimization_barrier((first, kept))
        sent = jnp.where(odd, chip_e, chip_a) + f_chip * first
        near = lax.ppermute(sent, "ctx", [(2, 4), (3, 5), (4, 2), (5, 3)])
        kept = beside[1](sent, kept)
        near, kept = lax.optimization_barrier((near, kept))
        far = lax.ppermute(near, "ctx", [(4, 6), (5, 7), (2, 0), (3, 1)])
        kept = beside[2](near, kept)
        far, kept = lax.optimization_barrier((far, kept))
        far = first + f_chip * far
        return jnp.where(odd, far, near), jnp.where(odd, near, far), kept
    kept = beside[2](chip_e, beside[1](chip_e, beside[0](chip_e, None)))
    before, after = jnp.zeros_like(chip_e), jnp.zeros_like(chip_a)
    reach = 1
    while reach < chips:
        early, late = shifted(chip_e, "ctx", 2 * reach), shifted(chip_a, "ctx", -2 * reach)
        factor = f_chip ** (reach - 1)
        before, after = before + factor * early, after + factor * late
        factor = f_chip**reach
        chip_e, chip_a = chip_e + factor * early, chip_a + factor * late
        reach = 2 * reach
    return before, after, kept


def summed(value):
    dp, parts = lax.axis_index("dp"), lax.axis_size("dp")
    low = lax.rem(lax.axis_index("ctx"), 2) == 0
    half = value.shape[0] // 2
    left, right = value[:half], value[half:]
    value = jnp.where(low, left, right) + swapped(jnp.where(low, right, left))
    size = half // parts
    piece = lambda k: lax.dynamic_slice_in_dim(value, jnp.bitwise_xor(dp, k) * size, size, 0)
    total = piece(0)
    for term in [paired(piece(k), "dp", k) for k in range(1, parts)]:
        total = total + term
    reach = 2
    while reach < lax.axis_size("ctx"):
        total = total + paired(total, "ctx", reach)
        reach = 2 * reach
    value = jnp.zeros((half,) + value.shape[1:], F32)
    for k in range(parts):
        term = paired(total, "dp", k) if k else total
        value = lax.dynamic_update_slice_in_dim(value, term, jnp.bitwise_xor(dp, k) * size, 0)
    other = swapped(value)
    return jnp.concatenate([jnp.where(low, value, other), jnp.where(low, other, value)], axis=0)


def local(projected, short_filter, residues, decay_rates, skip_gain, cotangent):
    rows = projected.shape[1]
    channels = projected.shape[3]
    taps = short_filter.shape[1]
    groups, poles = residues.shape
    width = channels // groups
    run = (rows + SUB) // SUB
    held = rows + SUB
    p = projected[0].transpose(1, 0, 2)
    u = cotangent[0]
    core = lax.rem(lax.axis_index("ctx"), 2)

    def edge(last):
        start = jnp.where(last, rows - SUB, 0)
        cut = lambda value, axis: lax.dynamic_slice_in_dim(value, start, SUB, axis)
        return jnp.concatenate([cut(p, 1), cut(u, 0)[None]], axis=0)

    devices = lax.axis_size("ctx")
    across = [(k, k + 1) for k in range(1, devices - 1, 2)]
    across = across + [(target, source) for source, target in across]
    hx = lax.ppermute(edge(core == 1), "ctx", across)
    hi = swapped(edge(core == 0))

    rate = decay_rates.T
    weight = residues.T
    sub = np.arange(SUB)
    powers = np.stack([run * (7 - sub) - SUB, run * sub, 1 + run * sub, rows - run * (sub + 1) + 1])
    table = jnp.exp(-rate[None, :, None, :] * powers.astype(np.float32)[:, None, :, None])
    we, wb = table[0], table[1]
    cz, cy = weight[:, None, :] * table[2], weight[:, None, :] * table[3]
    f1 = jnp.exp(-rate)
    f_all = jnp.exp(-rate * rows)
    steps = np.array([1, run, 2 * run, 4 * run], np.float32)
    factor = jnp.exp(-rate[None] * steps[:, None, None])
    factor = jnp.concatenate([weight[None] * factor[:1], factor[1:]], axis=0)
    reach = np.array([1, 1, 2, 4])[:, None]
    down, up = sub[None] >= reach, sub[None] < SUB - reach
    join_e = jnp.where(down[:, None, :, None], factor[:, :, None, :], 0.0)
    join_a = jnp.where(up[:, None, :, None], factor[:, :, None, :], 0.0)
    close = np.arange(-taps, run).astype(np.float32)
    near = jnp.sum(weight[:, None, :] * jnp.exp(-rate[:, None, :] * close[None, :, None]), axis=0)

    each = 1

    def by_w(*shape):
        axis = len(shape)
        return pl.BlockSpec(shape + (each * groups,), lambda w: (0,) * axis + (w,))

    def fixed(value):
        return pl.BlockSpec(
            value.shape, lambda w: (0,) * value.ndim, pipeline_mode=pl.Buffered(1)
        )

    params = pltpu.CompilerParams(vmem_limit_bytes=48 * 1024 * 1024)
    shape_of = jax.ShapeDtypeStruct
    ends_spec = pl.BlockSpec((2, each, poles, groups), lambda w: (0, w, 0, 0))
    halved = pl.BlockSpec(
        (2, each, poles, groups), lambda w: (0, lax.rem(w, width // each // 2), 0, 0)
    )
    early = (hx, near, join_e, join_a, cz, cy, f_all)
    hx, near, join_e, join_a, cz, cy, f_all = lax.optimization_barrier(early)
    state_shape = shape_of((width, poles, SUB, groups), F32)
    pair_shape = shape_of((width, 2, held, groups), F32)

    def by_block(*shape, count=each, first=0):
        return pl.BlockSpec((count,) + shape, lambda w: (w + first,) + (0,) * len(shape))

    state_spec = by_block(poles, SUB, groups)
    kv, xg, blocks_e, blocks_a, ends = pl.pallas_call(
        states_kernel,
        grid=(width // each,),
        in_specs=[
            pl.BlockSpec(memory_space=pltpu.SMEM),
            by_w(3, rows), by_w(4, SUB), by_w(4, SUB), by_w(rows), by_w(3, taps),
            fixed(f1), fixed(we), fixed(wb),
        ],
        out_specs=[
            by_block(2, held, groups), by_block(2, held, groups), state_spec, state_spec,
            ends_spec,
        ],
        out_shape=[
            pair_shape, pair_shape,
            state_shape, state_shape, shape_of((2, width, poles, groups), F32),
        ],
        scratch_shapes=[pltpu.VMEM((4, held + SUB, LANES), F32)],
        compiler_params=params,
        name="states",
    )(core[None], p, hx, hi, u, short_filter, f1, we, wb)

    many = 2 if width % 2 == 0 else 1

    def blocks(first, last):
        place = {"count": many, "first": first}
        states, pairs = by_block(poles, SUB, groups, **place), by_block(2, held, groups, **place)

        def call(sent, kept):
            close, _ = lax.optimization_barrier((near, sent))
            held_before = kept or (xg, blocks_e, blocks_a)
            out = pl.pallas_call(
                blocks_kernel,
                grid=(last - first,),
                in_specs=[
                    pairs, states, states, fixed(near),
                    pl.BlockSpec((1, many * groups), lambda w: (0, w + first)),
                    fixed(join_e), fixed(join_a),
                ],
                out_specs=[pairs, states, states, by_block(SUB, groups, count=many)],
                out_shape=[
                    pair_shape, state_shape, state_shape,
                    shape_of(((last - first) * many, SUB, groups), F32),
                ],
                input_output_aliases={0: 0, 1: 1, 2: 2},
                compiler_params=params,
                cost_estimate=pl.CostEstimate(
                    flops=60 * rows * channels, bytes_accessed=35 * 2**20, transcendentals=0
                ),
                name="blocks",
            )(*held_before[:3], close, skip_gain[None], join_e, join_a)
            return [*out[:3], jnp.concatenate([*held_before[3:], out[3]], axis=0)]

        return call

    steps = width // many
    cuts = (0, (3 * steps) // 8, (5 * steps) // 8, steps)
    other, chip_e, chip_a = joined(ends, f_all)
    before, after, (conv, from_e, from_a, skip_sum) = scanned(
        chip_e, chip_a, f_all, [blocks(cuts[k], cuts[k + 1]) for k in range(3)]
    )
    both = jnp.stack([before, after])
    found = swapped(both)

    count = 3 * SUB
    split = 2 if groups % (2 * LANES) == 0 else 1
    scratch = [
        pltpu.VMEM((3, held + SUB, LANES), F32),
        pltpu.VMEM((held, LANES), F32),
        pltpu.VMEM((3, held, LANES), F32),
        pltpu.VMEM((held, LANES), F32),
        pltpu.VMEM((2, poles, LANES), F32),
    ]
    output, grad_p, sums = pl.pallas_call(
        final_kernel,
        grid=(width // each,),
        in_specs=[
            pl.BlockSpec(memory_space=pltpu.SMEM),
            by_w(3, rows), by_w(4, SUB), by_w(4, SUB), by_w(rows),
            by_block(2, held, groups), by_block(2, held, groups), state_spec, state_spec,
            by_block(SUB, groups), halved, halved, ends_spec,
            by_w(3, taps), fixed(f1), fixed(f_all), fixed(cz), fixed(cy),
        ],
        out_specs=[
            by_w(rows), by_w(3, rows),
            pl.BlockSpec((each * split, count, groups // split), lambda w: (w, 0, 0)),
        ],
        out_shape=[
            shape_of((rows, channels), BF16),
            shape_of((3, rows, channels), BF16),
            shape_of((width * split, count, groups // split), F32),
        ],
        scratch_shapes=scratch,
        compiler_params=params,
        name="final",
    )(
        core[None], p, hx, hi, u, kv, conv, from_e, from_a, skip_sum, both, found, other, short_filter,
        f1, f_all, cz, cy,
    )

    total = summed(sums).transpose(1, 0, 2).reshape(3, SUB, channels)
    grad_short, grad_skip = total[:, :taps], total[0, taps]
    return output[None], grad_p.transpose(1, 0, 2)[None], grad_short, grad_skip


def solution(mesh):
    placed = (P("dp", "ctx", None, None), P(), P(), P(), P(), P("dp", "ctx", None))
    return jax.shard_map(
        local,
        mesh=mesh,
        in_specs=placed,
        out_specs=(P("dp", "ctx", None), P("dp", "ctx", None, None), P(), P()),
        check_vma=False,
    )
```

```python
import functools

import jax
import jax.numpy as jnp
import numpy as np
from jax import lax
from jax.experimental import pallas as pl
from jax.experimental.pallas import tpu as pltpu
from jax.sharding import PartitionSpec as P

LANES = 128
SUB = 8
F32 = jnp.float32
BF16 = jnp.bfloat16


def spread(row):
    return jnp.broadcast_to(row, (SUB, LANES))


def added(terms):
    while len(terms) > 1:
        pairs = [terms[k] + terms[k + 1] for k in range(0, len(terms) - 1, 2)]
        terms = pairs + terms[len(terms) - len(terms) % 2 :]
    return terms[0]


def folded(values):
    row = lax.broadcasted_iota(jnp.int32, (SUB, LANES), 0)
    upper = row < 4
    values = [
        jnp.where(upper, values[n], values[n + 4])
        + pltpu.roll(jnp.where(upper, values[n + 4], values[n]), 4, 0)
        for n in range(4)
    ]
    for step in (2, 1):
        even = (row // step) % 2 == 0
        values = [
            jnp.where(
                even,
                values[n] + pltpu.roll(values[n], SUB - step, 0),
                values[n + step] + pltpu.roll(values[n + step], step, 0),
            )
            for n in range(step)
        ]
    return values[0]


def phases(tap):
    even, odd = tap[0::2], tap[1::2]
    both = [even[k] + odd[k] if k < len(odd) else even[k] for k in range(len(even))]
    return even, odd, both


def weighted(tap, values):
    return added([tap[k] * values[k] for k in range(len(tap))])


def states_kernel(core, p, hx, hi, u, filt, f1, we, wb, qkv, xg, blocks_e, blocks_a, ends, xs):
    rows = p.shape[1]
    run = (rows + SUB) // SUB
    taps = filt.shape[1]
    poles, groups = f1.shape
    own = rows - run * (SUB - 1)
    tiles = groups // LANES
    first = core[0] == 0

    def tile(lt, carry):
        lanes = pl.ds(pl.multiple_of(lt * LANES, LANES), LANES)
        part = pl.ds(pl.multiple_of(lax.rem(lt, tiles) * LANES, LANES), LANES)
        which = lt // tiles
        inside = lax.broadcasted_iota(jnp.int32, (SUB, LANES), 0) < SUB - 1
        for j in range(3):
            across, within = hx[j, :, lanes].astype(F32), hi[j, :, lanes].astype(F32)
            xs[j, 0:SUB] = jnp.where(first, across, within)
            xs[j, SUB : SUB + rows] = p[j, :, lanes].astype(F32)
            xs[j, SUB + rows :] = jnp.where(first, within, across)
        xs[3, SUB : SUB + rows] = u[:, lanes].astype(F32)
        across, within = hx[3, :, lanes].astype(F32), hi[3, :, lanes].astype(F32)
        xs[3, SUB + rows :] = jnp.where(first, within, across)

        def mixed(j):
            even, odd, both = phases([spread(filt[j, i : i + 1, lanes]) for i in range(taps)])
            row = lambda a: xs[j, pl.ds(SUB + a, SUB, stride=run), :]
            reach = len(even)
            evens = [row(-2 * k) for k in range(1, reach)]
            odds = [row(1 - 2 * k) for k in range(1, reach)]
            pairs = [evens[k] + odds[k] for k in range(reach - 1)]
            before = weighted(odd, odds)
            for a in range(0, run, 2):
                evens = [row(a)] + evens[: reach - 1]
                first = weighted(even, evens)
                yield first + before
                if a + 1 < run:
                    odds = [row(a + 1)] + odds[: reach - 1]
                    pairs = [evens[0] + odds[0]] + pairs[: reach - 1]
                    before = weighted(odd, odds)
                    yield weighted(both, pairs) - first - before

        decay = [spread(f1[n : n + 1, part]) for n in range(poles)]
        for j in (1, 2, 0):
            for a, total in enumerate(mixed(j)):
                at = slice(SUB * a, SUB * a + SUB)
                qkv[which, j, at, part] = total
                if j == 2:
                    xg[which, 0, at, part] = qkv[which, 1, at, part] * total
                if j == 0:
                    xg[which, 1, at, part] = xs[3, pl.ds(SUB + a, SUB, stride=run), :] * total
        states = [None, None]
        for step in range(run):
            for side, a in ((0, step), (1, run - 1 - step)):
                x = xg[which, side, SUB * a : SUB * a + SUB, part]
                if a >= own:
                    x = jnp.where(inside, x, 0.0)
                if step == 0:
                    states[side] = [x] * poles
                else:
                    states[side] = [decay[n] * states[side][n] + x for n in range(poles)]
        for side, weight, blocks in ((0, we, blocks_e), (1, wb, blocks_a)):
            state = states[side]
            for n in range(poles):
                blocks[which, n, :, part] = state[n]
            state = [state[n] * weight[n, :, part] for n in range(poles)]
            for n in range(0, poles, SUB):
                ends[side, which, n : n + SUB, part] = folded(state[n : n + SUB])
        return carry

    lax.fori_loop(0, p.shape[2] // LANES, tile, 0)


def blocks_kernel(
    xg, blocks_e, blocks_a, near, skip, join_e, join_a, conv, from_e, from_a, skip_sum
):
    run = xg.shape[2] // SUB
    rows = xg.shape[2] - SUB
    taps = near.shape[0] - run
    poles, groups = blocks_e.shape[1], near.shape[1]
    own = rows - run * (SUB - 1)
    tiles = groups // LANES

    def tile(lt, carry):
        lanes = pl.ds(pl.multiple_of(lt * LANES, LANES), LANES)
        part = pl.ds(pl.multiple_of(lax.rem(lt, tiles) * LANES, LANES), LANES)
        which = lt // tiles
        inside = lax.broadcasted_iota(jnp.int32, (SUB, LANES), 0) < SUB - 1
        gain = spread(skip[0:1, lanes])
        lag = [spread(near[taps + m : taps + m + 1, part]) for m in range(run)]
        lag[0] = lag[0] + gain
        x = [xg[which, 0, SUB * a : SUB * a + SUB, part] for a in range(run)]
        for a in range(run):
            conv[which, 0, SUB * a : SUB * a + SUB, part] = added(
                [lag[m] * x[a - m] for m in range(a + 1)]
            )
        gated = x
        x = [xg[which, 1, SUB * a : SUB * a + SUB, part] for a in range(run)]
        masked = [x[a] if a < own else jnp.where(inside, x[a], 0.0) for a in range(run)]
        skip_sum[which, :, part] = added([masked[a] * gated[a] for a in range(run)])
        past = [jnp.where(inside, 0.0, gain)] + [
            jnp.where(inside, 0.0, -spread(near[taps - m : taps - m + 1, part]))
            for m in range(1, taps - 1)
        ]
        for a in range(run):
            terms = [lag[m] * masked[a + m] for m in range(run - a)]
            if own <= a < own + taps - 1:
                terms = terms + [past[m] * x[a - m] for m in range(a - own + 1)]
            conv[which, 1, SUB * a : SUB * a + SUB, part] = added(terms)
        for n in range(poles):
            value = pltpu.roll(blocks_e[which, n, :, part], 1, 0) * join_e[0, n, :, part]
            for k, step in ((1, 1), (2, 2), (3, 4)):
                value = value + pltpu.roll(value, step, 0) * join_e[k, n, :, part]
            from_e[which, n, :, part] = value
            value = pltpu.roll(blocks_a[which, n, :, part], SUB - 1, 0) * join_a[0, n, :, part]
            for k, step in ((1, 1), (2, 2), (3, 4)):
                value = value + pltpu.roll(value, SUB - step, 0) * join_a[k, n, :, part]
            from_a[which, n, :, part] = value
        return carry

    lax.fori_loop(0, xg.shape[0] * tiles, tile, 0)


def final_kernel(
    core, p, hx, hi, u, qkv, conv, from_e, from_a, skip_sum, both, found, other, filt, f1, f_all, cz, cy,
    output, grad_p, sums, ps, us, gs, os, es,
):
    rows = p.shape[1]
    run = (rows + SUB) // SUB
    taps = filt.shape[1]
    poles, groups = f1.shape
    own = rows - run * (SUB - 1)
    tiles = groups // LANES
    first = core[0] == 0
    halves = pl.num_programs(0) // 2
    kept = (pl.program_id(0) < halves) == first
    cut = sums.shape[2] // LANES

    def tile(lt, carry):
        lanes = pl.ds(pl.multiple_of(lt * LANES, LANES), LANES)
        part = pl.ds(pl.multiple_of(lax.rem(lt, tiles) * LANES, LANES), LANES)
        which = lt // tiles
        piece = lt // cut
        spot = pl.ds(pl.multiple_of(lax.rem(lt, cut) * LANES, LANES), LANES)
        inside = lax.broadcasted_iota(jnp.int32, (SUB, LANES), 0) < SUB - 1
        for side in range(2):
            far = jnp.where(kept, both[side, which, :, part], found[side, which, :, part])
            close = other[side, which, :, part] + f_all[:, part] * far
            es[side] = jnp.where(first == (side == 0), far, close)
        for j in range(3):
            across, within = hx[j, :, lanes].astype(F32), hi[j, :, lanes].astype(F32)
            ps[j, 0:SUB] = jnp.where(first, across, within)
            ps[j, SUB : SUB + rows] = p[j, :, lanes].astype(F32)
            ps[j, SUB + rows :] = jnp.where(first, within, across)
        us[0:rows] = u[:, lanes].astype(F32)
        across, within = hx[3, :, lanes].astype(F32), hi[3, :, lanes].astype(F32)
        us[rows:] = jnp.where(first, within, across)
        decay = [spread(f1[n : n + 1, part]) for n in range(poles)]

        state = [
            from_e[which, n, :, part] + cz[n, :, part] * spread(es[0, n : n + 1])
            for n in range(poles)
        ]
        for a in range(run):
            at = slice(SUB * a, SUB * a + SUB)
            query, upstream = qkv[which, 0, at, part], us[pl.ds(a, SUB, stride=run), :]
            filtered = conv[which, 0, at, part] + added(list(state))
            os[pl.ds(a, SUB, stride=run), :] = query * filtered
            gs[0, at] = upstream * filtered
            if a + 1 < run:
                state = [state[n] * decay[n] for n in range(poles)]
        output[:, lanes] = os[0:rows].astype(BF16)

        state = [
            from_a[which, n, :, part] + cy[n, :, part] * spread(es[1, n : n + 1])
            for n in range(poles)
        ]
        for a in range(run - 1, -1, -1):
            at = slice(SUB * a, SUB * a + SUB)
            grad = conv[which, 1, at, part] + added(list(state))
            gs[1, at] = grad * qkv[which, 2, at, part]
            gs[2, at] = grad * qkv[which, 1, at, part]
            if a:
                state = [state[n] * decay[n] for n in range(poles)]

        for j in range(3):
            even, odd, paired_taps = phases([spread(filt[j, i : i + 1, lanes]) for i in range(taps)])
            reach = len(even)
            grads = [gs[j, SUB * a : SUB * a + SUB] for a in range(taps - 1)]
            beyond = [pltpu.roll(value, SUB - 1, 0) for value in grads]

            def ahead(a):
                return gs[j, SUB * a : SUB * a + SUB] if a < run else beyond[a - run]

            def behind(a):
                return ps[j, pl.ds(SUB + a, SUB, stride=run), :]

            def own_rows(a):
                return grads[a] if a < own else jnp.where(inside, grads[a], 0.0)

            grads = {a: grads[a] for a in range(taps - 1)}
            joint = {k: grads[2 * k + 1] + grads[2 * k + 2] for k in range((taps - 3) // 2)}
            leading = weighted(even, [grads[2 * k] if 2 * k in grads else ahead(2 * k) for k in range(reach)])
            evens = [behind(-2 * k) for k in range(1, reach)]
            odds = [behind(1 - 2 * k) for k in range(1, reach)]
            pairs = [evens[k] + odds[k] for k in range(reach - 1)]
            sums_of = [[None] * reach for _ in range(3)]

            def collect(kind, grad, values, count):
                for k in range(count):
                    term = grad * values[k]
                    so_far = sums_of[kind][k]
                    sums_of[kind][k] = term if so_far is None else so_far + term

            previous = None
            for a in range(0, run, 2):
                for c in range(a, a + 2 * reach + 1):
                    if c not in grads and c < run + taps - 1:
                        grads[c] = ahead(c)
                here = own_rows(a)
                collect(1, here if previous is None else here - previous, odds, len(odd))
                second = weighted(odd, [grads[a + 2 * k + 1] for k in range(len(odd))])
                os[pl.ds(a, SUB, stride=run), :] = leading + second
                evens = [behind(a)] + evens[: reach - 1]
                if a + 1 < run:
                    previous = own_rows(a + 1)
                    for k in range(a // 2, a // 2 + reach):
                        if k not in joint:
                            joint[k] = grads[2 * k + 1] + grads[2 * k + 2]
                    following = weighted(even, [grads[a + 2 + 2 * k] for k in range(reach)])
                    total = weighted(paired_taps, [joint[a // 2 + k] for k in range(reach)])
                    os[pl.ds(a + 1, SUB, stride=run), :] = total - following - second
                    leading = following
                    odds = [behind(a + 1)] + odds[: reach - 1]
                    pairs = [evens[0] + odds[0]] + pairs[: reach - 1]
                    collect(0, here - previous, evens, reach)
                    collect(2, previous, pairs, reach)
                else:
                    collect(0, here, evens, reach)
            sums_of = [sums_of[i % 2][i // 2] + sums_of[2][i // 2] for i in range(taps)]
            grad_p[j, :, lanes] = os[0:rows].astype(BF16)
            extra = [skip_sum[which, :, part]] + [jnp.zeros((SUB, LANES), F32)] * (SUB - taps)
            extra = extra[: SUB - taps] if j == 0 else extra[1 : SUB - taps + 1]
            sums[piece, j * SUB : j * SUB + SUB, spot] = folded(sums_of + extra)
        return carry

    lax.fori_loop(0, p.shape[2] // LANES, tile, 0)


def shifted(value, axis, steps):
    count = lax.axis_size(axis)
    first, last = (max(0, -steps), min(count, count - steps))
    return lax.ppermute(value, axis, [(source, source + steps) for source in range(first, last)])


def swapped(value):
    count = lax.axis_size("ctx")
    return lax.ppermute(value, "ctx", [(s, s ^ 1) for s in range(count)])


def joined(ends, f_all):
    core = lax.rem(lax.axis_index("ctx"), 2)
    half = ends.shape[1] // 2
    other = swapped(ends)
    first = core == 0
    mine = lax.dynamic_slice_in_dim(ends, core * half, half, 1)
    theirs = lax.dynamic_slice_in_dim(other, core * half, half, 1)
    one, two = jnp.where(first, mine, theirs), jnp.where(first, theirs, mine)
    return other, f_all * one[0] + two[0], one[1] + f_all * two[1]


def paired(value, axis, step, lines=None):
    count = lax.axis_size(axis)
    return lax.ppermute(value, axis, [(source, source ^ step) for source in lines or range(count)])


def scanned(chip_e, chip_a, f_all, beside):
    chips = lax.axis_size("ctx") // 2
    f_chip = f_all * f_all
    if chips == 4:
        odd = lax.rem(lax.axis_index("ctx") // 2, 2) == 1
        sent = jnp.where(odd, chip_a, chip_e)
        first = paired(sent, "ctx", 2)
        kept = beside[0](sent, None)
        first, kept = lax.optimization_barrier((first, kept))
        sent = jnp.where(odd, chip_e, chip_a) + f_chip * first
        near = lax.ppermute(sent, "ctx", [(2, 4), (3, 5), (4, 2), (5, 3)])
        kept = beside[1](sent, kept)
        near, kept = lax.optimization_barrier((near, kept))
        far = lax.ppermute(near, "ctx", [(4, 6), (5, 7), (2, 0), (3, 1)])
        kept = beside[2](near, kept)
        far, kept = lax.optimization_barrier((far, kept))
        far = first + f_chip * far
        return jnp.where(odd, far, near), jnp.where(odd, near, far), kept
    kept = beside[2](chip_e, beside[1](chip_e, beside[0](chip_e, None)))
    before, after = jnp.zeros_like(chip_e), jnp.zeros_like(chip_a)
    reach = 1
    while reach < chips:
        early, late = shifted(chip_e, "ctx", 2 * reach), shifted(chip_a, "ctx", -2 * reach)
        factor = f_chip ** (reach - 1)
        before, after = before + factor * early, after + factor * late
        factor = f_chip**reach
        chip_e, chip_a = chip_e + factor * early, chip_a + factor * late
        reach = 2 * reach
    return before, after, kept


def summed(value):
    dp, parts = lax.axis_index("dp"), lax.axis_size("dp")
    low = lax.rem(lax.axis_index("ctx"), 2) == 0
    half = value.shape[0] // 2
    left, right = value[:half], value[half:]
    value = jnp.where(low, left, right) + swapped(jnp.where(low, right, left))
    size = half // parts
    piece = lambda k: lax.dynamic_slice_in_dim(value, jnp.bitwise_xor(dp, k) * size, size, 0)
    total = piece(0)
    for term in [paired(piece(k), "dp", k) for k in range(1, parts)]:
        total = total + term
    reach = 2
    while reach < lax.axis_size("ctx"):
        total = total + paired(total, "ctx", reach)
        reach = 2 * reach
    value = jnp.zeros((half,) + value.shape[1:], F32)
    for k in range(parts):
        term = paired(total, "dp", k) if k else total
        value = lax.dynamic_update_slice_in_dim(value, term, jnp.bitwise_xor(dp, k) * size, 0)
    other = swapped(value)
    return jnp.concatenate([jnp.where(low, value, other), jnp.where(low, other, value)], axis=0)


def local(projected, short_filter, residues, decay_rates, skip_gain, cotangent):
    rows = projected.shape[1]
    channels = projected.shape[3]
    taps = short_filter.shape[1]
    groups, poles = residues.shape
    width = channels // groups
    run = (rows + SUB) // SUB
    held = rows + SUB
    p = projected[0].transpose(1, 0, 2)
    u = cotangent[0]
    core = lax.rem(lax.axis_index("ctx"), 2)

    def edge(last):
        start = jnp.where(last, rows - SUB, 0)
        cut = lambda value, axis: lax.dynamic_slice_in_dim(value, start, SUB, axis)
        return jnp.concatenate([cut(p, 1), cut(u, 0)[None]], axis=0)

    devices = lax.axis_size("ctx")
    across = [(k, k + 1) for k in range(1, devices - 1, 2)]
    across = across + [(target, source) for source, target in across]
    hx = lax.ppermute(edge(core == 1), "ctx", across)
    hi = swapped(edge(core == 0))

    rate = decay_rates.T
    weight = residues.T
    sub = np.arange(SUB)
    powers = np.stack([run * (7 - sub) - SUB, run * sub, 1 + run * sub, rows - run * (sub + 1) + 1])
    table = jnp.exp(-rate[None, :, None, :] * powers.astype(np.float32)[:, None, :, None])
    we, wb = table[0], table[1]
    cz, cy = weight[:, None, :] * table[2], weight[:, None, :] * table[3]
    f1 = jnp.exp(-rate)
    f_all = jnp.exp(-rate * rows)
    steps = np.array([1, run, 2 * run, 4 * run], np.float32)
    factor = jnp.exp(-rate[None] * steps[:, None, None])
    factor = jnp.concatenate([weight[None] * factor[:1], factor[1:]], axis=0)
    reach = np.array([1, 1, 2, 4])[:, None]
    down, up = sub[None] >= reach, sub[None] < SUB - reach
    join_e = jnp.where(down[:, None, :, None], factor[:, :, None, :], 0.0)
    join_a = jnp.where(up[:, None, :, None], factor[:, :, None, :], 0.0)
    close = np.arange(-taps, run).astype(np.float32)
    near = jnp.sum(weight[:, None, :] * jnp.exp(-rate[:, None, :] * close[None, :, None]), axis=0)

    each = 1

    def by_w(*shape):
        axis = len(shape)
        return pl.BlockSpec(shape + (each * groups,), lambda w: (0,) * axis + (w,))

    def fixed(value):
        return pl.BlockSpec(
            value.shape, lambda w: (0,) * value.ndim, pipeline_mode=pl.Buffered(1)
        )

    params = pltpu.CompilerParams(vmem_limit_bytes=48 * 1024 * 1024)
    shape_of = jax.ShapeDtypeStruct
    ends_spec = pl.BlockSpec((2, each, poles, groups), lambda w: (0, w, 0, 0))
    halved = pl.BlockSpec(
        (2, each, poles, groups), lambda w: (0, lax.rem(w, width // each // 2), 0, 0)
    )
    early = (hx, near, join_e, join_a, cz, cy, f_all)
    hx, near, join_e, join_a, cz, cy, f_all = lax.optimization_barrier(early)
    state_shape = shape_of((width, poles, SUB, groups), F32)
    pair_shape = shape_of((width, 2, held, groups), F32)

    def by_block(*shape, count=each, first=0):
        return pl.BlockSpec((count,) + shape, lambda w: (w + first,) + (0,) * len(shape))

    state_spec = by_block(poles, SUB, groups)
    qkv, xg, blocks_e, blocks_a, ends = pl.pallas_call(
        states_kernel,
        grid=(width // each,),
        in_specs=[
            pl.BlockSpec(memory_space=pltpu.SMEM),
            by_w(3, rows), by_w(4, SUB), by_w(4, SUB), by_w(rows), by_w(3, taps),
            fixed(f1), fixed(we), fixed(wb),
        ],
        out_specs=[
            by_block(3, held, groups), by_block(2, held, groups), state_spec, state_spec,
            ends_spec,
        ],
        out_shape=[
            shape_of((width, 3, held, groups), F32), pair_shape,
            state_shape, state_shape, shape_of((2, width, poles, groups), F32),
        ],
        scratch_shapes=[pltpu.VMEM((4, held + SUB, LANES), F32)],
        compiler_params=params,
        name="states",
    )(core[None], p, hx, hi, u, short_filter, f1, we, wb)

    many = 2 if width % 2 == 0 else 1

    def blocks(first, last):
        place = {"count": many, "first": first}
        states, pairs = by_block(poles, SUB, groups, **place), by_block(2, held, groups, **place)

        def call(sent, kept):
            close, _ = lax.optimization_barrier((near, sent))
            held_before = kept or (xg, blocks_e, blocks_a)
            out = pl.pallas_call(
                blocks_kernel,
                grid=(last - first,),
                in_specs=[
                    pairs, states, states, fixed(near),
                    pl.BlockSpec((1, many * groups), lambda w: (0, w + first)),
                    fixed(join_e), fixed(join_a),
                ],
                out_specs=[pairs, states, states, by_block(SUB, groups, count=many)],
                out_shape=[
                    pair_shape, state_shape, state_shape,
                    shape_of(((last - first) * many, SUB, groups), F32),
                ],
                input_output_aliases={0: 0, 1: 1, 2: 2},
                compiler_params=params,
                cost_estimate=pl.CostEstimate(
                    flops=60 * rows * channels, bytes_accessed=35 * 2**20, transcendentals=0
                ),
                name="blocks",
            )(*held_before[:3], close, skip_gain[None], join_e, join_a)
            return [*out[:3], jnp.concatenate([*held_before[3:], out[3]], axis=0)]

        return call

    steps = width // many
    cuts = (0, (3 * steps) // 8, (5 * steps) // 8, steps)
    other, chip_e, chip_a = joined(ends, f_all)
    before, after, (conv, from_e, from_a, skip_sum) = scanned(
        chip_e, chip_a, f_all, [blocks(cuts[k], cuts[k + 1]) for k in range(3)]
    )
    both = jnp.stack([before, after])
    found = swapped(both)

    count = 3 * SUB
    split = 2 if groups % (2 * LANES) == 0 else 1
    scratch = [
        pltpu.VMEM((3, held + SUB, LANES), F32),
        pltpu.VMEM((held, LANES), F32),
        pltpu.VMEM((3, held, LANES), F32),
        pltpu.VMEM((held, LANES), F32),
        pltpu.VMEM((2, poles, LANES), F32),
    ]
    output, grad_p, sums = pl.pallas_call(
        final_kernel,
        grid=(width // each,),
        in_specs=[
            pl.BlockSpec(memory_space=pltpu.SMEM),
            by_w(3, rows), by_w(4, SUB), by_w(4, SUB), by_w(rows),
            by_block(3, held, groups), by_block(2, held, groups), state_spec, state_spec,
            by_block(SUB, groups), halved, halved, ends_spec,
            by_w(3, taps), fixed(f1), fixed(f_all), fixed(cz), fixed(cy),
        ],
        out_specs=[
            by_w(rows), by_w(3, rows),
            pl.BlockSpec((each * split, count, groups // split), lambda w: (w, 0, 0)),
        ],
        out_shape=[
            shape_of((rows, channels), BF16),
            shape_of((3, rows, channels), BF16),
            shape_of((width * split, count, groups // split), F32),
        ],
        scratch_shapes=scratch,
        compiler_params=params,
        name="final",
    )(
        core[None], p, hx, hi, u, qkv, conv, from_e, from_a, skip_sum, both, found, other, short_filter,
        f1, f_all, cz, cy,
    )

    total = summed(sums).transpose(1, 0, 2).reshape(3, SUB, channels)
    grad_short, grad_skip = total[:, :taps], total[0, taps]
    return output[None], grad_p.transpose(1, 0, 2)[None], grad_short, grad_skip


def solution(mesh):
    placed = (P("dp", "ctx", None, None), P(), P(), P(), P(), P("dp", "ctx", None))
    return jax.shard_map(
        local,
        mesh=mesh,
        in_specs=placed,
        out_specs=(P("dp", "ctx", None), P("dp", "ctx", None, None), P(), P()),
        check_vma=False,
    )
```

```python
import functools

import jax
import jax.numpy as jnp
import numpy as np
from jax import lax
from jax.experimental import pallas as pl
from jax.experimental.pallas import tpu as pltpu
from jax.sharding import PartitionSpec as P

LANES = 128
SUB = 8
F32 = jnp.float32
BF16 = jnp.bfloat16


def spread(row):
    return jnp.broadcast_to(row, (SUB, LANES))


def added(terms):
    while len(terms) > 1:
        pairs = [terms[k] + terms[k + 1] for k in range(0, len(terms) - 1, 2)]
        terms = pairs + terms[len(terms) - len(terms) % 2 :]
    return terms[0]


def folded(values):
    row = lax.broadcasted_iota(jnp.int32, (SUB, LANES), 0)
    upper = row < 4
    values = [
        jnp.where(upper, values[n], values[n + 4])
        + pltpu.roll(jnp.where(upper, values[n + 4], values[n]), 4, 0)
        for n in range(4)
    ]
    for step in (2, 1):
        even = (row // step) % 2 == 0
        values = [
            jnp.where(
                even,
                values[n] + pltpu.roll(values[n], SUB - step, 0),
                values[n + step] + pltpu.roll(values[n + step], step, 0),
            )
            for n in range(step)
        ]
    return values[0]


def phases(tap):
    even, odd = tap[0::2], tap[1::2]
    both = [even[k] + odd[k] if k < len(odd) else even[k] for k in range(len(even))]
    return even, odd, both


def weighted(tap, values):
    return added([tap[k] * values[k] for k in range(len(tap))])


def states_kernel(core, p, hx, hi, u, filt, f1, we, wb, qkv, xg, blocks_e, blocks_a, ends, xs):
    rows = p.shape[1]
    run = (rows + SUB) // SUB
    taps = filt.shape[1]
    poles, groups = f1.shape
    own = rows - run * (SUB - 1)
    tiles = groups // LANES
    first = core[0] == 0

    def tile(lt, carry):
        lanes = pl.ds(pl.multiple_of(lt * LANES, LANES), LANES)
        part = pl.ds(pl.multiple_of(lax.rem(lt, tiles) * LANES, LANES), LANES)
        which = lt // tiles
        inside = lax.broadcasted_iota(jnp.int32, (SUB, LANES), 0) < SUB - 1
        for j in range(3):
            across, within = hx[j, :, lanes].astype(F32), hi[j, :, lanes].astype(F32)
            xs[j, 0:SUB] = jnp.where(first, across, within)
            xs[j, SUB : SUB + rows] = p[j, :, lanes].astype(F32)
            xs[j, SUB + rows :] = jnp.where(first, within, across)
        xs[3, SUB : SUB + rows] = u[:, lanes].astype(F32)
        across, within = hx[3, :, lanes].astype(F32), hi[3, :, lanes].astype(F32)
        xs[3, SUB + rows :] = jnp.where(first, within, across)

        def mixed(j):
            even, odd, both = phases([spread(filt[j, i : i + 1, lanes]) for i in range(taps)])
            row = lambda a: xs[j, pl.ds(SUB + a, SUB, stride=run), :]
            reach = len(even)
            evens = [row(-2 * k) for k in range(1, reach)]
            odds = [row(1 - 2 * k) for k in range(1, reach)]
            pairs = [evens[k] + odds[k] for k in range(reach - 1)]
            before = weighted(odd, odds)
            for a in range(0, run, 2):
                evens = [row(a)] + evens[: reach - 1]
                first = weighted(even, evens)
                yield first + before
                if a + 1 < run:
                    odds = [row(a + 1)] + odds[: reach - 1]
                    pairs = [evens[0] + odds[0]] + pairs[: reach - 1]
                    before = weighted(odd, odds)
                    yield weighted(both, pairs) - first - before

        decay = [spread(f1[n : n + 1, part]) for n in range(poles)]
        for j in (1, 2, 0):
            for a, total in enumerate(mixed(j)):
                at = slice(SUB * a, SUB * a + SUB)
                qkv[which, j, at, part] = total
                if j == 2:
                    xg[which, 0, at, part] = qkv[which, 1, at, part] * total
                if j == 0:
                    xg[which, 1, at, part] = xs[3, pl.ds(SUB + a, SUB, stride=run), :] * total
        for side, order, weight, blocks in (
            (0, range(run), we, blocks_e),
            (1, range(run - 1, -1, -1), wb, blocks_a),
        ):
            state = None
            for a in order:
                x = xg[which, side, SUB * a : SUB * a + SUB, part]
                if a >= own:
                    x = jnp.where(inside, x, 0.0)
                state = [x] * poles if state is None else [decay[n] * state[n] + x for n in range(poles)]
            for n in range(poles):
                blocks[which, n, :, part] = state[n]
            state = [state[n] * weight[n, :, part] for n in range(poles)]
            for n in range(0, poles, SUB):
                ends[side, which, n : n + SUB, part] = folded(state[n : n + SUB])
        return carry

    lax.fori_loop(0, p.shape[2] // LANES, tile, 0)


def blocks_kernel(
    xg, blocks_e, blocks_a, near, skip, join_e, join_a, conv, from_e, from_a, skip_sum
):
    run = xg.shape[2] // SUB
    rows = xg.shape[2] - SUB
    taps = near.shape[0] - run
    poles, groups = blocks_e.shape[1], near.shape[1]
    own = rows - run * (SUB - 1)
    tiles = groups // LANES

    def tile(lt, carry):
        lanes = pl.ds(pl.multiple_of(lt * LANES, LANES), LANES)
        part = pl.ds(pl.multiple_of(lax.rem(lt, tiles) * LANES, LANES), LANES)
        which = lt // tiles
        inside = lax.broadcasted_iota(jnp.int32, (SUB, LANES), 0) < SUB - 1
        gain = spread(skip[0:1, lanes])
        lag = [spread(near[taps + m : taps + m + 1, part]) for m in range(run)]
        lag[0] = lag[0] + gain
        x = [xg[which, 0, SUB * a : SUB * a + SUB, part] for a in range(run)]
        for a in range(run):
            conv[which, 0, SUB * a : SUB * a + SUB, part] = added(
                [lag[m] * x[a - m] for m in range(a + 1)]
            )
        gated = x
        x = [xg[which, 1, SUB * a : SUB * a + SUB, part] for a in range(run)]
        masked = [x[a] if a < own else jnp.where(inside, x[a], 0.0) for a in range(run)]
        skip_sum[which, :, part] = added([masked[a] * gated[a] for a in range(run)])
        past = [jnp.where(inside, 0.0, gain)] + [
            jnp.where(inside, 0.0, -spread(near[taps - m : taps - m + 1, part]))
            for m in range(1, taps - 1)
        ]
        for a in range(run):
            terms = [lag[m] * masked[a + m] for m in range(run - a)]
            if own <= a < own + taps - 1:
                terms = terms + [past[m] * x[a - m] for m in range(a - own + 1)]
            conv[which, 1, SUB * a : SUB * a + SUB, part] = added(terms)
        for n in range(poles):
            value = pltpu.roll(blocks_e[which, n, :, part], 1, 0) * join_e[0, n, :, part]
            for k, step in ((1, 1), (2, 2), (3, 4)):
                value = value + pltpu.roll(value, step, 0) * join_e[k, n, :, part]
            from_e[which, n, :, part] = value
            value = pltpu.roll(blocks_a[which, n, :, part], SUB - 1, 0) * join_a[0, n, :, part]
            for k, step in ((1, 1), (2, 2), (3, 4)):
                value = value + pltpu.roll(value, SUB - step, 0) * join_a[k, n, :, part]
            from_a[which, n, :, part] = value
        return carry

    lax.fori_loop(0, xg.shape[0] * tiles, tile, 0)


def final_kernel(
    core, p, hx, hi, u, qkv, conv, from_e, from_a, skip_sum, both, found, other, filt, f1, f_all, cz, cy,
    output, grad_p, sums, ps, us, gs, os, es,
):
    rows = p.shape[1]
    run = (rows + SUB) // SUB
    taps = filt.shape[1]
    poles, groups = f1.shape
    own = rows - run * (SUB - 1)
    tiles = groups // LANES
    first = core[0] == 0
    halves = pl.num_programs(0) // 2
    kept = (pl.program_id(0) < halves) == first
    cut = sums.shape[2] // LANES

    def tile(lt, carry):
        lanes = pl.ds(pl.multiple_of(lt * LANES, LANES), LANES)
        part = pl.ds(pl.multiple_of(lax.rem(lt, tiles) * LANES, LANES), LANES)
        which = lt // tiles
        piece = lt // cut
        spot = pl.ds(pl.multiple_of(lax.rem(lt, cut) * LANES, LANES), LANES)
        inside = lax.broadcasted_iota(jnp.int32, (SUB, LANES), 0) < SUB - 1
        for side in range(2):
            far = jnp.where(kept, both[side, which, :, part], found[side, which, :, part])
            close = other[side, which, :, part] + f_all[:, part] * far
            es[side] = jnp.where(first == (side == 0), far, close)
        for j in range(3):
            across, within = hx[j, :, lanes].astype(F32), hi[j, :, lanes].astype(F32)
            ps[j, 0:SUB] = jnp.where(first, across, within)
            ps[j, SUB : SUB + rows] = p[j, :, lanes].astype(F32)
            ps[j, SUB + rows :] = jnp.where(first, within, across)
        us[0:rows] = u[:, lanes].astype(F32)
        across, within = hx[3, :, lanes].astype(F32), hi[3, :, lanes].astype(F32)
        us[rows:] = jnp.where(first, within, across)
        decay = [spread(f1[n : n + 1, part]) for n in range(poles)]

        state = [
            from_e[which, n, :, part] + cz[n, :, part] * spread(es[0, n : n + 1])
            for n in range(poles)
        ]
        for a in range(run):
            at = slice(SUB * a, SUB * a + SUB)
            query, upstream = qkv[which, 0, at, part], us[pl.ds(a, SUB, stride=run), :]
            filtered = conv[which, 0, at, part] + added(list(state))
            os[pl.ds(a, SUB, stride=run), :] = query * filtered
            gs[0, at] = upstream * filtered
            if a + 1 < run:
                state = [state[n] * decay[n] for n in range(poles)]
        output[:, lanes] = os[0:rows].astype(BF16)

        state = [
            from_a[which, n, :, part] + cy[n, :, part] * spread(es[1, n : n + 1])
            for n in range(poles)
        ]
        for a in range(run - 1, -1, -1):
            at = slice(SUB * a, SUB * a + SUB)
            grad = conv[which, 1, at, part] + added(list(state))
            gs[1, at] = grad * qkv[which, 2, at, part]
            gs[2, at] = grad * qkv[which, 1, at, part]
            if a:
                state = [state[n] * decay[n] for n in range(poles)]

        for j in range(3):
            even, odd, paired_taps = phases([spread(filt[j, i : i + 1, lanes]) for i in range(taps)])
            reach = len(even)
            grads = [gs[j, SUB * a : SUB * a + SUB] for a in range(taps - 1)]
            beyond = [pltpu.roll(value, SUB - 1, 0) for value in grads]

            def ahead(a):
                return gs[j, SUB * a : SUB * a + SUB] if a < run else beyond[a - run]

            def behind(a):
                return ps[j, pl.ds(SUB + a, SUB, stride=run), :]

            def own_rows(a):
                return grads[a] if a < own else jnp.where(inside, grads[a], 0.0)

            grads = {a: grads[a] for a in range(taps - 1)}
            joint = {k: grads[2 * k + 1] + grads[2 * k + 2] for k in range((taps - 3) // 2)}
            leading = weighted(even, [grads[2 * k] if 2 * k in grads else ahead(2 * k) for k in range(reach)])
            evens = [behind(-2 * k) for k in range(1, reach)]
            odds = [behind(1 - 2 * k) for k in range(1, reach)]
            pairs = [evens[k] + odds[k] for k in range(reach - 1)]
            sums_of = [[None] * reach for _ in range(3)]

            def collect(kind, grad, values, count):
                for k in range(count):
                    term = grad * values[k]
                    so_far = sums_of[kind][k]
                    sums_of[kind][k] = term if so_far is None else so_far + term

            previous = None
            for a in range(0, run, 2):
                for c in range(a, a + 2 * reach + 1):
                    if c not in grads and c < run + taps - 1:
                        grads[c] = ahead(c)
                here = own_rows(a)
                collect(1, here if previous is None else here - previous, odds, len(odd))
                second = weighted(odd, [grads[a + 2 * k + 1] for k in range(len(odd))])
                os[pl.ds(a, SUB, stride=run), :] = leading + second
                evens = [behind(a)] + evens[: reach - 1]
                if a + 1 < run:
                    previous = own_rows(a + 1)
                    for k in range(a // 2, a // 2 + reach):
                        if k not in joint:
                            joint[k] = grads[2 * k + 1] + grads[2 * k + 2]
                    following = weighted(even, [grads[a + 2 + 2 * k] for k in range(reach)])
                    total = weighted(paired_taps, [joint[a // 2 + k] for k in range(reach)])
                    os[pl.ds(a + 1, SUB, stride=run), :] = total - following - second
                    leading = following
                    odds = [behind(a + 1)] + odds[: reach - 1]
                    pairs = [evens[0] + odds[0]] + pairs[: reach - 1]
                    collect(0, here - previous, evens, reach)
                    collect(2, previous, pairs, reach)
                else:
                    collect(0, here, evens, reach)
            sums_of = [sums_of[i % 2][i // 2] + sums_of[2][i // 2] for i in range(taps)]
            grad_p[j, :, lanes] = os[0:rows].astype(BF16)
            extra = [skip_sum[which, :, part]] + [jnp.zeros((SUB, LANES), F32)] * (SUB - taps)
            extra = extra[: SUB - taps] if j == 0 else extra[1 : SUB - taps + 1]
            sums[piece, j * SUB : j * SUB + SUB, spot] = folded(sums_of + extra)
        return carry

    lax.fori_loop(0, p.shape[2] // LANES, tile, 0)


def shifted(value, axis, steps):
    count = lax.axis_size(axis)
    first, last = (max(0, -steps), min(count, count - steps))
    return lax.ppermute(value, axis, [(source, source + steps) for source in range(first, last)])


def swapped(value):
    count = lax.axis_size("ctx")
    return lax.ppermute(value, "ctx", [(s, s ^ 1) for s in range(count)])


def joined(ends, f_all):
    core = lax.rem(lax.axis_index("ctx"), 2)
    half = ends.shape[1] // 2
    other = swapped(ends)
    first = core == 0
    mine = lax.dynamic_slice_in_dim(ends, core * half, half, 1)
    theirs = lax.dynamic_slice_in_dim(other, core * half, half, 1)
    one, two = jnp.where(first, mine, theirs), jnp.where(first, theirs, mine)
    return other, f_all * one[0] + two[0], one[1] + f_all * two[1]


def paired(value, axis, step, lines=None):
    count = lax.axis_size(axis)
    return lax.ppermute(value, axis, [(source, source ^ step) for source in lines or range(count)])


def scanned(chip_e, chip_a, f_all, beside):
    chips = lax.axis_size("ctx") // 2
    f_chip = f_all * f_all
    if chips == 4:
        odd = lax.rem(lax.axis_index("ctx") // 2, 2) == 1
        sent = jnp.where(odd, chip_a, chip_e)
        first = paired(sent, "ctx", 2)
        kept = beside[0](sent, None)
        first, kept = lax.optimization_barrier((first, kept))
        sent = jnp.where(odd, chip_e, chip_a) + f_chip * first
        near = lax.ppermute(sent, "ctx", [(2, 4), (3, 5), (4, 2), (5, 3)])
        kept = beside[1](sent, kept)
        near, kept = lax.optimization_barrier((near, kept))
        far = lax.ppermute(near, "ctx", [(4, 6), (5, 7), (2, 0), (3, 1)])
        kept = beside[2](near, kept)
        far, kept = lax.optimization_barrier((far, kept))
        far = first + f_chip * far
        return jnp.where(odd, far, near), jnp.where(odd, near, far), kept
    kept = beside[2](chip_e, beside[1](chip_e, beside[0](chip_e, None)))
    before, after = jnp.zeros_like(chip_e), jnp.zeros_like(chip_a)
    reach = 1
    while reach < chips:
        early, late = shifted(chip_e, "ctx", 2 * reach), shifted(chip_a, "ctx", -2 * reach)
        factor = f_chip ** (reach - 1)
        before, after = before + factor * early, after + factor * late
        factor = f_chip**reach
        chip_e, chip_a = chip_e + factor * early, chip_a + factor * late
        reach = 2 * reach
    return before, after, kept


def summed(value):
    dp, parts = lax.axis_index("dp"), lax.axis_size("dp")
    low = lax.rem(lax.axis_index("ctx"), 2) == 0
    half = value.shape[0] // 2
    left, right = value[:half], value[half:]
    value = jnp.where(low, left, right) + swapped(jnp.where(low, right, left))
    size = half // parts
    piece = lambda k: lax.dynamic_slice_in_dim(value, jnp.bitwise_xor(dp, k) * size, size, 0)
    total = piece(0)
    for term in [paired(piece(k), "dp", k) for k in range(1, parts)]:
        total = total + term
    reach = 2
    while reach < lax.axis_size("ctx"):
        total = total + paired(total, "ctx", reach)
        reach = 2 * reach
    value = jnp.zeros((half,) + value.shape[1:], F32)
    for k in range(parts):
        term = paired(total, "dp", k) if k else total
        value = lax.dynamic_update_slice_in_dim(value, term, jnp.bitwise_xor(dp, k) * size, 0)
    other = swapped(value)
    return jnp.concatenate([jnp.where(low, value, other), jnp.where(low, other, value)], axis=0)


def local(projected, short_filter, residues, decay_rates, skip_gain, cotangent):
    rows = projected.shape[1]
    channels = projected.shape[3]
    taps = short_filter.shape[1]
    groups, poles = residues.shape
    width = channels // groups
    run = (rows + SUB) // SUB
    held = rows + SUB
    p = projected[0].transpose(1, 0, 2)
    u = cotangent[0]
    core = lax.rem(lax.axis_index("ctx"), 2)

    def edge(last):
        start = jnp.where(last, rows - SUB, 0)
        cut = lambda value, axis: lax.dynamic_slice_in_dim(value, start, SUB, axis)
        return jnp.concatenate([cut(p, 1), cut(u, 0)[None]], axis=0)

    devices = lax.axis_size("ctx")
    across = [(k, k + 1) for k in range(1, devices - 1, 2)]
    across = across + [(target, source) for source, target in across]
    hx = lax.ppermute(edge(core == 1), "ctx", across)
    hi = swapped(edge(core == 0))

    rate = decay_rates.T
    weight = residues.T
    sub = np.arange(SUB)
    powers = np.stack([run * (7 - sub) - SUB, run * sub, 1 + run * sub, rows - run * (sub + 1) + 1])
    table = jnp.exp(-rate[None, :, None, :] * powers.astype(np.float32)[:, None, :, None])
    we, wb = table[0], table[1]
    cz, cy = weight[:, None, :] * table[2], weight[:, None, :] * table[3]
    f1 = jnp.exp(-rate)
    f_all = jnp.exp(-rate * rows)
    steps = np.array([1, run, 2 * run, 4 * run], np.float32)
    factor = jnp.exp(-rate[None] * steps[:, None, None])
    factor = jnp.concatenate([weight[None] * factor[:1], factor[1:]], axis=0)
    reach = np.array([1, 1, 2, 4])[:, None]
    down, up = sub[None] >= reach, sub[None] < SUB - reach
    join_e = jnp.where(down[:, None, :, None], factor[:, :, None, :], 0.0)
    join_a = jnp.where(up[:, None, :, None], factor[:, :, None, :], 0.0)
    close = np.arange(-taps, run).astype(np.float32)
    near = jnp.sum(weight[:, None, :] * jnp.exp(-rate[:, None, :] * close[None, :, None]), axis=0)

    each = 1

    def by_w(*shape):
        axis = len(shape)
        return pl.BlockSpec(shape + (each * groups,), lambda w: (0,) * axis + (w,))

    def fixed(value):
        return pl.BlockSpec(
            value.shape, lambda w: (0,) * value.ndim, pipeline_mode=pl.Buffered(1)
        )

    params = pltpu.CompilerParams(vmem_limit_bytes=48 * 1024 * 1024)
    shape_of = jax.ShapeDtypeStruct
    ends_spec = pl.BlockSpec((2, each, poles, groups), lambda w: (0, w, 0, 0))
    halved = pl.BlockSpec(
        (2, each, poles, groups), lambda w: (0, lax.rem(w, width // each // 2), 0, 0)
    )
    early = (hx, near, join_e, join_a, cz, cy, f_all)
    hx, near, join_e, join_a, cz, cy, f_all = lax.optimization_barrier(early)
    state_shape = shape_of((width, poles, SUB, groups), F32)
    pair_shape = shape_of((width, 2, held, groups), F32)

    def by_block(*shape, count=each, first=0):
        return pl.BlockSpec((count,) + shape, lambda w: (w + first,) + (0,) * len(shape))

    state_spec = by_block(poles, SUB, groups)
    qkv, xg, blocks_e, blocks_a, ends = pl.pallas_call(
        states_kernel,
        grid=(width // each,),
        in_specs=[
            pl.BlockSpec(memory_space=pltpu.SMEM),
            by_w(3, rows), by_w(4, SUB), by_w(4, SUB), by_w(rows), by_w(3, taps),
            fixed(f1), fixed(we), fixed(wb),
        ],
        out_specs=[
            by_block(3, held, groups), by_block(2, held, groups), state_spec, state_spec,
            ends_spec,
        ],
        out_shape=[
            shape_of((width, 3, held, groups), F32), pair_shape,
            state_shape, state_shape, shape_of((2, width, poles, groups), F32),
        ],
        scratch_shapes=[pltpu.VMEM((4, held + SUB, LANES), F32)],
        compiler_params=params,
        name="states",
    )(core[None], p, hx, hi, u, short_filter, f1, we, wb)

    many = 2 if width % 2 == 0 else 1

    def blocks(first, last):
        place = {"count": many, "first": first}
        states, pairs = by_block(poles, SUB, groups, **place), by_block(2, held, groups, **place)

        def call(sent, kept):
            close, _ = lax.optimization_barrier((near, sent))
            held_before = kept or (xg, blocks_e, blocks_a)
            out = pl.pallas_call(
                blocks_kernel,
                grid=(last - first,),
                in_specs=[
                    pairs, states, states, fixed(near),
                    pl.BlockSpec((1, many * groups), lambda w: (0, w + first)),
                    fixed(join_e), fixed(join_a),
                ],
                out_specs=[pairs, states, states, by_block(SUB, groups, count=many)],
                out_shape=[
                    pair_shape, state_shape, state_shape,
                    shape_of(((last - first) * many, SUB, groups), F32),
                ],
                input_output_aliases={0: 0, 1: 1, 2: 2},
                compiler_params=params,
                cost_estimate=pl.CostEstimate(
                    flops=60 * rows * channels, bytes_accessed=35 * 2**20, transcendentals=0
                ),
                name="blocks",
            )(*held_before[:3], close, skip_gain[None], join_e, join_a)
            return [*out[:3], jnp.concatenate([*held_before[3:], out[3]], axis=0)]

        return call

    steps = width // many
    cuts = (0, (3 * steps) // 8, (5 * steps) // 8, steps)
    other, chip_e, chip_a = joined(ends, f_all)
    before, after, (conv, from_e, from_a, skip_sum) = scanned(
        chip_e, chip_a, f_all, [blocks(cuts[k], cuts[k + 1]) for k in range(3)]
    )
    both = jnp.stack([before, after])
    found = swapped(both)

    count = 3 * SUB
    split = 2 if groups % (2 * LANES) == 0 else 1
    scratch = [
        pltpu.VMEM((3, held + SUB, LANES), F32),
        pltpu.VMEM((held, LANES), F32),
        pltpu.VMEM((3, held, LANES), F32),
        pltpu.VMEM((held, LANES), F32),
        pltpu.VMEM((2, poles, LANES), F32),
    ]
    output, grad_p, sums = pl.pallas_call(
        final_kernel,
        grid=(width // each,),
        in_specs=[
            pl.BlockSpec(memory_space=pltpu.SMEM),
            by_w(3, rows), by_w(4, SUB), by_w(4, SUB), by_w(rows),
            by_block(3, held, groups), by_block(2, held, groups), state_spec, state_spec,
            by_block(SUB, groups), halved, halved, ends_spec,
            by_w(3, taps), fixed(f1), fixed(f_all), fixed(cz), fixed(cy),
        ],
        out_specs=[
            by_w(rows), by_w(3, rows),
            pl.BlockSpec((each * split, count, groups // split), lambda w: (w, 0, 0)),
        ],
        out_shape=[
            shape_of((rows, channels), BF16),
            shape_of((3, rows, channels), BF16),
            shape_of((width * split, count, groups // split), F32),
        ],
        scratch_shapes=scratch,
        compiler_params=params,
        name="final",
    )(
        core[None], p, hx, hi, u, qkv, conv, from_e, from_a, skip_sum, both, found, other, short_filter,
        f1, f_all, cz, cy,
    )

    total = summed(sums).transpose(1, 0, 2).reshape(3, SUB, channels)
    grad_short, grad_skip = total[:, :taps], total[0, taps]
    return output[None], grad_p.transpose(1, 0, 2)[None], grad_short, grad_skip


def solution(mesh):
    placed = (P("dp", "ctx", None, None), P(), P(), P(), P(), P("dp", "ctx", None))
    return jax.shard_map(
        local,
        mesh=mesh,
        in_specs=placed,
        out_specs=(P("dp", "ctx", None), P("dp", "ctx", None, None), P(), P()),
        check_vma=False,
    )
```

```python
import functools

import jax
import jax.numpy as jnp
import numpy as np
from jax import lax
from jax.experimental import pallas as pl
from jax.experimental.pallas import tpu as pltpu
from jax.sharding import PartitionSpec as P

LANES = 128
SUB = 8
F32 = jnp.float32
BF16 = jnp.bfloat16


def spread(row):
    return jnp.broadcast_to(row, (SUB, LANES))


def added(terms):
    while len(terms) > 1:
        pairs = [terms[k] + terms[k + 1] for k in range(0, len(terms) - 1, 2)]
        terms = pairs + terms[len(terms) - len(terms) % 2 :]
    return terms[0]


def folded(values):
    row = lax.broadcasted_iota(jnp.int32, (SUB, LANES), 0)
    upper = row < 4
    values = [
        jnp.where(upper, values[n], values[n + 4])
        + pltpu.roll(jnp.where(upper, values[n + 4], values[n]), 4, 0)
        for n in range(4)
    ]
    for step in (2, 1):
        even = (row // step) % 2 == 0
        values = [
            jnp.where(
                even,
                values[n] + pltpu.roll(values[n], SUB - step, 0),
                values[n + step] + pltpu.roll(values[n + step], step, 0),
            )
            for n in range(step)
        ]
    return values[0]


def phases(tap):
    even, odd = tap[0::2], tap[1::2]
    both = [even[k] + odd[k] if k < len(odd) else even[k] for k in range(len(even))]
    return even, odd, both


def weighted(tap, values):
    return added([tap[k] * values[k] for k in range(len(tap))])


def states_kernel(core, p, hx, hi, u, filt, f1, we, wb, qkv, xg, blocks_e, blocks_a, ends, xs):
    rows = p.shape[1]
    run = (rows + SUB) // SUB
    taps = filt.shape[1]
    poles, groups = f1.shape
    own = rows - run * (SUB - 1)
    tiles = groups // LANES
    first = core[0] == 0

    def tile(lt, carry):
        lanes = pl.ds(pl.multiple_of(lt * LANES, LANES), LANES)
        part = pl.ds(pl.multiple_of(lax.rem(lt, tiles) * LANES, LANES), LANES)
        which = lt // tiles
        inside = lax.broadcasted_iota(jnp.int32, (SUB, LANES), 0) < SUB - 1
        for j in range(3):
            across, within = hx[j, :, lanes].astype(F32), hi[j, :, lanes].astype(F32)
            xs[j, 0:SUB] = jnp.where(first, across, within)
            xs[j, SUB : SUB + rows] = p[j, :, lanes].astype(F32)
            xs[j, SUB + rows : 2 * SUB + rows] = jnp.where(first, within, across)
        xs[3, SUB : SUB + rows] = u[:, lanes].astype(F32)
        across, within = hx[3, :, lanes].astype(F32), hi[3, :, lanes].astype(F32)
        xs[3, SUB + rows : 2 * SUB + rows] = jnp.where(first, within, across)

        def mixed(j):
            even, odd, both = phases([spread(filt[j, i : i + 1, lanes]) for i in range(taps)])
            row = lambda a: xs[j, pl.ds(SUB + a, SUB, stride=run), :]
            reach = len(even)
            evens = [row(-2 * k) for k in range(1, reach)]
            odds = [row(1 - 2 * k) for k in range(1, reach)]
            pairs = [evens[k] + odds[k] for k in range(reach - 1)]
            before = weighted(odd, odds)
            for a in range(0, run, 2):
                evens = [row(a)] + evens[: reach - 1]
                first = weighted(even, evens)
                yield first + before
                if a + 1 < run:
                    odds = [row(a + 1)] + odds[: reach - 1]
                    pairs = [evens[0] + odds[0]] + pairs[: reach - 1]
                    before = weighted(odd, odds)
                    yield weighted(both, pairs) - first - before

        decay = [spread(f1[n : n + 1, part]) for n in range(poles)]
        for j in (1, 2, 0):
            for a, total in enumerate(mixed(j)):
                at = slice(SUB * a, SUB * a + SUB)
                qkv[which, j, at, part] = total
                if j == 2:
                    xg[which, 0, at, part] = qkv[which, 1, at, part] * total
                if j == 0:
                    xg[which, 1, at, part] = xs[3, pl.ds(SUB + a, SUB, stride=run), :] * total
        for side, order, weight, blocks in (
            (0, range(run), we, blocks_e),
            (1, range(run - 1, -1, -1), wb, blocks_a),
        ):
            state = None
            for a in order:
                x = xg[which, side, SUB * a : SUB * a + SUB, part]
                if a >= own:
                    x = jnp.where(inside, x, 0.0)
                state = [x] * poles if state is None else [decay[n] * state[n] + x for n in range(poles)]
            for n in range(poles):
                blocks[which, n, :, part] = state[n]
            state = [state[n] * weight[n, :, part] for n in range(poles)]
            for n in range(0, poles, SUB):
                ends[side, which, n : n + SUB, part] = folded(state[n : n + SUB])
        return carry

    lax.fori_loop(0, p.shape[2] // LANES, tile, 0)


def blocks_kernel(
    xg, blocks_e, blocks_a, near, skip, join_e, join_a, conv, from_e, from_a, skip_sum
):
    run = xg.shape[2] // SUB
    rows = xg.shape[2] - SUB
    taps = near.shape[0] - run
    poles, groups = blocks_e.shape[1], near.shape[1]
    own = rows - run * (SUB - 1)
    tiles = groups // LANES

    def tile(lt, carry):
        lanes = pl.ds(pl.multiple_of(lt * LANES, LANES), LANES)
        part = pl.ds(pl.multiple_of(lax.rem(lt, tiles) * LANES, LANES), LANES)
        which = lt // tiles
        inside = lax.broadcasted_iota(jnp.int32, (SUB, LANES), 0) < SUB - 1
        gain = spread(skip[0:1, lanes])
        lag = [spread(near[taps + m : taps + m + 1, part]) for m in range(run)]
        lag[0] = lag[0] + gain
        x = [xg[which, 0, SUB * a : SUB * a + SUB, part] for a in range(run)]
        for a in range(run):
            conv[which, 0, SUB * a : SUB * a + SUB, part] = added(
                [lag[m] * x[a - m] for m in range(a + 1)]
            )
        gated = x
        x = [xg[which, 1, SUB * a : SUB * a + SUB, part] for a in range(run)]
        masked = [x[a] if a < own else jnp.where(inside, x[a], 0.0) for a in range(run)]
        skip_sum[which, :, part] = added([masked[a] * gated[a] for a in range(run)])
        past = [jnp.where(inside, 0.0, gain)] + [
            jnp.where(inside, 0.0, -spread(near[taps - m : taps - m + 1, part]))
            for m in range(1, taps - 1)
        ]
        for a in range(run):
            terms = [lag[m] * masked[a + m] for m in range(run - a)]
            if own <= a < own + taps - 1:
                terms = terms + [past[m] * x[a - m] for m in range(a - own + 1)]
            conv[which, 1, SUB * a : SUB * a + SUB, part] = added(terms)
        for n in range(poles):
            value = pltpu.roll(blocks_e[which, n, :, part], 1, 0) * join_e[0, n, :, part]
            for k, step in ((1, 1), (2, 2), (3, 4)):
                value = value + pltpu.roll(value, step, 0) * join_e[k, n, :, part]
            from_e[which, n, :, part] = value
            value = pltpu.roll(blocks_a[which, n, :, part], SUB - 1, 0) * join_a[0, n, :, part]
            for k, step in ((1, 1), (2, 2), (3, 4)):
                value = value + pltpu.roll(value, SUB - step, 0) * join_a[k, n, :, part]
            from_a[which, n, :, part] = value
        return carry

    lax.fori_loop(0, xg.shape[0] * tiles, tile, 0)


def final_kernel(
    core, p, hx, hi, u, qkv, conv, from_e, from_a, skip_sum, both, found, other, filt, f1, f_all, cz, cy,
    output, grad_p, sums, ps, us, gs, os, es,
):
    rows = p.shape[1]
    run = (rows + SUB) // SUB
    taps = filt.shape[1]
    poles, groups = f1.shape
    own = rows - run * (SUB - 1)
    tiles = groups // LANES
    first = core[0] == 0
    halves = pl.num_programs(0) // 2
    kept = (pl.program_id(0) < halves) == first
    cut = sums.shape[2] // LANES

    def tile(lt, carry):
        lanes = pl.ds(pl.multiple_of(lt * LANES, LANES), LANES)
        part = pl.ds(pl.multiple_of(lax.rem(lt, tiles) * LANES, LANES), LANES)
        which = lt // tiles
        piece = lt // cut
        spot = pl.ds(pl.multiple_of(lax.rem(lt, cut) * LANES, LANES), LANES)
        inside = lax.broadcasted_iota(jnp.int32, (SUB, LANES), 0) < SUB - 1
        for side in range(2):
            far = jnp.where(kept, both[side, which, :, part], found[side, which, :, part])
            close = other[side, which, :, part] + f_all[:, part] * far
            es[side] = jnp.where(first == (side == 0), far, close)
        for j in range(3):
            across, within = hx[j, :, lanes].astype(F32), hi[j, :, lanes].astype(F32)
            ps[j, 0:SUB] = jnp.where(first, across, within)
            ps[j, SUB : SUB + rows] = p[j, :, lanes].astype(F32)
            ps[j, SUB + rows : 2 * SUB + rows] = jnp.where(first, within, across)
        us[0:rows] = u[:, lanes].astype(F32)
        across, within = hx[3, :, lanes].astype(F32), hi[3, :, lanes].astype(F32)
        us[rows : SUB + rows] = jnp.where(first, within, across)
        decay = [spread(f1[n : n + 1, part]) for n in range(poles)]

        state = [
            from_e[which, n, :, part] + cz[n, :, part] * spread(es[0, n : n + 1])
            for n in range(poles)
        ]
        for a in range(run):
            at = slice(SUB * a, SUB * a + SUB)
            query, upstream = qkv[which, 0, at, part], us[pl.ds(a, SUB, stride=run), :]
            filtered = conv[which, 0, at, part] + added(list(state))
            os[pl.ds(a, SUB, stride=run), :] = query * filtered
            gs[0, at] = upstream * filtered
            if a + 1 < run:
                state = [state[n] * decay[n] for n in range(poles)]
        output[:, lanes] = os[0:rows].astype(BF16)

        state = [
            from_a[which, n, :, part] + cy[n, :, part] * spread(es[1, n : n + 1])
            for n in range(poles)
        ]
        for a in range(run - 1, -1, -1):
            at = slice(SUB * a, SUB * a + SUB)
            grad = conv[which, 1, at, part] + added(list(state))
            gs[1, at] = grad * qkv[which, 2, at, part]
            gs[2, at] = grad * qkv[which, 1, at, part]
            if a:
                state = [state[n] * decay[n] for n in range(poles)]

        for j in range(3):
            even, odd, paired_taps = phases([spread(filt[j, i : i + 1, lanes]) for i in range(taps)])
            reach = len(even)
            grads = [gs[j, SUB * a : SUB * a + SUB] for a in range(taps - 1)]
            beyond = [pltpu.roll(value, SUB - 1, 0) for value in grads]

            def ahead(a):
                return gs[j, SUB * a : SUB * a + SUB] if a < run else beyond[a - run]

            def behind(a):
                return ps[j, pl.ds(SUB + a, SUB, stride=run), :]

            def own_rows(a):
                return grads[a] if a < own else jnp.where(inside, grads[a], 0.0)

            grads = {a: grads[a] for a in range(taps - 1)}
            joint = {k: grads[2 * k + 1] + grads[2 * k + 2] for k in range((taps - 3) // 2)}
            leading = weighted(even, [grads[2 * k] if 2 * k in grads else ahead(2 * k) for k in range(reach)])
            evens = [behind(-2 * k) for k in range(1, reach)]
            odds = [behind(1 - 2 * k) for k in range(1, reach)]
            pairs = [evens[k] + odds[k] for k in range(reach - 1)]
            sums_of = [[None] * reach for _ in range(3)]

            def collect(kind, grad, values, count):
                for k in range(count):
                    term = grad * values[k]
                    so_far = sums_of[kind][k]
                    sums_of[kind][k] = term if so_far is None else so_far + term

            previous = None
            for a in range(0, run, 2):
                for c in range(a, a + 2 * reach + 1):
                    if c not in grads and c < run + taps - 1:
                        grads[c] = ahead(c)
                here = own_rows(a)
                collect(1, here if previous is None else here - previous, odds, len(odd))
                second = weighted(odd, [grads[a + 2 * k + 1] for k in range(len(odd))])
                os[pl.ds(a, SUB, stride=run), :] = leading + second
                evens = [behind(a)] + evens[: reach - 1]
                if a + 1 < run:
                    previous = own_rows(a + 1)
                    for k in range(a // 2, a // 2 + reach):
                        if k not in joint:
                            joint[k] = grads[2 * k + 1] + grads[2 * k + 2]
                    following = weighted(even, [grads[a + 2 + 2 * k] for k in range(reach)])
                    total = weighted(paired_taps, [joint[a // 2 + k] for k in range(reach)])
                    os[pl.ds(a + 1, SUB, stride=run), :] = total - following - second
                    leading = following
                    odds = [behind(a + 1)] + odds[: reach - 1]
                    pairs = [evens[0] + odds[0]] + pairs[: reach - 1]
                    collect(0, here - previous, evens, reach)
                    collect(2, previous, pairs, reach)
                else:
                    collect(0, here, evens, reach)
            sums_of = [sums_of[i % 2][i // 2] + sums_of[2][i // 2] for i in range(taps)]
            grad_p[j, :, lanes] = os[0:rows].astype(BF16)
            extra = [skip_sum[which, :, part]] + [jnp.zeros((SUB, LANES), F32)] * (SUB - taps)
            extra = extra[: SUB - taps] if j == 0 else extra[1 : SUB - taps + 1]
            sums[piece, j * SUB : j * SUB + SUB, spot] = folded(sums_of + extra)
        return carry

    lax.fori_loop(0, p.shape[2] // LANES, tile, 0)


def shifted(value, axis, steps):
    count = lax.axis_size(axis)
    first, last = (max(0, -steps), min(count, count - steps))
    return lax.ppermute(value, axis, [(source, source + steps) for source in range(first, last)])


def swapped(value):
    count = lax.axis_size("ctx")
    return lax.ppermute(value, "ctx", [(s, s ^ 1) for s in range(count)])


def joined(ends, f_all):
    core = lax.rem(lax.axis_index("ctx"), 2)
    half = ends.shape[1] // 2
    other = swapped(ends)
    first = core == 0
    mine = lax.dynamic_slice_in_dim(ends, core * half, half, 1)
    theirs = lax.dynamic_slice_in_dim(other, core * half, half, 1)
    one, two = jnp.where(first, mine, theirs), jnp.where(first, theirs, mine)
    return other, f_all * one[0] + two[0], one[1] + f_all * two[1]


def paired(value, axis, step, lines=None):
    count = lax.axis_size(axis)
    return lax.ppermute(value, axis, [(source, source ^ step) for source in lines or range(count)])


def scanned(chip_e, chip_a, f_all, beside):
    chips = lax.axis_size("ctx") // 2
    f_chip = f_all * f_all
    if chips == 4:
        odd = lax.rem(lax.axis_index("ctx") // 2, 2) == 1
        sent = jnp.where(odd, chip_a, chip_e)
        first = paired(sent, "ctx", 2)
        kept = beside[0](sent, None)
        first, kept = lax.optimization_barrier((first, kept))
        sent = jnp.where(odd, chip_e, chip_a) + f_chip * first
        near = lax.ppermute(sent, "ctx", [(2, 4), (3, 5), (4, 2), (5, 3)])
        kept = beside[1](sent, kept)
        near, kept = lax.optimization_barrier((near, kept))
        far = lax.ppermute(near, "ctx", [(4, 6), (5, 7), (2, 0), (3, 1)])
        kept = beside[2](near, kept)
        far, kept = lax.optimization_barrier((far, kept))
        far = first + f_chip * far
        return jnp.where(odd, far, near), jnp.where(odd, near, far), kept
    kept = beside[2](chip_e, beside[1](chip_e, beside[0](chip_e, None)))
    before, after = jnp.zeros_like(chip_e), jnp.zeros_like(chip_a)
    reach = 1
    while reach < chips:
        early, late = shifted(chip_e, "ctx", 2 * reach), shifted(chip_a, "ctx", -2 * reach)
        factor = f_chip ** (reach - 1)
        before, after = before + factor * early, after + factor * late
        factor = f_chip**reach
        chip_e, chip_a = chip_e + factor * early, chip_a + factor * late
        reach = 2 * reach
    return before, after, kept


def summed(value):
    dp, parts = lax.axis_index("dp"), lax.axis_size("dp")
    low = lax.rem(lax.axis_index("ctx"), 2) == 0
    half = value.shape[0] // 2
    left, right = value[:half], value[half:]
    value = jnp.where(low, left, right) + swapped(jnp.where(low, right, left))
    size = half // parts
    piece = lambda k: lax.dynamic_slice_in_dim(value, jnp.bitwise_xor(dp, k) * size, size, 0)
    total = piece(0)
    for term in [paired(piece(k), "dp", k) for k in range(1, parts)]:
        total = total + term
    count = lax.axis_size("ctx")
    reaches = [2 << k for k in range((count // 2).bit_length() - 1)]
    for near, far in zip(reaches, reversed(reaches)):
        pairs = [(s, s ^ (far if s % 2 else near)) for s in range(count)]
        total = total + lax.ppermute(total, "ctx", pairs)
    value = jnp.zeros((half,) + value.shape[1:], F32)
    for k in range(parts):
        term = paired(total, "dp", k) if k else total
        value = lax.dynamic_update_slice_in_dim(value, term, jnp.bitwise_xor(dp, k) * size, 0)
    other = swapped(value)
    return jnp.concatenate([jnp.where(low, value, other), jnp.where(low, other, value)], axis=0)


def local(projected, short_filter, residues, decay_rates, skip_gain, cotangent):
    rows = projected.shape[1]
    channels = projected.shape[3]
    taps = short_filter.shape[1]
    groups, poles = residues.shape
    width = channels // groups
    run = (rows + SUB) // SUB
    held = rows + SUB
    p = projected[0].transpose(1, 0, 2)
    u = cotangent[0]
    core = lax.rem(lax.axis_index("ctx"), 2)

    def edge(last):
        start = jnp.where(last, rows - SUB, 0)
        cut = lambda value, axis: lax.dynamic_slice_in_dim(value, start, SUB, axis)
        return jnp.concatenate([cut(p, 1), cut(u, 0)[None]], axis=0)

    devices = lax.axis_size("ctx")
    across = [(k, k + 1) for k in range(1, devices - 1, 2)]
    across = across + [(target, source) for source, target in across]
    hx = lax.ppermute(edge(core == 1), "ctx", across)
    hi = swapped(edge(core == 0))

    rate = decay_rates.T
    weight = residues.T
    sub = np.arange(SUB)
    powers = np.stack([run * (7 - sub) - SUB, run * sub, 1 + run * sub, rows - run * (sub + 1) + 1])
    table = jnp.exp(-rate[None, :, None, :] * powers.astype(np.float32)[:, None, :, None])
    we, wb = table[0], table[1]
    cz, cy = weight[:, None, :] * table[2], weight[:, None, :] * table[3]
    f1 = jnp.exp(-rate)
    f_all = jnp.exp(-rate * rows)
    steps = np.array([1, run, 2 * run, 4 * run], np.float32)
    factor = jnp.exp(-rate[None] * steps[:, None, None])
    factor = jnp.concatenate([weight[None] * factor[:1], factor[1:]], axis=0)
    reach = np.array([1, 1, 2, 4])[:, None]
    down, up = sub[None] >= reach, sub[None] < SUB - reach
    join_e = jnp.where(down[:, None, :, None], factor[:, :, None, :], 0.0)
    join_a = jnp.where(up[:, None, :, None], factor[:, :, None, :], 0.0)
    close = np.arange(-taps, run).astype(np.float32)
    near = jnp.sum(weight[:, None, :] * jnp.exp(-rate[:, None, :] * close[None, :, None]), axis=0)

    each = 1

    def by_w(*shape):
        axis = len(shape)
        return pl.BlockSpec(shape + (each * groups,), lambda w: (0,) * axis + (w,))

    def fixed(value):
        return pl.BlockSpec(
            value.shape, lambda w: (0,) * value.ndim, pipeline_mode=pl.Buffered(1)
        )

    params = pltpu.CompilerParams(vmem_limit_bytes=48 * 1024 * 1024)
    shape_of = jax.ShapeDtypeStruct
    ends_spec = pl.BlockSpec((2, each, poles, groups), lambda w: (0, w, 0, 0))
    halved = pl.BlockSpec(
        (2, each, poles, groups), lambda w: (0, lax.rem(w, width // each // 2), 0, 0)
    )
    early = (hx, near, join_e, join_a, cz, cy, f_all)
    hx, near, join_e, join_a, cz, cy, f_all = lax.optimization_barrier(early)
    state_shape = shape_of((width, poles, SUB, groups), F32)
    pair_shape = shape_of((width, 2, held, groups), F32)

    def by_block(*shape, count=each, first=0):
        return pl.BlockSpec((count,) + shape, lambda w: (w + first,) + (0,) * len(shape))

    state_spec = by_block(poles, SUB, groups)
    qkv, xg, blocks_e, blocks_a, ends = pl.pallas_call(
        states_kernel,
        grid=(width // each,),
        in_specs=[
            pl.BlockSpec(memory_space=pltpu.SMEM),
            by_w(3, rows), by_w(4, SUB), by_w(4, SUB), by_w(rows), by_w(3, taps),
            fixed(f1), fixed(we), fixed(wb),
        ],
        out_specs=[
            by_block(3, held, groups), by_block(2, held, groups), state_spec, state_spec,
            ends_spec,
        ],
        out_shape=[
            shape_of((width, 3, held, groups), F32), pair_shape,
            state_shape, state_shape, shape_of((2, width, poles, groups), F32),
        ],
        scratch_shapes=[pltpu.VMEM((4, held + 4 * SUB, LANES), F32)],
        compiler_params=params,
        name="states",
    )(core[None], p, hx, hi, u, short_filter, f1, we, wb)

    many = 2 if width % 2 == 0 else 1

    def blocks(first, last):
        place = {"count": many, "first": first}
        states, pairs = by_block(poles, SUB, groups, **place), by_block(2, held, groups, **place)

        def call(sent, kept):
            close, _ = lax.optimization_barrier((near, sent))
            held_before = kept or (xg, blocks_e, blocks_a)
            out = pl.pallas_call(
                blocks_kernel,
                grid=(last - first,),
                in_specs=[
                    pairs, states, states, fixed(near),
                    pl.BlockSpec((1, many * groups), lambda w: (0, w + first)),
                    fixed(join_e), fixed(join_a),
                ],
                out_specs=[pairs, states, states, by_block(SUB, groups, count=many)],
                out_shape=[
                    pair_shape, state_shape, state_shape,
                    shape_of(((last - first) * many, SUB, groups), F32),
                ],
                input_output_aliases={0: 0, 1: 1, 2: 2},
                compiler_params=params,
                cost_estimate=pl.CostEstimate(
                    flops=60 * rows * channels, bytes_accessed=35 * 2**20, transcendentals=0
                ),
                name="blocks",
            )(*held_before[:3], close, skip_gain[None], join_e, join_a)
            return [*out[:3], jnp.concatenate([*held_before[3:], out[3]], axis=0)]

        return call

    steps = width // many
    cuts = (0, (3 * steps) // 8, (5 * steps) // 8, steps)
    other, chip_e, chip_a = joined(ends, f_all)
    before, after, (conv, from_e, from_a, skip_sum) = scanned(
        chip_e, chip_a, f_all, [blocks(cuts[k], cuts[k + 1]) for k in range(3)]
    )
    both = jnp.stack([before, after])
    found = swapped(both)

    count = 3 * SUB
    split = 2 if groups % (2 * LANES) == 0 else 1
    scratch = [
        pltpu.VMEM((3, held + 4 * SUB, LANES), F32),
        pltpu.VMEM((held + 4 * SUB, LANES), F32),
        pltpu.VMEM((3, held, LANES), F32),
        pltpu.VMEM((held + 4 * SUB, LANES), F32),
        pltpu.VMEM((2, poles, LANES), F32),
    ]
    output, grad_p, sums = pl.pallas_call(
        final_kernel,
        grid=(width // each,),
        in_specs=[
            pl.BlockSpec(memory_space=pltpu.SMEM),
            by_w(3, rows), by_w(4, SUB), by_w(4, SUB), by_w(rows),
            by_block(3, held, groups), by_block(2, held, groups), state_spec, state_spec,
            by_block(SUB, groups), halved, halved, ends_spec,
            by_w(3, taps), fixed(f1), fixed(f_all), fixed(cz), fixed(cy),
        ],
        out_specs=[
            by_w(rows), by_w(3, rows),
            pl.BlockSpec((each * split, count, groups // split), lambda w: (w, 0, 0)),
        ],
        out_shape=[
            shape_of((rows, channels), BF16),
            shape_of((3, rows, channels), BF16),
            shape_of((width * split, count, groups // split), F32),
        ],
        scratch_shapes=scratch,
        compiler_params=params,
        name="final",
    )(
        core[None], p, hx, hi, u, qkv, conv, from_e, from_a, skip_sum, both, found, other, short_filter,
        f1, f_all, cz, cy,
    )

    total = summed(sums).transpose(1, 0, 2).reshape(3, SUB, channels)
    grad_short, grad_skip = total[:, :taps], total[0, taps]
    return output[None], grad_p.transpose(1, 0, 2)[None], grad_short, grad_skip


def solution(mesh):
    placed = (P("dp", "ctx", None, None), P(), P(), P(), P(), P("dp", "ctx", None))
    return jax.shard_map(
        local,
        mesh=mesh,
        in_specs=placed,
        out_specs=(P("dp", "ctx", None), P("dp", "ctx", None, None), P(), P()),
        check_vma=False,
    )
```
